32 devices in a mesh: dp: 8 (over z, core), tensor: 4 (over y, x).
Axes of the slice: x: 2, y: 2, z: 4, core: 2. Of those that a mesh axis runs over, the one named last changes fastest.
Arguments:
- tokens: bfloat16 [8192, 2048], P('dp'), may hold values from -6 to 6
- lengths: int32 [64], P('dp'), may hold values from 1 to 64, 2560 in all
- cotangent: bfloat16 [8192, 2048], P('dp'), may hold values from -6 to 6
- pre_gain: float32 [2048], replicated, may hold values from 0.5 to 1.5
- pre_shift: float32 [2048], replicated, may hold values from -1.5 to 1.5
- qkv_weight: bfloat16 [3, 2048, 2048], P(None, None, 'tensor'), may hold values from -0.125 to 0.125
- qkv_bias: float32 [3, 2048], P(None, 'tensor'), may hold values from -1.5 to 1.5
- mix_gain: float32 [2048], P('tensor'), may hold values from 0.5 to 1.5
- mix_shift: float32 [2048], P('tensor'), may hold values from -1.5 to 1.5
- out_weight: bfloat16 [2048, 2048], P('tensor'), may hold values from -0.125 to 0.125
- out_bias: float32 [2048], replicated, may hold values from -1.5 to 1.5
- ffn_gain: float32 [2048], replicated, may hold values from 0.5 to 1.5
- ffn_shift: float32 [2048], replicated, may hold values from -1.5 to 1.5
- up_weight: bfloat16 [2048, 8192], P(None, 'tensor'), may hold values from -0.125 to 0.125
- up_bias: float32 [8192], P('tensor'), may hold values from -2.5 to 2.5
- hid_gain: float32 [8192], P('tensor'), may hold values from 0.5 to 1.5
- hid_shift: float32 [8192], P('tensor'), may hold values from -1.5 to 1.5
- down_weight: bfloat16 [8192, 2048], P('tensor'), may hold values from -0.0625 to 0.0625
- down_bias: float32 [2048], replicated, may hold values from -1.5 to 1.5
Outputs:
- output: bfloat16 [8192, 2048], P('dp')
- tokens_grad: float32 [8192, 2048], P('dp')
- pre_gain_grad: float32 [2048], replicated
- pre_shift_grad: float32 [2048], replicated
- qkv_weight_grad: float32 [3, 2048, 2048], P(None, 'dp', 'tensor')
- qkv_bias_grad: float32 [3, 2048], P(None, 'tensor')
- mix_gain_grad: float32 [2048], P('tensor')
- mix_shift_grad: float32 [2048], P('tensor')
- out_weight_grad: float32 [2048, 2048], P('tensor', 'dp')
- out_bias_grad: float32 [2048], replicated
- ffn_gain_grad: float32 [2048], replicated
- ffn_shift_grad: float32 [2048], replicated
- up_weight_grad: float32 [2048, 8192], P('dp', 'tensor')
- up_bias_grad: float32 [8192], P('tensor')
- hid_gain_grad: float32 [8192], P('tensor')
- hid_shift_grad: float32 [8192], P('tensor')
- down_weight_grad: float32 [8192, 2048], P('tensor', 'dp')
- down_bias_grad: float32 [2048], replicated
The draws below stay inside these ranges and needn't reach their ends.
Inputs may be any that keep to these rules, and one draw needn't show every extreme that they name: Caption length of each pair; the lengths sum to 2560 and the longest is 64.
All inputs are finite; a program needn't handle non-finite values. No bound on the sum of `lengths` on one device may be relied on, other than what follows from the above.
Results may differ from the reference program's by a relative error of at most 0.013.
Values sent between devices are 32-bit elements; how exact they have to be, the bound alone decides.
No kernel may reach another device: no remote copies, remote signals or barrier semaphores. Data moves between devices by JAX's collectives and lax.ppermute only.
A program may use at most 256 MiB of HBM per device.

```python
import functools
import math
import jax
import jax.numpy as jnp
import numpy as np
from jax import lax

D = 2048
HEADS = 32
HD = 64
FF = 8192
SLOT = 128
IMG = 64
SCALE_BASE = 512
CAP = 64
PAIRS = 64
TOKENS = 8192


def levels(own_key, dims, pieces, smallest, high):
    factor_of, own = 1.0, jax.random.fold_in(own_key, 6)
    for axis_at, parts in pieces:
        heights = jnp.exp(jax.random.uniform(jax.random.fold_in(own, axis_at), (parts,), jnp.float32, smallest / len(pieces), high / len(pieces)))
        factor_of = factor_of * jnp.repeat(heights, dims[axis_at] // parts).reshape([-1 if axis == axis_at else 1 for axis in range(len(dims))])
    return factor_of


def split_up(number_of, total, most, slope):
    loads = [(1 << 20) // math.isqrt(rank ** slope) + 1 for rank in range(2, number_of + 1)]
    rest, counts = total - most - (number_of - 1), [1] * (number_of - 1)
    while rest > 0:
        candidates = [i for i in range(number_of - 1) if counts[i] < most]
        pool, budget = sum([loads[i] for i in candidates]), rest
        for i in candidates:
            extra = min(most - counts[i], max(1, budget * loads[i] // pool), rest)
            counts[i] = counts[i] + extra
            rest = rest - extra
    return np.array([most] + counts)


def uneven_parts(stream_key, number_of, total, reach, skew):
    if number_of == 2:
        one = jax.random.randint(stream_key, (), max(1, total - reach), min(reach, total - 1) + 1)
        return jnp.stack([one, total - one])
    tallies = jnp.asarray(split_up(number_of, total, reach, skew), jnp.int32)
    couples = (number_of - 1) // 2
    giver, receiver = tallies[1:1 + 2 * couples:2], tallies[2:2 + 2 * couples:2]
    room = jnp.minimum(giver - 1, reach - receiver)
    moved = jax.random.randint(jax.random.fold_in(stream_key, 1), (couples,), 0, 1 << 20) % (room + 1)
    tallies = tallies.at[1:1 + 2 * couples:2].set(giver - moved).at[2:2 + 2 * couples:2].set(receiver + moved)
    return tallies[jax.random.permutation(jax.random.fold_in(stream_key, 2), number_of)]


def centred(stream_key, extent, deviation, limit, cuts=(), kind=jnp.bfloat16):
    entries = deviation * jax.random.normal(stream_key, extent, jnp.float32)
    if cuts:
        entries = entries * levels(stream_key, extent, cuts, -0.22, 0.18)
    return jnp.clip(entries, -limit, limit).astype(kind)


def setup_inputs(seed: int = 0) -> dict:
    key_of = jax.random.split(jax.random.key(seed), 20)
    tokens = centred(key_of[0], (TOKENS, D), 1.0, 6.0, ((0, 8),))
    lengths = uneven_parts(key_of[1], PAIRS, PAIRS * CAP * 5 // 8, CAP, 1).astype(jnp.int32)
    cotangent = centred(key_of[2], (TOKENS, D), 1.0, 6.0, ((0, 8),))
    pre_gain = jnp.clip(1.0 + 0.1 * jax.random.normal(key_of[3], (D,), jnp.float32), 0.5, 1.5)
    pre_shift = centred(key_of[4], (D,), 0.3, 1.5, (), jnp.float32)
    qkv_weight = centred(key_of[5], (3, D, D), D ** -0.5, 0.125, ((2, 4),))
    qkv_bias = centred(key_of[6], (3, D), 0.3, 1.5, ((1, 4),), jnp.float32)
    mix_gain = jnp.clip(1.0 + 0.1 * jax.random.normal(key_of[7], (D,), jnp.float32), 0.5, 1.5)
    mix_shift = centred(key_of[8], (D,), 0.3, 1.5, ((0, 4),), jnp.float32)
    out_weight = centred(key_of[9], (D, D), D ** -0.5, 0.125, ((0, 4),))
    out_bias = centred(key_of[10], (D,), 0.3, 1.5, (), jnp.float32)
    ffn_gain = jnp.clip(1.0 + 0.1 * jax.random.normal(key_of[11], (D,), jnp.float32), 0.5, 1.5)
    ffn_shift = centred(key_of[12], (D,), 0.3, 1.5, (), jnp.float32)
    up_weight = centred(key_of[13], (D, FF), D ** -0.5, 0.125, ((1, 4),))
    up_bias = centred(key_of[14], (FF,), 0.5, 2.5, ((0, 4),), jnp.float32)
    hid_gain = jnp.clip(1.0 + 0.1 * jax.random.normal(key_of[15], (FF,), jnp.float32), 0.5, 1.5)
    hid_shift = centred(key_of[16], (FF,), 0.3, 1.5, ((0, 4),), jnp.float32)
    down_weight = centred(key_of[17], (FF, D), FF ** -0.5, 0.0625, ((0, 4),))
    down_bias = centred(key_of[18], (D,), 0.3, 1.5, (), jnp.float32)
    return {"tokens": tokens, "lengths": lengths, "cotangent": cotangent, "pre_gain": pre_gain, "pre_shift": pre_shift, "qkv_weight": qkv_weight, "qkv_bias": qkv_bias, "mix_gain": mix_gain, "mix_shift": mix_shift, "out_weight": out_weight, "out_bias": out_bias, "ffn_gain": ffn_gain, "ffn_shift": ffn_shift, "up_weight": up_weight, "up_bias": up_bias, "hid_gain": hid_gain, "hid_shift": hid_shift, "down_weight": down_weight, "down_bias": down_bias}


@jax.custom_vjp
def low(v):
    return lax.optimization_barrier(v.astype(jnp.bfloat16)).astype(jnp.float32)

@jax.custom_vjp
def low_back(v):
    return v

def low_keep(v):
    return (low(v), None)

def low_pass(kept, grad):
    return (grad,)

def back_keep(v):
    return (v, None)

def back_low(kept, grad):
    return (low(grad),)
low.defvjp(low_keep, low_pass)
low_back.defvjp(back_keep, back_low)
eps = 1e-05
highest = lax.Precision.HIGHEST

def normalize(value, gain, shift):
    mean = lax.optimization_barrier(jnp.mean(value, axis=-1, keepdims=True))
    var = lax.optimization_barrier(jnp.mean(value * value, axis=-1, keepdims=True)) - mean * mean
    return (value - mean) * lax.rsqrt(var + eps) * gain + shift

def tables():
    place = jnp.arange(SLOT, dtype=jnp.float32)
    index = jnp.arange(HD // 2, dtype=jnp.float32)
    theta = 10000.0 ** (-2.0 * index / HD)
    angle = place[:, None] * theta[None, :]
    zeta = (2.0 * index + 0.4 * HD) / (1.4 * HD)
    growth = zeta[None, :] ** ((place[:, None] - SLOT // 2) / SCALE_BASE)
    return (jnp.cos(angle), jnp.sin(angle), growth)

def rotate(value, cosine, sine, factor):
    shape = value.shape
    pairs = value.reshape(shape[:-1] + (shape[-1] // 2, 2))
    even = pairs[..., 0]
    odd = pairs[..., 1]
    cos_b = cosine[:, None, :]
    sin_b = sine[:, None, :]
    fac_b = factor[:, None, :]
    new_even = (even * cos_b - odd * sin_b) * fac_b
    new_odd = (odd * cos_b + even * sin_b) * fac_b
    return jnp.stack([new_even, new_odd], axis=-1).reshape(shape)

def attend(block):
    query, key, value, length = block
    scale = 1.0 / math.sqrt(HD)
    scores = jnp.einsum('gqhd,gkhd->ghqk', query, key, precision=highest) * scale
    scores = low_back(scores)
    place = jnp.arange(SLOT, dtype=jnp.int32)
    causal = (place[None, :] <= place[:, None])[None, None]
    valid = place[None, None, None, :] < (IMG + length)[:, None, None, None]
    scores = jnp.where(causal & valid, scores, -1e+30)
    probs = jax.nn.softmax(scores, axis=-1)
    return jnp.einsum('ghqk,gkhd->gqhd', low(probs), value, precision=highest)

def forward(lengths, tokens, pre_gain, pre_shift, qkv_weight, qkv_bias, mix_gain, mix_shift, out_weight, out_bias, ffn_gain, ffn_shift, up_weight, up_bias, hid_gain, hid_shift, down_weight, down_bias):
    cosine, sine, growth = tables()
    first = low(normalize(tokens, pre_gain, pre_shift))
    proj = jnp.einsum('td,cde->cte', first, qkv_weight, precision=highest) + qkv_bias[:, None, :]
    proj = low_back(proj)
    shaped = proj.reshape(3, PAIRS, SLOT, HEADS, HD)
    query = low(rotate(shaped[0], cosine, sine, growth))
    key = low(rotate(shaped[1], cosine, sine, 1.0 / growth))
    value = low(shaped[2])
    group = math.gcd(PAIRS, max(1, 4096 // SLOT))
    count = PAIRS // group

    def split(v):
        return v.reshape((count, group) + v.shape[1:])
    mixed = lax.map(jax.checkpoint(attend), (split(query), split(key), split(value), split(lengths)))
    mixed = low_back(mixed.reshape(TOKENS, D))
    mix_low = low(normalize(mixed, mix_gain, mix_shift))
    branch = low_back(jnp.dot(mix_low, out_weight, precision=highest, preferred_element_type=jnp.float32))
    middle = tokens + branch + out_bias
    second = low(normalize(middle, ffn_gain, ffn_shift))
    hidden = low_back(jnp.dot(second, up_weight, precision=highest, preferred_element_type=jnp.float32) + up_bias)
    active = jax.nn.gelu(hidden, approximate=False)
    hid_low = low(normalize(active, hid_gain, hid_shift))
    result = low_back(jnp.dot(hid_low, down_weight, precision=highest, preferred_element_type=jnp.float32))
    return middle + result + down_bias

def reference(tokens, lengths, cotangent, pre_gain, pre_shift, qkv_weight, qkv_bias, mix_gain, mix_shift, out_weight, out_bias, ffn_gain, ffn_shift, up_weight, up_bias, hid_gain, hid_shift, down_weight, down_bias):
    params = [tokens, pre_gain, pre_shift, qkv_weight, qkv_bias, mix_gain, mix_shift, out_weight, out_bias, ffn_gain, ffn_shift, up_weight, up_bias, hid_gain, hid_shift, down_weight, down_bias]
    params = [p.astype(jnp.float32) for p in params]
    final, pull = jax.vjp(functools.partial(forward, lengths), *params)
    grads = pull(cotangent.astype(jnp.float32))
    return (final.astype(jnp.bfloat16), grads[0], grads[1], grads[2], grads[3], grads[4], grads[5], grads[6], grads[7], grads[8], grads[9], grads[10], grads[11], grads[12], grads[13], grads[14], grads[15], grads[16])
```

```python
import functools
import math

import jax
import jax.numpy as jnp
import numpy as np
from jax import lax
from jax.experimental import pallas as pl
from jax.experimental.pallas import tpu as pltpu
from jax.sharding import PartitionSpec as P

D = 2048
HD = 64
FF = 8192
SLOT = 128
IMG = 64
SCALE_BASE = 512
HALF = D // 2

eps = 1e-05
root_half = 0.7071067811865476
inv_root_two_pi = 0.3989422804014327
masked_score = -1e30
MEGA = 1 << 20

F32 = jnp.float32
BF16 = jnp.bfloat16
NN = (((1,), (0,)), ((), ()))
NT = (((1,), (1,)), ((), ()))
TN = (((0,), (0,)), ((), ()))


def rounded(value):
    return value.astype(BF16)


def mul(left, right, dims=NN):
    return lax.dot_general(left, right, dims, preferred_element_type=F32)


def xpos_tables():
    place = np.arange(SLOT, dtype=np.float64)[:, None]
    lane = np.arange(128)[None, :]
    index = (lane % HD) // 2
    angle = place * 10000.0 ** (-2.0 * index / HD)
    zeta = (2.0 * index + 0.4 * HD) / (1.4 * HD)
    growth = zeta ** ((place - SLOT // 2) / SCALE_BASE)
    even = lane % 2 == 0
    found = []
    for factor in (growth / math.sqrt(HD), 1.0 / growth):
        found += [
            np.cos(angle) * factor,
            np.where(even, -np.sin(angle), 0.0) * factor,
            np.where(even, 0.0, np.sin(angle)) * factor,
        ]
    return jnp.asarray(np.tile(np.stack(found), (1, 2, 1)).astype(np.float32))


def rotate(value, tables, base, sign):
    up = pltpu.roll(value, 127, axis=1)
    down = pltpu.roll(value, 1, axis=1)
    turned = up * tables[base + 1] + down * tables[base + 2]
    return value * tables[base] + turned if sign > 0 else value * tables[base] - turned


def columns_of(parts):
    return jnp.transpose(parts)


def rows_of(columns):
    size = columns[0].shape[0]
    lane = lax.broadcasted_iota(jnp.int32, (size, 128), 1)
    tile = jnp.zeros((size, 128), F32)
    for at, column in enumerate(columns):
        tile = jnp.where(lane == at, column, tile)
    return jnp.transpose(tile)[:8]


def norm_parts(value):
    mean = jnp.mean(value, axis=-1, keepdims=True)
    var = jnp.mean(value * value, axis=-1, keepdims=True) - mean * mean
    inverse = lax.rsqrt(var + eps)
    return (value - mean) * inverse, inverse


def sum_rows(value):
    return jnp.sum(value, axis=0, keepdims=True)


def whole(array, **kw):
    rank = array.ndim
    return (array, array.shape, lambda *at: (0,) * rank)


def run(kernel, grid, ins, outs, scratch=(), prefetch=(), after=(), alias=None, limit=56, name=None):
    prefetch = tuple(prefetch)

    def body(*refs):
        refs = list(refs)
        first = len(prefetch) + len(ins)
        del refs[first : first + len(after)]
        kernel(*refs)

    in_specs = []
    for array, block, where in ins:
        if block is None:
            in_specs.append(pl.BlockSpec(memory_space=pl.ANY))
        elif tuple(block) == tuple(array.shape):
            in_specs.append(pl.BlockSpec(block, where, pipeline_mode=pl.Buffered(1)))
        else:
            in_specs.append(pl.BlockSpec(block, where))
    in_specs += [pl.BlockSpec(memory_space=pl.ANY)] * len(after)
    out_specs = [pl.BlockSpec(block, where) for shape, dtype, block, where in outs]
    out_shape = [jax.ShapeDtypeStruct(shape, dtype) for shape, dtype, block, where in outs]
    return pl.pallas_call(
        body,
        grid_spec=pltpu.PrefetchScalarGridSpec(
            num_scalar_prefetch=len(prefetch),
            grid=grid,
            in_specs=in_specs,
            out_specs=out_specs,
            scratch_shapes=list(scratch),
        ),
        out_shape=out_shape,
        input_output_aliases=alias or {},
        compiler_params=pltpu.CompilerParams(
            dimension_semantics=("arbitrary",) * len(grid), vmem_limit_bytes=limit * MEGA
        ),
        cost_estimate=pl.CostEstimate(flops=1000, bytes_accessed=1000, transcendentals=0),
        name=name,
    )(*prefetch, *[array for array, block, where in ins], *after)


def flip(value, bit, size):
    return lax.ppermute(value, "tensor", [(t, t ^ (1 << bit)) for t in range(size)])


def gather_pieces(own, bits, order):
    pieces = {0: own}
    for bit in order:
        for block in list(pieces):
            pieces[block | 1 << bit] = flip(pieces[block], bit, 1 << bits)
    return [pieces[block] for block in range(1 << bits)]


class Line:
    def __init__(self):
        self.last = None

    def tie(self, value):
        if self.last is None:
            return value
        return lax.optimization_barrier((value, self.last))[0]

    def mark(self, value):
        self.last = value


class Total:
    def __init__(self, line, parts, bits):
        self.line, self.bits = line, bits
        self.orders = [list(range(bits)), list(range(bits))[::-1]]
        self.left = [[bit for bit in range(bits) if bit != order[0]] for order in self.orders]
        self.keep = [parts[0], parts[2]]
        self.got = [flip(parts[1], self.orders[0][0], 1 << bits), flip(parts[3], self.orders[1][0], 1 << bits)]
        self.step = 1

    def advance(self):
        line, size = self.line, 1 << self.bits
        if self.step == self.bits:
            for half in range(2):
                self.keep[half] = line.tie(self.keep[half]) + self.got[half]
                line.mark(self.keep[half])
            return
        picks = []
        for half in range(2):
            left, bit = self.left[half], self.orders[half][self.step]
            keep, got = self.keep[half], self.got[half]
            cube = (2,) * len(left) + keep.shape[1:]
            axis = len(left) - 1 - left.index(bit)
            shape = (keep.shape[0] // 2,) + keep.shape[1:]
            pick = lambda value, at, cube=cube, axis=axis, shape=shape: lax.index_in_dim(
                value.reshape(cube), at, axis, keepdims=False
            ).reshape(shape)
            send = pick(line.tie(keep), 1) + pick(got, 1)
            line.mark(send)
            picks.append((pick, keep, got))
            self.got[half] = flip(send, bit, size)
            left.remove(bit)
        for half in range(2):
            pick, keep, got = picks[half]
            self.keep[half] = pick(line.tie(keep), 0) + pick(got, 0)
            line.mark(self.keep[half])
        self.step += 1

    def pieces(self):
        up, down = self.orders
        return gather_pieces(self.keep[0], self.bits, down), gather_pieces(self.keep[1], self.bits, up)


class Ring:
    def __init__(self, line, first, rest, size):
        self.line, self.rest, self.size = line, rest, size
        self.step = 0
        self.got = self.send(first)

    def send(self, value):
        return lax.ppermute(value, "dp", [(d, (d + 2) % self.size) for d in range(self.size)])

    def advance(self):
        value = self.line.tie(self.rest)[self.step] + self.got
        self.line.mark(value)
        self.step += 1
        if self.step < self.size // 2 - 1:
            self.got = self.send(value)
        return value


def butterfly(value, bits):
    for bit in range(bits):
        value = value + flip(value, bit, 1 << bits)
    return value


def tree_sum(value):
    while value.shape[0] > 1:
        value = value.reshape((value.shape[0] // 2, 2) + value.shape[1:])
        value = value[:, 0] + value[:, 1]
    return value[0]


def combine(pieces, block, blocks):
    level = [pieces[other][:, (block ^ other) * SLOT : (block ^ other) * SLOT + SLOT] for other in range(blocks)]
    while len(level) > 1:
        level = [level[at] + level[at + 1] for at in range(0, len(level), 2)]
    return level[0]


def attention_scores(query, both_keys, length):
    scores = mul(query, both_keys, NT)
    row = lax.broadcasted_iota(jnp.int32, scores.shape, 0)
    place = lax.broadcasted_iota(jnp.int32, scores.shape, 1) % SLOT
    scores = jnp.where((place <= row) & (place < IMG + length), scores, masked_score)
    parts = []
    for at in range(2):
        part = scores[:, at * SLOT : (at + 1) * SLOT]
        expd = jnp.exp(part - jnp.max(part, axis=-1, keepdims=True))
        parts.append(expd / jnp.sum(expd, axis=-1, keepdims=True))
    return parts


def split_heads(value, mask):
    return jnp.concatenate([value * mask[0:1], value * mask[1:2]], axis=0)


def store_parts(refs, value, step, steps, only=None):
    left_keep, left_send, right_keep, right_send = refs
    left_keep[0] = value[:SLOT, :HALF]
    left_send[0] = value[SLOT:, :HALF]

    @pl.when(step < steps // 2)
    def _():
        right_keep[0] = value[:SLOT, HALF:]
        right_keep[1] = value[SLOT:, HALF:]

    @pl.when(step >= steps // 2)
    def _():
        right_send[0] = value[:SLOT, HALF:]
        right_send[1] = value[SLOT:, HALF:]


def part_outs(blocks):
    half = blocks // 2
    steps = blocks // 2
    shape = (half, SLOT, HALF)
    low = max(steps // 2, 1)
    return [
        (shape, F32, (1, SLOT, HALF), lambda s, *_: (s, 0, 0)),
        (shape, F32, (1, SLOT, HALF), lambda s, *_: (s, 0, 0)),
        (shape, F32, (2, SLOT, HALF), lambda s, *_: (jnp.minimum(s, low - 1), 0, 0)),
        (shape, F32, (2, SLOT, HALF), lambda s, *_: (jnp.maximum(s - steps // 2, 0), 0, 0)),
    ]


def front(order, lengths, tokens, gain, shift, weight, bias, tables, mask, mix_gain, uw_rows, out_weight, after=()):
    blocks = order.shape[0]
    steps = blocks // 2
    width = weight.shape[2]
    groups = width // 128
    rows = blocks * SLOT

    def kernel(order_ref, length_ref, x0, x1, g, b, w, wb, tab, msk, mg, uwr, ow, own, first, qkv, mixed, sums, uw, *parts):
        step = pl.program_id(0)

        @pl.when(step == 0)
        def _():
            found = mul(uwr[...], ow[...])
            uw[...] = jnp.concatenate(
                [found[0:1] + found[1:2] + found[2:3], found[3:4] + found[4:5] + found[5:6], found[6:8], jnp.zeros((4, D), F32)],
                axis=0,
            )

        x = jnp.concatenate([x0[0], x1[0]], axis=0)
        own[...] = x
        hat, _ = norm_parts(x.astype(F32))
        one = rounded(hat * g[...] + b[...])
        first[...] = one
        for c in range(3):
            proj = mul(one, w[c]) + wb[c : c + 1]
            for group in range(groups):
                part = proj[:, group * 128 : group * 128 + 128]
                if c < 2:
                    part = rotate(part, tab, 3 * c, 1)
                at = c * width + group * 128
                qkv[:, at : at + 128] = rounded(part)
        for pair in range(2):
            r = slice(pair * SLOT, pair * SLOT + SLOT)
            length = length_ref[order_ref[2 * step + pair]]
            for group in range(groups):
                at = group * 128
                query = qkv[r, at : at + 128]
                keys = split_heads(qkv[r, width + at : width + at + 128], msk)
                values = split_heads(qkv[r, 2 * width + at : 2 * width + at + 128], msk)
                probs = attention_scores(query, keys, length)
                mixed[r, at : at + 128] = mul(rounded(jnp.concatenate(probs, axis=1)), values)
        m = mixed[...]
        total = jnp.sum(m, axis=-1, keepdims=True)
        sums[...] = rows_of([total, jnp.sum(m * m, axis=-1, keepdims=True)])
        middle = total * (1.0 / width)
        partial = mul(rounded((m - middle) * mg[...]), ow[...]) + middle * uw[0:1]
        store_parts(parts, partial, step, steps)

    row2 = lambda s, *_: (s, 0)
    pair_of = lambda offset: lambda s, order_ref, length_ref: (order_ref[2 * s + offset], 0, 0)
    return run(
        kernel,
        (steps,),
        [
            (tokens, (1, SLOT, D), pair_of(0)),
            (tokens, (1, SLOT, D), pair_of(1)),
            whole(gain), whole(shift), whole(weight), whole(bias), whole(tables), whole(mask),
            whole(mix_gain), whole(uw_rows), whole(out_weight),
        ],
        [
            ((rows, D), BF16, (2 * SLOT, D), row2),
            ((rows, D), BF16, (2 * SLOT, D), row2),
            ((rows, 3 * width), BF16, (2 * SLOT, 3 * width), row2),
            ((rows, width), F32, (2 * SLOT, width), row2),
            ((8, rows), F32, (8, 2 * SLOT), lambda s, *_: (0, s)),
            ((8, D), F32, (8, D), lambda s, *_: (0, 0)),
        ]
        + part_outs(blocks),
        prefetch=(order, lengths),
        after=after,
        name="front",
    )


def pieces_in(pieces):
    return [whole(piece) for half in pieces for piece in half]


def load_pieces(refs, total, step, blocks):
    for block in range(blocks):

        @pl.when(step == block)
        def _(block=block):
            total[:, :HALF] = refs[block][0]
            total[:, HALF:] = refs[blocks + block][0]


def middle_norm(own, pieces, sums, uw, out_bias, gain, shift, after=()):
    blocks = len(pieces[0])
    rows = blocks * SLOT

    def kernel(*refs):
        x, parts, stats = refs[0], refs[1 : 1 + 2 * blocks], refs[1 + 2 * blocks : 1 + 3 * blocks]
        uw_ref, bias, g, b, mid, second, stat, total, tot8 = refs[1 + 3 * blocks :]
        step = pl.program_id(0)
        load_pieces(parts, total, step, blocks)
        for block in range(blocks):

            @pl.when(step == block)
            def _(block=block):
                tot8[...] = combine(stats, block, blocks)

        cols = columns_of(tot8[...])
        mean = cols[:, 0:1] * (1.0 / D)
        inverse = lax.rsqrt(cols[:, 1:2] * (1.0 / D) - mean * mean + eps)
        branch = inverse * (total[...] - mean * uw_ref[0:1]) + uw_ref[1:2]
        value = x[...].astype(F32) + branch + bias[...]
        mid[...] = value
        hat, _ = norm_parts(value)
        second[...] = rounded(hat * g[...] + b[...])
        lane = lax.broadcasted_iota(jnp.int32, (SLOT, 128), 1)
        stat[...] = jnp.where(lane == 0, mean, inverse)

    row = lambda k, *_: (k, 0)
    return run(
        kernel,
        (blocks,),
        [(own, (SLOT, D), row)]
        + pieces_in(pieces)
        + [whole(part) for part in sums]
        + [whole(uw), whole(out_bias), whole(gain), whole(shift)],
        [
            ((rows, D), F32, (SLOT, D), row),
            ((rows, D), BF16, (SLOT, D), row),
            ((rows, 128), F32, (SLOT, 128), row),
        ],
        scratch=[pltpu.VMEM((SLOT, D), F32), pltpu.VMEM((8, SLOT), F32)],
        after=after,
        name="middle_norm",
    )


def hidden_back(cot, down_weight, after=()):
    rows, units = cot.shape[0], down_weight.shape[0]
    tile = min(512, units)

    def kernel(c, w, out):
        out[...] = rounded(mul(c[...], w[...], NT))

    return run(
        kernel,
        (units // tile,),
        [whole(cot), (down_weight, (tile, D), lambda j: (j, 0))],
        [((rows, units), BF16, (rows, tile), lambda j: (0, j))],
        after=after,
        name="hidden_back",
    )[0]


def hidden_front(chunk, second, up_weight, up_bias, back, gain, after=()):
    rows, units = second.shape[0], up_weight.shape[1]
    tile = 256
    steps = units // tile

    def kernel(s_ref, w, b, hb, g, act, slp, sums, acc):
        step = pl.program_id(0)
        hidden = mul(s_ref[...], w[...]) + b[...]
        tail = jnp.exp(-0.5 * hidden * hidden)
        t = 1.0 / (1.0 + (0.3275911 * root_half) * jnp.abs(hidden))
        poly = 1.061405429 * t - 1.453152027
        poly = poly * t + 1.421413741
        poly = poly * t - 0.284496736
        poly = poly * t + 0.254829592
        half = 0.5 * poly * t * tail
        phi = jnp.where(hidden >= 0.0, 1.0 - half, half)
        active = hidden * phi
        act[...] = rounded(active)
        slp[...] = rounded(phi + hidden * (inv_root_two_pi * tail))
        scaled = hb[...].astype(F32) * g[...]
        for at, value in enumerate((active, active * active, scaled, scaled * active)):
            part = value[:, :128] + value[:, 128:]

            @pl.when(step == 0)
            def _():
                acc[at] = part

            @pl.when(step > 0)
            def _():
                acc[at] += part

        @pl.when(step == steps - 1)
        def _():
            for block in range(rows // SLOT):
                r = slice(block * SLOT, block * SLOT + SLOT)
                sums[:, r] = rows_of([jnp.sum(acc[at, r], axis=-1, keepdims=True) for at in range(4)])

    return run(
        kernel,
        (steps,),
        [
            whole(second),
            (up_weight, (D, tile), lambda j: (0, j)),
            (up_bias, (1, tile), lambda j: (0, j)),
            (back, (rows, tile), lambda j: (chunk, j)),
            (gain, (1, tile), lambda j: (0, j)),
        ],
        [
            ((rows, units), BF16, (rows, tile), lambda j: (0, j)),
            ((rows, units), BF16, (rows, tile), lambda j: (0, j)),
            ((8, rows), F32, (8, rows), lambda j: (0, 0)),
        ],
        scratch=[pltpu.VMEM((4, rows, 128), F32)],
        after=after,
        name="hidden_front",
    )


def hidden_grad(chunk, active, slope, back, sums, gain, shift, up_weight, after=()):
    blocks = len(sums)
    rows, units = active.shape
    tile = 256
    steps = D // tile
    half = steps // 2

    def kernel(act, slp, hb, *refs):
        stats = refs[:blocks]
        g, b, w, low, grad, vecs, left_keep, left_send, right_keep, right_send, acc = refs[blocks:]
        step = pl.program_id(0)

        @pl.when(step == 0)
        def _():
            for block in range(blocks):
                r = slice(block * SLOT, block * SLOT + SLOT)
                cols = columns_of(combine(stats, block, blocks)) * (1.0 / FF)
                mean = cols[:, 0:1]
                inverse = lax.rsqrt(cols[:, 1:2] - mean * mean + eps)
                one = cols[:, 2:3]
                two = inverse * (cols[:, 3:4] - mean * one)
                for at in range(0, units, 512):
                    c = slice(at, at + 512)
                    hat = (act[r, c].astype(F32) - mean) * inverse
                    low[r, c] = rounded(hat * g[:, c] + b[:, c])
                    raw = hb[r, c].astype(F32)
                    grown = rounded(inverse * (raw * g[:, c] - one - hat * two) * slp[r, c].astype(F32))
                    grad[r, c] = grown
                    found = [sum_rows(raw * hat), sum_rows(raw), sum_rows(grown.astype(F32))]
                    for i, value in enumerate(found):
                        if block == 0:
                            vecs[i : i + 1, c] = value
                        else:
                            vecs[i : i + 1, c] += value

        value = mul(grad[...], w[...], NT)

        @pl.when(step < half)
        def _():
            for block in range(blocks):
                r = slice(block * SLOT, block * SLOT + SLOT)
                (left_send if block & 1 else left_keep)[block // 2] = value[r]

        @pl.when(step >= half)
        def _():
            for block in range(blocks):
                r = slice(block * SLOT, block * SLOT + SLOT)
                (right_send if block >= blocks // 2 else right_keep)[block % (blocks // 2)] = value[r]

    shape = (blocks // 2, SLOT, HALF)
    block_shape = (blocks // 2, SLOT, tile)
    lefts = lambda j: (0, 0, jnp.minimum(j, half - 1))
    rights = lambda j: (0, 0, jnp.maximum(j - half, 0))
    fixed = lambda j: (0, 0)
    return run(
        kernel,
        (steps,),
        [whole(active), whole(slope), (back, (rows, units), lambda j: (chunk, 0))]
        + [whole(part) for part in sums]
        + [whole(gain), whole(shift), (up_weight, (tile, units), lambda j: (j, 0))],
        [
            ((rows, units), BF16, (rows, units), fixed),
            ((rows, units), BF16, (rows, units), fixed),
            ((8, units), F32, (8, units), fixed),
            (shape, F32, block_shape, lefts),
            (shape, F32, block_shape, lefts),
            (shape, F32, block_shape, rights),
            (shape, F32, block_shape, rights),
        ],
        scratch=[pltpu.VMEM((8, 128), F32)],
        after=after,
        name="hidden_grad",
    )


def result_part(order, lows, down_weight, after=()):
    blocks = order.shape[0]
    units = down_weight.shape[0]

    def kernel(order_ref, low, w, out):
        out[0] = mul(low[...], w[...])

    return run(
        kernel,
        (blocks,),
        [(lows, (SLOT, units), lambda k, *_: (k, 0)), whole(down_weight)],
        [((blocks, SLOT, D), F32, (1, SLOT, D), lambda k, o: (o[k], 0, 0))],
        prefetch=(order,),
        after=after,
        name="result_part",
    )[0]


def middle_back(own, cot, pieces, middle, stat, uw, out_bias, gain, after=()):
    blocks = len(pieces[0])
    rows = blocks * SLOT

    def kernel(*refs):
        x, c, parts = refs[0], refs[1], refs[2 : 2 + 2 * blocks]
        mid, st, uw_ref, bias, g, grad, low, stat2, vecs, total = refs[2 + 2 * blocks :]
        load_pieces(parts, total, pl.program_id(0), blocks)
        value = mid[...]
        hat, inverse = norm_parts(value)
        sec = total[...]
        scaled = sec * g[...]
        up = c[...].astype(F32)
        out = up + inverse * (
            scaled
            - jnp.mean(scaled, axis=-1, keepdims=True)
            - hat * jnp.mean(scaled * hat, axis=-1, keepdims=True)
        )
        grad[...] = out
        lowered = rounded(out)
        low[...] = lowered
        low32 = lowered.astype(F32)
        one = jnp.mean(low32 * uw_ref[0:1], axis=-1, keepdims=True)
        moved = value - x[...].astype(F32) - bias[...] - uw_ref[1:2]
        two = jnp.mean(low32 * moved, axis=-1, keepdims=True)
        lane = lax.broadcasted_iota(jnp.int32, (SLOT, 128), 1)
        stat2[...] = jnp.where(lane == 2, one, jnp.where(lane == 3, two, st[...]))
        vecs[0, 0:1] = sum_rows(sec * hat)
        vecs[0, 1:2] = sum_rows(sec)
        vecs[0, 2:3] = sum_rows(out)
        vecs[0, 3:4] = sum_rows(up)

    row = lambda k, *_: (k, 0)
    return run(
        kernel,
        (blocks,),
        [(own, (SLOT, D), row), (cot, (SLOT, D), row)]
        + pieces_in(pieces)
        + [(middle, (SLOT, D), row), (stat, (SLOT, 128), row), whole(uw), whole(out_bias), whole(gain)],
        [
            ((rows, D), F32, (SLOT, D), row),
            ((rows, D), BF16, (SLOT, D), row),
            ((rows, 128), F32, (SLOT, 128), row),
            ((blocks, 8, D), F32, (1, 8, D), lambda k, *_: (k, 0, 0)),
        ],
        scratch=[pltpu.VMEM((SLOT, D), F32)],
        after=after,
        name="middle_back",
    )


def attention_back(order, lengths, low, stat, mixed, qkv, own, mix_gain, mix_shift, out_weight, weight, tables, mask, after=()):
    blocks = order.shape[0]
    steps = blocks // 2
    width = out_weight.shape[0]
    groups = width // 128
    rows = blocks * SLOT

    def kernel(
        order_ref, length_ref, low_ref, st, mx, qkv_ref, x, mg, ms, ow, w, tab, msk,
        mix_low, dproj, vecs, wide, left_keep, left_send, right_keep, right_send, dmixed,
    ):
        step = pl.program_id(0)
        mean, inverse, one, two = (st[:, at : at + 1] for at in range(4))
        back = mul(low_ref[...], ow[...], NT)
        hat = (mx[...] - mean) * inverse
        mix_low[...] = rounded(hat * mg[...] + ms[...])
        dmixed[...] = rounded(inverse * (back * mg[...] - one - hat * two))
        vecs[0, 0:1, :width] = sum_rows(back * hat)
        vecs[0, 1:2, :width] = sum_rows(back)
        first_half = lax.broadcasted_iota(jnp.int32, (SLOT, 128), 1) < HD
        for pair in range(2):
            r = slice(pair * SLOT, pair * SLOT + SLOT)
            length = length_ref[order_ref[2 * step + pair]]
            for group in range(groups):
                at = group * 128
                query = qkv_ref[r, at : at + 128]
                keys = split_heads(qkv_ref[r, width + at : width + at + 128], msk)
                values = split_heads(qkv_ref[r, 2 * width + at : 2 * width + at + 128], msk)
                grad = dmixed[r, at : at + 128]
                probs = attention_scores(query, keys, length)
                dprobs = mul(grad, values, NT)
                dscores = []
                for i in range(2):
                    dp = dprobs[:, i * SLOT : (i + 1) * SLOT]
                    carried = jnp.sum(probs[i] * dp, axis=-1, keepdims=True)
                    dscores.append(rounded(probs[i] * (dp - carried)))
                dscores = jnp.concatenate(dscores, axis=1)
                dquery = mul(dscores, keys)
                dkey = mul(dscores, query, TN)
                dvalue = mul(rounded(jnp.concatenate(probs, axis=1)), grad, TN)
                dkey = jnp.where(first_half, dkey[:SLOT], dkey[SLOT:])
                dvalue = jnp.where(first_half, dvalue[:SLOT], dvalue[SLOT:])
                tabs = [tab[i, :SLOT] for i in range(6)]
                dproj[r, at : at + 128] = rounded(rotate(dquery, tabs, 0, -1))
                dproj[r, width + at : width + at + 128] = rounded(rotate(dkey, tabs, 3, -1))
                dproj[r, 2 * width + at : 2 * width + at + 128] = rounded(dvalue)
        vecs[0, 2:3] = sum_rows(dproj[...].astype(F32))
        partial = mul(dproj[:, :width], w[0], NT)
        for c in (1, 2):
            partial += mul(dproj[:, c * width : (c + 1) * width], w[c], NT)
        pre_hat, _ = norm_parts(x[...].astype(F32))
        grown = partial * pre_hat
        wide[0, 0:1] = sum_rows(grown[:SLOT]) + sum_rows(grown[SLOT:])
        wide[0, 1:2] = sum_rows(partial[:SLOT]) + sum_rows(partial[SLOT:])
        store_parts((left_keep, left_send, right_keep, right_send), partial, step, steps)

    row2 = lambda s, *_: (s, 0)
    return run(
        kernel,
        (steps,),
        [
            (low, (2 * SLOT, D), row2),
            (stat, (2 * SLOT, 128), row2),
            (mixed, (2 * SLOT, width), row2),
            (qkv, (2 * SLOT, 3 * width), row2),
            (own, (2 * SLOT, D), row2),
            whole(mix_gain), whole(mix_shift), whole(out_weight), whole(weight), whole(tables), whole(mask),
        ],
        [
            ((rows, width), BF16, (2 * SLOT, width), row2),
            ((rows, 3 * width), BF16, (2 * SLOT, 3 * width), row2),
            ((steps, 8, 3 * width), F32, (1, 8, 3 * width), lambda s, *_: (s, 0, 0)),
            ((steps, 8, D), F32, (1, 8, D), lambda s, *_: (s, 0, 0)),
        ]
        + part_outs(blocks),
        scratch=[pltpu.VMEM((2 * SLOT, width), BF16)],
        prefetch=(order, lengths),
        after=after,
        name="attention_back",
    )


def tokens_back(order, own, grad, pieces, gain, before, pairs, after=()):
    blocks = len(pieces[0])

    def kernel(order_ref, x, gr, *refs):
        parts = refs[: 2 * blocks]
        g = refs[2 * blocks]
        out, total = refs[-2:]
        load_pieces(parts, total, pl.program_id(0), blocks)
        hat, inverse = norm_parts(x[...].astype(F32))
        scaled = total[...] * g[...]
        out[0] = gr[...] + inverse * (
            scaled
            - jnp.mean(scaled, axis=-1, keepdims=True)
            - hat * jnp.mean(scaled * hat, axis=-1, keepdims=True)
        )

    row = lambda k, *_: (k, 0)
    ins = [(own, (SLOT, D), row), (grad, (SLOT, D), row)] + pieces_in(pieces) + [whole(gain)]
    alias = None
    if before is not None:
        alias = {1 + len(ins): 0}
        ins = ins + [(before, None, None)]
    return run(
        kernel,
        (blocks,),
        ins,
        [((pairs, SLOT, D), F32, (1, SLOT, D), lambda k, o: (o[k], 0, 0))],
        scratch=[pltpu.VMEM((SLOT, D), F32)],
        prefetch=(order,),
        after=after,
        alias=alias,
        name="tokens_back",
    )[0]


def output_of(order, middle, result, bias, before, after=()):
    blocks = order.shape[0]

    def kernel(order_ref, mid, res, b, *refs):
        out = refs[-1]
        out[0] = rounded(mid[...] + res[0] + b[...])

    ins = [
        (middle, (SLOT, D), lambda k, *_: (k, 0)),
        (result, (1, SLOT, D), lambda k, o: (o[k], 0, 0)),
        whole(bias),
    ]
    alias = None
    if before is not None:
        alias = {1 + len(ins): 0}
        ins = ins + [(before, None, None)]
    return run(
        kernel,
        (blocks,),
        ins,
        [(result.shape, BF16, (1, SLOT, D), lambda k, o: (o[k], 0, 0))],
        prefetch=(order,),
        after=after,
        alias=alias,
        name="output",
    )[0]


def weight_grad(ids, lefts, rights, left_blocked, got=None):
    count = ids.shape[0]
    rows = lefts[0].shape[0]
    many = len(lefts)
    wide, tall = lefts[0].shape[1], rights[0].shape[1]
    block = D // (2 * count)
    shape = (block, tall) if left_blocked else (wide, block)

    def kernel(ids_ref, *refs):
        left, right = refs[:many], refs[many : 2 * many]
        outs = refs[2 * many + (got is not None) :]
        value = mul(left[0][...], right[0][...], TN)
        for at in range(1, many):
            value += mul(left[at][...], right[at][...], TN)
        if got is None:
            outs[0][0] = value
            return
        value += refs[2 * many][0]
        step = pl.program_id(0)

        @pl.when(step == 0)
        def _():
            outs[0][...] = value

        @pl.when(step > 0)
        def _():
            outs[1][0] = value

    fixed = lambda i, *_: (0, 0)
    moving = lambda i, ids_ref: (0, ids_ref[i])
    lead = lambda i, *_: (i, 0, 0)
    ins = [(left, (rows, block), moving) if left_blocked else (left, (rows, wide), fixed) for left in lefts]
    ins += [(right, (rows, tall), fixed) if left_blocked else (right, (rows, block), moving) for right in rights]
    if got is None:
        outs = [((count,) + shape, F32, (1,) + shape, lead)]
    else:
        ins += [(got, (1,) + shape, lead)]
        outs = [
            (shape, F32, shape, fixed),
            ((count - 1,) + shape, F32, (1,) + shape, lambda i, *_: (jnp.maximum(i - 1, 0), 0, 0)),
        ]
    return run(kernel, (count,), ins, outs, prefetch=(ids,), name="weight_grad")


def split_rows(value):
    found = []
    for _ in range(3):
        part = lax.reduce_precision(value, 8, 7)
        found.append(part.astype(BF16))
        value = value - part
    return found


def body(
    tokens,
    lengths,
    cotangent,
    pre_gain,
    pre_shift,
    qkv_weight,
    qkv_bias,
    mix_gain,
    mix_shift,
    out_weight,
    out_bias,
    ffn_gain,
    ffn_shift,
    up_weight,
    up_bias,
    hid_gain,
    hid_shift,
    down_weight,
    down_bias,
):
    pairs = lengths.shape[0]
    blocks = lax.axis_size("tensor")
    bits = blocks.bit_length() - 1
    chunks = pairs // blocks
    width = qkv_weight.shape[2]
    mine = lax.axis_index("tensor").astype(jnp.int32)
    orders = [jnp.arange(c * blocks, (c + 1) * blocks, dtype=jnp.int32) ^ mine for c in range(chunks)]
    tokens3 = tokens.reshape(pairs, SLOT, D)
    row = lambda v: v.reshape(1, -1)
    pre_gain, pre_shift, mix_gain, mix_shift = map(row, (pre_gain, pre_shift, mix_gain, mix_shift))
    out_bias, ffn_gain, ffn_shift, up_bias = map(row, (out_bias, ffn_gain, ffn_shift, up_bias))
    hid_gain, hid_shift, down_bias = map(row, (hid_gain, hid_shift, down_bias))
    tables = xpos_tables()
    lane = np.arange(128)[None, :] < HD
    mask = jnp.asarray(np.concatenate([lane, ~lane], 0).astype(np.float32)).astype(BF16)
    zero = jnp.zeros((2, width), BF16)
    uw_rows = jnp.concatenate(split_rows(mix_gain) + split_rows(mix_shift) + [zero], 0)

    line = Line()
    dp_size = lax.axis_size("dp")
    place = lax.axis_index("dp").astype(jnp.int32)
    count = dp_size // 2
    around = lax.rem(place // 2 + count - 1 - jnp.arange(count, dtype=jnp.int32), count)
    mine_ids, other_ids = 2 * around + lax.rem(place, 2), 2 * around + 1 - lax.rem(place, 2)

    def send_half(lefts, rights, left_blocked):
        sent = weight_grad(other_ids, [line.tie(lefts[0])] + lefts[1:], rights, left_blocked)[0]
        line.mark(sent)
        return lax.ppermute(sent, "dp", [(d, d ^ 1) for d in range(dp_size)])

    def keep_half(lefts, rights, left_blocked, got):
        first, rest = weight_grad(mine_ids, [line.tie(lefts[0])] + lefts[1:], rights, left_blocked, got)
        line.mark(rest)
        return Ring(line, first, rest, dp_size)

    ones, twos, threes = [], [], []
    up_order = list(range(bits))
    for c in range(chunks):
        found = front(
            orders[c], lengths, line.tie(tokens3), pre_gain, pre_shift, qkv_weight, qkv_bias, tables, mask, mix_gain, uw_rows,
            out_weight,
        )
        own, first, qkv, mixed, sums, uw = found[:6]
        line.mark(sums)
        if c == 0:
            uw_total = butterfly(uw, bits)
        one = dict(own=own, first=first, qkv=qkv, mixed=mixed, parts=found[6:])
        one["sums"] = gather_pieces(sums, bits, up_order)
        if c == 0:
            one["branch"] = Total(line, one["parts"], bits)
        ones.append(one)
    cot3 = cotangent.reshape(pairs, SLOT, D)
    cot_own = line.tie(cot3)[jnp.concatenate(orders)].reshape(chunks, -1, D)
    cots = [cot_own[c] for c in range(chunks)]
    back = hidden_back(cot_own.reshape(-1, D), down_weight)
    line.mark(back)
    for c in range(chunks):
        one = ones[c]
        if c > 0:
            one["branch"] = Total(line, [line.tie(part) for part in one["parts"]], bits)
        for step in range(bits):
            one["branch"].advance()
        one["pieces"] = one["branch"].pieces()

    for c in range(chunks):
        one = ones[c]
        mid, second, stat = middle_norm(
            line.tie(one["own"]), one["pieces"], one["sums"], uw_total, out_bias, ffn_gain, ffn_shift
        )
        line.mark(stat)
        active, slope, sums = hidden_front(c, line.tie(second), up_weight, up_bias, back, hid_gain)
        line.mark(sums)
        twos.append(
            dict(middle=mid, second=second, stat=stat, active=active, slope=slope, sums=gather_pieces(sums, bits, up_order))
        )
    for c in range(chunks):
        two = twos[c]
        found = hidden_grad(c, line.tie(two["active"]), two["slope"], back, two["sums"], hid_gain, hid_shift, up_weight)
        line.mark(found[2])
        two.update(low=found[0], grad=found[1], vecs=found[2], parts=found[3:])
        two["total"] = Total(line, two["parts"], bits)
    every = lambda items, name: [item[name] for item in items]
    down_args = (every(twos, "low"), cots, False)
    up_args = (every(twos, "second"), every(twos, "grad"), True)
    down_got = send_half(*down_args)
    up_got = send_half(*up_args)
    twos[0]["total"].advance()
    down_ring = keep_half(*down_args, down_got)
    up_ring = keep_half(*up_args, up_got)
    for step in range(1, bits):
        twos[0]["total"].advance()
    twos[0]["pieces"] = twos[0]["total"].pieces()
    for c in range(1, chunks):
        for step in range(bits):
            twos[c]["total"].advance()
        twos[c]["pieces"] = twos[c]["total"].pieces()
    result = result_part(jnp.concatenate(orders), line.tie(jnp.concatenate(every(twos, "low"), 0)), down_weight)
    line.mark(result)
    result = lax.psum(result, "tensor")

    for c in range(chunks):
        one, two = ones[c], twos[c]
        grad, low, stat2, vecs = middle_back(
            line.tie(one["own"]), cots[c], two["pieces"], two["middle"], two["stat"], uw_total, out_bias, ffn_gain
        )
        line.mark(stat2)
        found = attention_back(
            orders[c], lengths, line.tie(low), stat2, one["mixed"], one["qkv"], one["own"], mix_gain, mix_shift, out_weight,
            qkv_weight, tables, mask,
        )
        line.mark(found[2])
        three = dict(grad=grad, low=low, vecs=tree_sum(vecs), mix_low=found[0], dproj=found[1])
        three["narrow"] = tree_sum(found[2])
        three["wide"] = tree_sum(found[3])
        three["total"] = Total(line, found[4:], bits)
        threes.append(three)
        if c == 0:
            down_ring.advance()
            up_ring.advance()

    out_args = (every(threes, "mix_low"), every(threes, "low"), False)
    qkv_args = (every(ones, "first"), every(threes, "dproj"), True)
    out_got = send_half(*out_args)
    threes[0]["total"].advance()
    qkv_got = send_half(*qkv_args)
    out_ring = keep_half(*out_args, out_got)
    for step in range(1, bits):
        threes[0]["total"].advance()
    threes[0]["pieces"] = threes[0]["total"].pieces()
    qkv_ring = keep_half(*qkv_args, qkv_got)
    for c in range(1, chunks):
        threes[c]["total"].advance()

    add = lambda items, name, size: functools.reduce(jnp.add, [item[name] for item in items])[:size]
    hid_vecs, mid_vecs, narrow = add(twos, "vecs", 3), add(threes, "vecs", 4), add(threes, "narrow", 3)
    wide = butterfly(line.tie(add(threes, "wide", 2)), bits)
    line.mark(wide)
    pad = lambda v: jnp.pad(v, ((0, 0), (0, D - v.shape[1])))
    vecs = jnp.concatenate([pad(hid_vecs), mid_vecs, pad(narrow), wide], 0)
    for bit in range(dp_size.bit_length() - 1):
        vecs = vecs + lax.ppermute(vecs, "dp", [(d, d ^ (1 << bit)) for d in range(dp_size)])
    hid_vecs, mid_vecs, narrow, wide = vecs[:3], vecs[3:7], vecs[7:10], vecs[10:12]
    for c in range(1, chunks):
        for step in range(1, bits):
            threes[c]["total"].advance()
        threes[c]["pieces"] = threes[c]["total"].pieces()
    for step in range(1, count - 1):
        down_part, up_part = down_ring.advance(), up_ring.advance()
        if step == 1:
            out_ring.advance()
            qkv_ring.advance()
    tokens_grad, output = None, None
    for c in range(chunks):
        tokens_grad = tokens_back(
            orders[c], line.tie(ones[c]["own"]), threes[c]["grad"], threes[c]["pieces"], pre_gain, tokens_grad, pairs
        )
        line.mark(tokens_grad)
        output = output_of(orders[c], line.tie(twos[c]["middle"]), result, down_bias, output)
        line.mark(output)
    for step in range(1, count - 1):
        out_part, qkv_part = out_ring.advance(), qkv_ring.advance()
    qkv_part = jnp.swapaxes(qkv_part.reshape(-1, 3, width), 0, 1)
    units = hid_gain.shape[1]
    return (
        output.reshape(-1, D),
        tokens_grad.reshape(-1, D),
        wide[0],
        wide[1],
        qkv_part,
        narrow[2, : 3 * width].reshape(3, width),
        narrow[0, :width],
        narrow[1, :width],
        out_part,
        mid_vecs[2],
        mid_vecs[0],
        mid_vecs[1],
        up_part,
        hid_vecs[2, :units],
        hid_vecs[0, :units],
        hid_vecs[1, :units],
        down_part,
        mid_vecs[3],
    )


def solution(mesh):
    in_specs = (
        P("dp", None),
        P("dp"),
        P("dp", None),
        P(),
        P(),
        P(None, None, "tensor"),
        P(None, "tensor"),
        P("tensor"),
        P("tensor"),
        P("tensor", None),
        P(),
        P(),
        P(),
        P(None, "tensor"),
        P("tensor"),
        P("tensor"),
        P("tensor"),
        P("tensor", None),
        P(),
    )
    out_specs = (
        P("dp", None),
        P("dp", None),
        P(),
        P(),
        P(None, "dp", "tensor"),
        P(None, "tensor"),
        P("tensor"),
        P("tensor"),
        P("tensor", "dp"),
        P(),
        P(),
        P(),
        P("dp", "tensor"),
        P("tensor"),
        P("tensor"),
        P("tensor"),
        P("tensor", "dp"),
        P(),
    )
    return jax.shard_map(body, mesh=mesh, in_specs=in_specs, out_specs=out_specs, check_vma=False)
```

```python
import functools
import math

import jax
import jax.numpy as jnp
import numpy as np
from jax import lax
from jax.experimental import pallas as pl
from jax.experimental.pallas import tpu as pltpu
from jax.sharding import PartitionSpec as P

D = 2048
HD = 64
FF = 8192
SLOT = 128
IMG = 64
SCALE_BASE = 512
HALF = D // 2

eps = 1e-05
root_half = 0.7071067811865476
inv_root_two_pi = 0.3989422804014327
masked_score = -1e30
MEGA = 1 << 20

COST = {
    "front": 15.6,
    "middle_norm": 7.5,
    "hidden_back": 400.0,
    "hidden_front": 14.7,
    "hidden_mid": 6.0,
    "hidden_grad": 7.0,
    "full_grad": 15.0,
    "attention_grads": 12.0,
    "result_part": 400.0,
    "middle_back": 11.0,
    "attention_back": 21.7,
    "tokens_back": 8.5,
    "output": 6.0,
}
WORK = 5.5e+07

F32 = jnp.float32
BF16 = jnp.bfloat16
NN = (((1,), (0,)), ((), ()))
NT = (((1,), (1,)), ((), ()))
TN = (((0,), (0,)), ((), ()))


def rounded(value):
    return value.astype(BF16)


def mul(left, right, dims=NN):
    return lax.dot_general(left, right, dims, preferred_element_type=F32)


def xpos_tables():
    place = np.arange(SLOT, dtype=np.float64)[:, None]
    lane = np.arange(128)[None, :]
    index = (lane % HD) // 2
    angle = place * 10000.0 ** (-2.0 * index / HD)
    zeta = (2.0 * index + 0.4 * HD) / (1.4 * HD)
    growth = zeta ** ((place - SLOT // 2) / SCALE_BASE)
    even = lane % 2 == 0
    found = []
    for factor in (growth / math.sqrt(HD), 1.0 / growth):
        found += [
            np.cos(angle) * factor,
            np.where(even, -np.sin(angle), 0.0) * factor,
            np.where(even, 0.0, np.sin(angle)) * factor,
        ]
    return jnp.asarray(np.tile(np.stack(found), (1, 2, 1)).astype(np.float32))


def rotate(value, tables, base, sign):
    up = pltpu.roll(value, 127, axis=1)
    down = pltpu.roll(value, 1, axis=1)
    turned = up * tables[base + 1] + down * tables[base + 2]
    return value * tables[base] + turned if sign > 0 else value * tables[base] - turned


def columns_of(parts):
    return jnp.transpose(parts)


def rows_of(columns):
    size = columns[0].shape[0]
    lane = lax.broadcasted_iota(jnp.int32, (size, 128), 1)
    tile = jnp.zeros((size, 128), F32)
    for at, column in enumerate(columns):
        tile = jnp.where(lane == at, column, tile)
    return jnp.transpose(tile)[:8]


def norm_parts(value):
    mean = jnp.mean(value, axis=-1, keepdims=True)
    var = jnp.mean(value * value, axis=-1, keepdims=True) - mean * mean
    inverse = lax.rsqrt(var + eps)
    return (value - mean) * inverse, inverse


def sum_rows(value):
    return jnp.sum(value, axis=0, keepdims=True)


def whole(array, **kw):
    rank = array.ndim
    return (array, array.shape, lambda *at: (0,) * rank)


def run(kernel, grid, ins, outs, scratch=(), prefetch=(), after=(), alias=None, limit=56, name=None):
    prefetch = tuple(prefetch)

    def body(*refs):
        refs = list(refs)
        first = len(prefetch) + len(ins)
        del refs[first : first + len(after)]
        kernel(*refs)

    in_specs = []
    for array, block, where in ins:
        if block is None:
            in_specs.append(pl.BlockSpec(memory_space=pl.ANY))
        elif tuple(block) == tuple(array.shape):
            in_specs.append(pl.BlockSpec(block, where, pipeline_mode=pl.Buffered(1)))
        else:
            in_specs.append(pl.BlockSpec(block, where))
    in_specs += [pl.BlockSpec(memory_space=pl.ANY)] * len(after)
    out_specs = [pl.BlockSpec(block, where) for shape, dtype, block, where in outs]
    out_shape = [jax.ShapeDtypeStruct(shape, dtype) for shape, dtype, block, where in outs]
    return pl.pallas_call(
        body,
        grid_spec=pltpu.PrefetchScalarGridSpec(
            num_scalar_prefetch=len(prefetch),
            grid=grid,
            in_specs=in_specs,
            out_specs=out_specs,
            scratch_shapes=list(scratch),
        ),
        out_shape=out_shape,
        input_output_aliases=alias or {},
        compiler_params=pltpu.CompilerParams(
            dimension_semantics=("arbitrary",) * len(grid), vmem_limit_bytes=limit * MEGA
        ),
        cost_estimate=pl.CostEstimate(flops=int(COST[name] * WORK), bytes_accessed=1000, transcendentals=0),
        name=name,
    )(*prefetch, *[array for array, block, where in ins], *after)


def flip(value, bit, size):
    return lax.ppermute(value, "tensor", [(t, t ^ (1 << bit)) for t in range(size)])


def all_pieces(own, bits):
    size = 1 << bits
    return [own] + [lax.ppermute(own, "tensor", [(t, t ^ k) for t in range(size)]) for k in range(1, size)]


class Line:
    def __init__(self):
        self.last = None

    def tie(self, value):
        if self.last is None:
            return value
        return lax.optimization_barrier((value,) + self.last)[0]

    def mark(self, *values):
        self.last = values


class Total:
    def __init__(self, line, parts, bits):
        self.line, self.bits = line, bits
        self.orders = [list(range(bits)), list(range(bits))[::-1]]
        self.left = [[bit for bit in range(bits) if bit != order[0]] for order in self.orders]
        self.keep = [parts[0], parts[2]]
        self.got = [flip(parts[1], self.orders[0][0], 1 << bits), flip(parts[3], self.orders[1][0], 1 << bits)]
        self.step = 1

    def advance(self):
        line, size = self.line, 1 << self.bits
        if self.step == self.bits:
            for half in range(2):
                self.keep[half] = line.tie(self.keep[half]) + self.got[half]
                line.mark(self.keep[half])
            return
        picks = []
        for half in range(2):
            left, bit = self.left[half], self.orders[half][self.step]
            keep, got = self.keep[half], self.got[half]
            cube = (2,) * len(left) + keep.shape[1:]
            axis = len(left) - 1 - left.index(bit)
            shape = (keep.shape[0] // 2,) + keep.shape[1:]
            pick = lambda value, at, cube=cube, axis=axis, shape=shape: lax.index_in_dim(
                value.reshape(cube), at, axis, keepdims=False
            ).reshape(shape)
            send = pick(line.tie(keep), 1) + pick(got, 1)
            line.mark(send)
            picks.append((pick, keep, got))
            self.got[half] = flip(send, bit, size)
            left.remove(bit)
        for half in range(2):
            pick, keep, got = picks[half]
            self.keep[half] = pick(line.tie(keep), 0) + pick(got, 0)
            line.mark(self.keep[half])
        self.step += 1

    def gather(self):
        size = 1 << self.bits
        if self.step == self.bits:
            self.held = [[0], [0]]
            self.step += 1
        else:
            for half in range(2):
                self.keep[half] = jnp.concatenate([self.line.tie(self.keep[half]), self.got[half]], 0)
                self.line.mark(self.keep[half])
                self.held[half] = self.held[half] + [block | self.last[half] for block in self.held[half]]
        self.last = [1 << self.orders[half].pop() for half in range(2)]
        self.got = [flip(self.keep[half], self.last[half].bit_length() - 1, size) for half in range(2)]

    def pieces(self):
        arrays, where = [], []
        for half in range(2):
            arrays += [self.keep[half], self.got[half]]
            found = {block: (2 * half, at) for at, block in enumerate(self.held[half])}
            found.update({block | self.last[half]: (2 * half + 1, at) for at, block in enumerate(self.held[half])})
            where.append(found)
        return arrays, where


class Ring:
    def __init__(self, line, first, rest, size):
        self.line, self.rest, self.size = line, rest, size
        self.step = 0
        self.got = self.send(first)

    def send(self, value):
        return lax.ppermute(value, "dp", [(d, (d + 2) % self.size) for d in range(self.size)])

    def advance(self):
        value = self.line.tie(self.rest)[self.step] + self.got
        self.line.mark(value)
        self.step += 1
        if self.step < self.size // 2 - 1:
            self.got = self.send(value)
        return value


def butterfly(value, bits):
    for bit in range(bits):
        value = value + flip(value, bit, 1 << bits)
    return value


def tree_sum(value):
    while value.shape[0] > 1:
        value = value.reshape((value.shape[0] // 2, 2) + value.shape[1:])
        value = value[:, 0] + value[:, 1]
    return value[0]


class Small:
    def __init__(self, own, bits):
        self.bits, self.bit, self.held = bits, 0, [own]
        self.got = None
        self.step()

    def step(self):
        if self.got is not None:
            many = len(self.held)
            self.held = self.held + [self.got[at] for at in range(many)]
        if self.bit < self.bits:
            self.got = flip(jnp.stack(self.held), self.bit, 1 << self.bits)
            self.bit += 1

    def pieces(self):
        while len(self.held) < 1 << self.bits:
            self.step()
        return self.held


def both_vectors(pieces):
    level = [piece[8:] for piece in pieces]
    while len(level) > 1:
        level = [level[at] + level[at + 1] for at in range(0, len(level), 2)]
    many = D // level[0].shape[1]
    return jnp.stack([level[0][:many].reshape(-1), level[0][4 : 4 + many].reshape(-1)])


def combine(pieces, block, blocks):
    level = [pieces[other][:8, (block ^ other) * SLOT : (block ^ other) * SLOT + SLOT] for other in range(blocks)]
    while len(level) > 1:
        level = [level[at] + level[at + 1] for at in range(0, len(level), 2)]
    return level[0]


def attention_scores(query, both_keys, length):
    scores = mul(query, both_keys, NT)
    row = lax.broadcasted_iota(jnp.int32, scores.shape, 0)
    place = lax.broadcasted_iota(jnp.int32, scores.shape, 1) % SLOT
    scores = jnp.where((place <= row) & (place < IMG + length), scores, masked_score)
    parts = []
    for at in range(2):
        part = scores[:, at * SLOT : (at + 1) * SLOT]
        expd = jnp.exp(part - jnp.max(part, axis=-1, keepdims=True))
        parts.append(expd / jnp.sum(expd, axis=-1, keepdims=True))
    return parts


def split_heads(value, mask):
    return jnp.concatenate([value * mask[0:1], value * mask[1:2]], axis=0)


def store_parts(refs, value, step, steps, only=None):
    left_keep, left_send, right_keep, right_send = refs
    left_keep[0] = value[:SLOT, :HALF]
    left_send[0] = value[SLOT:, :HALF]

    @pl.when(step < steps // 2)
    def _():
        right_keep[0] = value[:SLOT, HALF:]
        right_keep[1] = value[SLOT:, HALF:]

    @pl.when(step >= steps // 2)
    def _():
        right_send[0] = value[:SLOT, HALF:]
        right_send[1] = value[SLOT:, HALF:]


def part_outs(blocks):
    half = blocks // 2
    steps = blocks // 2
    shape = (half, SLOT, HALF)
    low = max(steps // 2, 1)
    return [
        (shape, F32, (1, SLOT, HALF), lambda s, *_: (s, 0, 0)),
        (shape, F32, (1, SLOT, HALF), lambda s, *_: (s, 0, 0)),
        (shape, F32, (2, SLOT, HALF), lambda s, *_: (jnp.minimum(s, low - 1), 0, 0)),
        (shape, F32, (2, SLOT, HALF), lambda s, *_: (jnp.maximum(s - steps // 2, 0), 0, 0)),
    ]


def front(order, lengths, tokens, gain, shift, weight, bias, tables, mask, mix_gain, uw_rows, out_weight, after=()):
    blocks = order.shape[0]
    steps = blocks // 2
    width = weight.shape[2]
    groups = width // 128
    rows = blocks * SLOT

    def kernel(order_ref, length_ref, x0, x1, g, b, w, wb, tab, msk, mg, uwr, ow, own, first, qkv, mixed, small, *parts_uw):
        step = pl.program_id(0)
        parts, uw = parts_uw[:4], parts_uw[4]

        @pl.when(step == 0)
        def _():
            found = mul(uwr[...], ow[...])
            uw[0:1] = found[0:1] + found[1:2] + found[2:3]
            uw[1:2] = found[3:4] + found[4:5] + found[5:6]
            small[8:] = jnp.zeros((8, rows), F32)
            for at in range(D // rows):
                c = slice(at * rows, at * rows + rows)
                small[8 + at : 9 + at] = uw[0:1, c]
                small[12 + at : 13 + at] = uw[1:2, c]

        x = jnp.concatenate([x0[0], x1[0]], axis=0)
        own[...] = x
        hat, _ = norm_parts(x.astype(F32))
        one = rounded(hat * g[...] + b[...])
        first[...] = one
        for c in range(3):
            proj = mul(one, w[c]) + wb[c : c + 1]
            for group in range(groups):
                part = proj[:, group * 128 : group * 128 + 128]
                if c < 2:
                    part = rotate(part, tab, 3 * c, 1)
                at = c * width + group * 128
                qkv[:, at : at + 128] = rounded(part)
        for pair in range(2):
            r = slice(pair * SLOT, pair * SLOT + SLOT)
            length = length_ref[order_ref[2 * step + pair]]
            for group in range(groups):
                at = group * 128
                query = qkv[r, at : at + 128]
                keys = split_heads(qkv[r, width + at : width + at + 128], msk)
                values = split_heads(qkv[r, 2 * width + at : 2 * width + at + 128], msk)
                probs = attention_scores(query, keys, length)
                mixed[r, at : at + 128] = mul(rounded(jnp.concatenate(probs, axis=1)), values)
        m = mixed[...]
        total = jnp.sum(m, axis=-1, keepdims=True)
        here = pl.ds(pl.multiple_of(step * 2 * SLOT, 2 * SLOT), 2 * SLOT)
        small[:8, here] = rows_of([total, jnp.sum(m * m, axis=-1, keepdims=True)])
        middle = total * (1.0 / width)
        partial = mul(rounded((m - middle) * mg[...]), ow[...]) + middle * uw[0:1]
        store_parts(parts, partial, step, steps)

    row2 = lambda s, *_: (s, 0)
    pair_of = lambda offset: lambda s, order_ref, length_ref: (order_ref[2 * s + offset], 0, 0)
    return run(
        kernel,
        (steps,),
        [
            (tokens, (1, SLOT, D), pair_of(0)),
            (tokens, (1, SLOT, D), pair_of(1)),
            whole(gain), whole(shift), whole(weight), whole(bias), whole(tables), whole(mask),
            whole(mix_gain), whole(uw_rows), whole(out_weight),
        ],
        [
            ((rows, D), BF16, (2 * SLOT, D), row2),
            ((rows, D), BF16, (2 * SLOT, D), row2),
            ((rows, 3 * width), BF16, (2 * SLOT, 3 * width), row2),
            ((rows, width), F32, (2 * SLOT, width), row2),
            ((16, rows), F32, (16, rows), lambda s, *_: (0, 0)),
        ]
        + part_outs(blocks),
        scratch=[pltpu.VMEM((8, D), F32)],
        prefetch=(order, lengths),
        after=after,
        name="front",
    )


def pieces_in(pieces):
    return [whole(piece) for piece in pieces[0]]


def load_pieces(refs, where, total, step, blocks):
    for block in range(blocks):

        @pl.when(step == block)
        def _(block=block):
            for half in range(2):
                array, at = where[half][block]
                total[:, half * HALF : half * HALF + HALF] = refs[array][at]


def middle_norm(own, pieces, sums, uw, out_bias, gain, shift, after=()):
    blocks = len(pieces[1][0])
    rows = blocks * SLOT

    def kernel(*refs):
        x, parts, stats = refs[0], refs[1:5], refs[5 : 5 + blocks]
        uw_ref, bias, g, b, mid, second, stat, total, tot8 = refs[5 + blocks :]
        step = pl.program_id(0)
        load_pieces(parts, pieces[1], total, step, blocks)
        for block in range(blocks):

            @pl.when(step == block)
            def _(block=block):
                tot8[...] = combine(stats, block, blocks)

        cols = columns_of(tot8[...])
        mean = cols[:, 0:1] * (1.0 / D)
        inverse = lax.rsqrt(cols[:, 1:2] * (1.0 / D) - mean * mean + eps)
        branch = inverse * (total[...] - mean * uw_ref[0:1]) + uw_ref[1:2]
        value = x[...].astype(F32) + branch + bias[...]
        mid[...] = value
        hat, _ = norm_parts(value)
        second[...] = rounded(hat * g[...] + b[...])
        lane = lax.broadcasted_iota(jnp.int32, (SLOT, 128), 1)
        stat[...] = jnp.where(lane == 0, mean, inverse)

    row = lambda k, *_: (k, 0)
    return run(
        kernel,
        (blocks,),
        [(own, (SLOT, D), row)]
        + pieces_in(pieces)
        + [whole(part) for part in sums]
        + [whole(uw), whole(out_bias), whole(gain), whole(shift)],
        [
            ((rows, D), F32, (SLOT, D), row),
            ((rows, D), BF16, (SLOT, D), row),
            ((rows, 128), F32, (SLOT, 128), row),
        ],
        scratch=[pltpu.VMEM((SLOT, D), F32), pltpu.VMEM((8, SLOT), F32)],
        after=after,
        name="middle_norm",
    )


def hidden_back(cots, down_weight):
    many, rows, units = len(cots), cots[0].shape[0], down_weight.shape[0]
    tile = min(512, units)

    def kernel(*refs):
        w, out = refs[many:]
        for at in range(many):
            out[at * rows : at * rows + rows] = rounded(mul(refs[at][...], w[...], NT))

    return run(
        kernel,
        (units // tile,),
        [whole(cot) for cot in cots] + [(down_weight, (tile, D), lambda j: (j, 0))],
        [((many * rows, units), BF16, (many * rows, tile), lambda j: (0, j))],
        name="hidden_back",
    )[0]


def hidden_front(chunk, second, up_weight, up_bias, back, gain, after=()):
    rows, units = second.shape[0], up_weight.shape[1]
    tile = 512
    steps = units // tile

    def part_of(c, s_ref, w, b, hb, g, act, slp):
        hidden = mul(s_ref[...], w[:, c]) + b[:, c]
        tail = jnp.exp(-0.5 * hidden * hidden)
        t = 1.0 / (1.0 + (0.3275911 * root_half) * jnp.abs(hidden))
        poly = 1.061405429 * t - 1.453152027
        poly = poly * t + 1.421413741
        poly = poly * t - 0.284496736
        poly = poly * t + 0.254829592
        half = 0.5 * poly * t * tail
        phi = jnp.where(hidden >= 0.0, 1.0 - half, half)
        active = hidden * phi
        act[:, c] = rounded(active)
        slp[:, c] = rounded(phi + hidden * (inv_root_two_pi * tail))
        scaled = hb[:, c].astype(F32) * g[:, c]
        return [value[:, :128] + value[:, 128:] for value in (active, active * active, scaled, scaled * active)]

    def kernel(s_ref, w, b, hb, g, act, slp, sums, acc):
        step = pl.program_id(0)
        found = [part_of(slice(at, at + 256), s_ref, w, b, hb, g, act, slp) for at in range(0, tile, 256)]

        @pl.when(step == 0)
        def _():
            for at in range(4):
                acc[at] = found[0][at] + found[1][at]

        @pl.when(step > 0)
        def _():
            for at in range(4):
                acc[at] += found[0][at] + found[1][at]

        @pl.when(step == steps - 1)
        def _():
            for block in range(rows // SLOT):
                r = slice(block * SLOT, block * SLOT + SLOT)
                sums[:, r] = rows_of([jnp.sum(acc[at, r], axis=-1, keepdims=True) for at in range(4)])

    return run(
        kernel,
        (steps,),
        [
            whole(second),
            (up_weight, (D, tile), lambda j: (0, j)),
            (up_bias, (1, tile), lambda j: (0, j)),
            (back, (rows, tile), lambda j: (chunk, j)),
            (gain, (1, tile), lambda j: (0, j)),
        ],
        [
            ((rows, units), BF16, (rows, tile), lambda j: (0, j)),
            ((rows, units), BF16, (rows, tile), lambda j: (0, j)),
            ((8, rows), F32, (8, rows), lambda j: (0, 0)),
        ],
        scratch=[pltpu.VMEM((4, rows, 128), F32)],
        after=after,
        name="hidden_front",
    )


def hidden_mid(chunk, active, slope, back, sums, gain, shift):
    blocks = len(sums)
    rows, units = active.shape

    def kernel(act, slp, hb, *refs):
        stats = refs[:blocks]
        g, b, low, grad, vecs, tot8 = refs[blocks:]
        step = pl.program_id(0)
        for block in range(blocks):

            @pl.when(step == block)
            def _(block=block):
                tot8[...] = combine(stats, block, blocks)

        cols = columns_of(tot8[...]) * (1.0 / FF)
        mean = cols[:, 0:1]
        inverse = lax.rsqrt(cols[:, 1:2] - mean * mean + eps)
        one = cols[:, 2:3]
        two = inverse * (cols[:, 3:4] - mean * one)
        for at in range(0, units, 256):
            c = slice(at, at + 256)
            hat = (act[:, c].astype(F32) - mean) * inverse
            low[:, c] = rounded(hat * g[:, c] + b[:, c])
            raw = hb[:, c].astype(F32)
            grown = rounded(inverse * (raw * g[:, c] - one - hat * two) * slp[:, c].astype(F32))
            grad[:, c] = grown
            vecs[0, 0:1, c] = sum_rows(raw * hat)
            vecs[0, 1:2, c] = sum_rows(raw)
            vecs[0, 2:3, c] = sum_rows(grown.astype(F32))

    row = lambda k: (k, 0)
    return run(
        kernel,
        (blocks,),
        [
            (active, (SLOT, units), row),
            (slope, (SLOT, units), row),
            (back, (SLOT, units), lambda k: (chunk * blocks + k, 0)),
        ]
        + [whole(part) for part in sums]
        + [whole(gain), whole(shift)],
        [
            ((rows, units), BF16, (SLOT, units), row),
            ((rows, units), BF16, (SLOT, units), row),
            ((blocks, 8, units), F32, (1, 8, units), lambda k: (k, 0, 0)),
        ],
        scratch=[pltpu.VMEM((8, SLOT), F32)],
        name="hidden_mid",
    )


def hidden_grad(grad, up_weight):
    rows, units = grad.shape
    blocks = rows // SLOT
    tile = 256
    steps = D // tile
    half = steps // 2

    def kernel(gr, w, left_keep, left_send, right_keep, right_send):
        step = pl.program_id(0)
        value = mul(gr[...], w[...], NT)

        @pl.when(step < half)
        def _():
            for block in range(blocks):
                r = slice(block * SLOT, block * SLOT + SLOT)
                (left_send if block & 1 else left_keep)[block // 2] = value[r]

        @pl.when(step >= half)
        def _():
            for block in range(blocks):
                r = slice(block * SLOT, block * SLOT + SLOT)
                (right_send if block >= blocks // 2 else right_keep)[block % (blocks // 2)] = value[r]

    shape = (blocks // 2, SLOT, HALF)
    block_shape = (blocks // 2, SLOT, tile)
    lefts = lambda j: (0, 0, jnp.minimum(j, half - 1))
    rights = lambda j: (0, 0, jnp.maximum(j - half, 0))
    return run(
        kernel,
        (steps,),
        [whole(grad), (up_weight, (tile, units), lambda j: (j, 0))],
        [
            (shape, F32, block_shape, lefts),
            (shape, F32, block_shape, lefts),
            (shape, F32, block_shape, rights),
            (shape, F32, block_shape, rights),
        ],
        name="hidden_grad",
    )


def result_part(order, lows, down_weight):
    pairs = order.shape[0]
    units = down_weight.shape[0]
    many = len(lows)
    rows = lows[0].shape[0]
    each = rows // SLOT
    tile = 256

    def kernel(order_ref, *refs):
        w, out = refs[many:]
        for at in range(many):
            value = mul(refs[at][...], w[...])
            for block in range(each):
                out[order_ref[at * each + block]] = value[block * SLOT : block * SLOT + SLOT]

    return run(
        kernel,
        (D // tile,),
        [whole(low) for low in lows] + [(down_weight, (units, tile), lambda j, *_: (0, j))],
        [((pairs, SLOT, D), F32, (pairs, SLOT, tile), lambda j, *_: (0, 0, j))],
        prefetch=(order,),
        name="result_part",
    )[0]


def middle_back(own, cot, pieces, middle, stat, uw, out_bias, gain, after=()):
    blocks = len(pieces[1][0])
    rows = blocks * SLOT

    def kernel(*refs):
        x, c, parts = refs[0], refs[1], refs[2:6]
        mid, st, uw_ref, bias, g, grad, low, stat2, vecs, total = refs[6:]
        load_pieces(parts, pieces[1], total, pl.program_id(0), blocks)
        value = mid[...]
        hat, inverse = norm_parts(value)
        sec = total[...]
        scaled = sec * g[...]
        up = c[...].astype(F32)
        out = up + inverse * (
            scaled
            - jnp.mean(scaled, axis=-1, keepdims=True)
            - hat * jnp.mean(scaled * hat, axis=-1, keepdims=True)
        )
        grad[...] = out
        lowered = rounded(out)
        low[...] = lowered
        low32 = lowered.astype(F32)
        one = jnp.mean(low32 * uw_ref[0:1], axis=-1, keepdims=True)
        moved = value - x[...].astype(F32) - bias[...] - uw_ref[1:2]
        two = jnp.mean(low32 * moved, axis=-1, keepdims=True)
        lane = lax.broadcasted_iota(jnp.int32, (SLOT, 128), 1)
        stat2[...] = jnp.where(lane == 2, one, jnp.where(lane == 3, two, st[...]))
        vecs[0, 0:1] = sum_rows(sec * hat)
        vecs[0, 1:2] = sum_rows(sec)
        vecs[0, 2:3] = sum_rows(out)
        vecs[0, 3:4] = sum_rows(up)

    row = lambda k, *_: (k, 0)
    return run(
        kernel,
        (blocks,),
        [(own, (SLOT, D), row), (cot, (SLOT, D), row)]
        + pieces_in(pieces)
        + [(middle, (SLOT, D), row), (stat, (SLOT, 128), row), whole(uw), whole(out_bias), whole(gain)],
        [
            ((rows, D), F32, (SLOT, D), row),
            ((rows, D), BF16, (SLOT, D), row),
            ((rows, 128), F32, (SLOT, 128), row),
            ((blocks, 8, D), F32, (1, 8, D), lambda k, *_: (k, 0, 0)),
        ],
        scratch=[pltpu.VMEM((SLOT, D), F32)],
        after=after,
        name="middle_back",
    )


def attention_back(order, lengths, low, stat, mixed, qkv, own, mix_gain, mix_shift, out_weight, weight, tables, mask, after=()):
    blocks = order.shape[0]
    steps = blocks // 2
    width = out_weight.shape[0]
    groups = width // 128
    rows = blocks * SLOT

    def kernel(
        order_ref, length_ref, low_ref, st, mx, qkv_ref, x, mg, ms, ow, w, tab, msk,
        mix_low, dproj, vecs, wide, left_keep, left_send, right_keep, right_send, dmixed,
    ):
        step = pl.program_id(0)
        mean, inverse, one, two = (st[:, at : at + 1] for at in range(4))
        back = mul(low_ref[...], ow[...], NT)
        hat = (mx[...] - mean) * inverse
        mix_low[...] = rounded(hat * mg[...] + ms[...])
        dmixed[...] = rounded(inverse * (back * mg[...] - one - hat * two))
        vecs[0, 0:1, :width] = sum_rows(back * hat)
        vecs[0, 1:2, :width] = sum_rows(back)
        first_half = lax.broadcasted_iota(jnp.int32, (SLOT, 128), 1) < HD
        for pair in range(2):
            r = slice(pair * SLOT, pair * SLOT + SLOT)
            length = length_ref[order_ref[2 * step + pair]]
            for group in range(groups):
                at = group * 128
                query = qkv_ref[r, at : at + 128]
                keys = split_heads(qkv_ref[r, width + at : width + at + 128], msk)
                values = split_heads(qkv_ref[r, 2 * width + at : 2 * width + at + 128], msk)
                grad = dmixed[r, at : at + 128]
                probs = attention_scores(query, keys, length)
                dprobs = mul(grad, values, NT)
                dscores = []
                for i in range(2):
                    dp = dprobs[:, i * SLOT : (i + 1) * SLOT]
                    carried = jnp.sum(probs[i] * dp, axis=-1, keepdims=True)
                    dscores.append(rounded(probs[i] * (dp - carried)))
                dscores = jnp.concatenate(dscores, axis=1)
                dquery = mul(dscores, keys)
                dkey = mul(dscores, query, TN)
                dvalue = mul(rounded(jnp.concatenate(probs, axis=1)), grad, TN)
                dkey = jnp.where(first_half, dkey[:SLOT], dkey[SLOT:])
                dvalue = jnp.where(first_half, dvalue[:SLOT], dvalue[SLOT:])
                tabs = [tab[i, :SLOT] for i in range(6)]
                dproj[r, at : at + 128] = rounded(rotate(dquery, tabs, 0, -1))
                dproj[r, width + at : width + at + 128] = rounded(rotate(dkey, tabs, 3, -1))
                dproj[r, 2 * width + at : 2 * width + at + 128] = rounded(dvalue)
        vecs[0, 2:3] = sum_rows(dproj[...].astype(F32))
        partial = mul(dproj[:, :width], w[0], NT)
        for c in (1, 2):
            partial += mul(dproj[:, c * width : (c + 1) * width], w[c], NT)
        pre_hat, _ = norm_parts(x[...].astype(F32))
        grown = partial * pre_hat
        wide[0, 0:1] = sum_rows(grown[:SLOT]) + sum_rows(grown[SLOT:])
        wide[0, 1:2] = sum_rows(partial[:SLOT]) + sum_rows(partial[SLOT:])
        store_parts((left_keep, left_send, right_keep, right_send), partial, step, steps)

    row2 = lambda s, *_: (s, 0)
    return run(
        kernel,
        (steps,),
        [
            (low, (2 * SLOT, D), row2),
            (stat, (2 * SLOT, 128), row2),
            (mixed, (2 * SLOT, width), row2),
            (qkv, (2 * SLOT, 3 * width), row2),
            (own, (2 * SLOT, D), row2),
            whole(mix_gain), whole(mix_shift), whole(out_weight), whole(weight), whole(tables), whole(mask),
        ],
        [
            ((rows, width), BF16, (2 * SLOT, width), row2),
            ((rows, 3 * width), BF16, (2 * SLOT, 3 * width), row2),
            ((steps, 8, 3 * width), F32, (1, 8, 3 * width), lambda s, *_: (s, 0, 0)),
            ((steps, 8, D), F32, (1, 8, D), lambda s, *_: (s, 0, 0)),
        ]
        + part_outs(blocks),
        scratch=[pltpu.VMEM((2 * SLOT, width), BF16)],
        prefetch=(order, lengths),
        after=after,
        name="attention_back",
    )


def tokens_back(order, own, grad, pieces, gain, before, pairs, after=()):
    blocks = len(pieces[1][0])

    def kernel(order_ref, x, gr, *refs):
        parts = refs[:4]
        g = refs[4]
        out, total = refs[-2:]
        load_pieces(parts, pieces[1], total, pl.program_id(0), blocks)
        hat, inverse = norm_parts(x[...].astype(F32))
        scaled = total[...] * g[...]
        out[0] = gr[...] + inverse * (
            scaled
            - jnp.mean(scaled, axis=-1, keepdims=True)
            - hat * jnp.mean(scaled * hat, axis=-1, keepdims=True)
        )

    row = lambda k, *_: (k, 0)
    ins = [(own, (SLOT, D), row), (grad, (SLOT, D), row)] + pieces_in(pieces) + [whole(gain)]
    alias = None
    if before is not None:
        alias = {1 + len(ins): 0}
        ins = ins + [(before, None, None)]
    return run(
        kernel,
        (blocks,),
        ins,
        [((pairs, SLOT, D), F32, (1, SLOT, D), lambda k, o: (o[k], 0, 0))],
        scratch=[pltpu.VMEM((SLOT, D), F32)],
        prefetch=(order,),
        after=after,
        alias=alias,
        name="tokens_back",
    )[0]


def output_of(order, middle, result, bias, before, after=()):
    blocks = order.shape[0]

    def kernel(order_ref, mid, res, b, *refs):
        out = refs[-1]
        out[0] = rounded(mid[...] + res[0] + b[...])

    ins = [
        (middle, (SLOT, D), lambda k, *_: (k, 0)),
        (result, (1, SLOT, D), lambda k, o: (o[k], 0, 0)),
        whole(bias),
    ]
    alias = None
    if before is not None:
        alias = {1 + len(ins): 0}
        ins = ins + [(before, None, None)]
    return run(
        kernel,
        (blocks,),
        ins,
        [(result.shape, BF16, (1, SLOT, D), lambda k, o: (o[k], 0, 0))],
        prefetch=(order,),
        after=after,
        alias=alias,
        name="output",
    )[0]


def attention_grads(ids, firsts, dprojs, lows, mixes, got=None):
    count, many = ids.shape[0], len(firsts)
    rows = firsts[0].shape[0]
    wide, tall = dprojs[0].shape[1], mixes[0].shape[1]
    block = D // (2 * count)
    shape = (block, wide + tall)

    def kernel(ids_ref, *refs):
        parts = [refs[at * many : (at + 1) * many] for at in range(4)]
        outs = refs[4 * many + (got is not None) :]
        total = []
        for left, right in ((parts[0], parts[1]), (parts[2], parts[3])):
            value = mul(left[0][...], right[0][...], TN)
            for at in range(1, many):
                value += mul(left[at][...], right[at][...], TN)
            total.append(value)
        if got is None:
            outs[0][0, :, :wide] = total[0]
            outs[0][0, :, wide:] = total[1]
            return
        more = refs[4 * many]
        step = pl.program_id(0)

        @pl.when(step == 0)
        def _():
            outs[0][:, :wide] = total[0] + more[0, :, :wide]
            outs[0][:, wide:] = total[1] + more[0, :, wide:]

        @pl.when(step > 0)
        def _():
            outs[1][0, :, :wide] = total[0] + more[0, :, :wide]
            outs[1][0, :, wide:] = total[1] + more[0, :, wide:]

    fixed = lambda i, *_: (0, 0)
    moving = lambda i, ids_ref: (0, ids_ref[i])
    lead = lambda i, *_: (i, 0, 0)
    ins = [(left, (rows, block), moving) for left in firsts] + [(right, (rows, wide), fixed) for right in dprojs]
    ins += [(left, (rows, block), moving) for left in lows] + [(right, (rows, tall), fixed) for right in mixes]
    if got is None:
        outs = [((count,) + shape, F32, (1,) + shape, lead)]
    else:
        ins += [(got, (1,) + shape, lead)]
        outs = [
            (shape, F32, shape, fixed),
            ((count - 1,) + shape, F32, (1,) + shape, lambda i, *_: (jnp.maximum(i - 1, 0), 0, 0)),
        ]
    return run(kernel, (count,), ins, outs, prefetch=(ids,), name="attention_grads")


def full_grad(lefts, rights):
    rows, many, block = lefts[0].shape[0], len(lefts), 512
    wide, tall = lefts[0].shape[1], rights[0].shape[1]

    def kernel(*refs):
        left, right, out = refs[:many], refs[many : 2 * many], refs[2 * many]
        value = mul(left[0][...], right[0][...], TN)
        for at in range(1, many):
            value += mul(left[at][...], right[at][...], TN)
        out[...] = value

    ins = [(left, (rows, block), lambda i: (0, i)) for left in lefts]
    ins += [(right, (rows, tall), lambda i: (0, 0)) for right in rights]
    return run(
        kernel, (wide // block,), ins, [((wide, tall), F32, (block, tall), lambda i: (i, 0))], name="full_grad"
    )[0]


def steps_of(totals, bits, done, until):
    done = list(done)

    def step(at):
        if done[at] < bits:
            totals[at].advance()
        else:
            totals[at].gather()
        done[at] += 1
        if done[at] == bits and until == 2 * bits:
            totals[at].gather()
            done[at] += 1

    limits = [until] + [until if until == 2 * bits else bits - 1] * (len(totals) - 1)
    while any(have < limit for have, limit in zip(done, limits)):
        for at in range(len(totals)):
            if done[at] < limits[at]:
                step(at)


def split_rows(value):
    found = []
    for _ in range(3):
        part = lax.reduce_precision(value, 8, 7)
        found.append(part.astype(BF16))
        value = value - part
    return found


def body(
    tokens,
    lengths,
    cotangent,
    pre_gain,
    pre_shift,
    qkv_weight,
    qkv_bias,
    mix_gain,
    mix_shift,
    out_weight,
    out_bias,
    ffn_gain,
    ffn_shift,
    up_weight,
    up_bias,
    hid_gain,
    hid_shift,
    down_weight,
    down_bias,
):
    pairs = lengths.shape[0]
    blocks = lax.axis_size("tensor")
    bits = blocks.bit_length() - 1
    chunks = pairs // blocks
    width = qkv_weight.shape[2]
    mine = lax.axis_index("tensor").astype(jnp.int32)
    orders = [jnp.arange(c * blocks, (c + 1) * blocks, dtype=jnp.int32) ^ mine for c in range(chunks)]
    tokens3 = tokens.reshape(pairs, SLOT, D)
    row = lambda v: v.reshape(1, -1)
    pre_gain, pre_shift, mix_gain, mix_shift = map(row, (pre_gain, pre_shift, mix_gain, mix_shift))
    out_bias, ffn_gain, ffn_shift, up_bias = map(row, (out_bias, ffn_gain, ffn_shift, up_bias))
    hid_gain, hid_shift, down_bias = map(row, (hid_gain, hid_shift, down_bias))
    tables = xpos_tables()
    lane = np.arange(128)[None, :] < HD
    mask = jnp.asarray(np.concatenate([lane, ~lane], 0).astype(np.float32)).astype(BF16)
    zero = jnp.zeros((2, width), BF16)
    uw_rows = jnp.concatenate(split_rows(mix_gain) + split_rows(mix_shift) + [zero], 0)

    line = Line()
    dp_size = lax.axis_size("dp")
    place = lax.axis_index("dp").astype(jnp.int32)
    count = dp_size // 2
    around = lax.rem(place // 2 + count - 1 - jnp.arange(count, dtype=jnp.int32), count)
    mine_ids, other_ids = 2 * around + lax.rem(place, 2), 2 * around + 1 - lax.rem(place, 2)

    def full(lefts, rights):
        grad = full_grad([line.tie(lefts[0])] + lefts[1:], rights)
        line.mark(grad)
        return grad

    every = lambda items, name: [item[name] for item in items]

    ones, twos, threes = [], [], []
    for c in range(chunks):
        found = front(
            orders[c], lengths, line.tie(tokens3), pre_gain, pre_shift, qkv_weight, qkv_bias, tables, mask, mix_gain, uw_rows,
            out_weight,
        )
        own, first, qkv, mixed, small = found[:5]
        one = dict(own=own, first=first, qkv=qkv, mixed=mixed, parts=found[5:])
        line.mark(small)
        one["small"] = small
        if c == 0:
            one["total"] = Total(line, one["parts"], bits)
            one["sums"] = Small(small, bits)
        ones.append(one)
    sums0 = ones[0]["sums"]
    if bits > 1:
        ones[0]["total"].advance()
    for c in range(1, chunks):
        ones[c]["total"] = Total(line, [line.tie(part) for part in ones[c]["parts"]], bits)
    sums0.held[0] = line.tie(sums0.held[0])
    sums0.step()
    cot3 = cotangent.reshape(pairs, SLOT, D)
    cots = []
    for c in range(chunks):
        cots.append(line.tie(cot3)[orders[c]].reshape(-1, D))
        line.mark(cots[-1])
    totals = every(ones, "total")
    for step in range(1, bits):
        totals[0].advance()
    back = hidden_back([line.tie(cots[0])] + cots[1:], down_weight)
    line.mark(back)
    for one in ones[1:]:
        one["sums"] = Small(line.tie(one["small"]), bits)
    done = [bits] + [0] * (chunks - 1)
    steps_of(totals, bits, done, 2 * bits - 1)
    for one in ones[1:]:
        line.mark(*line.last, one["sums"].got)
        one["sums"].step()
    uw_total = both_vectors(sums0.pieces())

    for c in range(chunks):
        one = ones[c]
        if c == 0:
            totals[0].gather()
            for total in totals[1:]:
                total.advance()
                total.gather()
            for other in ones[1:]:
                line.mark(*line.last, *other["sums"].pieces())
        mid, second, stat = middle_norm(
            line.tie(one["own"]), totals[c].pieces(), one["sums"].pieces(), uw_total, out_bias, ffn_gain, ffn_shift
        )
        line.mark(stat)
        if c == 0:
            for total in totals[1:]:
                for step in range(1, bits):
                    total.gather()
        else:
            line.mark(stat, *twos[c - 1]["sums"][1:])
        active, slope, sums = hidden_front(c, line.tie(second), up_weight, up_bias, back, hid_gain)
        line.mark(sums)
        twos.append(dict(middle=mid, second=second, stat=stat, active=active, slope=slope, sums=all_pieces(sums, bits)))
    for c in range(chunks):
        two = twos[c]
        low, grad, vecs = hidden_mid(c, line.tie(two["active"]), two["slope"], back, two["sums"], hid_gain, hid_shift)
        two.update(low=low, grad=grad, vecs=functools.reduce(jnp.add, [vecs[k] for k in range(blocks)]))
        line.mark(vecs)
    lows = every(twos, "low")
    down_grad = full(lows, cots)
    down_part = lax.psum_scatter(down_grad, "dp", scatter_dimension=1, tiled=True)
    up_grad = full(every(twos, "second"), every(twos, "grad"))
    up_part = lax.psum_scatter(up_grad, "dp", scatter_dimension=0, tiled=True)
    parts = []
    for two in twos:
        parts.append(hidden_grad(line.tie(two["grad"]), up_weight))
        line.mark(parts[-1][0])
        if not totals[1:] or two is twos[0]:
            twos[0]["total"] = Total(line, parts[0], bits)
    for step in range(bits):
        twos[0]["total"].advance()
    twos[0]["total"].gather()
    for c in range(1, chunks):
        twos[c]["total"] = Total(line, [line.tie(part) for part in parts[c]], bits)
    totals = every(twos, "total")
    for step in range(1, bits):
        totals[0].gather()
    result = result_part(jnp.concatenate(orders), [line.tie(lows[0])] + lows[1:], down_weight)
    line.mark(result)
    steps_of(totals, bits, [2 * bits] + [0] * (chunks - 1), 2 * bits)
    result = lax.psum(line.tie(result), "tensor")
    for two in twos:
        two["pieces"] = two["total"].pieces()

    for c in range(chunks):
        one, two = ones[c], twos[c]
        grad, low, stat2, vecs = middle_back(
            line.tie(one["own"]), cots[c], two["pieces"], two["middle"], two["stat"], uw_total, out_bias, ffn_gain
        )
        line.mark(stat2)
        found = attention_back(
            orders[c], lengths, line.tie(low), stat2, one["mixed"], one["qkv"], one["own"], mix_gain, mix_shift, out_weight,
            qkv_weight, tables, mask,
        )
        line.mark(found[2])
        three = dict(grad=grad, low=low, vecs=tree_sum(vecs), mix_low=found[0], dproj=found[1])
        three["narrow"] = tree_sum(found[2])
        three["wide"] = tree_sum(found[3])
        three["total"] = Total(line, found[4:], bits)
        threes.append(three)

    first, last = threes[0]["total"], threes[-1]["total"]
    if chunks > 1:
        first.advance()
    add = lambda items, name, size: functools.reduce(jnp.add, [item[name] for item in items])[:size]
    pad = lambda v: jnp.pad(v, ((0, 0), (0, D - v.shape[1])))
    wide = add(threes, "wide", 2)
    got = flip(wide, 0, blocks)
    grads_of = lambda ids, sent: attention_grads(
        ids, [line.tie(ones[0]["first"])] + every(ones, "first")[1:], every(threes, "dproj"), every(threes, "low"),
        every(threes, "mix_low"), sent,
    )
    sent = grads_of(other_ids, None)[0]
    line.mark(sent)
    sent = lax.ppermute(sent, "dp", [(d, d ^ 1) for d in range(dp_size)])
    for step in range(1 if chunks > 1 else 0, bits):
        first.advance()
    first.gather()
    line.mark(*line.last, down_part)
    ring_first, ring_rest = grads_of(mine_ids, sent)
    line.mark(ring_rest)
    ring = Ring(line, ring_first, ring_rest, dp_size)
    for bit in range(1, bits):
        wide = line.tie(wide) + got
        got = flip(wide, bit, blocks)
        line.mark(wide)
    if chunks > 1:
        last.advance()
    for step in range(1, bits):
        first.gather()
    wide = line.tie(wide) + got
    vecs = jnp.concatenate([pad(add(twos, "vecs", 3)), add(threes, "vecs", 4), pad(add(threes, "narrow", 3)), wide], 0)
    line.mark(vecs)
    hop = lambda v, bit: lax.ppermute(v, "dp", [(d, d ^ (1 << bit)) for d in range(dp_size)])
    dp_bits = dp_size.bit_length() - 1
    got = hop(vecs, 0)
    if chunks > 1:
        for step in range(1, bits):
            last.advance()
        last.gather()
        line.mark(*line.last, *last.got)
    vecs = line.tie(vecs) + got
    line.mark(vecs)
    got = hop(vecs, 1)
    attention_part = ring.advance()
    tokens_grad, output = None, None
    for c in range(chunks):
        tokens_grad = tokens_back(
            orders[c], line.tie(ones[c]["own"]), threes[c]["grad"], threes[c]["total"].pieces(), pre_gain, tokens_grad, pairs
        )
        line.mark(tokens_grad)
        if c == 0:
            if chunks > 1:
                for step in range(1, bits):
                    last.gather()
    for bit in range(2, dp_bits):
        vecs = line.tie(vecs) + got
        line.mark(vecs)
        got = hop(vecs, bit)
        attention_part = ring.advance()
    line.mark(attention_part, up_part)
    for step in range(dp_bits - 1, count - 1):
        attention_part = ring.advance()
    vecs = vecs + got
    hid_vecs, mid_vecs, narrow, wide = vecs[:3], vecs[3:7], vecs[7:10], vecs[10:12]
    for c in range(chunks):
        output = output_of(orders[c], line.tie(twos[c]["middle"]), result, down_bias, output)
        line.mark(output)
    qkv_part = jnp.swapaxes(attention_part[:, : 3 * width].reshape(-1, 3, width), 0, 1)
    out_part = jnp.transpose(attention_part[:, 3 * width :])
    units = hid_gain.shape[1]
    return (
        output.reshape(-1, D),
        tokens_grad.reshape(-1, D),
        wide[0],
        wide[1],
        qkv_part,
        narrow[2, : 3 * width].reshape(3, width),
        narrow[0, :width],
        narrow[1, :width],
        out_part,
        mid_vecs[2],
        mid_vecs[0],
        mid_vecs[1],
        up_part,
        hid_vecs[2, :units],
        hid_vecs[0, :units],
        hid_vecs[1, :units],
        down_part,
        mid_vecs[3],
    )


def solution(mesh):
    in_specs = (
        P("dp", None),
        P("dp"),
        P("dp", None),
        P(),
        P(),
        P(None, None, "tensor"),
        P(None, "tensor"),
        P("tensor"),
        P("tensor"),
        P("tensor", None),
        P(),
        P(),
        P(),
        P(None, "tensor"),
        P("tensor"),
        P("tensor"),
        P("tensor"),
        P("tensor", None),
        P(),
    )
    out_specs = (
        P("dp", None),
        P("dp", None),
        P(),
        P(),
        P(None, "dp", "tensor"),
        P(None, "tensor"),
        P("tensor"),
        P("tensor"),
        P("tensor", "dp"),
        P(),
        P(),
        P(),
        P("dp", "tensor"),
        P("tensor"),
        P("tensor"),
        P("tensor"),
        P("tensor", "dp"),
        P(),
    )
    return jax.shard_map(body, mesh=mesh, in_specs=in_specs, out_specs=out_specs, check_vma=False)
```

```python
import functools
import math

import jax
import jax.numpy as jnp
import numpy as np
from jax import lax
from jax.experimental import pallas as pl
from jax.experimental.pallas import tpu as pltpu
from jax.sharding import PartitionSpec as P

D = 2048
HD = 64
FF = 8192
SLOT = 128
IMG = 64
SCALE_BASE = 512
HALF = D // 2

eps = 1e-05
root_half = 0.7071067811865476
inv_root_two_pi = 0.3989422804014327
masked_score = -1e30
MEGA = 1 << 20

COST = {
    "front": 15.6,
    "middle_norm": 7.5,
    "hidden_back": 400.0,
    "hidden_front": 14.7,
    "hidden_mid": 6.0,
    "hidden_grad": 7.0,
    "full_grad": 15.0,
    "attention_grads": 12.0,
    "result_part": 400.0,
    "middle_back": 11.0,
    "attention_back": 21.7,
    "tokens_back": 8.5,
    "output": 6.0,
}
WORK = 5.5e+07

F32 = jnp.float32
BF16 = jnp.bfloat16
NN = (((1,), (0,)), ((), ()))
NT = (((1,), (1,)), ((), ()))
TN = (((0,), (0,)), ((), ()))


def rounded(value):
    return value.astype(BF16)


def mul(left, right, dims=NN):
    return lax.dot_general(left, right, dims, preferred_element_type=F32)


def xpos_tables():
    place = np.arange(SLOT, dtype=np.float64)[:, None]
    lane = np.arange(128)[None, :]
    index = (lane % HD) // 2
    angle = place * 10000.0 ** (-2.0 * index / HD)
    zeta = (2.0 * index + 0.4 * HD) / (1.4 * HD)
    growth = zeta ** ((place - SLOT // 2) / SCALE_BASE)
    even = lane % 2 == 0
    found = []
    for factor in (growth / math.sqrt(HD), 1.0 / growth):
        found += [
            np.cos(angle) * factor,
            np.where(even, -np.sin(angle), 0.0) * factor,
            np.where(even, 0.0, np.sin(angle)) * factor,
        ]
    return jnp.asarray(np.tile(np.stack(found), (1, 2, 1)).astype(np.float32))


def rotate(value, tables, base, sign):
    up = pltpu.roll(value, 127, axis=1)
    down = pltpu.roll(value, 1, axis=1)
    turned = up * tables[base + 1] + down * tables[base + 2]
    return value * tables[base] + turned if sign > 0 else value * tables[base] - turned


def columns_of(parts):
    return jnp.transpose(parts)


def rows_of(columns):
    size = columns[0].shape[0]
    lane = lax.broadcasted_iota(jnp.int32, (size, 128), 1)
    tile = jnp.zeros((size, 128), F32)
    for at, column in enumerate(columns):
        tile = jnp.where(lane == at, column, tile)
    return jnp.transpose(tile)[:8]


def norm_parts(value):
    mean = jnp.mean(value, axis=-1, keepdims=True)
    var = jnp.mean(value * value, axis=-1, keepdims=True) - mean * mean
    inverse = lax.rsqrt(var + eps)
    return (value - mean) * inverse, inverse


def sum_rows(value):
    return jnp.sum(value, axis=0, keepdims=True)


def whole(array, **kw):
    rank = array.ndim
    return (array, array.shape, lambda *at: (0,) * rank)


def run(kernel, grid, ins, outs, scratch=(), prefetch=(), after=(), alias=None, limit=56, name=None):
    prefetch = tuple(prefetch)

    def body(*refs):
        refs = list(refs)
        first = len(prefetch) + len(ins)
        del refs[first : first + len(after)]
        kernel(*refs)

    in_specs = []
    for array, block, where in ins:
        if block is None:
            in_specs.append(pl.BlockSpec(memory_space=pl.ANY))
        elif tuple(block) == tuple(array.shape):
            in_specs.append(pl.BlockSpec(block, where, pipeline_mode=pl.Buffered(1)))
        else:
            in_specs.append(pl.BlockSpec(block, where))
    in_specs += [pl.BlockSpec(memory_space=pl.ANY)] * len(after)
    out_specs = [pl.BlockSpec(block, where) for shape, dtype, block, where in outs]
    out_shape = [jax.ShapeDtypeStruct(shape, dtype) for shape, dtype, block, where in outs]
    return pl.pallas_call(
        body,
        grid_spec=pltpu.PrefetchScalarGridSpec(
            num_scalar_prefetch=len(prefetch),
            grid=grid,
            in_specs=in_specs,
            out_specs=out_specs,
            scratch_shapes=list(scratch),
        ),
        out_shape=out_shape,
        input_output_aliases=alias or {},
        compiler_params=pltpu.CompilerParams(
            dimension_semantics=("arbitrary",) * len(grid), vmem_limit_bytes=limit * MEGA
        ),
        cost_estimate=pl.CostEstimate(flops=int(COST[name] * WORK), bytes_accessed=1000, transcendentals=0),
        name=name,
    )(*prefetch, *[array for array, block, where in ins], *after)


def flip(value, bit, size):
    return lax.ppermute(value, "tensor", [(t, t ^ (1 << bit)) for t in range(size)])


def all_pieces(own, bits):
    size = 1 << bits
    return [own] + [lax.ppermute(own, "tensor", [(t, t ^ k) for t in range(size)]) for k in range(1, size)]


class Line:
    def __init__(self):
        self.last = None

    def tie(self, value):
        if self.last is None:
            return value
        return lax.optimization_barrier((value,) + self.last)[0]

    def mark(self, *values):
        self.last = values


class Total:
    def __init__(self, line, parts, bits):
        self.line, self.bits = line, bits
        self.orders = [list(range(bits)), list(range(bits))[::-1]]
        self.left = [[bit for bit in range(bits) if bit != order[0]] for order in self.orders]
        self.keep = [parts[0], parts[2]]
        self.got = [flip(parts[1], self.orders[0][0], 1 << bits), flip(parts[3], self.orders[1][0], 1 << bits)]
        self.step = 1

    def advance(self):
        line, size = self.line, 1 << self.bits
        if self.step == self.bits:
            for half in range(2):
                self.keep[half] = line.tie(self.keep[half]) + self.got[half]
                line.mark(self.keep[half])
            return
        picks = []
        for half in range(2):
            left, bit = self.left[half], self.orders[half][self.step]
            keep, got = self.keep[half], self.got[half]
            cube = (2,) * len(left) + keep.shape[1:]
            axis = len(left) - 1 - left.index(bit)
            shape = (keep.shape[0] // 2,) + keep.shape[1:]
            pick = lambda value, at, cube=cube, axis=axis, shape=shape: lax.index_in_dim(
                value.reshape(cube), at, axis, keepdims=False
            ).reshape(shape)
            send = pick(line.tie(keep), 1) + pick(got, 1)
            line.mark(send)
            picks.append((pick, keep, got))
            self.got[half] = flip(send, bit, size)
            left.remove(bit)
        for half in range(2):
            pick, keep, got = picks[half]
            self.keep[half] = pick(line.tie(keep), 0) + pick(got, 0)
            line.mark(self.keep[half])
        self.step += 1

    def gather(self):
        size = 1 << self.bits
        if self.step == self.bits:
            self.held = [[0], [0]]
            self.step += 1
        else:
            for half in range(2):
                self.keep[half] = jnp.concatenate([self.line.tie(self.keep[half]), self.got[half]], 0)
                self.line.mark(self.keep[half])
                self.held[half] = self.held[half] + [block | self.last[half] for block in self.held[half]]
        self.last = [1 << self.orders[half].pop() for half in range(2)]
        self.got = [flip(self.keep[half], self.last[half].bit_length() - 1, size) for half in range(2)]

    def pieces(self):
        arrays, where = [], []
        for half in range(2):
            arrays += [self.keep[half], self.got[half]]
            found = {block: (2 * half, at) for at, block in enumerate(self.held[half])}
            found.update({block | self.last[half]: (2 * half + 1, at) for at, block in enumerate(self.held[half])})
            where.append(found)
        return arrays, where


class Ring:
    def __init__(self, line, first, rest, size):
        self.line, self.rest, self.size = line, rest, size
        self.step = 0
        self.got = self.send(first)

    def send(self, value):
        return lax.ppermute(value, "dp", [(d, (d + 2) % self.size) for d in range(self.size)])

    def advance(self):
        value = self.line.tie(self.rest)[self.step] + self.got
        self.line.mark(value)
        self.step += 1
        if self.step < self.size // 2 - 1:
            self.got = self.send(value)
        return value


def butterfly(value, bits):
    for bit in range(bits):
        value = value + flip(value, bit, 1 << bits)
    return value


def tree_sum(value):
    while value.shape[0] > 1:
        value = value.reshape((value.shape[0] // 2, 2) + value.shape[1:])
        value = value[:, 0] + value[:, 1]
    return value[0]


class Small:
    def __init__(self, own, bits):
        self.bits, self.bit, self.held = bits, 0, [own]
        self.got = None
        self.step()

    def step(self):
        if self.got is not None:
            many = len(self.held)
            self.held = self.held + [self.got[at] for at in range(many)]
        if self.bit < self.bits:
            self.got = flip(jnp.stack(self.held), self.bit, 1 << self.bits)
            self.bit += 1

    def pieces(self):
        while len(self.held) < 1 << self.bits:
            self.step()
        return self.held


def both_vectors(pieces):
    level = [piece[8:] for piece in pieces]
    while len(level) > 1:
        level = [level[at] + level[at + 1] for at in range(0, len(level), 2)]
    many = D // level[0].shape[1]
    return jnp.stack([level[0][:many].reshape(-1), level[0][4 : 4 + many].reshape(-1)])


def combine(pieces, block, blocks):
    level = [pieces[other][:8, (block ^ other) * SLOT : (block ^ other) * SLOT + SLOT] for other in range(blocks)]
    while len(level) > 1:
        level = [level[at] + level[at + 1] for at in range(0, len(level), 2)]
    return level[0]


def attention_scores(query, both_keys, length):
    scores = mul(query, both_keys, NT)
    row = lax.broadcasted_iota(jnp.int32, scores.shape, 0)
    place = lax.broadcasted_iota(jnp.int32, scores.shape, 1) % SLOT
    scores = jnp.where((place <= row) & (place < IMG + length), scores, masked_score)
    parts = []
    for at in range(2):
        part = scores[:, at * SLOT : (at + 1) * SLOT]
        expd = jnp.exp(part - jnp.max(part, axis=-1, keepdims=True))
        parts.append(expd / jnp.sum(expd, axis=-1, keepdims=True))
    return parts


def split_heads(value, mask):
    return jnp.concatenate([value * mask[0:1], value * mask[1:2]], axis=0)


def store_parts(refs, value, step, steps, only=None):
    left_keep, left_send, right_keep, right_send = refs
    left_keep[0] = value[:SLOT, :HALF]
    left_send[0] = value[SLOT:, :HALF]

    @pl.when(step < steps // 2)
    def _():
        right_keep[0] = value[:SLOT, HALF:]
        right_keep[1] = value[SLOT:, HALF:]

    @pl.when(step >= steps // 2)
    def _():
        right_send[0] = value[:SLOT, HALF:]
        right_send[1] = value[SLOT:, HALF:]


def part_outs(blocks):
    half = blocks // 2
    steps = blocks // 2
    shape = (half, SLOT, HALF)
    low = max(steps // 2, 1)
    return [
        (shape, F32, (1, SLOT, HALF), lambda s, *_: (s, 0, 0)),
        (shape, F32, (1, SLOT, HALF), lambda s, *_: (s, 0, 0)),
        (shape, F32, (2, SLOT, HALF), lambda s, *_: (jnp.minimum(s, low - 1), 0, 0)),
        (shape, F32, (2, SLOT, HALF), lambda s, *_: (jnp.maximum(s - steps // 2, 0), 0, 0)),
    ]


def front(order, lengths, tokens, gain, shift, weight, bias, tables, mask, mix_gain, uw_rows, out_weight, after=()):
    blocks = order.shape[0]
    steps = blocks // 2
    width = weight.shape[2]
    groups = width // 128
    rows = blocks * SLOT

    def kernel(order_ref, length_ref, x0, x1, g, b, w, wb, tab, msk, mg, uwr, ow, own, first, qkv, mixed, small, *parts_uw):
        step = pl.program_id(0)
        parts, uw = parts_uw[:4], parts_uw[4]

        @pl.when(step == 0)
        def _():
            found = mul(uwr[...], ow[...])
            uw[0:1] = found[0:1] + found[1:2] + found[2:3]
            uw[1:2] = found[3:4] + found[4:5] + found[5:6]
            small[8:] = jnp.zeros((8, rows), F32)
            for at in range(D // rows):
                c = slice(at * rows, at * rows + rows)
                small[8 + at : 9 + at] = uw[0:1, c]
                small[12 + at : 13 + at] = uw[1:2, c]

        x = jnp.concatenate([x0[0], x1[0]], axis=0)
        own[...] = x
        hat, _ = norm_parts(x.astype(F32))
        one = rounded(hat * g[...] + b[...])
        first[...] = one
        for c in range(3):
            proj = mul(one, w[c]) + wb[c : c + 1]
            for group in range(groups):
                part = proj[:, group * 128 : group * 128 + 128]
                if c < 2:
                    part = rotate(part, tab, 3 * c, 1)
                at = c * width + group * 128
                qkv[:, at : at + 128] = rounded(part)
        for pair in range(2):
            r = slice(pair * SLOT, pair * SLOT + SLOT)
            length = length_ref[order_ref[2 * step + pair]]
            for group in range(groups):
                at = group * 128
                query = qkv[r, at : at + 128]
                keys = split_heads(qkv[r, width + at : width + at + 128], msk)
                values = split_heads(qkv[r, 2 * width + at : 2 * width + at + 128], msk)
                probs = attention_scores(query, keys, length)
                mixed[r, at : at + 128] = mul(rounded(jnp.concatenate(probs, axis=1)), values)
        m = mixed[...]
        total = jnp.sum(m, axis=-1, keepdims=True)
        here = pl.ds(pl.multiple_of(step * 2 * SLOT, 2 * SLOT), 2 * SLOT)
        small[:8, here] = rows_of([total, jnp.sum(m * m, axis=-1, keepdims=True)])
        middle = total * (1.0 / width)
        partial = mul(rounded((m - middle) * mg[...]), ow[...]) + middle * uw[0:1]
        store_parts(parts, partial, step, steps)

    row2 = lambda s, *_: (s, 0)
    pair_of = lambda offset: lambda s, order_ref, length_ref: (order_ref[2 * s + offset], 0, 0)
    return run(
        kernel,
        (steps,),
        [
            (tokens, (1, SLOT, D), pair_of(0)),
            (tokens, (1, SLOT, D), pair_of(1)),
            whole(gain), whole(shift), whole(weight), whole(bias), whole(tables), whole(mask),
            whole(mix_gain), whole(uw_rows), whole(out_weight),
        ],
        [
            ((rows, D), BF16, (2 * SLOT, D), row2),
            ((rows, D), BF16, (2 * SLOT, D), row2),
            ((rows, 3 * width), BF16, (2 * SLOT, 3 * width), row2),
            ((rows, width), F32, (2 * SLOT, width), row2),
            ((16, rows), F32, (16, rows), lambda s, *_: (0, 0)),
        ]
        + part_outs(blocks),
        scratch=[pltpu.VMEM((8, D), F32)],
        prefetch=(order, lengths),
        after=after,
        name="front",
    )


def pieces_in(pieces):
    return [whole(piece) for piece in pieces[0]]


def load_pieces(refs, where, total, step, blocks):
    for block in range(blocks):

        @pl.when(step == block)
        def _(block=block):
            for half in range(2):
                array, at = where[half][block]
                total[:, half * HALF : half * HALF + HALF] = refs[array][at]


def middle_norm(own, pieces, sums, uw, out_bias, gain, shift, after=()):
    blocks = len(pieces[1][0])
    rows = blocks * SLOT

    def kernel(*refs):
        x, parts, stats = refs[0], refs[1:5], refs[5 : 5 + blocks]
        uw_ref, bias, g, b, mid, second, stat, total, tot8 = refs[5 + blocks :]
        step = pl.program_id(0)
        load_pieces(parts, pieces[1], total, step, blocks)
        for block in range(blocks):

            @pl.when(step == block)
            def _(block=block):
                tot8[...] = combine(stats, block, blocks)

        cols = columns_of(tot8[...])
        mean = cols[:, 0:1] * (1.0 / D)
        inverse = lax.rsqrt(cols[:, 1:2] * (1.0 / D) - mean * mean + eps)
        branch = inverse * (total[...] - mean * uw_ref[0:1]) + uw_ref[1:2]
        value = x[...].astype(F32) + branch + bias[...]
        mid[...] = value
        hat, _ = norm_parts(value)
        second[...] = rounded(hat * g[...] + b[...])
        lane = lax.broadcasted_iota(jnp.int32, (SLOT, 128), 1)
        stat[...] = jnp.where(lane == 0, mean, inverse)

    row = lambda k, *_: (k, 0)
    return run(
        kernel,
        (blocks,),
        [(own, (SLOT, D), row)]
        + pieces_in(pieces)
        + [whole(part) for part in sums]
        + [whole(uw), whole(out_bias), whole(gain), whole(shift)],
        [
            ((rows, D), F32, (SLOT, D), row),
            ((rows, D), BF16, (SLOT, D), row),
            ((rows, 128), F32, (SLOT, 128), row),
        ],
        scratch=[pltpu.VMEM((SLOT, D), F32), pltpu.VMEM((8, SLOT), F32)],
        after=after,
        name="middle_norm",
    )


def hidden_back(cots, down_weight):
    many, rows, units = len(cots), cots[0].shape[0], down_weight.shape[0]
    tile = min(512, units)

    def kernel(*refs):
        w, out = refs[many:]
        for at in range(many):
            out[at * rows : at * rows + rows] = rounded(mul(refs[at][...], w[...], NT))

    return run(
        kernel,
        (units // tile,),
        [whole(cot) for cot in cots] + [(down_weight, (tile, D), lambda j: (j, 0))],
        [((many * rows, units), BF16, (many * rows, tile), lambda j: (0, j))],
        name="hidden_back",
    )[0]


def hidden_front(chunk, second, up_weight, up_bias, back, gain, after=()):
    rows, units = second.shape[0], up_weight.shape[1]
    tile = 512
    steps = units // tile

    def part_of(c, s_ref, w, b, hb, g, act, slp):
        hidden = mul(s_ref[...], w[:, c]) + b[:, c]
        tail = jnp.exp(-0.5 * hidden * hidden)
        t = 1.0 / (1.0 + (0.3275911 * root_half) * jnp.abs(hidden))
        poly = 1.061405429 * t - 1.453152027
        poly = poly * t + 1.421413741
        poly = poly * t - 0.284496736
        poly = poly * t + 0.254829592
        half = 0.5 * poly * t * tail
        phi = jnp.where(hidden >= 0.0, 1.0 - half, half)
        active = hidden * phi
        act[:, c] = rounded(active)
        slp[:, c] = rounded(phi + hidden * (inv_root_two_pi * tail))
        scaled = hb[:, c].astype(F32) * g[:, c]
        return [value[:, :128] + value[:, 128:] for value in (active, active * active, scaled, scaled * active)]

    def kernel(s_ref, w, b, hb, g, act, slp, sums, acc):
        step = pl.program_id(0)
        found = [part_of(slice(at, at + 256), s_ref, w, b, hb, g, act, slp) for at in range(0, tile, 256)]

        @pl.when(step == 0)
        def _():
            for at in range(4):
                acc[at] = found[0][at] + found[1][at]

        @pl.when(step > 0)
        def _():
            for at in range(4):
                acc[at] += found[0][at] + found[1][at]

        @pl.when(step == steps - 1)
        def _():
            for block in range(rows // SLOT):
                r = slice(block * SLOT, block * SLOT + SLOT)
                sums[:, r] = rows_of([jnp.sum(acc[at, r], axis=-1, keepdims=True) for at in range(4)])

    return run(
        kernel,
        (steps,),
        [
            whole(second),
            (up_weight, (D, tile), lambda j: (0, j)),
            (up_bias, (1, tile), lambda j: (0, j)),
            (back, (rows, tile), lambda j: (chunk, j)),
            (gain, (1, tile), lambda j: (0, j)),
        ],
        [
            ((rows, units), BF16, (rows, tile), lambda j: (0, j)),
            ((rows, units), BF16, (rows, tile), lambda j: (0, j)),
            ((8, rows), F32, (8, rows), lambda j: (0, 0)),
        ],
        scratch=[pltpu.VMEM((4, rows, 128), F32)],
        after=after,
        name="hidden_front",
    )


def hidden_mid(chunk, active, slope, back, sums, gain, shift):
    blocks = len(sums)
    rows, units = active.shape

    def kernel(act, slp, hb, *refs):
        stats = refs[:blocks]
        g, b, low, grad, vecs, tot8 = refs[blocks:]
        step = pl.program_id(0)
        for block in range(blocks):

            @pl.when(step == block)
            def _(block=block):
                tot8[...] = combine(stats, block, blocks)

        cols = columns_of(tot8[...]) * (1.0 / FF)
        mean = cols[:, 0:1]
        inverse = lax.rsqrt(cols[:, 1:2] - mean * mean + eps)
        one = cols[:, 2:3]
        two = inverse * (cols[:, 3:4] - mean * one)
        for at in range(0, units, 256):
            c = slice(at, at + 256)
            hat = (act[:, c].astype(F32) - mean) * inverse
            low[:, c] = rounded(hat * g[:, c] + b[:, c])
            raw = hb[:, c].astype(F32)
            grown = rounded(inverse * (raw * g[:, c] - one - hat * two) * slp[:, c].astype(F32))
            grad[:, c] = grown
            vecs[0, 0:1, c] = sum_rows(raw * hat)
            vecs[0, 1:2, c] = sum_rows(raw)
            vecs[0, 2:3, c] = sum_rows(grown.astype(F32))

    row = lambda k: (k, 0)
    return run(
        kernel,
        (blocks,),
        [
            (active, (SLOT, units), row),
            (slope, (SLOT, units), row),
            (back, (SLOT, units), lambda k: (chunk * blocks + k, 0)),
        ]
        + [whole(part) for part in sums]
        + [whole(gain), whole(shift)],
        [
            ((rows, units), BF16, (SLOT, units), row),
            ((rows, units), BF16, (SLOT, units), row),
            ((blocks, 8, units), F32, (1, 8, units), lambda k: (k, 0, 0)),
        ],
        scratch=[pltpu.VMEM((8, SLOT), F32)],
        name="hidden_mid",
    )


def hidden_grad(grad, up_weight):
    rows, units = grad.shape
    blocks = rows // SLOT
    tile = 512
    steps = D // tile
    half = steps // 2

    def kernel(gr, w, left_keep, left_send, right_keep, right_send):
        step = pl.program_id(0)
        value = mul(gr[...], w[...], NT)

        @pl.when(step < half)
        def _():
            for block in range(blocks):
                r = slice(block * SLOT, block * SLOT + SLOT)
                (left_send if block & 1 else left_keep)[block // 2] = value[r]

        @pl.when(step >= half)
        def _():
            for block in range(blocks):
                r = slice(block * SLOT, block * SLOT + SLOT)
                (right_send if block >= blocks // 2 else right_keep)[block % (blocks // 2)] = value[r]

    shape = (blocks // 2, SLOT, HALF)
    block_shape = (blocks // 2, SLOT, tile)
    lefts = lambda j: (0, 0, jnp.minimum(j, half - 1))
    rights = lambda j: (0, 0, jnp.maximum(j - half, 0))
    return run(
        kernel,
        (steps,),
        [whole(grad), (up_weight, (tile, units), lambda j: (j, 0))],
        [
            (shape, F32, block_shape, lefts),
            (shape, F32, block_shape, lefts),
            (shape, F32, block_shape, rights),
            (shape, F32, block_shape, rights),
        ],
        name="hidden_grad",
    )


def result_part(order, lows, down_weight):
    pairs = order.shape[0]
    units = down_weight.shape[0]
    many = len(lows)
    rows = lows[0].shape[0]
    each = rows // SLOT
    tile = 256

    def kernel(order_ref, *refs):
        w, out = refs[many:]
        for at in range(many):
            value = mul(refs[at][...], w[...])
            for block in range(each):
                out[order_ref[at * each + block]] = value[block * SLOT : block * SLOT + SLOT]

    return run(
        kernel,
        (D // tile,),
        [whole(low) for low in lows] + [(down_weight, (units, tile), lambda j, *_: (0, j))],
        [((pairs, SLOT, D), F32, (pairs, SLOT, tile), lambda j, *_: (0, 0, j))],
        prefetch=(order,),
        name="result_part",
    )[0]


def middle_back(own, cot, pieces, middle, stat, uw, out_bias, gain, after=()):
    blocks = len(pieces[1][0])
    rows = blocks * SLOT

    def kernel(*refs):
        x, c, parts = refs[0], refs[1], refs[2:6]
        mid, st, uw_ref, bias, g, grad, low, stat2, vecs, total = refs[6:]
        load_pieces(parts, pieces[1], total, pl.program_id(0), blocks)
        value = mid[...]
        hat, inverse = norm_parts(value)
        sec = total[...]
        scaled = sec * g[...]
        up = c[...].astype(F32)
        out = up + inverse * (
            scaled
            - jnp.mean(scaled, axis=-1, keepdims=True)
            - hat * jnp.mean(scaled * hat, axis=-1, keepdims=True)
        )
        grad[...] = out
        lowered = rounded(out)
        low[...] = lowered
        low32 = lowered.astype(F32)
        one = jnp.mean(low32 * uw_ref[0:1], axis=-1, keepdims=True)
        moved = value - x[...].astype(F32) - bias[...] - uw_ref[1:2]
        two = jnp.mean(low32 * moved, axis=-1, keepdims=True)
        lane = lax.broadcasted_iota(jnp.int32, (SLOT, 128), 1)
        stat2[...] = jnp.where(lane == 2, one, jnp.where(lane == 3, two, st[...]))
        vecs[0, 0:1] = sum_rows(sec * hat)
        vecs[0, 1:2] = sum_rows(sec)
        vecs[0, 2:3] = sum_rows(out)
        vecs[0, 3:4] = sum_rows(up)

    row = lambda k, *_: (k, 0)
    return run(
        kernel,
        (blocks,),
        [(own, (SLOT, D), row), (cot, (SLOT, D), row)]
        + pieces_in(pieces)
        + [(middle, (SLOT, D), row), (stat, (SLOT, 128), row), whole(uw), whole(out_bias), whole(gain)],
        [
            ((rows, D), F32, (SLOT, D), row),
            ((rows, D), BF16, (SLOT, D), row),
            ((rows, 128), F32, (SLOT, 128), row),
            ((blocks, 8, D), F32, (1, 8, D), lambda k, *_: (k, 0, 0)),
        ],
        scratch=[pltpu.VMEM((SLOT, D), F32)],
        after=after,
        name="middle_back",
    )


def attention_back(order, lengths, low, stat, mixed, qkv, own, mix_gain, mix_shift, out_weight, weight, tables, mask, after=()):
    blocks = order.shape[0]
    steps = blocks // 2
    width = out_weight.shape[0]
    groups = width // 128
    rows = blocks * SLOT

    def kernel(
        order_ref, length_ref, low_ref, st, mx, qkv_ref, x, mg, ms, ow, w, tab, msk,
        mix_low, dproj, vecs, wide, left_keep, left_send, right_keep, right_send, dmixed,
    ):
        step = pl.program_id(0)
        mean, inverse, one, two = (st[:, at : at + 1] for at in range(4))
        back = mul(low_ref[...], ow[...], NT)
        hat = (mx[...] - mean) * inverse
        mix_low[...] = rounded(hat * mg[...] + ms[...])
        dmixed[...] = rounded(inverse * (back * mg[...] - one - hat * two))
        vecs[0, 0:1, :width] = sum_rows(back * hat)
        vecs[0, 1:2, :width] = sum_rows(back)
        first_half = lax.broadcasted_iota(jnp.int32, (SLOT, 128), 1) < HD
        for pair in range(2):
            r = slice(pair * SLOT, pair * SLOT + SLOT)
            length = length_ref[order_ref[2 * step + pair]]
            for group in range(groups):
                at = group * 128
                query = qkv_ref[r, at : at + 128]
                keys = split_heads(qkv_ref[r, width + at : width + at + 128], msk)
                values = split_heads(qkv_ref[r, 2 * width + at : 2 * width + at + 128], msk)
                grad = dmixed[r, at : at + 128]
                probs = attention_scores(query, keys, length)
                dprobs = mul(grad, values, NT)
                dscores = []
                for i in range(2):
                    dp = dprobs[:, i * SLOT : (i + 1) * SLOT]
                    carried = jnp.sum(probs[i] * dp, axis=-1, keepdims=True)
                    dscores.append(rounded(probs[i] * (dp - carried)))
                dscores = jnp.concatenate(dscores, axis=1)
                dquery = mul(dscores, keys)
                dkey = mul(dscores, query, TN)
                dvalue = mul(rounded(jnp.concatenate(probs, axis=1)), grad, TN)
                dkey = jnp.where(first_half, dkey[:SLOT], dkey[SLOT:])
                dvalue = jnp.where(first_half, dvalue[:SLOT], dvalue[SLOT:])
                tabs = [tab[i, :SLOT] for i in range(6)]
                dproj[r, at : at + 128] = rounded(rotate(dquery, tabs, 0, -1))
                dproj[r, width + at : width + at + 128] = rounded(rotate(dkey, tabs, 3, -1))
                dproj[r, 2 * width + at : 2 * width + at + 128] = rounded(dvalue)
        vecs[0, 2:3] = sum_rows(dproj[...].astype(F32))
        partial = mul(dproj[:, :width], w[0], NT)
        for c in (1, 2):
            partial += mul(dproj[:, c * width : (c + 1) * width], w[c], NT)
        pre_hat, _ = norm_parts(x[...].astype(F32))
        grown = partial * pre_hat
        wide[0, 0:1] = sum_rows(grown[:SLOT]) + sum_rows(grown[SLOT:])
        wide[0, 1:2] = sum_rows(partial[:SLOT]) + sum_rows(partial[SLOT:])
        store_parts((left_keep, left_send, right_keep, right_send), partial, step, steps)

    row2 = lambda s, *_: (s, 0)
    return run(
        kernel,
        (steps,),
        [
            (low, (2 * SLOT, D), row2),
            (stat, (2 * SLOT, 128), row2),
            (mixed, (2 * SLOT, width), row2),
            (qkv, (2 * SLOT, 3 * width), row2),
            (own, (2 * SLOT, D), row2),
            whole(mix_gain), whole(mix_shift), whole(out_weight), whole(weight), whole(tables), whole(mask),
        ],
        [
            ((rows, width), BF16, (2 * SLOT, width), row2),
            ((rows, 3 * width), BF16, (2 * SLOT, 3 * width), row2),
            ((steps, 8, 3 * width), F32, (1, 8, 3 * width), lambda s, *_: (s, 0, 0)),
            ((steps, 8, D), F32, (1, 8, D), lambda s, *_: (s, 0, 0)),
        ]
        + part_outs(blocks),
        scratch=[pltpu.VMEM((2 * SLOT, width), BF16)],
        prefetch=(order, lengths),
        after=after,
        name="attention_back",
    )


def tokens_back(order, own, grad, pieces, gain, before, pairs, after=()):
    blocks = len(pieces[1][0])

    def kernel(order_ref, x, gr, *refs):
        parts = refs[:4]
        g = refs[4]
        out, total = refs[-2:]
        load_pieces(parts, pieces[1], total, pl.program_id(0), blocks)
        hat, inverse = norm_parts(x[...].astype(F32))
        scaled = total[...] * g[...]
        out[0] = gr[...] + inverse * (
            scaled
            - jnp.mean(scaled, axis=-1, keepdims=True)
            - hat * jnp.mean(scaled * hat, axis=-1, keepdims=True)
        )

    row = lambda k, *_: (k, 0)
    ins = [(own, (SLOT, D), row), (grad, (SLOT, D), row)] + pieces_in(pieces) + [whole(gain)]
    alias = None
    if before is not None:
        alias = {1 + len(ins): 0}
        ins = ins + [(before, None, None)]
    return run(
        kernel,
        (blocks,),
        ins,
        [((pairs, SLOT, D), F32, (1, SLOT, D), lambda k, o: (o[k], 0, 0))],
        scratch=[pltpu.VMEM((SLOT, D), F32)],
        prefetch=(order,),
        after=after,
        alias=alias,
        name="tokens_back",
    )[0]


def output_of(order, middle, result, bias, before, after=()):
    blocks = order.shape[0]

    def kernel(order_ref, mid, res, b, *refs):
        out = refs[-1]
        out[0] = rounded(mid[...] + res[0] + b[...])

    ins = [
        (middle, (SLOT, D), lambda k, *_: (k, 0)),
        (result, (1, SLOT, D), lambda k, o: (o[k], 0, 0)),
        whole(bias),
    ]
    alias = None
    if before is not None:
        alias = {1 + len(ins): 0}
        ins = ins + [(before, None, None)]
    return run(
        kernel,
        (blocks,),
        ins,
        [(result.shape, BF16, (1, SLOT, D), lambda k, o: (o[k], 0, 0))],
        prefetch=(order,),
        after=after,
        alias=alias,
        name="output",
    )[0]


def attention_grads(ids, firsts, dprojs, lows, mixes, got=None):
    count, many = ids.shape[0], len(firsts)
    rows = firsts[0].shape[0]
    wide, tall = dprojs[0].shape[1], mixes[0].shape[1]
    block = D // (2 * count)
    shape = (block, wide + tall)

    def kernel(ids_ref, *refs):
        parts = [refs[at * many : (at + 1) * many] for at in range(4)]
        outs = refs[4 * many + (got is not None) :]
        total = []
        for left, right in ((parts[0], parts[1]), (parts[2], parts[3])):
            value = mul(left[0][...], right[0][...], TN)
            for at in range(1, many):
                value += mul(left[at][...], right[at][...], TN)
            total.append(value)
        if got is None:
            outs[0][0, :, :wide] = total[0]
            outs[0][0, :, wide:] = total[1]
            return
        more = refs[4 * many]
        step = pl.program_id(0)

        @pl.when(step == 0)
        def _():
            outs[0][:, :wide] = total[0] + more[0, :, :wide]
            outs[0][:, wide:] = total[1] + more[0, :, wide:]

        @pl.when(step > 0)
        def _():
            outs[1][0, :, :wide] = total[0] + more[0, :, :wide]
            outs[1][0, :, wide:] = total[1] + more[0, :, wide:]

    fixed = lambda i, *_: (0, 0)
    moving = lambda i, ids_ref: (0, ids_ref[i])
    lead = lambda i, *_: (i, 0, 0)
    ins = [(left, (rows, block), moving) for left in firsts] + [(right, (rows, wide), fixed) for right in dprojs]
    ins += [(left, (rows, block), moving) for left in lows] + [(right, (rows, tall), fixed) for right in mixes]
    if got is None:
        outs = [((count,) + shape, F32, (1,) + shape, lead)]
    else:
        ins += [(got, (1,) + shape, lead)]
        outs = [
            (shape, F32, shape, fixed),
            ((count - 1,) + shape, F32, (1,) + shape, lambda i, *_: (jnp.maximum(i - 1, 0), 0, 0)),
        ]
    return run(kernel, (count,), ins, outs, prefetch=(ids,), name="attention_grads")


def full_grad(lefts, rights):
    rows, many, block = lefts[0].shape[0], len(lefts), 512
    wide, tall = lefts[0].shape[1], rights[0].shape[1]

    def kernel(*refs):
        left, right, out = refs[:many], refs[many : 2 * many], refs[2 * many]
        value = mul(left[0][...], right[0][...], TN)
        for at in range(1, many):
            value += mul(left[at][...], right[at][...], TN)
        out[...] = value

    ins = [(left, (rows, block), lambda i: (0, i)) for left in lefts]
    ins += [(right, (rows, tall), lambda i: (0, 0)) for right in rights]
    return run(
        kernel, (wide // block,), ins, [((wide, tall), F32, (block, tall), lambda i: (i, 0))], name="full_grad"
    )[0]


def steps_of(totals, bits, done, until):
    done = list(done)

    def step(at):
        if done[at] < bits:
            totals[at].advance()
        else:
            totals[at].gather()
        done[at] += 1
        if done[at] == bits and until == 2 * bits:
            totals[at].gather()
            done[at] += 1

    limits = [until] + [until if until == 2 * bits else bits - 1] * (len(totals) - 1)
    while any(have < limit for have, limit in zip(done, limits)):
        for at in range(len(totals)):
            if done[at] < limits[at]:
                step(at)


def split_rows(value):
    found = []
    for _ in range(3):
        part = lax.reduce_precision(value, 8, 7)
        found.append(part.astype(BF16))
        value = value - part
    return found


def body(
    tokens,
    lengths,
    cotangent,
    pre_gain,
    pre_shift,
    qkv_weight,
    qkv_bias,
    mix_gain,
    mix_shift,
    out_weight,
    out_bias,
    ffn_gain,
    ffn_shift,
    up_weight,
    up_bias,
    hid_gain,
    hid_shift,
    down_weight,
    down_bias,
):
    pairs = lengths.shape[0]
    blocks = lax.axis_size("tensor")
    bits = blocks.bit_length() - 1
    chunks = pairs // blocks
    width = qkv_weight.shape[2]
    mine = lax.axis_index("tensor").astype(jnp.int32)
    orders = [jnp.arange(c * blocks, (c + 1) * blocks, dtype=jnp.int32) ^ mine for c in range(chunks)]
    tokens3 = tokens.reshape(pairs, SLOT, D)
    row = lambda v: v.reshape(1, -1)
    pre_gain, pre_shift, mix_gain, mix_shift = map(row, (pre_gain, pre_shift, mix_gain, mix_shift))
    out_bias, ffn_gain, ffn_shift, up_bias = map(row, (out_bias, ffn_gain, ffn_shift, up_bias))
    hid_gain, hid_shift, down_bias = map(row, (hid_gain, hid_shift, down_bias))
    tables = xpos_tables()
    lane = np.arange(128)[None, :] < HD
    mask = jnp.asarray(np.concatenate([lane, ~lane], 0).astype(np.float32)).astype(BF16)
    zero = jnp.zeros((2, width), BF16)
    uw_rows = jnp.concatenate(split_rows(mix_gain) + split_rows(mix_shift) + [zero], 0)

    line = Line()
    dp_size = lax.axis_size("dp")
    place = lax.axis_index("dp").astype(jnp.int32)
    count = dp_size // 2
    around = lax.rem(place // 2 + count - 1 - jnp.arange(count, dtype=jnp.int32), count)
    mine_ids, other_ids = 2 * around + lax.rem(place, 2), 2 * around + 1 - lax.rem(place, 2)

    def full(lefts, rights):
        grad = full_grad([line.tie(lefts[0])] + lefts[1:], rights)
        line.mark(grad)
        return grad

    every = lambda items, name: [item[name] for item in items]

    ones, twos, threes = [], [], []
    for c in range(chunks):
        found = front(
            orders[c], lengths, line.tie(tokens3), pre_gain, pre_shift, qkv_weight, qkv_bias, tables, mask, mix_gain, uw_rows,
            out_weight,
        )
        own, first, qkv, mixed, small = found[:5]
        one = dict(own=own, first=first, qkv=qkv, mixed=mixed, parts=found[5:])
        line.mark(small)
        one["small"] = small
        if c == 0:
            one["total"] = Total(line, one["parts"], bits)
            one["sums"] = Small(small, bits)
        ones.append(one)
    sums0 = ones[0]["sums"]
    if bits > 1:
        ones[0]["total"].advance()
    for c in range(1, chunks):
        ones[c]["total"] = Total(line, [line.tie(part) for part in ones[c]["parts"]], bits)
    sums0.held[0] = line.tie(sums0.held[0])
    sums0.step()
    cot3 = cotangent.reshape(pairs, SLOT, D)
    cots = []
    for c in range(chunks):
        cots.append(line.tie(cot3)[orders[c]].reshape(-1, D))
        line.mark(cots[-1])
    totals = every(ones, "total")
    line.mark(*line.last, *sums0.pieces())
    for step in range(1, bits):
        totals[0].advance()
    back = hidden_back([line.tie(cots[0])] + cots[1:], down_weight)
    line.mark(back)
    for one in ones[1:]:
        one["sums"] = Small(line.tie(one["small"]), bits)
    done = [bits] + [0] * (chunks - 1)
    steps_of(totals, bits, done, 2 * bits - 1)
    for one in ones[1:]:
        line.mark(*line.last, one["sums"].got)
        one["sums"].step()
    uw_total = both_vectors(sums0.pieces())

    def mid_of(c):
        two = twos[c]
        low, grad, vecs = hidden_mid(c, line.tie(two["active"]), two["slope"], back, two["sums"], hid_gain, hid_shift)
        two.update(low=low, grad=grad, vecs=functools.reduce(jnp.add, [vecs[k] for k in range(blocks)]))
        line.mark(vecs)

    totals[0].gather()
    for other in ones[1:]:
        line.mark(*line.last, *other["sums"].pieces())
    for c in range(chunks):
        one = ones[c]
        mid, second, stat = middle_norm(
            line.tie(one["own"]), totals[c].pieces(), one["sums"].pieces(), uw_total, out_bias, ffn_gain, ffn_shift
        )
        line.mark(stat)
        if c == 0:
            for total in totals[1:]:
                total.advance()
                total.gather()
        active, slope, sums = hidden_front(c, line.tie(second), up_weight, up_bias, back, hid_gain)
        line.mark(sums)
        twos.append(dict(middle=mid, second=second, stat=stat, active=active, slope=slope, sums=all_pieces(sums, bits)))
        if c == 0:
            for total in totals[1:]:
                for step in range(1, bits):
                    total.gather()
        if c > 0:
            line.mark(sums, *twos[c - 1]["sums"][1:])
    for c in range(chunks):
        mid_of(c)
    lows = every(twos, "low")
    down_grad = full(lows, cots)
    down_part = lax.psum_scatter(down_grad, "dp", scatter_dimension=1, tiled=True)
    up_grad = full(every(twos, "second"), every(twos, "grad"))
    up_part = lax.psum_scatter(up_grad, "dp", scatter_dimension=0, tiled=True)
    parts = []
    for two in twos:
        parts.append(hidden_grad(line.tie(two["grad"]), up_weight))
        line.mark(parts[-1][0])
        if not totals[1:] or two is twos[0]:
            twos[0]["total"] = Total(line, parts[0], bits)
    for step in range(bits):
        twos[0]["total"].advance()
    twos[0]["total"].gather()
    for c in range(1, chunks):
        twos[c]["total"] = Total(line, [line.tie(part) for part in parts[c]], bits)
    totals = every(twos, "total")
    for step in range(1, bits):
        totals[0].gather()
    result = result_part(jnp.concatenate(orders), [line.tie(lows[0])] + lows[1:], down_weight)
    line.mark(result)
    steps_of(totals, bits, [2 * bits] + [0] * (chunks - 1), bits)
    result = lax.psum(line.tie(result), "tensor")

    for c in range(chunks):
        one, two = ones[c], twos[c]
        grad, low, stat2, vecs = middle_back(
            line.tie(one["own"]), cots[c], two["total"].pieces(), two["middle"], two["stat"], uw_total, out_bias, ffn_gain
        )
        line.mark(stat2)
        if c == 0:
            for total in totals[1:]:
                total.advance()
                for step in range(bits):
                    total.gather()
        found = attention_back(
            orders[c], lengths, line.tie(low), stat2, one["mixed"], one["qkv"], one["own"], mix_gain, mix_shift, out_weight,
            qkv_weight, tables, mask,
        )
        line.mark(found[2])
        three = dict(grad=grad, low=low, vecs=tree_sum(vecs), mix_low=found[0], dproj=found[1])
        three["narrow"] = tree_sum(found[2])
        three["wide"] = tree_sum(found[3])
        three["total"] = Total(line, found[4:], bits)
        threes.append(three)

    first, last = threes[0]["total"], threes[-1]["total"]
    if chunks > 1:
        first.advance()
    add = lambda items, name, size: functools.reduce(jnp.add, [item[name] for item in items])[:size]
    pad = lambda v: jnp.pad(v, ((0, 0), (0, D - v.shape[1])))
    wide = add(threes, "wide", 2)
    got = flip(wide, 0, blocks)
    grads_of = lambda ids, sent: attention_grads(
        ids, [line.tie(ones[0]["first"])] + every(ones, "first")[1:], every(threes, "dproj"), every(threes, "low"),
        every(threes, "mix_low"), sent,
    )
    sent = grads_of(other_ids, None)[0]
    line.mark(sent)
    sent = lax.ppermute(sent, "dp", [(d, d ^ 1) for d in range(dp_size)])
    line.mark(*line.last, down_part)
    ring_first, ring_rest = grads_of(mine_ids, sent)
    line.mark(ring_rest)
    ring = Ring(line, ring_first, ring_rest, dp_size)
    for step in range(1 if chunks > 1 else 0, bits):
        first.advance()
    first.gather()
    if chunks > 1:
        last.advance()
    for step in range(1, bits):
        first.gather()
    attention_part = ring.advance()
    if chunks > 1:
        for step in range(1, bits):
            last.advance()
        last.gather()
    for bit in range(1, bits):
        wide = line.tie(wide) + got
        got = flip(wide, bit, blocks)
        line.mark(wide)
    if chunks > 1:
        line.mark(*line.last, *last.got)
    hop = lambda v, bit: lax.ppermute(v, "dp", [(d, d ^ (1 << bit)) for d in range(dp_size)])
    dp_bits = dp_size.bit_length() - 1
    tokens_grad, output = None, None
    for c in range(chunks):
        tokens_grad = tokens_back(
            orders[c], line.tie(ones[c]["own"]), threes[c]["grad"], threes[c]["total"].pieces(), pre_gain, tokens_grad, pairs
        )
        line.mark(tokens_grad)
        if c == 0:
            wide = line.tie(wide) + got
            vecs = jnp.concatenate(
                [pad(add(twos, "vecs", 3)), add(threes, "vecs", 4), pad(add(threes, "narrow", 3)), wide], 0
            )
            line.mark(vecs)
            got = hop(vecs, 0)
            if chunks > 1:
                for step in range(1, bits):
                    last.gather()
            vecs = line.tie(vecs) + got
            line.mark(vecs)
            got = hop(vecs, 1)
            attention_part = ring.advance()
    for bit in range(2, dp_bits):
        vecs = line.tie(vecs) + got
        line.mark(vecs)
        got = hop(vecs, bit)
    line.mark(*line.last, up_part)
    for step in range(2, count - 1):
        attention_part = ring.advance()
    vecs = vecs + got
    hid_vecs, mid_vecs, narrow, wide = vecs[:3], vecs[3:7], vecs[7:10], vecs[10:12]
    for c in range(chunks):
        output = output_of(orders[c], line.tie(twos[c]["middle"]), result, down_bias, output)
        line.mark(output)
    qkv_part = jnp.swapaxes(attention_part[:, : 3 * width].reshape(-1, 3, width), 0, 1)
    out_part = jnp.transpose(attention_part[:, 3 * width :])
    units = hid_gain.shape[1]
    return (
        output.reshape(-1, D),
        tokens_grad.reshape(-1, D),
        wide[0],
        wide[1],
        qkv_part,
        narrow[2, : 3 * width].reshape(3, width),
        narrow[0, :width],
        narrow[1, :width],
        out_part,
        mid_vecs[2],
        mid_vecs[0],
        mid_vecs[1],
        up_part,
        hid_vecs[2, :units],
        hid_vecs[0, :units],
        hid_vecs[1, :units],
        down_part,
        mid_vecs[3],
    )


def solution(mesh):
    in_specs = (
        P("dp", None),
        P("dp"),
        P("dp", None),
        P(),
        P(),
        P(None, None, "tensor"),
        P(None, "tensor"),
        P("tensor"),
        P("tensor"),
        P("tensor", None),
        P(),
        P(),
        P(),
        P(None, "tensor"),
        P("tensor"),
        P("tensor"),
        P("tensor"),
        P("tensor", None),
        P(),
    )
    out_specs = (
        P("dp", None),
        P("dp", None),
        P(),
        P(),
        P(None, "dp", "tensor"),
        P(None, "tensor"),
        P("tensor"),
        P("tensor"),
        P("tensor", "dp"),
        P(),
        P(),
        P(),
        P("dp", "tensor"),
        P("tensor"),
        P("tensor"),
        P("tensor"),
        P("tensor", "dp"),
        P(),
    )
    return jax.shard_map(body, mesh=mesh, in_specs=in_specs, out_specs=out_specs, check_vma=False)
```

```python
import functools
import math

import jax
import jax.numpy as jnp
import numpy as np
from jax import lax
from jax.experimental import pallas as pl
from jax.experimental.pallas import tpu as pltpu
from jax.sharding import PartitionSpec as P

D = 2048
HD = 64
FF = 8192
SLOT = 128
IMG = 64
SCALE_BASE = 512
HALF = D // 2

eps = 1e-05
root_half = 0.7071067811865476
inv_root_two_pi = 0.3989422804014327
masked_score = -1e30
MEGA = 1 << 20

COST = {
    "front": 15.6,
    "middle_norm": 7.5,
    "hidden_back": 400.0,
    "hidden_front": 14.7,
    "hidden_mid": 6.0,
    "hidden_grad": 7.0,
    "full_grad": 15.0,
    "attention_grads": 12.0,
    "result_part": 400.0,
    "middle_back": 11.0,
    "attention_back": 21.7,
    "tokens_back": 8.5,
    "output": 6.0,
}
WORK = 5.5e+07

F32 = jnp.float32
BF16 = jnp.bfloat16
NN = (((1,), (0,)), ((), ()))
NT = (((1,), (1,)), ((), ()))
TN = (((0,), (0,)), ((), ()))


def rounded(value):
    return value.astype(BF16)


def mul(left, right, dims=NN):
    return lax.dot_general(left, right, dims, preferred_element_type=F32)


def xpos_tables():
    place = np.arange(SLOT, dtype=np.float64)[:, None]
    lane = np.arange(128)[None, :]
    index = (lane % HD) // 2
    angle = place * 10000.0 ** (-2.0 * index / HD)
    zeta = (2.0 * index + 0.4 * HD) / (1.4 * HD)
    growth = zeta ** ((place - SLOT // 2) / SCALE_BASE)
    even = lane % 2 == 0
    found = []
    for factor in (growth / math.sqrt(HD), 1.0 / growth):
        found += [
            np.cos(angle) * factor,
            np.where(even, -np.sin(angle), 0.0) * factor,
            np.where(even, 0.0, np.sin(angle)) * factor,
        ]
    return jnp.asarray(np.tile(np.stack(found), (1, 2, 1)).astype(np.float32))


def rotate(value, tables, base, sign):
    up = pltpu.roll(value, 127, axis=1)
    down = pltpu.roll(value, 1, axis=1)
    turned = up * tables[base + 1] + down * tables[base + 2]
    return value * tables[base] + turned if sign > 0 else value * tables[base] - turned


def columns_of(parts):
    return jnp.transpose(parts)


def rows_of(columns):
    size = columns[0].shape[0]
    lane = lax.broadcasted_iota(jnp.int32, (size, 128), 1)
    tile = jnp.zeros((size, 128), F32)
    for at, column in enumerate(columns):
        tile = jnp.where(lane == at, column, tile)
    return jnp.transpose(tile)[:8]


def norm_parts(value):
    mean = jnp.mean(value, axis=-1, keepdims=True)
    var = jnp.mean(value * value, axis=-1, keepdims=True) - mean * mean
    inverse = lax.rsqrt(var + eps)
    return (value - mean) * inverse, inverse


def sum_rows(value):
    return jnp.sum(value, axis=0, keepdims=True)


def whole(array, **kw):
    rank = array.ndim
    return (array, array.shape, lambda *at: (0,) * rank)


def run(kernel, grid, ins, outs, scratch=(), prefetch=(), after=(), alias=None, limit=56, name=None):
    prefetch = tuple(prefetch)

    def body(*refs):
        refs = list(refs)
        first = len(prefetch) + len(ins)
        del refs[first : first + len(after)]
        kernel(*refs)

    in_specs = []
    for array, block, where in ins:
        if block is None:
            in_specs.append(pl.BlockSpec(memory_space=pl.ANY))
        elif tuple(block) == tuple(array.shape):
            in_specs.append(pl.BlockSpec(block, where, pipeline_mode=pl.Buffered(1)))
        else:
            in_specs.append(pl.BlockSpec(block, where))
    in_specs += [pl.BlockSpec(memory_space=pl.ANY)] * len(after)
    out_specs = [pl.BlockSpec(block, where) for shape, dtype, block, where in outs]
    out_shape = [jax.ShapeDtypeStruct(shape, dtype) for shape, dtype, block, where in outs]
    return pl.pallas_call(
        body,
        grid_spec=pltpu.PrefetchScalarGridSpec(
            num_scalar_prefetch=len(prefetch),
            grid=grid,
            in_specs=in_specs,
            out_specs=out_specs,
            scratch_shapes=list(scratch),
        ),
        out_shape=out_shape,
        input_output_aliases=alias or {},
        compiler_params=pltpu.CompilerParams(
            dimension_semantics=("arbitrary",) * len(grid), vmem_limit_bytes=limit * MEGA
        ),
        cost_estimate=pl.CostEstimate(flops=int(COST[name] * WORK), bytes_accessed=1000, transcendentals=0),
        name=name,
    )(*prefetch, *[array for array, block, where in ins], *after)


def flip(value, bit, size):
    return lax.ppermute(value, "tensor", [(t, t ^ (1 << bit)) for t in range(size)])


def all_pieces(own, bits):
    size = 1 << bits
    return [own] + [lax.ppermute(own, "tensor", [(t, t ^ k) for t in range(size)]) for k in range(1, size)]


class Line:
    def __init__(self):
        self.last = None

    def tie(self, value):
        if self.last is None:
            return value
        return lax.optimization_barrier((value,) + self.last)[0]

    def mark(self, *values):
        self.last = values


class Total:
    def __init__(self, line, parts, bits):
        self.line, self.bits = line, bits
        self.orders = [list(range(bits)), list(range(bits))[::-1]]
        self.left = [[bit for bit in range(bits) if bit != order[0]] for order in self.orders]
        self.keep = [parts[0], parts[2]]
        self.got = [flip(parts[1], self.orders[0][0], 1 << bits), flip(parts[3], self.orders[1][0], 1 << bits)]
        self.step = 1

    def advance(self):
        line, size = self.line, 1 << self.bits
        if self.step == self.bits:
            for half in range(2):
                self.keep[half] = line.tie(self.keep[half]) + self.got[half]
                line.mark(self.keep[half])
            return
        picks = []
        for half in range(2):
            left, bit = self.left[half], self.orders[half][self.step]
            keep, got = self.keep[half], self.got[half]
            cube = (2,) * len(left) + keep.shape[1:]
            axis = len(left) - 1 - left.index(bit)
            shape = (keep.shape[0] // 2,) + keep.shape[1:]
            pick = lambda value, at, cube=cube, axis=axis, shape=shape: lax.index_in_dim(
                value.reshape(cube), at, axis, keepdims=False
            ).reshape(shape)
            send = pick(line.tie(keep), 1) + pick(got, 1)
            line.mark(send)
            picks.append((pick, keep, got))
            self.got[half] = flip(send, bit, size)
            left.remove(bit)
        for half in range(2):
            pick, keep, got = picks[half]
            self.keep[half] = pick(line.tie(keep), 0) + pick(got, 0)
            line.mark(self.keep[half])
        self.step += 1

    def gather(self):
        size = 1 << self.bits
        if self.step == self.bits:
            self.held = [[0], [0]]
            self.step += 1
        else:
            for half in range(2):
                self.keep[half] = jnp.concatenate([self.line.tie(self.keep[half]), self.got[half]], 0)
                self.line.mark(self.keep[half])
                self.held[half] = self.held[half] + [block | self.last[half] for block in self.held[half]]
        self.last = [1 << self.orders[half].pop() for half in range(2)]
        self.got = [flip(self.keep[half], self.last[half].bit_length() - 1, size) for half in range(2)]

    def pieces(self):
        arrays, where = [], []
        for half in range(2):
            arrays += [self.keep[half], self.got[half]]
            found = {block: (2 * half, at) for at, block in enumerate(self.held[half])}
            found.update({block | self.last[half]: (2 * half + 1, at) for at, block in enumerate(self.held[half])})
            where.append(found)
        return arrays, where


class Ring:
    def __init__(self, line, first, rest, size):
        self.line, self.rest, self.size = line, rest, size
        self.step = 0
        self.got = self.send(first)

    def send(self, value):
        return lax.ppermute(value, "dp", [(d, (d + 2) % self.size) for d in range(self.size)])

    def advance(self):
        value = self.line.tie(self.rest)[self.step] + self.got
        self.line.mark(value)
        self.step += 1
        if self.step < self.size // 2 - 1:
            self.got = self.send(value)
        return value


def butterfly(value, bits):
    for bit in range(bits):
        value = value + flip(value, bit, 1 << bits)
    return value


def tree_sum(value):
    while value.shape[0] > 1:
        value = value.reshape((value.shape[0] // 2, 2) + value.shape[1:])
        value = value[:, 0] + value[:, 1]
    return value[0]


class Small:
    def __init__(self, own, bits):
        self.bits, self.bit, self.held = bits, 0, [own]
        self.got = None
        self.step()

    def step(self):
        if self.got is not None:
            many = len(self.held)
            self.held = self.held + [self.got[at] for at in range(many)]
        if self.bit < self.bits:
            self.got = flip(jnp.stack(self.held), self.bit, 1 << self.bits)
            self.bit += 1

    def pieces(self):
        while len(self.held) < 1 << self.bits:
            self.step()
        return self.held


def both_vectors(pieces):
    level = [piece[8:] for piece in pieces]
    while len(level) > 1:
        level = [level[at] + level[at + 1] for at in range(0, len(level), 2)]
    many = D // level[0].shape[1]
    return jnp.stack([level[0][:many].reshape(-1), level[0][4 : 4 + many].reshape(-1)])


def combine(pieces, block, blocks):
    level = [pieces[other][:8, (block ^ other) * SLOT : (block ^ other) * SLOT + SLOT] for other in range(blocks)]
    while len(level) > 1:
        level = [level[at] + level[at + 1] for at in range(0, len(level), 2)]
    return level[0]


def attention_scores(query, both_keys, length):
    scores = mul(query, both_keys, NT)
    row = lax.broadcasted_iota(jnp.int32, scores.shape, 0)
    place = lax.broadcasted_iota(jnp.int32, scores.shape, 1) % SLOT
    scores = jnp.where((place <= row) & (place < IMG + length), scores, masked_score)
    parts = []
    for at in range(2):
        part = scores[:, at * SLOT : (at + 1) * SLOT]
        expd = jnp.exp(part - jnp.max(part, axis=-1, keepdims=True))
        parts.append(expd / jnp.sum(expd, axis=-1, keepdims=True))
    return parts


def split_heads(value, mask):
    return jnp.concatenate([value * mask[0:1], value * mask[1:2]], axis=0)


def store_parts(refs, value, step, steps, only=None):
    left_keep, left_send, right_keep, right_send = refs
    left_keep[0] = value[:SLOT, :HALF]
    left_send[0] = value[SLOT:, :HALF]

    @pl.when(step < steps // 2)
    def _():
        right_keep[0] = value[:SLOT, HALF:]
        right_keep[1] = value[SLOT:, HALF:]

    @pl.when(step >= steps // 2)
    def _():
        right_send[0] = value[:SLOT, HALF:]
        right_send[1] = value[SLOT:, HALF:]


def part_outs(blocks):
    half = blocks // 2
    steps = blocks // 2
    shape = (half, SLOT, HALF)
    low = max(steps // 2, 1)
    return [
        (shape, F32, (1, SLOT, HALF), lambda s, *_: (s, 0, 0)),
        (shape, F32, (1, SLOT, HALF), lambda s, *_: (s, 0, 0)),
        (shape, F32, (2, SLOT, HALF), lambda s, *_: (jnp.minimum(s, low - 1), 0, 0)),
        (shape, F32, (2, SLOT, HALF), lambda s, *_: (jnp.maximum(s - steps // 2, 0), 0, 0)),
    ]


def front(order, lengths, tokens, gain, shift, weight, bias, tables, mask, mix_gain, uw_rows, out_weight, after=()):
    blocks = order.shape[0]
    steps = blocks // 2
    width = weight.shape[2]
    groups = width // 128
    rows = blocks * SLOT

    def kernel(order_ref, length_ref, x0, x1, g, b, w, wb, tab, msk, mg, uwr, ow, own, first, qkv, mixed, small, *parts_uw):
        step = pl.program_id(0)
        parts, uw = parts_uw[:4], parts_uw[4]

        @pl.when(step == 0)
        def _():
            found = mul(uwr[...], ow[...])
            uw[0:1] = found[0:1] + found[1:2] + found[2:3]
            uw[1:2] = found[3:4] + found[4:5] + found[5:6]
            small[8:] = jnp.zeros((8, rows), F32)
            for at in range(D // rows):
                c = slice(at * rows, at * rows + rows)
                small[8 + at : 9 + at] = uw[0:1, c]
                small[12 + at : 13 + at] = uw[1:2, c]

        x = jnp.concatenate([x0[0], x1[0]], axis=0)
        own[...] = x
        hat, _ = norm_parts(x.astype(F32))
        one = rounded(hat * g[...] + b[...])
        first[...] = one
        for c in range(3):
            proj = mul(one, w[c]) + wb[c : c + 1]
            for group in range(groups):
                part = proj[:, group * 128 : group * 128 + 128]
                if c < 2:
                    part = rotate(part, tab, 3 * c, 1)
                at = c * width + group * 128
                qkv[:, at : at + 128] = rounded(part)
        for pair in range(2):
            r = slice(pair * SLOT, pair * SLOT + SLOT)
            length = length_ref[order_ref[2 * step + pair]]
            for group in range(groups):
                at = group * 128
                query = qkv[r, at : at + 128]
                keys = split_heads(qkv[r, width + at : width + at + 128], msk)
                values = split_heads(qkv[r, 2 * width + at : 2 * width + at + 128], msk)
                probs = attention_scores(query, keys, length)
                mixed[r, at : at + 128] = mul(rounded(jnp.concatenate(probs, axis=1)), values)
        m = mixed[...]
        total = jnp.sum(m, axis=-1, keepdims=True)
        here = pl.ds(pl.multiple_of(step * 2 * SLOT, 2 * SLOT), 2 * SLOT)
        small[:8, here] = rows_of([total, jnp.sum(m * m, axis=-1, keepdims=True)])
        middle = total * (1.0 / width)
        partial = mul(rounded((m - middle) * mg[...]), ow[...]) + middle * uw[0:1]
        store_parts(parts, partial, step, steps)

    row2 = lambda s, *_: (s, 0)
    pair_of = lambda offset: lambda s, order_ref, length_ref: (order_ref[2 * s + offset], 0, 0)
    return run(
        kernel,
        (steps,),
        [
            (tokens, (1, SLOT, D), pair_of(0)),
            (tokens, (1, SLOT, D), pair_of(1)),
            whole(gain), whole(shift), whole(weight), whole(bias), whole(tables), whole(mask),
            whole(mix_gain), whole(uw_rows), whole(out_weight),
        ],
        [
            ((rows, D), BF16, (2 * SLOT, D), row2),
            ((rows, D), BF16, (2 * SLOT, D), row2),
            ((rows, 3 * width), BF16, (2 * SLOT, 3 * width), row2),
            ((rows, width), F32, (2 * SLOT, width), row2),
            ((16, rows), F32, (16, rows), lambda s, *_: (0, 0)),
        ]
        + part_outs(blocks),
        scratch=[pltpu.VMEM((8, D), F32)],
        prefetch=(order, lengths),
        after=after,
        name="front",
    )


def pieces_in(pieces):
    return [whole(piece) for piece in pieces[0]]


def load_pieces(refs, where, total, step, blocks):
    for block in range(blocks):

        @pl.when(step == block)
        def _(block=block):
            for half in range(2):
                array, at = where[half][block]
                total[:, half * HALF : half * HALF + HALF] = refs[array][at]


def middle_norm(own, pieces, sums, uw, out_bias, gain, shift, after=()):
    blocks = len(pieces[1][0])
    rows = blocks * SLOT

    def kernel(*refs):
        x, parts, stats = refs[0], refs[1:5], refs[5 : 5 + blocks]
        uw_ref, bias, g, b, mid, second, stat, total, tot8 = refs[5 + blocks :]
        step = pl.program_id(0)
        load_pieces(parts, pieces[1], total, step, blocks)
        for block in range(blocks):

            @pl.when(step == block)
            def _(block=block):
                tot8[...] = combine(stats, block, blocks)

        cols = columns_of(tot8[...])
        mean = cols[:, 0:1] * (1.0 / D)
        inverse = lax.rsqrt(cols[:, 1:2] * (1.0 / D) - mean * mean + eps)
        branch = inverse * (total[...] - mean * uw_ref[0:1]) + uw_ref[1:2]
        value = x[...].astype(F32) + branch + bias[...]
        mid[...] = value
        hat, _ = norm_parts(value)
        second[...] = rounded(hat * g[...] + b[...])
        lane = lax.broadcasted_iota(jnp.int32, (SLOT, 128), 1)
        stat[...] = jnp.where(lane == 0, mean, inverse)

    row = lambda k, *_: (k, 0)
    return run(
        kernel,
        (blocks,),
        [(own, (SLOT, D), row)]
        + pieces_in(pieces)
        + [whole(part) for part in sums]
        + [whole(uw), whole(out_bias), whole(gain), whole(shift)],
        [
            ((rows, D), F32, (SLOT, D), row),
            ((rows, D), BF16, (SLOT, D), row),
            ((rows, 128), F32, (SLOT, 128), row),
        ],
        scratch=[pltpu.VMEM((SLOT, D), F32), pltpu.VMEM((8, SLOT), F32)],
        after=after,
        name="middle_norm",
    )


def hidden_back(cots, down_weight):
    many, rows, units = len(cots), cots[0].shape[0], down_weight.shape[0]
    tile = min(512, units)

    def kernel(*refs):
        w, out = refs[many:]
        for at in range(many):
            out[at * rows : at * rows + rows] = rounded(mul(refs[at][...], w[...], NT))

    return run(
        kernel,
        (units // tile,),
        [whole(cot) for cot in cots] + [(down_weight, (tile, D), lambda j: (j, 0))],
        [((many * rows, units), BF16, (many * rows, tile), lambda j: (0, j))],
        name="hidden_back",
    )[0]


def hidden_front(chunk, second, up_weight, up_bias, back, gain, after=()):
    rows, units = second.shape[0], up_weight.shape[1]
    tile = 512
    steps = units // tile

    def part_of(c, s_ref, w, b, hb, g, act, slp):
        hidden = mul(s_ref[...], w[:, c]) + b[:, c]
        tail = jnp.exp(-0.5 * hidden * hidden)
        t = 1.0 / (1.0 + (0.3275911 * root_half) * jnp.abs(hidden))
        poly = 1.061405429 * t - 1.453152027
        poly = poly * t + 1.421413741
        poly = poly * t - 0.284496736
        poly = poly * t + 0.254829592
        half = 0.5 * poly * t * tail
        phi = jnp.where(hidden >= 0.0, 1.0 - half, half)
        active = hidden * phi
        act[:, c] = rounded(active)
        slp[:, c] = rounded(phi + hidden * (inv_root_two_pi * tail))
        scaled = hb[:, c].astype(F32) * g[:, c]
        return [value[:, :128] + value[:, 128:] for value in (active, active * active, scaled, scaled * active)]

    def kernel(s_ref, w, b, hb, g, act, slp, sums, acc):
        step = pl.program_id(0)
        found = [part_of(slice(at, at + 256), s_ref, w, b, hb, g, act, slp) for at in range(0, tile, 256)]

        @pl.when(step == 0)
        def _():
            for at in range(4):
                acc[at] = found[0][at] + found[1][at]

        @pl.when(step > 0)
        def _():
            for at in range(4):
                acc[at] += found[0][at] + found[1][at]

        @pl.when(step == steps - 1)
        def _():
            for block in range(rows // SLOT):
                r = slice(block * SLOT, block * SLOT + SLOT)
                sums[:, r] = rows_of([jnp.sum(acc[at, r], axis=-1, keepdims=True) for at in range(4)])

    return run(
        kernel,
        (steps,),
        [
            whole(second),
            (up_weight, (D, tile), lambda j: (0, j)),
            (up_bias, (1, tile), lambda j: (0, j)),
            (back, (rows, tile), lambda j: (chunk, j)),
            (gain, (1, tile), lambda j: (0, j)),
        ],
        [
            ((rows, units), BF16, (rows, tile), lambda j: (0, j)),
            ((rows, units), BF16, (rows, tile), lambda j: (0, j)),
            ((8, rows), F32, (8, rows), lambda j: (0, 0)),
        ],
        scratch=[pltpu.VMEM((4, rows, 128), F32)],
        after=after,
        name="hidden_front",
    )


def hidden_mid(chunk, active, slope, back, sums, gain, shift):
    blocks = len(sums)
    rows, units = active.shape

    def kernel(act, slp, hb, *refs):
        stats = refs[:blocks]
        g, b, low, grad, vecs, tot8 = refs[blocks:]
        step = pl.program_id(0)
        for block in range(blocks):

            @pl.when(step == block)
            def _(block=block):
                tot8[...] = combine(stats, block, blocks)

        cols = columns_of(tot8[...]) * (1.0 / FF)
        mean = cols[:, 0:1]
        inverse = lax.rsqrt(cols[:, 1:2] - mean * mean + eps)
        one = cols[:, 2:3]
        two = inverse * (cols[:, 3:4] - mean * one)
        for at in range(0, units, 256):
            c = slice(at, at + 256)
            hat = (act[:, c].astype(F32) - mean) * inverse
            low[:, c] = rounded(hat * g[:, c] + b[:, c])
            raw = hb[:, c].astype(F32)
            grown = rounded(inverse * (raw * g[:, c] - one - hat * two) * slp[:, c].astype(F32))
            grad[:, c] = grown
            vecs[0, 0:1, c] = sum_rows(raw * hat)
            vecs[0, 1:2, c] = sum_rows(raw)
            vecs[0, 2:3, c] = sum_rows(grown.astype(F32))

    row = lambda k: (k, 0)
    return run(
        kernel,
        (blocks,),
        [
            (active, (SLOT, units), row),
            (slope, (SLOT, units), row),
            (back, (SLOT, units), lambda k: (chunk * blocks + k, 0)),
        ]
        + [whole(part) for part in sums]
        + [whole(gain), whole(shift)],
        [
            ((rows, units), BF16, (SLOT, units), row),
            ((rows, units), BF16, (SLOT, units), row),
            ((blocks, 8, units), F32, (1, 8, units), lambda k: (k, 0, 0)),
        ],
        scratch=[pltpu.VMEM((8, SLOT), F32)],
        name="hidden_mid",
    )


def hidden_grad(grad, up_weight):
    rows, units = grad.shape
    blocks = rows // SLOT
    tile = 512
    steps = D // tile
    half = steps // 2

    def kernel(gr, w, left_keep, left_send, right_keep, right_send):
        step = pl.program_id(0)
        value = mul(gr[...], w[...], NT)

        @pl.when(step < half)
        def _():
            for block in range(blocks):
                r = slice(block * SLOT, block * SLOT + SLOT)
                (left_send if block & 1 else left_keep)[block // 2] = value[r]

        @pl.when(step >= half)
        def _():
            for block in range(blocks):
                r = slice(block * SLOT, block * SLOT + SLOT)
                (right_send if block >= blocks // 2 else right_keep)[block % (blocks // 2)] = value[r]

    shape = (blocks // 2, SLOT, HALF)
    block_shape = (blocks // 2, SLOT, tile)
    lefts = lambda j: (0, 0, jnp.minimum(j, half - 1))
    rights = lambda j: (0, 0, jnp.maximum(j - half, 0))
    return run(
        kernel,
        (steps,),
        [whole(grad), (up_weight, (tile, units), lambda j: (j, 0))],
        [
            (shape, F32, block_shape, lefts),
            (shape, F32, block_shape, lefts),
            (shape, F32, block_shape, rights),
            (shape, F32, block_shape, rights),
        ],
        name="hidden_grad",
    )


def result_part(order, lows, down_weight):
    pairs = order.shape[0]
    units = down_weight.shape[0]
    many = len(lows)
    rows = lows[0].shape[0]
    each = rows // SLOT
    tile = 256

    def kernel(order_ref, *refs):
        w, out = refs[many:]
        for at in range(many):
            value = mul(refs[at][...], w[...])
            for block in range(each):
                out[order_ref[at * each + block]] = value[block * SLOT : block * SLOT + SLOT]

    return run(
        kernel,
        (D // tile,),
        [whole(low) for low in lows] + [(down_weight, (units, tile), lambda j, *_: (0, j))],
        [((pairs, SLOT, D), F32, (pairs, SLOT, tile), lambda j, *_: (0, 0, j))],
        prefetch=(order,),
        name="result_part",
    )[0]


def middle_back(own, cot, pieces, middle, stat, uw, out_bias, gain, after=()):
    blocks = len(pieces[1][0])
    rows = blocks * SLOT

    def kernel(*refs):
        x, c, parts = refs[0], refs[1], refs[2:6]
        mid, st, uw_ref, bias, g, grad, low, stat2, vecs, total = refs[6:]
        load_pieces(parts, pieces[1], total, pl.program_id(0), blocks)
        value = mid[...]
        hat, inverse = norm_parts(value)
        sec = total[...]
        scaled = sec * g[...]
        up = c[...].astype(F32)
        out = up + inverse * (
            scaled
            - jnp.mean(scaled, axis=-1, keepdims=True)
            - hat * jnp.mean(scaled * hat, axis=-1, keepdims=True)
        )
        grad[...] = out
        lowered = rounded(out)
        low[...] = lowered
        low32 = lowered.astype(F32)
        one = jnp.mean(low32 * uw_ref[0:1], axis=-1, keepdims=True)
        moved = value - x[...].astype(F32) - bias[...] - uw_ref[1:2]
        two = jnp.mean(low32 * moved, axis=-1, keepdims=True)
        lane = lax.broadcasted_iota(jnp.int32, (SLOT, 128), 1)
        stat2[...] = jnp.where(lane == 2, one, jnp.where(lane == 3, two, st[...]))
        vecs[0, 0:1] = sum_rows(sec * hat)
        vecs[0, 1:2] = sum_rows(sec)
        vecs[0, 2:3] = sum_rows(out)
        vecs[0, 3:4] = sum_rows(up)

    row = lambda k, *_: (k, 0)
    return run(
        kernel,
        (blocks,),
        [(own, (SLOT, D), row), (cot, (SLOT, D), row)]
        + pieces_in(pieces)
        + [(middle, (SLOT, D), row), (stat, (SLOT, 128), row), whole(uw), whole(out_bias), whole(gain)],
        [
            ((rows, D), F32, (SLOT, D), row),
            ((rows, D), BF16, (SLOT, D), row),
            ((rows, 128), F32, (SLOT, 128), row),
            ((blocks, 8, D), F32, (1, 8, D), lambda k, *_: (k, 0, 0)),
        ],
        scratch=[pltpu.VMEM((SLOT, D), F32)],
        after=after,
        name="middle_back",
    )


def attention_back(order, lengths, low, stat, mixed, qkv, own, mix_gain, mix_shift, out_weight, weight, tables, mask, after=()):
    blocks = order.shape[0]
    steps = blocks // 2
    width = out_weight.shape[0]
    groups = width // 128
    rows = blocks * SLOT

    def kernel(
        order_ref, length_ref, low_ref, st, mx, qkv_ref, x, mg, ms, ow, w, tab, msk,
        mix_low, dproj, vecs, wide, left_keep, left_send, right_keep, right_send, dmixed,
    ):
        step = pl.program_id(0)
        mean, inverse, one, two = (st[:, at : at + 1] for at in range(4))
        back = mul(low_ref[...], ow[...], NT)
        hat = (mx[...] - mean) * inverse
        mix_low[...] = rounded(hat * mg[...] + ms[...])
        dmixed[...] = rounded(inverse * (back * mg[...] - one - hat * two))
        vecs[0, 0:1, :width] = sum_rows(back * hat)
        vecs[0, 1:2, :width] = sum_rows(back)
        first_half = lax.broadcasted_iota(jnp.int32, (SLOT, 128), 1) < HD
        for pair in range(2):
            r = slice(pair * SLOT, pair * SLOT + SLOT)
            length = length_ref[order_ref[2 * step + pair]]
            for group in range(groups):
                at = group * 128
                query = qkv_ref[r, at : at + 128]
                keys = split_heads(qkv_ref[r, width + at : width + at + 128], msk)
                values = split_heads(qkv_ref[r, 2 * width + at : 2 * width + at + 128], msk)
                grad = dmixed[r, at : at + 128]
                probs = attention_scores(query, keys, length)
                dprobs = mul(grad, values, NT)
                dscores = []
                for i in range(2):
                    dp = dprobs[:, i * SLOT : (i + 1) * SLOT]
                    carried = jnp.sum(probs[i] * dp, axis=-1, keepdims=True)
                    dscores.append(rounded(probs[i] * (dp - carried)))
                dscores = jnp.concatenate(dscores, axis=1)
                dquery = mul(dscores, keys)
                dkey = mul(dscores, query, TN)
                dvalue = mul(rounded(jnp.concatenate(probs, axis=1)), grad, TN)
                dkey = jnp.where(first_half, dkey[:SLOT], dkey[SLOT:])
                dvalue = jnp.where(first_half, dvalue[:SLOT], dvalue[SLOT:])
                tabs = [tab[i, :SLOT] for i in range(6)]
                dproj[r, at : at + 128] = rounded(rotate(dquery, tabs, 0, -1))
                dproj[r, width + at : width + at + 128] = rounded(rotate(dkey, tabs, 3, -1))
                dproj[r, 2 * width + at : 2 * width + at + 128] = rounded(dvalue)
        vecs[0, 2:3] = sum_rows(dproj[...].astype(F32))
        partial = mul(dproj[:, :width], w[0], NT)
        for c in (1, 2):
            partial += mul(dproj[:, c * width : (c + 1) * width], w[c], NT)
        pre_hat, _ = norm_parts(x[...].astype(F32))
        grown = partial * pre_hat
        wide[0, 0:1] = sum_rows(grown[:SLOT]) + sum_rows(grown[SLOT:])
        wide[0, 1:2] = sum_rows(partial[:SLOT]) + sum_rows(partial[SLOT:])
        store_parts((left_keep, left_send, right_keep, right_send), partial, step, steps)

    row2 = lambda s, *_: (s, 0)
    return run(
        kernel,
        (steps,),
        [
            (low, (2 * SLOT, D), row2),
            (stat, (2 * SLOT, 128), row2),
            (mixed, (2 * SLOT, width), row2),
            (qkv, (2 * SLOT, 3 * width), row2),
            (own, (2 * SLOT, D), row2),
            whole(mix_gain), whole(mix_shift), whole(out_weight), whole(weight), whole(tables), whole(mask),
        ],
        [
            ((rows, width), BF16, (2 * SLOT, width), row2),
            ((rows, 3 * width), BF16, (2 * SLOT, 3 * width), row2),
            ((steps, 8, 3 * width), F32, (1, 8, 3 * width), lambda s, *_: (s, 0, 0)),
            ((steps, 8, D), F32, (1, 8, D), lambda s, *_: (s, 0, 0)),
        ]
        + part_outs(blocks),
        scratch=[pltpu.VMEM((2 * SLOT, width), BF16)],
        prefetch=(order, lengths),
        after=after,
        name="attention_back",
    )


def tokens_back(order, own, grad, pieces, gain, before, pairs, after=()):
    blocks = len(pieces[1][0])

    def kernel(order_ref, x, gr, *refs):
        parts = refs[:4]
        g = refs[4]
        out, total = refs[-2:]
        load_pieces(parts, pieces[1], total, pl.program_id(0), blocks)
        hat, inverse = norm_parts(x[...].astype(F32))
        scaled = total[...] * g[...]
        out[0] = gr[...] + inverse * (
            scaled
            - jnp.mean(scaled, axis=-1, keepdims=True)
            - hat * jnp.mean(scaled * hat, axis=-1, keepdims=True)
        )

    row = lambda k, *_: (k, 0)
    ins = [(own, (SLOT, D), row), (grad, (SLOT, D), row)] + pieces_in(pieces) + [whole(gain)]
    alias = None
    if before is not None:
        alias = {1 + len(ins): 0}
        ins = ins + [(before, None, None)]
    return run(
        kernel,
        (blocks,),
        ins,
        [((pairs, SLOT, D), F32, (1, SLOT, D), lambda k, o: (o[k], 0, 0))],
        scratch=[pltpu.VMEM((SLOT, D), F32)],
        prefetch=(order,),
        after=after,
        alias=alias,
        name="tokens_back",
    )[0]


def output_of(order, middle, result, bias, before, after=()):
    blocks = order.shape[0]

    def kernel(order_ref, mid, res, b, *refs):
        out = refs[-1]
        out[0] = rounded(mid[...] + res[0] + b[...])

    ins = [
        (middle, (SLOT, D), lambda k, *_: (k, 0)),
        (result, (1, SLOT, D), lambda k, o: (o[k], 0, 0)),
        whole(bias),
    ]
    alias = None
    if before is not None:
        alias = {1 + len(ins): 0}
        ins = ins + [(before, None, None)]
    return run(
        kernel,
        (blocks,),
        ins,
        [(result.shape, BF16, (1, SLOT, D), lambda k, o: (o[k], 0, 0))],
        prefetch=(order,),
        after=after,
        alias=alias,
        name="output",
    )[0]


def attention_grads(ids, firsts, dprojs, lows, mixes, got=None):
    count, many = ids.shape[0], len(firsts)
    rows = firsts[0].shape[0]
    wide, tall = dprojs[0].shape[1], mixes[0].shape[1]
    block = D // (2 * count)
    shape = (block, wide + tall)

    def kernel(ids_ref, *refs):
        parts = [refs[at * many : (at + 1) * many] for at in range(4)]
        outs = refs[4 * many + (got is not None) :]
        total = []
        for left, right in ((parts[0], parts[1]), (parts[2], parts[3])):
            value = mul(left[0][...], right[0][...], TN)
            for at in range(1, many):
                value += mul(left[at][...], right[at][...], TN)
            total.append(value)
        if got is None:
            outs[0][0, :, :wide] = total[0]
            outs[0][0, :, wide:] = total[1]
            return
        more = refs[4 * many]
        step = pl.program_id(0)

        @pl.when(step == 0)
        def _():
            outs[0][:, :wide] = total[0] + more[0, :, :wide]
            outs[0][:, wide:] = total[1] + more[0, :, wide:]

        @pl.when(step > 0)
        def _():
            outs[1][0, :, :wide] = total[0] + more[0, :, :wide]
            outs[1][0, :, wide:] = total[1] + more[0, :, wide:]

    fixed = lambda i, *_: (0, 0)
    moving = lambda i, ids_ref: (0, ids_ref[i])
    lead = lambda i, *_: (i, 0, 0)
    ins = [(left, (rows, block), moving) for left in firsts] + [(right, (rows, wide), fixed) for right in dprojs]
    ins += [(left, (rows, block), moving) for left in lows] + [(right, (rows, tall), fixed) for right in mixes]
    if got is None:
        outs = [((count,) + shape, F32, (1,) + shape, lead)]
    else:
        ins += [(got, (1,) + shape, lead)]
        outs = [
            (shape, F32, shape, fixed),
            ((count - 1,) + shape, F32, (1,) + shape, lambda i, *_: (jnp.maximum(i - 1, 0), 0, 0)),
        ]
    return run(kernel, (count,), ins, outs, prefetch=(ids,), name="attention_grads")


def full_grad(lefts, rights):
    rows, many, block = lefts[0].shape[0], len(lefts), 512
    wide, tall = lefts[0].shape[1], rights[0].shape[1]

    def kernel(*refs):
        left, right, out = refs[:many], refs[many : 2 * many], refs[2 * many]
        value = mul(left[0][...], right[0][...], TN)
        for at in range(1, many):
            value += mul(left[at][...], right[at][...], TN)
        out[...] = value

    ins = [(left, (rows, block), lambda i: (0, i)) for left in lefts]
    ins += [(right, (rows, tall), lambda i: (0, 0)) for right in rights]
    return run(
        kernel, (wide // block,), ins, [((wide, tall), F32, (block, tall), lambda i: (i, 0))], name="full_grad"
    )[0]


def steps_of(totals, bits, done, until):
    done = list(done)

    def step(at):
        if done[at] < bits:
            totals[at].advance()
        else:
            totals[at].gather()
        done[at] += 1
        if done[at] == bits and until == 2 * bits:
            totals[at].gather()
            done[at] += 1

    limits = [until] + [until if until == 2 * bits else bits - 1] * (len(totals) - 1)
    while any(have < limit for have, limit in zip(done, limits)):
        for at in range(len(totals)):
            if done[at] < limits[at]:
                step(at)


def split_rows(value):
    found = []
    for _ in range(3):
        part = lax.reduce_precision(value, 8, 7)
        found.append(part.astype(BF16))
        value = value - part
    return found


def body(
    tokens,
    lengths,
    cotangent,
    pre_gain,
    pre_shift,
    qkv_weight,
    qkv_bias,
    mix_gain,
    mix_shift,
    out_weight,
    out_bias,
    ffn_gain,
    ffn_shift,
    up_weight,
    up_bias,
    hid_gain,
    hid_shift,
    down_weight,
    down_bias,
):
    pairs = lengths.shape[0]
    blocks = lax.axis_size("tensor")
    bits = blocks.bit_length() - 1
    chunks = pairs // blocks
    width = qkv_weight.shape[2]
    mine = lax.axis_index("tensor").astype(jnp.int32)
    orders = [jnp.arange(c * blocks, (c + 1) * blocks, dtype=jnp.int32) ^ mine for c in range(chunks)]
    tokens3 = tokens.reshape(pairs, SLOT, D)
    row = lambda v: v.reshape(1, -1)
    pre_gain, pre_shift, mix_gain, mix_shift = map(row, (pre_gain, pre_shift, mix_gain, mix_shift))
    out_bias, ffn_gain, ffn_shift, up_bias = map(row, (out_bias, ffn_gain, ffn_shift, up_bias))
    hid_gain, hid_shift, down_bias = map(row, (hid_gain, hid_shift, down_bias))
    tables = xpos_tables()
    lane = np.arange(128)[None, :] < HD
    mask = jnp.asarray(np.concatenate([lane, ~lane], 0).astype(np.float32)).astype(BF16)
    zero = jnp.zeros((2, width), BF16)
    uw_rows = jnp.concatenate(split_rows(mix_gain) + split_rows(mix_shift) + [zero], 0)

    line = Line()
    dp_size = lax.axis_size("dp")
    place = lax.axis_index("dp").astype(jnp.int32)
    count = dp_size // 2
    around = lax.rem(place // 2 + count - 1 - jnp.arange(count, dtype=jnp.int32), count)
    mine_ids, other_ids = 2 * around + lax.rem(place, 2), 2 * around + 1 - lax.rem(place, 2)

    def full(lefts, rights):
        grad = full_grad([line.tie(lefts[0])] + lefts[1:], rights)
        line.mark(grad)
        return grad

    every = lambda items, name: [item[name] for item in items]

    ones, twos, threes = [], [], []
    for c in range(chunks):
        found = front(
            orders[c], lengths, line.tie(tokens3), pre_gain, pre_shift, qkv_weight, qkv_bias, tables, mask, mix_gain, uw_rows,
            out_weight,
        )
        own, first, qkv, mixed, small = found[:5]
        one = dict(own=own, first=first, qkv=qkv, mixed=mixed, parts=found[5:])
        line.mark(small)
        one["small"] = small
        if c == 0:
            one["total"] = Total(line, one["parts"], bits)
            one["sums"] = Small(small, bits)
        ones.append(one)
    sums0 = ones[0]["sums"]
    if bits > 1:
        ones[0]["total"].advance()
    for c in range(1, chunks):
        ones[c]["total"] = Total(line, [line.tie(part) for part in ones[c]["parts"]], bits)
    sums0.held[0] = line.tie(sums0.held[0])
    sums0.step()
    cot3 = cotangent.reshape(pairs, SLOT, D)
    cots = []
    for c in range(chunks):
        cots.append(line.tie(cot3)[orders[c]].reshape(-1, D))
        line.mark(cots[-1])
    totals = every(ones, "total")
    line.mark(*line.last, *sums0.pieces())
    for step in range(1, bits):
        totals[0].advance()
    back = hidden_back([line.tie(cots[0])] + cots[1:], down_weight)
    line.mark(back)
    for one in ones[1:]:
        one["sums"] = Small(line.tie(one["small"]), bits)
    done = [bits] + [0] * (chunks - 1)
    steps_of(totals, bits, done, 2 * bits - 1)
    for one in ones[1:]:
        line.mark(*line.last, one["sums"].got)
        one["sums"].step()
    uw_total = both_vectors(sums0.pieces())

    def mid_of(c):
        two = twos[c]
        low, grad, vecs = hidden_mid(c, line.tie(two["active"]), two["slope"], back, two["sums"], hid_gain, hid_shift)
        two.update(low=low, grad=grad, vecs=functools.reduce(jnp.add, [vecs[k] for k in range(blocks)]))
        line.mark(vecs)

    def hidden_of(c):
        parts = hidden_grad(line.tie(twos[c]["grad"]), up_weight)
        line.mark(parts[0])
        return parts

    totals[0].gather()
    for other in ones[1:]:
        line.mark(*line.last, *other["sums"].pieces())
    for c in range(chunks):
        one = ones[c]
        mid, second, stat = middle_norm(
            line.tie(one["own"]), totals[c].pieces(), one["sums"].pieces(), uw_total, out_bias, ffn_gain, ffn_shift
        )
        line.mark(stat)
        if c == 0:
            for total in totals[1:]:
                total.advance()
                total.gather()
        active, slope, sums = hidden_front(c, line.tie(second), up_weight, up_bias, back, hid_gain)
        line.mark(sums)
        twos.append(dict(middle=mid, second=second, stat=stat, active=active, slope=slope, sums=all_pieces(sums, bits)))
        if c == 0:
            line.mark(sums, *twos[0]["sums"][1:])
            for total in totals[1:]:
                for step in range(1, bits):
                    total.gather()
        else:
            twos[0]["total"].advance()
            line.mark(*line.last, *twos[c]["sums"][1:], *twos[0]["total"].got)
        mid_of(c)
        if c == 0 and chunks > 1:
            twos[0]["total"] = Total(line, hidden_of(0), bits)
    lows = every(twos, "low")
    down_grad = full(lows, cots)
    down_part = lax.psum_scatter(down_grad, "dp", scatter_dimension=1, tiled=True)
    up_grad = full(every(twos, "second"), every(twos, "grad"))
    up_part = lax.psum_scatter(up_grad, "dp", scatter_dimension=0, tiled=True)
    if chunks > 1:
        for step in range(1, bits):
            twos[0]["total"].advance()
        twos[0]["total"].gather()
        parts = [None] + [hidden_of(c) for c in range(1, chunks)]
    else:
        twos[0]["total"] = Total(line, hidden_of(0), bits)
        for step in range(bits):
            twos[0]["total"].advance()
        twos[0]["total"].gather()
    for step in range(1, bits):
        twos[0]["total"].gather()
    for c in range(1, chunks):
        twos[c]["total"] = Total(line, [line.tie(part) for part in parts[c]], bits)
    totals = every(twos, "total")
    result = result_part(jnp.concatenate(orders), [line.tie(lows[0])] + lows[1:], down_weight)
    line.mark(result)
    result = lax.psum(line.tie(result), "tensor")

    for c in range(chunks):
        one, two = ones[c], twos[c]
        grad, low, stat2, vecs = middle_back(
            line.tie(one["own"]), cots[c], two["total"].pieces(), two["middle"], two["stat"], uw_total, out_bias, ffn_gain
        )
        line.mark(stat2)
        if c == 0:
            for total in totals[1:]:
                total.advance()
        found = attention_back(
            orders[c], lengths, line.tie(low), stat2, one["mixed"], one["qkv"], one["own"], mix_gain, mix_shift, out_weight,
            qkv_weight, tables, mask,
        )
        line.mark(found[2])
        three = dict(grad=grad, low=low, vecs=tree_sum(vecs), mix_low=found[0], dproj=found[1])
        three["narrow"] = tree_sum(found[2])
        three["wide"] = tree_sum(found[3])
        parts = found[4:]
        if c == 0 and chunks > 1:
            for total in totals[1:]:
                for step in range(1, bits):
                    total.advance()
                for step in range(bits):
                    total.gather()
            parts = [line.tie(part) for part in parts]
        three["total"] = Total(line, parts, bits)
        threes.append(three)

    first, last = threes[0]["total"], threes[-1]["total"]
    if chunks > 1:
        first.advance()
    add = lambda items, name, size: functools.reduce(jnp.add, [item[name] for item in items])[:size]
    pad = lambda v: jnp.pad(v, ((0, 0), (0, D - v.shape[1])))
    wide = add(threes, "wide", 2)
    got = flip(wide, 0, blocks)
    grads_of = lambda ids, sent: attention_grads(
        ids, [line.tie(ones[0]["first"])] + every(ones, "first")[1:], every(threes, "dproj"), every(threes, "low"),
        every(threes, "mix_low"), sent,
    )
    sent = grads_of(other_ids, None)[0]
    line.mark(sent)
    sent = lax.ppermute(sent, "dp", [(d, d ^ 1) for d in range(dp_size)])
    line.mark(*line.last, down_part)
    ring_first, ring_rest = grads_of(mine_ids, sent)
    line.mark(ring_rest)
    ring = Ring(line, ring_first, ring_rest, dp_size)
    for step in range(1 if chunks > 1 else 0, bits):
        first.advance()
    first.gather()
    if chunks > 1:
        last.advance()
    for step in range(1, bits):
        first.gather()
    attention_part = ring.advance()
    if chunks > 1:
        for step in range(1, bits):
            last.advance()
        last.gather()
    for bit in range(1, bits):
        wide = line.tie(wide) + got
        got = flip(wide, bit, blocks)
        line.mark(wide)
    if chunks > 1:
        line.mark(*line.last, *last.got)
    hop = lambda v, bit: lax.ppermute(v, "dp", [(d, d ^ (1 << bit)) for d in range(dp_size)])
    dp_bits = dp_size.bit_length() - 1
    tokens_grad, output = None, None
    for c in range(chunks):
        tokens_grad = tokens_back(
            orders[c], line.tie(ones[c]["own"]), threes[c]["grad"], threes[c]["total"].pieces(), pre_gain, tokens_grad, pairs
        )
        line.mark(tokens_grad)
        if c == 0:
            wide = line.tie(wide) + got
            vecs = jnp.concatenate(
                [pad(add(twos, "vecs", 3)), add(threes, "vecs", 4), pad(add(threes, "narrow", 3)), wide], 0
            )
            line.mark(vecs)
            got = hop(vecs, 0)
            if chunks > 1:
                for step in range(1, bits):
                    last.gather()
            vecs = line.tie(vecs) + got
            line.mark(vecs)
            got = hop(vecs, 1)
            attention_part = ring.advance()
    for bit in range(2, dp_bits):
        vecs = line.tie(vecs) + got
        line.mark(vecs)
        got = hop(vecs, bit)
    line.mark(*line.last, up_part)
    for step in range(2, count - 1):
        attention_part = ring.advance()
    vecs = vecs + got
    hid_vecs, mid_vecs, narrow, wide = vecs[:3], vecs[3:7], vecs[7:10], vecs[10:12]
    for c in range(chunks):
        output = output_of(orders[c], line.tie(twos[c]["middle"]), result, down_bias, output)
        line.mark(output)
    qkv_part = jnp.swapaxes(attention_part[:, : 3 * width].reshape(-1, 3, width), 0, 1)
    out_part = jnp.transpose(attention_part[:, 3 * width :])
    units = hid_gain.shape[1]
    return (
        output.reshape(-1, D),
        tokens_grad.reshape(-1, D),
        wide[0],
        wide[1],
        qkv_part,
        narrow[2, : 3 * width].reshape(3, width),
        narrow[0, :width],
        narrow[1, :width],
        out_part,
        mid_vecs[2],
        mid_vecs[0],
        mid_vecs[1],
        up_part,
        hid_vecs[2, :units],
        hid_vecs[0, :units],
        hid_vecs[1, :units],
        down_part,
        mid_vecs[3],
    )


def solution(mesh):
    in_specs = (
        P("dp", None),
        P("dp"),
        P("dp", None),
        P(),
        P(),
        P(None, None, "tensor"),
        P(None, "tensor"),
        P("tensor"),
        P("tensor"),
        P("tensor", None),
        P(),
        P(),
        P(),
        P(None, "tensor"),
        P("tensor"),
        P("tensor"),
        P("tensor"),
        P("tensor", None),
        P(),
    )
    out_specs = (
        P("dp", None),
        P("dp", None),
        P(),
        P(),
        P(None, "dp", "tensor"),
        P(None, "tensor"),
        P("tensor"),
        P("tensor"),
        P("tensor", "dp"),
        P(),
        P(),
        P(),
        P("dp", "tensor"),
        P("tensor"),
        P("tensor"),
        P("tensor"),
        P("tensor", "dp"),
        P(),
    )
    return jax.shard_map(body, mesh=mesh, in_specs=in_specs, out_specs=out_specs, check_vma=False)
```

```python
import functools
import math

import jax
import jax.numpy as jnp
import numpy as np
from jax import lax
from jax.experimental import pallas as pl
from jax.experimental.pallas import tpu as pltpu
from jax.sharding import PartitionSpec as P

D = 2048
HD = 64
FF = 8192
SLOT = 128
IMG = 64
SCALE_BASE = 512
HALF = D // 2

eps = 1e-05
root_half = 0.7071067811865476
inv_root_two_pi = 0.3989422804014327
masked_score = -1e30
MEGA = 1 << 20

COST = {
    "front": 15.6,
    "middle_norm": 7.5,
    "hidden_back": 400.0,
    "hidden_front": 14.7,
    "hidden_mid": 6.0,
    "hidden_grad": 7.0,
    "full_grad": 15.0,
    "attention_grads": 12.0,
    "result_part": 400.0,
    "middle_back": 11.0,
    "attention_back": 21.7,
    "tokens_back": 8.5,
    "output": 6.0,
}
WORK = 5.5e+07

F32 = jnp.float32
BF16 = jnp.bfloat16
NN = (((1,), (0,)), ((), ()))
NT = (((1,), (1,)), ((), ()))
TN = (((0,), (0,)), ((), ()))


def rounded(value):
    return value.astype(BF16)


def mul(left, right, dims=NN):
    return lax.dot_general(left, right, dims, preferred_element_type=F32)


def xpos_tables():
    place = np.arange(SLOT, dtype=np.float64)[:, None]
    lane = np.arange(128)[None, :]
    index = (lane % HD) // 2
    angle = place * 10000.0 ** (-2.0 * index / HD)
    zeta = (2.0 * index + 0.4 * HD) / (1.4 * HD)
    growth = zeta ** ((place - SLOT // 2) / SCALE_BASE)
    even = lane % 2 == 0
    found = []
    for factor in (growth / math.sqrt(HD), 1.0 / growth):
        found += [
            np.cos(angle) * factor,
            np.where(even, -np.sin(angle), 0.0) * factor,
            np.where(even, 0.0, np.sin(angle)) * factor,
        ]
    return jnp.asarray(np.tile(np.stack(found), (1, 2, 1)).astype(np.float32))


def rotate(value, tables, base, sign):
    up = pltpu.roll(value, 127, axis=1)
    down = pltpu.roll(value, 1, axis=1)
    turned = up * tables[base + 1] + down * tables[base + 2]
    return value * tables[base] + turned if sign > 0 else value * tables[base] - turned


def columns_of(parts):
    return jnp.transpose(parts)


def rows_of(columns):
    size = columns[0].shape[0]
    lane = lax.broadcasted_iota(jnp.int32, (size, 128), 1)
    tile = jnp.zeros((size, 128), F32)
    for at, column in enumerate(columns):
        tile = jnp.where(lane == at, column, tile)
    return jnp.transpose(tile)[:8]


def norm_parts(value):
    mean = jnp.mean(value, axis=-1, keepdims=True)
    var = jnp.mean(value * value, axis=-1, keepdims=True) - mean * mean
    inverse = lax.rsqrt(var + eps)
    return (value - mean) * inverse, inverse


def sum_rows(value):
    return jnp.sum(value, axis=0, keepdims=True)


def whole(array, **kw):
    rank = array.ndim
    return (array, array.shape, lambda *at: (0,) * rank)


def run(kernel, grid, ins, outs, scratch=(), prefetch=(), after=(), alias=None, limit=56, name=None):
    prefetch = tuple(prefetch)

    def body(*refs):
        refs = list(refs)
        first = len(prefetch) + len(ins)
        del refs[first : first + len(after)]
        kernel(*refs)

    in_specs = []
    for array, block, where in ins:
        if block is None:
            in_specs.append(pl.BlockSpec(memory_space=pl.ANY))
        elif tuple(block) == tuple(array.shape):
            in_specs.append(pl.BlockSpec(block, where, pipeline_mode=pl.Buffered(1)))
        else:
            in_specs.append(pl.BlockSpec(block, where))
    in_specs += [pl.BlockSpec(memory_space=pl.ANY)] * len(after)
    out_specs = [pl.BlockSpec(block, where) for shape, dtype, block, where in outs]
    out_shape = [jax.ShapeDtypeStruct(shape, dtype) for shape, dtype, block, where in outs]
    return pl.pallas_call(
        body,
        grid_spec=pltpu.PrefetchScalarGridSpec(
            num_scalar_prefetch=len(prefetch),
            grid=grid,
            in_specs=in_specs,
            out_specs=out_specs,
            scratch_shapes=list(scratch),
        ),
        out_shape=out_shape,
        input_output_aliases=alias or {},
        compiler_params=pltpu.CompilerParams(
            dimension_semantics=("arbitrary",) * len(grid), vmem_limit_bytes=limit * MEGA
        ),
        cost_estimate=pl.CostEstimate(flops=int(COST[name] * WORK), bytes_accessed=1000, transcendentals=0),
        name=name,
    )(*prefetch, *[array for array, block, where in ins], *after)


def flip(value, bit, size):
    return lax.ppermute(value, "tensor", [(t, t ^ (1 << bit)) for t in range(size)])


def all_pieces(own, bits):
    size = 1 << bits
    return [own] + [lax.ppermute(own, "tensor", [(t, t ^ k) for t in range(size)]) for k in range(1, size)]


class Line:
    def __init__(self):
        self.last = None

    def tie(self, value):
        if self.last is None:
            return value
        return lax.optimization_barrier((value,) + self.last)[0]

    def mark(self, *values):
        self.last = values


class Total:
    def __init__(self, line, parts, bits):
        self.line, self.bits = line, bits
        self.orders = [list(range(bits)), list(range(bits))[::-1]]
        self.left = [[bit for bit in range(bits) if bit != order[0]] for order in self.orders]
        self.keep = [parts[0], parts[2]]
        self.got = [flip(parts[1], self.orders[0][0], 1 << bits), flip(parts[3], self.orders[1][0], 1 << bits)]
        self.step = 1

    def advance(self):
        line, size = self.line, 1 << self.bits
        if self.step == self.bits:
            for half in range(2):
                self.keep[half] = line.tie(self.keep[half]) + self.got[half]
                line.mark(self.keep[half])
            return
        picks = []
        for half in range(2):
            left, bit = self.left[half], self.orders[half][self.step]
            keep, got = self.keep[half], self.got[half]
            cube = (2,) * len(left) + keep.shape[1:]
            axis = len(left) - 1 - left.index(bit)
            shape = (keep.shape[0] // 2,) + keep.shape[1:]
            pick = lambda value, at, cube=cube, axis=axis, shape=shape: lax.index_in_dim(
                value.reshape(cube), at, axis, keepdims=False
            ).reshape(shape)
            send = pick(line.tie(keep), 1) + pick(got, 1)
            line.mark(send)
            picks.append((pick, keep, got))
            self.got[half] = flip(send, bit, size)
            left.remove(bit)
        for half in range(2):
            pick, keep, got = picks[half]
            self.keep[half] = pick(line.tie(keep), 0) + pick(got, 0)
            line.mark(self.keep[half])
        self.step += 1

    def gather(self):
        size = 1 << self.bits
        if self.step == self.bits:
            self.held = [[0], [0]]
            self.step += 1
        else:
            for half in range(2):
                self.keep[half] = jnp.concatenate([self.line.tie(self.keep[half]), self.got[half]], 0)
                self.line.mark(self.keep[half])
                self.held[half] = self.held[half] + [block | self.last[half] for block in self.held[half]]
        self.last = [1 << self.orders[half].pop() for half in range(2)]
        self.got = [flip(self.keep[half], self.last[half].bit_length() - 1, size) for half in range(2)]

    def pieces(self):
        arrays, where = [], []
        for half in range(2):
            arrays += [self.keep[half], self.got[half]]
            found = {block: (2 * half, at) for at, block in enumerate(self.held[half])}
            found.update({block | self.last[half]: (2 * half + 1, at) for at, block in enumerate(self.held[half])})
            where.append(found)
        return arrays, where


class Ring:
    def __init__(self, line, first, rest, size):
        self.line, self.rest, self.size = line, rest, size
        self.step = 0
        self.got = self.send(first)

    def send(self, value):
        return lax.ppermute(value, "dp", [(d, (d + 2) % self.size) for d in range(self.size)])

    def advance(self):
        value = self.line.tie(self.rest)[self.step] + self.got
        self.line.mark(value)
        self.step += 1
        if self.step < self.size // 2 - 1:
            self.got = self.send(value)
        return value


def butterfly(value, bits):
    for bit in range(bits):
        value = value + flip(value, bit, 1 << bits)
    return value


def tree_sum(value):
    while value.shape[0] > 1:
        value = value.reshape((value.shape[0] // 2, 2) + value.shape[1:])
        value = value[:, 0] + value[:, 1]
    return value[0]


class Small:
    def __init__(self, own, bits):
        self.bits, self.bit, self.held = bits, 0, [own]
        self.got = None
        self.step()

    def step(self):
        if self.got is not None:
            many = len(self.held)
            self.held = self.held + [self.got[at] for at in range(many)]
        if self.bit < self.bits:
            self.got = flip(jnp.stack(self.held), self.bit, 1 << self.bits)
            self.bit += 1

    def pieces(self):
        while len(self.held) < 1 << self.bits:
            self.step()
        return self.held


def both_vectors(pieces):
    level = [piece[8:] for piece in pieces]
    while len(level) > 1:
        level = [level[at] + level[at + 1] for at in range(0, len(level), 2)]
    many = D // level[0].shape[1]
    return jnp.stack([level[0][:many].reshape(-1), level[0][4 : 4 + many].reshape(-1)])


def combine(pieces, block, blocks):
    level = [pieces[other][:8, (block ^ other) * SLOT : (block ^ other) * SLOT + SLOT] for other in range(blocks)]
    while len(level) > 1:
        level = [level[at] + level[at + 1] for at in range(0, len(level), 2)]
    return level[0]


def attention_scores(query, both_keys, length):
    scores = mul(query, both_keys, NT)
    row = lax.broadcasted_iota(jnp.int32, scores.shape, 0)
    place = lax.broadcasted_iota(jnp.int32, scores.shape, 1) % SLOT
    scores = jnp.where((place <= row) & (place < IMG + length), scores, masked_score)
    parts = []
    for at in range(2):
        part = scores[:, at * SLOT : (at + 1) * SLOT]
        expd = jnp.exp(part - jnp.max(part, axis=-1, keepdims=True))
        parts.append(expd / jnp.sum(expd, axis=-1, keepdims=True))
    return parts


def split_heads(value, mask):
    return jnp.concatenate([value * mask[0:1], value * mask[1:2]], axis=0)


def store_parts(refs, value, step, steps, only=None):
    left_keep, left_send, right_keep, right_send = refs
    left_keep[0] = value[:SLOT, :HALF]
    left_send[0] = value[SLOT:, :HALF]

    @pl.when(step < steps // 2)
    def _():
        right_keep[0] = value[:SLOT, HALF:]
        right_keep[1] = value[SLOT:, HALF:]

    @pl.when(step >= steps // 2)
    def _():
        right_send[0] = value[:SLOT, HALF:]
        right_send[1] = value[SLOT:, HALF:]


def part_outs(blocks):
    half = blocks // 2
    steps = blocks // 2
    shape = (half, SLOT, HALF)
    low = max(steps // 2, 1)
    return [
        (shape, F32, (1, SLOT, HALF), lambda s, *_: (s, 0, 0)),
        (shape, F32, (1, SLOT, HALF), lambda s, *_: (s, 0, 0)),
        (shape, F32, (2, SLOT, HALF), lambda s, *_: (jnp.minimum(s, low - 1), 0, 0)),
        (shape, F32, (2, SLOT, HALF), lambda s, *_: (jnp.maximum(s - steps // 2, 0), 0, 0)),
    ]


def front(order, lengths, tokens, gain, shift, weight, bias, tables, mask, mix_gain, uw_rows, out_weight, after=()):
    blocks = order.shape[0]
    steps = blocks // 2
    width = weight.shape[2]
    groups = width // 128
    rows = blocks * SLOT

    def kernel(order_ref, length_ref, x0, x1, g, b, w, wb, tab, msk, mg, uwr, ow, own, first, qkv, mixed, small, *parts_uw):
        step = pl.program_id(0)
        parts, uw = parts_uw[:4], parts_uw[4]

        @pl.when(step == 0)
        def _():
            found = mul(uwr[...], ow[...])
            uw[0:1] = found[0:1] + found[1:2] + found[2:3]
            uw[1:2] = found[3:4] + found[4:5] + found[5:6]
            small[8:] = jnp.zeros((8, rows), F32)
            for at in range(D // rows):
                c = slice(at * rows, at * rows + rows)
                small[8 + at : 9 + at] = uw[0:1, c]
                small[12 + at : 13 + at] = uw[1:2, c]

        x = jnp.concatenate([x0[0], x1[0]], axis=0)
        own[...] = x
        hat, _ = norm_parts(x.astype(F32))
        one = rounded(hat * g[...] + b[...])
        first[...] = one
        for c in range(3):
            proj = mul(one, w[c]) + wb[c : c + 1]
            for group in range(groups):
                part = proj[:, group * 128 : group * 128 + 128]
                if c < 2:
                    part = rotate(part, tab, 3 * c, 1)
                at = c * width + group * 128
                qkv[:, at : at + 128] = rounded(part)
        for pair in range(2):
            r = slice(pair * SLOT, pair * SLOT + SLOT)
            length = length_ref[order_ref[2 * step + pair]]
            for group in range(groups):
                at = group * 128
                query = qkv[r, at : at + 128]
                keys = split_heads(qkv[r, width + at : width + at + 128], msk)
                values = split_heads(qkv[r, 2 * width + at : 2 * width + at + 128], msk)
                probs = attention_scores(query, keys, length)
                mixed[r, at : at + 128] = mul(rounded(jnp.concatenate(probs, axis=1)), values)
        m = mixed[...]
        total = jnp.sum(m, axis=-1, keepdims=True)
        here = pl.ds(pl.multiple_of(step * 2 * SLOT, 2 * SLOT), 2 * SLOT)
        small[:8, here] = rows_of([total, jnp.sum(m * m, axis=-1, keepdims=True)])
        middle = total * (1.0 / width)
        partial = mul(rounded((m - middle) * mg[...]), ow[...]) + middle * uw[0:1]
        store_parts(parts, partial, step, steps)

    row2 = lambda s, *_: (s, 0)
    pair_of = lambda offset: lambda s, order_ref, length_ref: (order_ref[2 * s + offset], 0, 0)
    return run(
        kernel,
        (steps,),
        [
            (tokens, (1, SLOT, D), pair_of(0)),
            (tokens, (1, SLOT, D), pair_of(1)),
            whole(gain), whole(shift), whole(weight), whole(bias), whole(tables), whole(mask),
            whole(mix_gain), whole(uw_rows), whole(out_weight),
        ],
        [
            ((rows, D), BF16, (2 * SLOT, D), row2),
            ((rows, D), BF16, (2 * SLOT, D), row2),
            ((rows, 3 * width), BF16, (2 * SLOT, 3 * width), row2),
            ((rows, width), F32, (2 * SLOT, width), row2),
            ((16, rows), F32, (16, rows), lambda s, *_: (0, 0)),
        ]
        + part_outs(blocks),
        scratch=[pltpu.VMEM((8, D), F32)],
        prefetch=(order, lengths),
        after=after,
        name="front",
    )


def pieces_in(pieces):
    return [whole(piece) for piece in pieces[0]]


def load_pieces(refs, where, total, step, blocks):
    for block in range(blocks):

        @pl.when(step == block)
        def _(block=block):
            for half in range(2):
                array, at = where[half][block]
                total[:, half * HALF : half * HALF + HALF] = refs[array][at]


def middle_norm(own, pieces, sums, uw, out_bias, gain, shift, after=()):
    blocks = len(pieces[1][0])
    rows = blocks * SLOT

    def kernel(*refs):
        x, parts, stats = refs[0], refs[1:5], refs[5 : 5 + blocks]
        uw_ref, bias, g, b, mid, second, stat, total, tot8 = refs[5 + blocks :]
        step = pl.program_id(0)
        load_pieces(parts, pieces[1], total, step, blocks)
        for block in range(blocks):

            @pl.when(step == block)
            def _(block=block):
                tot8[...] = combine(stats, block, blocks)

        cols = columns_of(tot8[...])
        mean = cols[:, 0:1] * (1.0 / D)
        inverse = lax.rsqrt(cols[:, 1:2] * (1.0 / D) - mean * mean + eps)
        branch = inverse * (total[...] - mean * uw_ref[0:1]) + uw_ref[1:2]
        value = x[...].astype(F32) + branch + bias[...]
        mid[...] = value
        hat, _ = norm_parts(value)
        second[...] = rounded(hat * g[...] + b[...])
        lane = lax.broadcasted_iota(jnp.int32, (SLOT, 128), 1)
        stat[...] = jnp.where(lane == 0, mean, inverse)

    row = lambda k, *_: (k, 0)
    return run(
        kernel,
        (blocks,),
        [(own, (SLOT, D), row)]
        + pieces_in(pieces)
        + [whole(part) for part in sums]
        + [whole(uw), whole(out_bias), whole(gain), whole(shift)],
        [
            ((rows, D), F32, (SLOT, D), row),
            ((rows, D), BF16, (SLOT, D), row),
            ((rows, 128), F32, (SLOT, 128), row),
        ],
        scratch=[pltpu.VMEM((SLOT, D), F32), pltpu.VMEM((8, SLOT), F32)],
        after=after,
        name="middle_norm",
    )


def hidden_back(cots, down_weight):
    many, rows, units = len(cots), cots[0].shape[0], down_weight.shape[0]
    tile = min(512, units)

    def kernel(*refs):
        w, out = refs[many:]
        for at in range(many):
            out[at * rows : at * rows + rows] = rounded(mul(refs[at][...], w[...], NT))

    return run(
        kernel,
        (units // tile,),
        [whole(cot) for cot in cots] + [(down_weight, (tile, D), lambda j: (j, 0))],
        [((many * rows, units), BF16, (many * rows, tile), lambda j: (0, j))],
        name="hidden_back",
    )[0]


def hidden_front(chunk, second, up_weight, up_bias, back, gain, after=()):
    rows, units = second.shape[0], up_weight.shape[1]
    tile = 512
    steps = units // tile

    def part_of(c, s_ref, w, b, hb, g, act, slp):
        hidden = mul(s_ref[...], w[:, c]) + b[:, c]
        tail = jnp.exp(-0.5 * hidden * hidden)
        t = 1.0 / (1.0 + (0.3275911 * root_half) * jnp.abs(hidden))
        poly = 1.061405429 * t - 1.453152027
        poly = poly * t + 1.421413741
        poly = poly * t - 0.284496736
        poly = poly * t + 0.254829592
        half = 0.5 * poly * t * tail
        phi = jnp.where(hidden >= 0.0, 1.0 - half, half)
        active = hidden * phi
        act[:, c] = rounded(active)
        slp[:, c] = rounded(phi + hidden * (inv_root_two_pi * tail))
        scaled = hb[:, c].astype(F32) * g[:, c]
        return [value[:, :128] + value[:, 128:] for value in (active, active * active, scaled, scaled * active)]

    def kernel(s_ref, w, b, hb, g, act, slp, sums, acc):
        step = pl.program_id(0)
        found = [part_of(slice(at, at + 256), s_ref, w, b, hb, g, act, slp) for at in range(0, tile, 256)]

        @pl.when(step == 0)
        def _():
            for at in range(4):
                acc[at] = found[0][at] + found[1][at]

        @pl.when(step > 0)
        def _():
            for at in range(4):
                acc[at] += found[0][at] + found[1][at]

        @pl.when(step == steps - 1)
        def _():
            for block in range(rows // SLOT):
                r = slice(block * SLOT, block * SLOT + SLOT)
                sums[:, r] = rows_of([jnp.sum(acc[at, r], axis=-1, keepdims=True) for at in range(4)])

    return run(
        kernel,
        (steps,),
        [
            whole(second),
            (up_weight, (D, tile), lambda j: (0, j)),
            (up_bias, (1, tile), lambda j: (0, j)),
            (back, (rows, tile), lambda j: (chunk, j)),
            (gain, (1, tile), lambda j: (0, j)),
        ],
        [
            ((rows, units), BF16, (rows, tile), lambda j: (0, j)),
            ((rows, units), BF16, (rows, tile), lambda j: (0, j)),
            ((8, rows), F32, (8, rows), lambda j: (0, 0)),
        ],
        scratch=[pltpu.VMEM((4, rows, 128), F32)],
        after=after,
        name="hidden_front",
    )


def hidden_mid(chunk, active, slope, back, sums, gain, shift):
    blocks = len(sums)
    rows, units = active.shape

    def kernel(act, slp, hb, *refs):
        stats = refs[:blocks]
        g, b, low, grad, vecs, tot8 = refs[blocks:]
        step = pl.program_id(0)
        for block in range(blocks):

            @pl.when(step == block)
            def _(block=block):
                tot8[...] = combine(stats, block, blocks)

        cols = columns_of(tot8[...]) * (1.0 / FF)
        mean = cols[:, 0:1]
        inverse = lax.rsqrt(cols[:, 1:2] - mean * mean + eps)
        one = cols[:, 2:3]
        two = inverse * (cols[:, 3:4] - mean * one)
        for at in range(0, units, 256):
            c = slice(at, at + 256)
            hat = (act[:, c].astype(F32) - mean) * inverse
            low[:, c] = rounded(hat * g[:, c] + b[:, c])
            raw = hb[:, c].astype(F32)
            grown = rounded(inverse * (raw * g[:, c] - one - hat * two) * slp[:, c].astype(F32))
            grad[:, c] = grown
            vecs[0, 0:1, c] = sum_rows(raw * hat)
            vecs[0, 1:2, c] = sum_rows(raw)
            vecs[0, 2:3, c] = sum_rows(grown.astype(F32))

    row = lambda k: (k, 0)
    return run(
        kernel,
        (blocks,),
        [
            (active, (SLOT, units), row),
            (slope, (SLOT, units), row),
            (back, (SLOT, units), lambda k: (chunk * blocks + k, 0)),
        ]
        + [whole(part) for part in sums]
        + [whole(gain), whole(shift)],
        [
            ((rows, units), BF16, (SLOT, units), row),
            ((rows, units), BF16, (SLOT, units), row),
            ((blocks, 8, units), F32, (1, 8, units), lambda k: (k, 0, 0)),
        ],
        scratch=[pltpu.VMEM((8, SLOT), F32)],
        name="hidden_mid",
    )


def hidden_grad(grad, up_weight):
    rows, units = grad.shape
    blocks = rows // SLOT
    tile = 512
    steps = D // tile
    half = steps // 2

    def kernel(gr, w, left_keep, left_send, right_keep, right_send):
        step = pl.program_id(0)
        value = mul(gr[...], w[...], NT)

        @pl.when(step < half)
        def _():
            for block in range(blocks):
                r = slice(block * SLOT, block * SLOT + SLOT)
                (left_send if block & 1 else left_keep)[block // 2] = value[r]

        @pl.when(step >= half)
        def _():
            for block in range(blocks):
                r = slice(block * SLOT, block * SLOT + SLOT)
                (right_send if block >= blocks // 2 else right_keep)[block % (blocks // 2)] = value[r]

    shape = (blocks // 2, SLOT, HALF)
    block_shape = (blocks // 2, SLOT, tile)
    lefts = lambda j: (0, 0, jnp.minimum(j, half - 1))
    rights = lambda j: (0, 0, jnp.maximum(j - half, 0))
    return run(
        kernel,
        (steps,),
        [whole(grad), (up_weight, (tile, units), lambda j: (j, 0))],
        [
            (shape, F32, block_shape, lefts),
            (shape, F32, block_shape, lefts),
            (shape, F32, block_shape, rights),
            (shape, F32, block_shape, rights),
        ],
        name="hidden_grad",
    )


def result_part(order, lows, down_weight):
    pairs = order.shape[0]
    units = down_weight.shape[0]
    many = len(lows)
    rows = lows[0].shape[0]
    each = rows // SLOT
    tile = 256

    def kernel(order_ref, *refs):
        w, out = refs[many:]
        for at in range(many):
            value = mul(refs[at][...], w[...])
            for block in range(each):
                out[order_ref[at * each + block]] = value[block * SLOT : block * SLOT + SLOT]

    return run(
        kernel,
        (D // tile,),
        [whole(low) for low in lows] + [(down_weight, (units, tile), lambda j, *_: (0, j))],
        [((pairs, SLOT, D), F32, (pairs, SLOT, tile), lambda j, *_: (0, 0, j))],
        prefetch=(order,),
        name="result_part",
    )[0]


def middle_back(own, cot, pieces, middle, stat, uw, out_bias, gain, after=()):
    blocks = len(pieces[1][0])
    rows = blocks * SLOT

    def kernel(*refs):
        x, c, parts = refs[0], refs[1], refs[2:6]
        mid, st, uw_ref, bias, g, grad, low, stat2, vecs, total = refs[6:]
        load_pieces(parts, pieces[1], total, pl.program_id(0), blocks)
        value = mid[...]
        hat, inverse = norm_parts(value)
        sec = total[...]
        scaled = sec * g[...]
        up = c[...].astype(F32)
        out = up + inverse * (
            scaled
            - jnp.mean(scaled, axis=-1, keepdims=True)
            - hat * jnp.mean(scaled * hat, axis=-1, keepdims=True)
        )
        grad[...] = out
        lowered = rounded(out)
        low[...] = lowered
        low32 = lowered.astype(F32)
        one = jnp.mean(low32 * uw_ref[0:1], axis=-1, keepdims=True)
        moved = value - x[...].astype(F32) - bias[...] - uw_ref[1:2]
        two = jnp.mean(low32 * moved, axis=-1, keepdims=True)
        lane = lax.broadcasted_iota(jnp.int32, (SLOT, 128), 1)
        stat2[...] = jnp.where(lane == 2, one, jnp.where(lane == 3, two, st[...]))
        vecs[0, 0:1] = sum_rows(sec * hat)
        vecs[0, 1:2] = sum_rows(sec)
        vecs[0, 2:3] = sum_rows(out)
        vecs[0, 3:4] = sum_rows(up)

    row = lambda k, *_: (k, 0)
    return run(
        kernel,
        (blocks,),
        [(own, (SLOT, D), row), (cot, (SLOT, D), row)]
        + pieces_in(pieces)
        + [(middle, (SLOT, D), row), (stat, (SLOT, 128), row), whole(uw), whole(out_bias), whole(gain)],
        [
            ((rows, D), F32, (SLOT, D), row),
            ((rows, D), BF16, (SLOT, D), row),
            ((rows, 128), F32, (SLOT, 128), row),
            ((blocks, 8, D), F32, (1, 8, D), lambda k, *_: (k, 0, 0)),
        ],
        scratch=[pltpu.VMEM((SLOT, D), F32)],
        after=after,
        name="middle_back",
    )


def attention_back(order, lengths, low, stat, mixed, qkv, own, mix_gain, mix_shift, out_weight, weight, tables, mask, after=()):
    blocks = order.shape[0]
    steps = blocks // 2
    width = out_weight.shape[0]
    groups = width // 128
    rows = blocks * SLOT

    def kernel(
        order_ref, length_ref, low_ref, st, mx, qkv_ref, x, mg, ms, ow, w, tab, msk,
        mix_low, dproj, vecs, wide, left_keep, left_send, right_keep, right_send, dmixed,
    ):
        step = pl.program_id(0)
        mean, inverse, one, two = (st[:, at : at + 1] for at in range(4))
        back = mul(low_ref[...], ow[...], NT)
        hat = (mx[...] - mean) * inverse
        mix_low[...] = rounded(hat * mg[...] + ms[...])
        dmixed[...] = rounded(inverse * (back * mg[...] - one - hat * two))
        vecs[0, 0:1, :width] = sum_rows(back * hat)
        vecs[0, 1:2, :width] = sum_rows(back)
        first_half = lax.broadcasted_iota(jnp.int32, (SLOT, 128), 1) < HD
        for pair in range(2):
            r = slice(pair * SLOT, pair * SLOT + SLOT)
            length = length_ref[order_ref[2 * step + pair]]
            for group in range(groups):
                at = group * 128
                query = qkv_ref[r, at : at + 128]
                keys = split_heads(qkv_ref[r, width + at : width + at + 128], msk)
                values = split_heads(qkv_ref[r, 2 * width + at : 2 * width + at + 128], msk)
                grad = dmixed[r, at : at + 128]
                probs = attention_scores(query, keys, length)
                dprobs = mul(grad, values, NT)
                dscores = []
                for i in range(2):
                    dp = dprobs[:, i * SLOT : (i + 1) * SLOT]
                    carried = jnp.sum(probs[i] * dp, axis=-1, keepdims=True)
                    dscores.append(rounded(probs[i] * (dp - carried)))
                dscores = jnp.concatenate(dscores, axis=1)
                dquery = mul(dscores, keys)
                dkey = mul(dscores, query, TN)
                dvalue = mul(rounded(jnp.concatenate(probs, axis=1)), grad, TN)
                dkey = jnp.where(first_half, dkey[:SLOT], dkey[SLOT:])
                dvalue = jnp.where(first_half, dvalue[:SLOT], dvalue[SLOT:])
                tabs = [tab[i, :SLOT] for i in range(6)]
                dproj[r, at : at + 128] = rounded(rotate(dquery, tabs, 0, -1))
                dproj[r, width + at : width + at + 128] = rounded(rotate(dkey, tabs, 3, -1))
                dproj[r, 2 * width + at : 2 * width + at + 128] = rounded(dvalue)
        vecs[0, 2:3] = sum_rows(dproj[...].astype(F32))
        partial = mul(dproj[:, :width], w[0], NT)
        for c in (1, 2):
            partial += mul(dproj[:, c * width : (c + 1) * width], w[c], NT)
        pre_hat, _ = norm_parts(x[...].astype(F32))
        grown = partial * pre_hat
        wide[0, 0:1] = sum_rows(grown[:SLOT]) + sum_rows(grown[SLOT:])
        wide[0, 1:2] = sum_rows(partial[:SLOT]) + sum_rows(partial[SLOT:])
        store_parts((left_keep, left_send, right_keep, right_send), partial, step, steps)

    row2 = lambda s, *_: (s, 0)
    return run(
        kernel,
        (steps,),
        [
            (low, (2 * SLOT, D), row2),
            (stat, (2 * SLOT, 128), row2),
            (mixed, (2 * SLOT, width), row2),
            (qkv, (2 * SLOT, 3 * width), row2),
            (own, (2 * SLOT, D), row2),
            whole(mix_gain), whole(mix_shift), whole(out_weight), whole(weight), whole(tables), whole(mask),
        ],
        [
            ((rows, width), BF16, (2 * SLOT, width), row2),
            ((rows, 3 * width), BF16, (2 * SLOT, 3 * width), row2),
            ((steps, 8, 3 * width), F32, (1, 8, 3 * width), lambda s, *_: (s, 0, 0)),
            ((steps, 8, D), F32, (1, 8, D), lambda s, *_: (s, 0, 0)),
        ]
        + part_outs(blocks),
        scratch=[pltpu.VMEM((2 * SLOT, width), BF16)],
        prefetch=(order, lengths),
        after=after,
        name="attention_back",
    )


def tokens_back(order, own, grad, pieces, gain, before, pairs, after=()):
    blocks = len(pieces[1][0])

    def kernel(order_ref, x, gr, *refs):
        parts = refs[:4]
        g = refs[4]
        out, total = refs[-2:]
        load_pieces(parts, pieces[1], total, pl.program_id(0), blocks)
        hat, inverse = norm_parts(x[...].astype(F32))
        scaled = total[...] * g[...]
        out[0] = gr[...] + inverse * (
            scaled
            - jnp.mean(scaled, axis=-1, keepdims=True)
            - hat * jnp.mean(scaled * hat, axis=-1, keepdims=True)
        )

    row = lambda k, *_: (k, 0)
    ins = [(own, (SLOT, D), row), (grad, (SLOT, D), row)] + pieces_in(pieces) + [whole(gain)]
    alias = None
    if before is not None:
        alias = {1 + len(ins): 0}
        ins = ins + [(before, None, None)]
    return run(
        kernel,
        (blocks,),
        ins,
        [((pairs, SLOT, D), F32, (1, SLOT, D), lambda k, o: (o[k], 0, 0))],
        scratch=[pltpu.VMEM((SLOT, D), F32)],
        prefetch=(order,),
        after=after,
        alias=alias,
        name="tokens_back",
    )[0]


def output_of(order, middle, result, bias, before, after=()):
    blocks = order.shape[0]

    def kernel(order_ref, mid, res, b, *refs):
        out = refs[-1]
        out[0] = rounded(mid[...] + res[0] + b[...])

    ins = [
        (middle, (SLOT, D), lambda k, *_: (k, 0)),
        (result, (1, SLOT, D), lambda k, o: (o[k], 0, 0)),
        whole(bias),
    ]
    alias = None
    if before is not None:
        alias = {1 + len(ins): 0}
        ins = ins + [(before, None, None)]
    return run(
        kernel,
        (blocks,),
        ins,
        [(result.shape, BF16, (1, SLOT, D), lambda k, o: (o[k], 0, 0))],
        prefetch=(order,),
        after=after,
        alias=alias,
        name="output",
    )[0]


def attention_grads(ids, firsts, dprojs, lows, mixes, got=None):
    count, many = ids.shape[0], len(firsts)
    rows = firsts[0].shape[0]
    wide, tall = dprojs[0].shape[1], mixes[0].shape[1]
    block = D // (2 * count)
    shape = (block, wide + tall)

    def kernel(ids_ref, *refs):
        parts = [refs[at * many : (at + 1) * many] for at in range(4)]
        outs = refs[4 * many + (got is not None) :]
        total = []
        for left, right in ((parts[0], parts[1]), (parts[2], parts[3])):
            value = mul(left[0][...], right[0][...], TN)
            for at in range(1, many):
                value += mul(left[at][...], right[at][...], TN)
            total.append(value)
        if got is None:
            outs[0][0, :, :wide] = total[0]
            outs[0][0, :, wide:] = total[1]
            return
        more = refs[4 * many]
        step = pl.program_id(0)

        @pl.when(step == 0)
        def _():
            outs[0][:, :wide] = total[0] + more[0, :, :wide]
            outs[0][:, wide:] = total[1] + more[0, :, wide:]

        @pl.when(step > 0)
        def _():
            outs[1][0, :, :wide] = total[0] + more[0, :, :wide]
            outs[1][0, :, wide:] = total[1] + more[0, :, wide:]

    fixed = lambda i, *_: (0, 0)
    moving = lambda i, ids_ref: (0, ids_ref[i])
    lead = lambda i, *_: (i, 0, 0)
    ins = [(left, (rows, block), moving) for left in firsts] + [(right, (rows, wide), fixed) for right in dprojs]
    ins += [(left, (rows, block), moving) for left in lows] + [(right, (rows, tall), fixed) for right in mixes]
    if got is None:
        outs = [((count,) + shape, F32, (1,) + shape, lead)]
    else:
        ins += [(got, (1,) + shape, lead)]
        outs = [
            (shape, F32, shape, fixed),
            ((count - 1,) + shape, F32, (1,) + shape, lambda i, *_: (jnp.maximum(i - 1, 0), 0, 0)),
        ]
    return run(kernel, (count,), ins, outs, prefetch=(ids,), name="attention_grads")


def full_grad(lefts, rights):
    rows, many, block = lefts[0].shape[0], len(lefts), 512
    wide, tall = lefts[0].shape[1], rights[0].shape[1]

    def kernel(*refs):
        left, right, out = refs[:many], refs[many : 2 * many], refs[2 * many]
        value = mul(left[0][...], right[0][...], TN)
        for at in range(1, many):
            value += mul(left[at][...], right[at][...], TN)
        out[...] = value

    ins = [(left, (rows, block), lambda i: (0, i)) for left in lefts]
    ins += [(right, (rows, tall), lambda i: (0, 0)) for right in rights]
    return run(
        kernel, (wide // block,), ins, [((wide, tall), F32, (block, tall), lambda i: (i, 0))], name="full_grad"
    )[0]


def steps_of(totals, bits, done, until):
    done = list(done)

    def step(at):
        if done[at] < bits:
            totals[at].advance()
        else:
            totals[at].gather()
        done[at] += 1
        if done[at] == bits and until == 2 * bits:
            totals[at].gather()
            done[at] += 1

    limits = [until] + [until if until == 2 * bits else bits - 1] * (len(totals) - 1)
    while any(have < limit for have, limit in zip(done, limits)):
        for at in range(len(totals)):
            if done[at] < limits[at]:
                step(at)


def split_rows(value):
    found = []
    for _ in range(3):
        part = lax.reduce_precision(value, 8, 7)
        found.append(part.astype(BF16))
        value = value - part
    return found


def body(
    tokens,
    lengths,
    cotangent,
    pre_gain,
    pre_shift,
    qkv_weight,
    qkv_bias,
    mix_gain,
    mix_shift,
    out_weight,
    out_bias,
    ffn_gain,
    ffn_shift,
    up_weight,
    up_bias,
    hid_gain,
    hid_shift,
    down_weight,
    down_bias,
):
    pairs = lengths.shape[0]
    blocks = lax.axis_size("tensor")
    bits = blocks.bit_length() - 1
    chunks = pairs // blocks
    width = qkv_weight.shape[2]
    mine = lax.axis_index("tensor").astype(jnp.int32)
    orders = [jnp.arange(c * blocks, (c + 1) * blocks, dtype=jnp.int32) ^ mine for c in range(chunks)]
    tokens3 = tokens.reshape(pairs, SLOT, D)
    row = lambda v: v.reshape(1, -1)
    pre_gain, pre_shift, mix_gain, mix_shift = map(row, (pre_gain, pre_shift, mix_gain, mix_shift))
    out_bias, ffn_gain, ffn_shift, up_bias = map(row, (out_bias, ffn_gain, ffn_shift, up_bias))
    hid_gain, hid_shift, down_bias = map(row, (hid_gain, hid_shift, down_bias))
    tables = xpos_tables()
    lane = np.arange(128)[None, :] < HD
    mask = jnp.asarray(np.concatenate([lane, ~lane], 0).astype(np.float32)).astype(BF16)
    zero = jnp.zeros((2, width), BF16)
    uw_rows = jnp.concatenate(split_rows(mix_gain) + split_rows(mix_shift) + [zero], 0)

    line = Line()
    dp_size = lax.axis_size("dp")
    place = lax.axis_index("dp").astype(jnp.int32)
    count = dp_size // 2
    around = lax.rem(place // 2 + count - 1 - jnp.arange(count, dtype=jnp.int32), count)
    mine_ids, other_ids = 2 * around + lax.rem(place, 2), 2 * around + 1 - lax.rem(place, 2)

    def full(lefts, rights):
        grad = full_grad([line.tie(lefts[0])] + lefts[1:], rights)
        line.mark(grad)
        return grad

    every = lambda items, name: [item[name] for item in items]

    ones, twos, threes = [], [], []
    for c in range(chunks):
        found = front(
            orders[c], lengths, line.tie(tokens3), pre_gain, pre_shift, qkv_weight, qkv_bias, tables, mask, mix_gain, uw_rows,
            out_weight,
        )
        own, first, qkv, mixed, small = found[:5]
        one = dict(own=own, first=first, qkv=qkv, mixed=mixed, parts=found[5:])
        line.mark(small)
        one["small"] = small
        if c == 0:
            one["total"] = Total(line, one["parts"], bits)
            one["sums"] = Small(small, bits)
        ones.append(one)
    sums0 = ones[0]["sums"]
    if bits > 1:
        ones[0]["total"].advance()
    for c in range(1, chunks):
        ones[c]["total"] = Total(line, [line.tie(part) for part in ones[c]["parts"]], bits)
    sums0.held[0] = line.tie(sums0.held[0])
    sums0.step()
    cot3 = cotangent.reshape(pairs, SLOT, D)
    cots = []
    for c in range(chunks):
        cots.append(line.tie(cot3)[orders[c]].reshape(-1, D))
        line.mark(cots[-1])
    totals = every(ones, "total")
    line.mark(*line.last, *sums0.pieces())
    for step in range(1, bits):
        totals[0].advance()
    back = hidden_back([line.tie(cots[0])] + cots[1:], down_weight)
    line.mark(back)
    for one in ones[1:]:
        one["sums"] = Small(line.tie(one["small"]), bits)
    done = [bits] + [0] * (chunks - 1)
    steps_of(totals, bits, done, 2 * bits - 1)
    for one in ones[1:]:
        line.mark(*line.last, one["sums"].got)
        one["sums"].step()
    uw_total = both_vectors(sums0.pieces())

    def mid_of(c):
        two = twos[c]
        low, grad, vecs = hidden_mid(c, line.tie(two["active"]), two["slope"], back, two["sums"], hid_gain, hid_shift)
        two.update(low=low, grad=grad, vecs=functools.reduce(jnp.add, [vecs[k] for k in range(blocks)]))
        line.mark(vecs)

    def hidden_of(c):
        parts = hidden_grad(line.tie(twos[c]["grad"]), up_weight)
        line.mark(parts[0])
        return parts

    totals[0].gather()
    for other in ones[1:]:
        line.mark(*line.last, *other["sums"].pieces())
    for c in range(chunks):
        one = ones[c]
        mid, second, stat = middle_norm(
            line.tie(one["own"]), totals[c].pieces(), one["sums"].pieces(), uw_total, out_bias, ffn_gain, ffn_shift
        )
        line.mark(stat)
        if c == 0:
            for total in totals[1:]:
                total.advance()
                total.gather()
        active, slope, sums = hidden_front(c, line.tie(second), up_weight, up_bias, back, hid_gain)
        line.mark(sums)
        twos.append(dict(middle=mid, second=second, stat=stat, active=active, slope=slope, sums=all_pieces(sums, bits)))
        if c == 0:
            line.mark(sums, *twos[0]["sums"][1:])
            for total in totals[1:]:
                for step in range(1, bits):
                    total.gather()
        else:
            twos[0]["total"].advance()
            line.mark(*line.last, *twos[c]["sums"][1:])
        mid_of(c)
        if c > 0:
            line.mark(*line.last, *twos[0]["total"].got)
        if c == 0 and chunks > 1:
            twos[0]["total"] = Total(line, hidden_of(0), bits)
    lows = every(twos, "low")
    down_grad = full(lows, cots)
    down_part = lax.psum_scatter(down_grad, "dp", scatter_dimension=1, tiled=True)
    up_grad = full(every(twos, "second"), every(twos, "grad"))
    up_part = lax.psum_scatter(up_grad, "dp", scatter_dimension=0, tiled=True)
    if chunks > 1:
        for step in range(1, bits):
            twos[0]["total"].advance()
        twos[0]["total"].gather()
        parts = [None] + [hidden_of(c) for c in range(1, chunks)]
    else:
        twos[0]["total"] = Total(line, hidden_of(0), bits)
        for step in range(bits):
            twos[0]["total"].advance()
        twos[0]["total"].gather()
    for step in range(1, bits):
        twos[0]["total"].gather()
    for c in range(1, chunks):
        twos[c]["total"] = Total(line, [line.tie(part) for part in parts[c]], bits)
    totals = every(twos, "total")
    result = result_part(jnp.concatenate(orders), [line.tie(lows[0])] + lows[1:], down_weight)
    line.mark(result)
    result = lax.psum(line.tie(result), "tensor")

    for c in range(chunks):
        one, two = ones[c], twos[c]
        grad, low, stat2, vecs = middle_back(
            line.tie(one["own"]), cots[c], two["total"].pieces(), two["middle"], two["stat"], uw_total, out_bias, ffn_gain
        )
        line.mark(stat2)
        if c == 0:
            for total in totals[1:]:
                total.advance()
        found = attention_back(
            orders[c], lengths, line.tie(low), stat2, one["mixed"], one["qkv"], one["own"], mix_gain, mix_shift, out_weight,
            qkv_weight, tables, mask,
        )
        line.mark(found[2])
        three = dict(grad=grad, low=low, vecs=tree_sum(vecs), mix_low=found[0], dproj=found[1])
        three["narrow"] = tree_sum(found[2])
        three["wide"] = tree_sum(found[3])
        parts = found[4:]
        if c == 0 and chunks > 1:
            for total in totals[1:]:
                for step in range(1, bits):
                    total.advance()
                for step in range(bits):
                    total.gather()
            parts = [line.tie(part) for part in parts]
        three["total"] = Total(line, parts, bits)
        threes.append(three)

    first, last = threes[0]["total"], threes[-1]["total"]
    if chunks > 1:
        first.advance()
    add = lambda items, name, size: functools.reduce(jnp.add, [item[name] for item in items])[:size]
    pad = lambda v: jnp.pad(v, ((0, 0), (0, D - v.shape[1])))
    wide = add(threes, "wide", 2)
    got = flip(wide, 0, blocks)
    grads_of = lambda ids, sent: attention_grads(
        ids, [line.tie(ones[0]["first"])] + every(ones, "first")[1:], every(threes, "dproj"), every(threes, "low"),
        every(threes, "mix_low"), sent,
    )
    sent = grads_of(other_ids, None)[0]
    line.mark(sent)
    sent = lax.ppermute(sent, "dp", [(d, d ^ 1) for d in range(dp_size)])
    line.mark(*line.last, down_part)
    ring_first, ring_rest = grads_of(mine_ids, sent)
    line.mark(ring_rest)
    ring = Ring(line, ring_first, ring_rest, dp_size)
    for step in range(1 if chunks > 1 else 0, bits):
        first.advance()
    first.gather()
    if chunks > 1:
        last.advance()
    for step in range(1, bits):
        first.gather()
    attention_part = ring.advance()
    if chunks > 1:
        for step in range(1, bits):
            last.advance()
        last.gather()
    for bit in range(1, bits):
        wide = line.tie(wide) + got
        got = flip(wide, bit, blocks)
        line.mark(wide)
    if chunks > 1:
        line.mark(*line.last, *last.got)
    hop = lambda v, bit: lax.ppermute(v, "dp", [(d, d ^ (1 << bit)) for d in range(dp_size)])
    dp_bits = dp_size.bit_length() - 1
    tokens_grad, output = None, None
    for c in range(chunks):
        tokens_grad = tokens_back(
            orders[c], line.tie(ones[c]["own"]), threes[c]["grad"], threes[c]["total"].pieces(), pre_gain, tokens_grad, pairs
        )
        line.mark(tokens_grad)
        if c == 0:
            wide = line.tie(wide) + got
            vecs = jnp.concatenate(
                [pad(add(twos, "vecs", 3)), add(threes, "vecs", 4), pad(add(threes, "narrow", 3)), wide], 0
            )
            line.mark(vecs)
            got = hop(vecs, 0)
            if chunks > 1:
                for step in range(1, bits):
                    last.gather()
            vecs = line.tie(vecs) + got
            line.mark(vecs)
            got = hop(vecs, 1)
            attention_part = ring.advance()
    for bit in range(2, dp_bits):
        vecs = line.tie(vecs) + got
        line.mark(vecs)
        got = hop(vecs, bit)
    for step in range(2, count - 2):
        attention_part = ring.advance()
    for c in range(chunks):
        output = output_of(orders[c], line.tie(twos[c]["middle"]), result, down_bias, output)
        line.mark(output)
    line.mark(*line.last, up_part)
    attention_part = ring.advance()
    vecs = vecs + got
    hid_vecs, mid_vecs, narrow, wide = vecs[:3], vecs[3:7], vecs[7:10], vecs[10:12]
    qkv_part = jnp.swapaxes(attention_part[:, : 3 * width].reshape(-1, 3, width), 0, 1)
    out_part = jnp.transpose(attention_part[:, 3 * width :])
    units = hid_gain.shape[1]
    return (
        output.reshape(-1, D),
        tokens_grad.reshape(-1, D),
        wide[0],
        wide[1],
        qkv_part,
        narrow[2, : 3 * width].reshape(3, width),
        narrow[0, :width],
        narrow[1, :width],
        out_part,
        mid_vecs[2],
        mid_vecs[0],
        mid_vecs[1],
        up_part,
        hid_vecs[2, :units],
        hid_vecs[0, :units],
        hid_vecs[1, :units],
        down_part,
        mid_vecs[3],
    )


def solution(mesh):
    in_specs = (
        P("dp", None),
        P("dp"),
        P("dp", None),
        P(),
        P(),
        P(None, None, "tensor"),
        P(None, "tensor"),
        P("tensor"),
        P("tensor"),
        P("tensor", None),
        P(),
        P(),
        P(),
        P(None, "tensor"),
        P("tensor"),
        P("tensor"),
        P("tensor"),
        P("tensor", None),
        P(),
    )
    out_specs = (
        P("dp", None),
        P("dp", None),
        P(),
        P(),
        P(None, "dp", "tensor"),
        P(None, "tensor"),
        P("tensor"),
        P("tensor"),
        P("tensor", "dp"),
        P(),
        P(),
        P(),
        P("dp", "tensor"),
        P("tensor"),
        P("tensor"),
        P("tensor"),
        P("tensor", "dp"),
        P(),
    )
    return jax.shard_map(body, mesh=mesh, in_specs=in_specs, out_specs=out_specs, check_vma=False)
```

```python
import functools
import math

import jax
import jax.numpy as jnp
import numpy as np
from jax import lax
from jax.experimental import pallas as pl
from jax.experimental.pallas import tpu as pltpu
from jax.sharding import PartitionSpec as P

D = 2048
HD = 64
FF = 8192
SLOT = 128
IMG = 64
SCALE_BASE = 512
HALF = D // 2

eps = 1e-05
root_half = 0.7071067811865476
inv_root_two_pi = 0.3989422804014327
masked_score = -1e30
MEGA = 1 << 20

COST = {
    "front": 15.6,
    "middle_norm": 7.5,
    "hidden_back": 400.0,
    "hidden_front": 14.7,
    "hidden_mid": 6.0,
    "hidden_grad": 7.0,
    "full_grad": 15.0,
    "ring_grads": 12.0,
    "result_part": 400.0,
    "middle_back": 11.0,
    "attention_back": 21.7,
    "tokens_back": 8.5,
    "output": 6.0,
}
WORK = 5.5e+07

F32 = jnp.float32
BF16 = jnp.bfloat16
NN = (((1,), (0,)), ((), ()))
NT = (((1,), (1,)), ((), ()))
TN = (((0,), (0,)), ((), ()))


def rounded(value):
    return value.astype(BF16)


def mul(left, right, dims=NN):
    return lax.dot_general(left, right, dims, preferred_element_type=F32)


def xpos_tables():
    place = np.arange(SLOT, dtype=np.float64)[:, None]
    lane = np.arange(128)[None, :]
    index = (lane % HD) // 2
    angle = place * 10000.0 ** (-2.0 * index / HD)
    zeta = (2.0 * index + 0.4 * HD) / (1.4 * HD)
    growth = zeta ** ((place - SLOT // 2) / SCALE_BASE)
    even = lane % 2 == 0
    found = []
    for factor in (growth / math.sqrt(HD), 1.0 / growth):
        found += [
            np.cos(angle) * factor,
            np.where(even, -np.sin(angle), 0.0) * factor,
            np.where(even, 0.0, np.sin(angle)) * factor,
        ]
    return jnp.asarray(np.tile(np.stack(found), (1, 2, 1)).astype(np.float32))


def rotate(value, tables, base, sign):
    up = pltpu.roll(value, 127, axis=1)
    down = pltpu.roll(value, 1, axis=1)
    turned = up * tables[base + 1] + down * tables[base + 2]
    return value * tables[base] + turned if sign > 0 else value * tables[base] - turned


def columns_of(parts):
    return jnp.transpose(parts)


def rows_of(columns):
    size = columns[0].shape[0]
    lane = lax.broadcasted_iota(jnp.int32, (size, 128), 1)
    tile = jnp.zeros((size, 128), F32)
    for at, column in enumerate(columns):
        tile = jnp.where(lane == at, column, tile)
    return jnp.transpose(tile)[:8]


def norm_parts(value):
    mean = jnp.mean(value, axis=-1, keepdims=True)
    var = jnp.mean(value * value, axis=-1, keepdims=True) - mean * mean
    inverse = lax.rsqrt(var + eps)
    return (value - mean) * inverse, inverse


def sum_rows(value):
    return jnp.sum(value, axis=0, keepdims=True)


def whole(array, **kw):
    rank = array.ndim
    return (array, array.shape, lambda *at: (0,) * rank)


def run(kernel, grid, ins, outs, scratch=(), prefetch=(), after=(), alias=None, limit=56, name=None):
    prefetch = tuple(prefetch)

    def body(*refs):
        refs = list(refs)
        first = len(prefetch) + len(ins)
        del refs[first : first + len(after)]
        kernel(*refs)

    in_specs = []
    for array, block, where in ins:
        if block is None:
            in_specs.append(pl.BlockSpec(memory_space=pl.ANY))
        elif tuple(block) == tuple(array.shape):
            in_specs.append(pl.BlockSpec(block, where, pipeline_mode=pl.Buffered(1)))
        else:
            in_specs.append(pl.BlockSpec(block, where))
    in_specs += [pl.BlockSpec(memory_space=pl.ANY)] * len(after)
    out_specs = [pl.BlockSpec(block, where) for shape, dtype, block, where in outs]
    out_shape = [jax.ShapeDtypeStruct(shape, dtype) for shape, dtype, block, where in outs]
    return pl.pallas_call(
        body,
        grid_spec=pltpu.PrefetchScalarGridSpec(
            num_scalar_prefetch=len(prefetch),
            grid=grid,
            in_specs=in_specs,
            out_specs=out_specs,
            scratch_shapes=list(scratch),
        ),
        out_shape=out_shape,
        input_output_aliases=alias or {},
        compiler_params=pltpu.CompilerParams(
            dimension_semantics=("arbitrary",) * len(grid), vmem_limit_bytes=limit * MEGA
        ),
        cost_estimate=pl.CostEstimate(flops=int(COST[name] * WORK), bytes_accessed=1000, transcendentals=0),
        name=name,
    )(*prefetch, *[array for array, block, where in ins], *after)


def flip(value, bit, size):
    return lax.ppermute(value, "tensor", [(t, t ^ (1 << bit)) for t in range(size)])


def all_pieces(own, bits):
    size = 1 << bits
    return [own] + [lax.ppermute(own, "tensor", [(t, t ^ k) for t in range(size)]) for k in range(1, size)]


class Line:
    def __init__(self):
        self.last = None

    def tie(self, value):
        if self.last is None:
            return value
        return lax.optimization_barrier((value,) + self.last)[0]

    def mark(self, *values):
        self.last = values


class Total:
    def __init__(self, line, parts, bits):
        self.line, self.bits = line, bits
        self.orders = [list(range(bits)), list(range(bits))[::-1]]
        self.left = [[bit for bit in range(bits) if bit != order[0]] for order in self.orders]
        self.keep = [parts[0], parts[2]]
        self.got = [flip(parts[1], self.orders[0][0], 1 << bits), flip(parts[3], self.orders[1][0], 1 << bits)]
        self.step = 1

    def advance(self):
        line, size = self.line, 1 << self.bits
        if self.step == self.bits:
            for half in range(2):
                self.keep[half] = line.tie(self.keep[half]) + self.got[half]
                line.mark(self.keep[half])
            return
        picks = []
        for half in range(2):
            left, bit = self.left[half], self.orders[half][self.step]
            keep, got = self.keep[half], self.got[half]
            cube = (2,) * len(left) + keep.shape[1:]
            axis = len(left) - 1 - left.index(bit)
            shape = (keep.shape[0] // 2,) + keep.shape[1:]
            pick = lambda value, at, cube=cube, axis=axis, shape=shape: lax.index_in_dim(
                value.reshape(cube), at, axis, keepdims=False
            ).reshape(shape)
            send = pick(line.tie(keep), 1) + pick(got, 1)
            line.mark(send)
            picks.append((pick, keep, got))
            self.got[half] = flip(send, bit, size)
            left.remove(bit)
        for half in range(2):
            pick, keep, got = picks[half]
            self.keep[half] = pick(line.tie(keep), 0) + pick(got, 0)
            line.mark(self.keep[half])
        self.step += 1

    def gather(self):
        size = 1 << self.bits
        if self.step == self.bits:
            self.held = [[0], [0]]
            self.step += 1
        else:
            for half in range(2):
                self.keep[half] = jnp.concatenate([self.line.tie(self.keep[half]), self.got[half]], 0)
                self.line.mark(self.keep[half])
                self.held[half] = self.held[half] + [block | self.last[half] for block in self.held[half]]
        self.last = [1 << self.orders[half].pop() for half in range(2)]
        self.got = [flip(self.keep[half], self.last[half].bit_length() - 1, size) for half in range(2)]

    def pieces(self):
        arrays, where = [], []
        for half in range(2):
            arrays += [self.keep[half], self.got[half]]
            found = {block: (2 * half, at) for at, block in enumerate(self.held[half])}
            found.update({block | self.last[half]: (2 * half + 1, at) for at, block in enumerate(self.held[half])})
            where.append(found)
        return arrays, where


class Ring:
    def __init__(self, line, first, rest, size):
        self.line, self.rest, self.size = line, rest, size
        self.step = 0
        self.got = self.send(first)

    def send(self, value):
        return lax.ppermute(value, "dp", [(d, (d + 2) % self.size) for d in range(self.size)])

    def advance(self):
        value = self.line.tie(self.rest)[self.step] + self.got
        self.line.mark(value)
        self.step += 1
        if self.step < self.size // 2 - 1:
            self.got = self.send(value)
        return value


def butterfly(value, bits):
    for bit in range(bits):
        value = value + flip(value, bit, 1 << bits)
    return value


def tree_sum(value):
    while value.shape[0] > 1:
        value = value.reshape((value.shape[0] // 2, 2) + value.shape[1:])
        value = value[:, 0] + value[:, 1]
    return value[0]


class Small:
    def __init__(self, own, bits):
        self.bits, self.bit, self.held = bits, 0, [own]
        self.got = None
        self.step()

    def step(self):
        if self.got is not None:
            many = len(self.held)
            self.held = self.held + [self.got[at] for at in range(many)]
        if self.bit < self.bits:
            self.got = flip(jnp.stack(self.held), self.bit, 1 << self.bits)
            self.bit += 1

    def pieces(self):
        while len(self.held) < 1 << self.bits:
            self.step()
        return self.held


def both_vectors(pieces):
    level = [piece[8:] for piece in pieces]
    while len(level) > 1:
        level = [level[at] + level[at + 1] for at in range(0, len(level), 2)]
    many = D // level[0].shape[1]
    return jnp.stack([level[0][:many].reshape(-1), level[0][4 : 4 + many].reshape(-1)])


def combine(pieces, block, blocks):
    level = [pieces[other][:8, (block ^ other) * SLOT : (block ^ other) * SLOT + SLOT] for other in range(blocks)]
    while len(level) > 1:
        level = [level[at] + level[at + 1] for at in range(0, len(level), 2)]
    return level[0]


def attention_scores(query, both_keys, length):
    scores = mul(query, both_keys, NT)
    row = lax.broadcasted_iota(jnp.int32, scores.shape, 0)
    place = lax.broadcasted_iota(jnp.int32, scores.shape, 1) % SLOT
    scores = jnp.where((place <= row) & (place < IMG + length), scores, masked_score)
    parts = []
    for at in range(2):
        part = scores[:, at * SLOT : (at + 1) * SLOT]
        expd = jnp.exp(part - jnp.max(part, axis=-1, keepdims=True))
        parts.append(expd / jnp.sum(expd, axis=-1, keepdims=True))
    return parts


def split_heads(value, mask):
    return jnp.concatenate([value * mask[0:1], value * mask[1:2]], axis=0)


def store_parts(refs, value, step, steps, only=None):
    left_keep, left_send, right_keep, right_send = refs
    left_keep[0] = value[:SLOT, :HALF]
    left_send[0] = value[SLOT:, :HALF]

    @pl.when(step < steps // 2)
    def _():
        right_keep[0] = value[:SLOT, HALF:]
        right_keep[1] = value[SLOT:, HALF:]

    @pl.when(step >= steps // 2)
    def _():
        right_send[0] = value[:SLOT, HALF:]
        right_send[1] = value[SLOT:, HALF:]


def part_outs(blocks):
    half = blocks // 2
    steps = blocks // 2
    shape = (half, SLOT, HALF)
    low = max(steps // 2, 1)
    return [
        (shape, F32, (1, SLOT, HALF), lambda s, *_: (s, 0, 0)),
        (shape, F32, (1, SLOT, HALF), lambda s, *_: (s, 0, 0)),
        (shape, F32, (2, SLOT, HALF), lambda s, *_: (jnp.minimum(s, low - 1), 0, 0)),
        (shape, F32, (2, SLOT, HALF), lambda s, *_: (jnp.maximum(s - steps // 2, 0), 0, 0)),
    ]


def front(order, lengths, tokens, gain, shift, weight, bias, tables, mask, mix_gain, uw_rows, out_weight, after=()):
    blocks = order.shape[0]
    steps = blocks // 2
    width = weight.shape[2]
    groups = width // 128
    rows = blocks * SLOT

    def kernel(order_ref, length_ref, x0, x1, g, b, w, wb, tab, msk, mg, uwr, ow, own, first, qkv, mixed, small, *parts_uw):
        step = pl.program_id(0)
        parts, uw = parts_uw[:4], parts_uw[4]

        @pl.when(step == 0)
        def _():
            found = mul(uwr[...], ow[...])
            uw[0:1] = found[0:1] + found[1:2] + found[2:3]
            uw[1:2] = found[3:4] + found[4:5] + found[5:6]
            small[8:] = jnp.zeros((8, rows), F32)
            for at in range(D // rows):
                c = slice(at * rows, at * rows + rows)
                small[8 + at : 9 + at] = uw[0:1, c]
                small[12 + at : 13 + at] = uw[1:2, c]

        x = jnp.concatenate([x0[0], x1[0]], axis=0)
        own[...] = x
        hat, _ = norm_parts(x.astype(F32))
        one = rounded(hat * g[...] + b[...])
        first[...] = one
        for c in range(3):
            proj = mul(one, w[c]) + wb[c : c + 1]
            for group in range(groups):
                part = proj[:, group * 128 : group * 128 + 128]
                if c < 2:
                    part = rotate(part, tab, 3 * c, 1)
                at = c * width + group * 128
                qkv[:, at : at + 128] = rounded(part)
        for pair in range(2):
            r = slice(pair * SLOT, pair * SLOT + SLOT)
            length = length_ref[order_ref[2 * step + pair]]
            for group in range(groups):
                at = group * 128
                query = qkv[r, at : at + 128]
                keys = split_heads(qkv[r, width + at : width + at + 128], msk)
                values = split_heads(qkv[r, 2 * width + at : 2 * width + at + 128], msk)
                probs = attention_scores(query, keys, length)
                mixed[r, at : at + 128] = mul(rounded(jnp.concatenate(probs, axis=1)), values)
        m = mixed[...]
        total = jnp.sum(m, axis=-1, keepdims=True)
        here = pl.ds(pl.multiple_of(step * 2 * SLOT, 2 * SLOT), 2 * SLOT)
        small[:8, here] = rows_of([total, jnp.sum(m * m, axis=-1, keepdims=True)])
        middle = total * (1.0 / width)
        partial = mul(rounded((m - middle) * mg[...]), ow[...]) + middle * uw[0:1]
        store_parts(parts, partial, step, steps)

    row2 = lambda s, *_: (s, 0)
    pair_of = lambda offset: lambda s, order_ref, length_ref: (order_ref[2 * s + offset], 0, 0)
    return run(
        kernel,
        (steps,),
        [
            (tokens, (1, SLOT, D), pair_of(0)),
            (tokens, (1, SLOT, D), pair_of(1)),
            whole(gain), whole(shift), whole(weight), whole(bias), whole(tables), whole(mask),
            whole(mix_gain), whole(uw_rows), whole(out_weight),
        ],
        [
            ((rows, D), BF16, (2 * SLOT, D), row2),
            ((rows, D), BF16, (2 * SLOT, D), row2),
            ((rows, 3 * width), BF16, (2 * SLOT, 3 * width), row2),
            ((rows, width), F32, (2 * SLOT, width), row2),
            ((16, rows), F32, (16, rows), lambda s, *_: (0, 0)),
        ]
        + part_outs(blocks),
        scratch=[pltpu.VMEM((8, D), F32)],
        prefetch=(order, lengths),
        after=after,
        name="front",
    )


def pieces_in(pieces):
    return [whole(piece) for piece in pieces[0]]


def load_pieces(refs, where, total, step, blocks):
    for block in range(blocks):

        @pl.when(step == block)
        def _(block=block):
            for half in range(2):
                array, at = where[half][block]
                total[:, half * HALF : half * HALF + HALF] = refs[array][at]


def middle_norm(own, pieces, sums, uw, out_bias, gain, shift, after=()):
    blocks = len(pieces[1][0])
    rows = blocks * SLOT

    def kernel(*refs):
        x, parts, stats = refs[0], refs[1:5], refs[5 : 5 + blocks]
        uw_ref, bias, g, b, mid, second, stat, total, tot8 = refs[5 + blocks :]
        step = pl.program_id(0)
        load_pieces(parts, pieces[1], total, step, blocks)
        for block in range(blocks):

            @pl.when(step == block)
            def _(block=block):
                tot8[...] = combine(stats, block, blocks)

        cols = columns_of(tot8[...])
        mean = cols[:, 0:1] * (1.0 / D)
        inverse = lax.rsqrt(cols[:, 1:2] * (1.0 / D) - mean * mean + eps)
        branch = inverse * (total[...] - mean * uw_ref[0:1]) + uw_ref[1:2]
        value = x[...].astype(F32) + branch + bias[...]
        mid[...] = value
        hat, _ = norm_parts(value)
        second[...] = rounded(hat * g[...] + b[...])
        lane = lax.broadcasted_iota(jnp.int32, (SLOT, 128), 1)
        stat[...] = jnp.where(lane == 0, mean, inverse)

    row = lambda k, *_: (k, 0)
    return run(
        kernel,
        (blocks,),
        [(own, (SLOT, D), row)]
        + pieces_in(pieces)
        + [whole(part) for part in sums]
        + [whole(uw), whole(out_bias), whole(gain), whole(shift)],
        [
            ((rows, D), F32, (SLOT, D), row),
            ((rows, D), BF16, (SLOT, D), row),
            ((rows, 128), F32, (SLOT, 128), row),
        ],
        scratch=[pltpu.VMEM((SLOT, D), F32), pltpu.VMEM((8, SLOT), F32)],
        after=after,
        name="middle_norm",
    )


def hidden_back(cots, down_weight):
    many, rows, units = len(cots), cots[0].shape[0], down_weight.shape[0]
    tile = min(512, units)

    def kernel(*refs):
        w, out = refs[many:]
        for at in range(many):
            out[at * rows : at * rows + rows] = rounded(mul(refs[at][...], w[...], NT))

    return run(
        kernel,
        (units // tile,),
        [whole(cot) for cot in cots] + [(down_weight, (tile, D), lambda j: (j, 0))],
        [((many * rows, units), BF16, (many * rows, tile), lambda j: (0, j))],
        name="hidden_back",
    )[0]


def hidden_front(chunk, second, up_weight, up_bias, back, gain, after=()):
    rows, units = second.shape[0], up_weight.shape[1]
    tile = 512
    steps = units // tile

    def part_of(c, s_ref, w, b, hb, g, act, slp):
        hidden = mul(s_ref[...], w[:, c]) + b[:, c]
        tail = jnp.exp(-0.5 * hidden * hidden)
        t = 1.0 / (1.0 + (0.3275911 * root_half) * jnp.abs(hidden))
        poly = 1.061405429 * t - 1.453152027
        poly = poly * t + 1.421413741
        poly = poly * t - 0.284496736
        poly = poly * t + 0.254829592
        half = 0.5 * poly * t * tail
        phi = jnp.where(hidden >= 0.0, 1.0 - half, half)
        active = hidden * phi
        act[:, c] = rounded(active)
        slp[:, c] = rounded(phi + hidden * (inv_root_two_pi * tail))
        scaled = hb[:, c].astype(F32) * g[:, c]
        return [value[:, :128] + value[:, 128:] for value in (active, active * active, scaled, scaled * active)]

    def kernel(s_ref, w, b, hb, g, act, slp, sums, acc):
        step = pl.program_id(0)
        found = [part_of(slice(at, at + 256), s_ref, w, b, hb, g, act, slp) for at in range(0, tile, 256)]

        @pl.when(step == 0)
        def _():
            for at in range(4):
                acc[at] = found[0][at] + found[1][at]

        @pl.when(step > 0)
        def _():
            for at in range(4):
                acc[at] += found[0][at] + found[1][at]

        @pl.when(step == steps - 1)
        def _():
            for block in range(rows // SLOT):
                r = slice(block * SLOT, block * SLOT + SLOT)
                sums[:, r] = rows_of([jnp.sum(acc[at, r], axis=-1, keepdims=True) for at in range(4)])

    return run(
        kernel,
        (steps,),
        [
            whole(second),
            (up_weight, (D, tile), lambda j: (0, j)),
            (up_bias, (1, tile), lambda j: (0, j)),
            (back, (rows, tile), lambda j: (chunk, j)),
            (gain, (1, tile), lambda j: (0, j)),
        ],
        [
            ((rows, units), BF16, (rows, tile), lambda j: (0, j)),
            ((rows, units), BF16, (rows, tile), lambda j: (0, j)),
            ((8, rows), F32, (8, rows), lambda j: (0, 0)),
        ],
        scratch=[pltpu.VMEM((4, rows, 128), F32)],
        after=after,
        name="hidden_front",
    )


def hidden_mid(chunk, active, slope, back, sums, gain, shift):
    blocks = len(sums)
    rows, units = active.shape

    def kernel(act, slp, hb, *refs):
        stats = refs[:blocks]
        g, b, low, grad, vecs, tot8 = refs[blocks:]
        step = pl.program_id(0)
        for block in range(blocks):

            @pl.when(step == block)
            def _(block=block):
                tot8[...] = combine(stats, block, blocks)

        cols = columns_of(tot8[...]) * (1.0 / FF)
        mean = cols[:, 0:1]
        inverse = lax.rsqrt(cols[:, 1:2] - mean * mean + eps)
        one = cols[:, 2:3]
        two = inverse * (cols[:, 3:4] - mean * one)
        for at in range(0, units, 256):
            c = slice(at, at + 256)
            hat = (act[:, c].astype(F32) - mean) * inverse
            low[:, c] = rounded(hat * g[:, c] + b[:, c])
            raw = hb[:, c].astype(F32)
            grown = rounded(inverse * (raw * g[:, c] - one - hat * two) * slp[:, c].astype(F32))
            grad[:, c] = grown
            vecs[0, 0:1, c] = sum_rows(raw * hat)
            vecs[0, 1:2, c] = sum_rows(raw)
            vecs[0, 2:3, c] = sum_rows(grown.astype(F32))

    row = lambda k: (k, 0)
    return run(
        kernel,
        (blocks,),
        [
            (active, (SLOT, units), row),
            (slope, (SLOT, units), row),
            (back, (SLOT, units), lambda k: (chunk * blocks + k, 0)),
        ]
        + [whole(part) for part in sums]
        + [whole(gain), whole(shift)],
        [
            ((rows, units), BF16, (SLOT, units), row),
            ((rows, units), BF16, (SLOT, units), row),
            ((blocks, 8, units), F32, (1, 8, units), lambda k: (k, 0, 0)),
        ],
        scratch=[pltpu.VMEM((8, SLOT), F32)],
        name="hidden_mid",
    )


def hidden_grad(grad, up_weight):
    rows, units = grad.shape
    blocks = rows // SLOT
    tile = 512
    steps = D // tile
    half = steps // 2

    def kernel(gr, w, left_keep, left_send, right_keep, right_send):
        step = pl.program_id(0)
        value = mul(gr[...], w[...], NT)

        @pl.when(step < half)
        def _():
            for block in range(blocks):
                r = slice(block * SLOT, block * SLOT + SLOT)
                (left_send if block & 1 else left_keep)[block // 2] = value[r]

        @pl.when(step >= half)
        def _():
            for block in range(blocks):
                r = slice(block * SLOT, block * SLOT + SLOT)
                (right_send if block >= blocks // 2 else right_keep)[block % (blocks // 2)] = value[r]

    shape = (blocks // 2, SLOT, HALF)
    block_shape = (blocks // 2, SLOT, tile)
    lefts = lambda j: (0, 0, jnp.minimum(j, half - 1))
    rights = lambda j: (0, 0, jnp.maximum(j - half, 0))
    return run(
        kernel,
        (steps,),
        [whole(grad), (up_weight, (tile, units), lambda j: (j, 0))],
        [
            (shape, F32, block_shape, lefts),
            (shape, F32, block_shape, lefts),
            (shape, F32, block_shape, rights),
            (shape, F32, block_shape, rights),
        ],
        name="hidden_grad",
    )


def result_part(order, lows, down_weight):
    pairs = order.shape[0]
    units = down_weight.shape[0]
    many = len(lows)
    rows = lows[0].shape[0]
    each = rows // SLOT
    tile = 256

    def kernel(order_ref, *refs):
        w, out = refs[many:]
        for at in range(many):
            value = mul(refs[at][...], w[...])
            for block in range(each):
                out[order_ref[at * each + block]] = value[block * SLOT : block * SLOT + SLOT]

    return run(
        kernel,
        (D // tile,),
        [whole(low) for low in lows] + [(down_weight, (units, tile), lambda j, *_: (0, j))],
        [((pairs, SLOT, D), F32, (pairs, SLOT, tile), lambda j, *_: (0, 0, j))],
        prefetch=(order,),
        name="result_part",
    )[0]


def middle_back(own, cot, pieces, middle, stat, uw, out_bias, gain, after=()):
    blocks = len(pieces[1][0])
    rows = blocks * SLOT

    def kernel(*refs):
        x, c, parts = refs[0], refs[1], refs[2:6]
        mid, st, uw_ref, bias, g, grad, low, stat2, vecs, total = refs[6:]
        load_pieces(parts, pieces[1], total, pl.program_id(0), blocks)
        value = mid[...]
        hat, inverse = norm_parts(value)
        sec = total[...]
        scaled = sec * g[...]
        up = c[...].astype(F32)
        out = up + inverse * (
            scaled
            - jnp.mean(scaled, axis=-1, keepdims=True)
            - hat * jnp.mean(scaled * hat, axis=-1, keepdims=True)
        )
        grad[...] = out
        lowered = rounded(out)
        low[...] = lowered
        low32 = lowered.astype(F32)
        one = jnp.mean(low32 * uw_ref[0:1], axis=-1, keepdims=True)
        moved = value - x[...].astype(F32) - bias[...] - uw_ref[1:2]
        two = jnp.mean(low32 * moved, axis=-1, keepdims=True)
        lane = lax.broadcasted_iota(jnp.int32, (SLOT, 128), 1)
        stat2[...] = jnp.where(lane == 2, one, jnp.where(lane == 3, two, st[...]))
        vecs[0, 0:1] = sum_rows(sec * hat)
        vecs[0, 1:2] = sum_rows(sec)
        vecs[0, 2:3] = sum_rows(out)
        vecs[0, 3:4] = sum_rows(up)

    row = lambda k, *_: (k, 0)
    return run(
        kernel,
        (blocks,),
        [(own, (SLOT, D), row), (cot, (SLOT, D), row)]
        + pieces_in(pieces)
        + [(middle, (SLOT, D), row), (stat, (SLOT, 128), row), whole(uw), whole(out_bias), whole(gain)],
        [
            ((rows, D), F32, (SLOT, D), row),
            ((rows, D), BF16, (SLOT, D), row),
            ((rows, 128), F32, (SLOT, 128), row),
            ((blocks, 8, D), F32, (1, 8, D), lambda k, *_: (k, 0, 0)),
        ],
        scratch=[pltpu.VMEM((SLOT, D), F32)],
        after=after,
        name="middle_back",
    )


def attention_back(order, lengths, low, stat, mixed, qkv, own, mix_gain, mix_shift, out_weight, weight, tables, mask, after=()):
    blocks = order.shape[0]
    steps = blocks // 2
    width = out_weight.shape[0]
    groups = width // 128
    rows = blocks * SLOT

    def kernel(
        order_ref, length_ref, low_ref, st, mx, qkv_ref, x, mg, ms, ow, w, tab, msk,
        mix_low, dproj, vecs, wide, left_keep, left_send, right_keep, right_send, dmixed,
    ):
        step = pl.program_id(0)
        mean, inverse, one, two = (st[:, at : at + 1] for at in range(4))
        back = mul(low_ref[...], ow[...], NT)
        hat = (mx[...] - mean) * inverse
        mix_low[...] = rounded(hat * mg[...] + ms[...])
        dmixed[...] = rounded(inverse * (back * mg[...] - one - hat * two))
        vecs[0, 0:1, :width] = sum_rows(back * hat)
        vecs[0, 1:2, :width] = sum_rows(back)
        first_half = lax.broadcasted_iota(jnp.int32, (SLOT, 128), 1) < HD
        for pair in range(2):
            r = slice(pair * SLOT, pair * SLOT + SLOT)
            length = length_ref[order_ref[2 * step + pair]]
            for group in range(groups):
                at = group * 128
                query = qkv_ref[r, at : at + 128]
                keys = split_heads(qkv_ref[r, width + at : width + at + 128], msk)
                values = split_heads(qkv_ref[r, 2 * width + at : 2 * width + at + 128], msk)
                grad = dmixed[r, at : at + 128]
                probs = attention_scores(query, keys, length)
                dprobs = mul(grad, values, NT)
                dscores = []
                for i in range(2):
                    dp = dprobs[:, i * SLOT : (i + 1) * SLOT]
                    carried = jnp.sum(probs[i] * dp, axis=-1, keepdims=True)
                    dscores.append(rounded(probs[i] * (dp - carried)))
                dscores = jnp.concatenate(dscores, axis=1)
                dquery = mul(dscores, keys)
                dkey = mul(dscores, query, TN)
                dvalue = mul(rounded(jnp.concatenate(probs, axis=1)), grad, TN)
                dkey = jnp.where(first_half, dkey[:SLOT], dkey[SLOT:])
                dvalue = jnp.where(first_half, dvalue[:SLOT], dvalue[SLOT:])
                tabs = [tab[i, :SLOT] for i in range(6)]
                dproj[r, at : at + 128] = rounded(rotate(dquery, tabs, 0, -1))
                dproj[r, width + at : width + at + 128] = rounded(rotate(dkey, tabs, 3, -1))
                dproj[r, 2 * width + at : 2 * width + at + 128] = rounded(dvalue)
        vecs[0, 2:3] = sum_rows(dproj[...].astype(F32))
        partial = mul(dproj[:, :width], w[0], NT)
        for c in (1, 2):
            partial += mul(dproj[:, c * width : (c + 1) * width], w[c], NT)
        pre_hat, _ = norm_parts(x[...].astype(F32))
        grown = partial * pre_hat
        wide[0, 0:1] = sum_rows(grown[:SLOT]) + sum_rows(grown[SLOT:])
        wide[0, 1:2] = sum_rows(partial[:SLOT]) + sum_rows(partial[SLOT:])
        store_parts((left_keep, left_send, right_keep, right_send), partial, step, steps)

    row2 = lambda s, *_: (s, 0)
    return run(
        kernel,
        (steps,),
        [
            (low, (2 * SLOT, D), row2),
            (stat, (2 * SLOT, 128), row2),
            (mixed, (2 * SLOT, width), row2),
            (qkv, (2 * SLOT, 3 * width), row2),
            (own, (2 * SLOT, D), row2),
            whole(mix_gain), whole(mix_shift), whole(out_weight), whole(weight), whole(tables), whole(mask),
        ],
        [
            ((rows, width), BF16, (2 * SLOT, width), row2),
            ((rows, 3 * width), BF16, (2 * SLOT, 3 * width), row2),
            ((steps, 8, 3 * width), F32, (1, 8, 3 * width), lambda s, *_: (s, 0, 0)),
            ((steps, 8, D), F32, (1, 8, D), lambda s, *_: (s, 0, 0)),
        ]
        + part_outs(blocks),
        scratch=[pltpu.VMEM((2 * SLOT, width), BF16)],
        prefetch=(order, lengths),
        after=after,
        name="attention_back",
    )


def tokens_back(order, own, grad, pieces, gain, before, pairs, after=()):
    blocks = len(pieces[1][0])

    def kernel(order_ref, x, gr, *refs):
        parts = refs[:4]
        g = refs[4]
        out, total = refs[-2:]
        load_pieces(parts, pieces[1], total, pl.program_id(0), blocks)
        hat, inverse = norm_parts(x[...].astype(F32))
        scaled = total[...] * g[...]
        out[0] = gr[...] + inverse * (
            scaled
            - jnp.mean(scaled, axis=-1, keepdims=True)
            - hat * jnp.mean(scaled * hat, axis=-1, keepdims=True)
        )

    row = lambda k, *_: (k, 0)
    ins = [(own, (SLOT, D), row), (grad, (SLOT, D), row)] + pieces_in(pieces) + [whole(gain)]
    alias = None
    if before is not None:
        alias = {1 + len(ins): 0}
        ins = ins + [(before, None, None)]
    return run(
        kernel,
        (blocks,),
        ins,
        [((pairs, SLOT, D), F32, (1, SLOT, D), lambda k, o: (o[k], 0, 0))],
        scratch=[pltpu.VMEM((SLOT, D), F32)],
        prefetch=(order,),
        after=after,
        alias=alias,
        name="tokens_back",
    )[0]


def output_of(order, middle, result, bias, before, after=()):
    blocks = order.shape[0]

    def kernel(order_ref, mid, res, b, *refs):
        out = refs[-1]
        out[0] = rounded(mid[...] + res[0] + b[...])

    ins = [
        (middle, (SLOT, D), lambda k, *_: (k, 0)),
        (result, (1, SLOT, D), lambda k, o: (o[k], 0, 0)),
        whole(bias),
    ]
    alias = None
    if before is not None:
        alias = {1 + len(ins): 0}
        ins = ins + [(before, None, None)]
    return run(
        kernel,
        (blocks,),
        ins,
        [(result.shape, BF16, (1, SLOT, D), lambda k, o: (o[k], 0, 0))],
        prefetch=(order,),
        after=after,
        alias=alias,
        name="output",
    )[0]


def ring_grads(ids, products, got=None):
    count, many = ids.shape[0], len(products[0][0])
    rows = products[0][0][0].shape[0]
    widths = [rights[0].shape[1] for lefts, rights in products]
    block = D // (2 * count)
    shape = (block, sum(widths))

    def kernel(ids_ref, *refs):
        outs = refs[2 * many * len(products) + (got is not None) :]
        step = pl.program_id(0)
        start = 0
        for at, width in enumerate(widths):
            left, right = (refs[(2 * at + side) * many : (2 * at + side + 1) * many] for side in range(2))
            value = mul(left[0][...], right[0][...], TN)
            for k in range(1, many):
                value += mul(left[k][...], right[k][...], TN)
            c = slice(start, start + width)
            start += width
            if got is None:
                outs[0][0, :, c] = value
                continue
            value += refs[2 * many * len(products)][0, :, c]

            @pl.when(step == 0)
            def _(value=value, c=c):
                outs[0][:, c] = value

            @pl.when(step > 0)
            def _(value=value, c=c):
                outs[1][0, :, c] = value

    fixed = lambda i, *_: (0, 0)
    moving = lambda i, ids_ref: (0, ids_ref[i])
    lead = lambda i, *_: (i, 0, 0)
    ins = []
    for lefts, rights in products:
        ins += [(left, (rows, block), moving) for left in lefts]
        ins += [(right, right.shape, fixed) for right in rights]
    if got is None:
        outs = [((count,) + shape, F32, (1,) + shape, lead)]
    else:
        ins += [(got, (1,) + shape, lead)]
        outs = [
            (shape, F32, shape, fixed),
            ((count - 1,) + shape, F32, (1,) + shape, lambda i, *_: (jnp.maximum(i - 1, 0), 0, 0)),
        ]
    return run(kernel, (count,), ins, outs, prefetch=(ids,), name="ring_grads")


def full_grad(products):
    many, block = len(products[0][0]), 512
    rows, tall = products[0][0][0].shape
    widths = [rights[0].shape[1] for lefts, rights in products]

    def kernel(*refs):
        out, start = refs[-1], 0
        for at, width in enumerate(widths):
            left, right = (refs[(2 * at + side) * many : (2 * at + side + 1) * many] for side in range(2))
            value = mul(left[0][...], right[0][...], TN)
            for k in range(1, many):
                value += mul(left[k][...], right[k][...], TN)
            out[:, start : start + width] = value
            start += width

    ins = []
    for lefts, rights in products:
        ins += [(left, (rows, block), lambda i: (0, i)) for left in lefts]
        ins += [(right, right.shape, lambda i: (0, 0)) for right in rights]
    wide = sum(widths)
    return run(
        kernel, (tall // block,), ins, [((tall, wide), F32, (block, wide), lambda i: (i, 0))], name="full_grad"
    )[0]


def steps_of(totals, bits, done, until):
    done = list(done)

    def step(at):
        if done[at] < bits:
            totals[at].advance()
        else:
            totals[at].gather()
        done[at] += 1
        if done[at] == bits and until == 2 * bits:
            totals[at].gather()
            done[at] += 1

    limits = [until] + [until if until == 2 * bits else bits - 1] * (len(totals) - 1)
    while any(have < limit for have, limit in zip(done, limits)):
        for at in range(len(totals)):
            if done[at] < limits[at]:
                step(at)


def split_rows(value):
    found = []
    for _ in range(3):
        part = lax.reduce_precision(value, 8, 7)
        found.append(part.astype(BF16))
        value = value - part
    return found


def body(
    tokens,
    lengths,
    cotangent,
    pre_gain,
    pre_shift,
    qkv_weight,
    qkv_bias,
    mix_gain,
    mix_shift,
    out_weight,
    out_bias,
    ffn_gain,
    ffn_shift,
    up_weight,
    up_bias,
    hid_gain,
    hid_shift,
    down_weight,
    down_bias,
):
    pairs = lengths.shape[0]
    blocks = lax.axis_size("tensor")
    bits = blocks.bit_length() - 1
    chunks = pairs // blocks
    width = qkv_weight.shape[2]
    mine = lax.axis_index("tensor").astype(jnp.int32)
    orders = [jnp.arange(c * blocks, (c + 1) * blocks, dtype=jnp.int32) ^ mine for c in range(chunks)]
    tokens3 = tokens.reshape(pairs, SLOT, D)
    row = lambda v: v.reshape(1, -1)
    pre_gain, pre_shift, mix_gain, mix_shift = map(row, (pre_gain, pre_shift, mix_gain, mix_shift))
    out_bias, ffn_gain, ffn_shift, up_bias = map(row, (out_bias, ffn_gain, ffn_shift, up_bias))
    hid_gain, hid_shift, down_bias = map(row, (hid_gain, hid_shift, down_bias))
    tables = xpos_tables()
    lane = np.arange(128)[None, :] < HD
    mask = jnp.asarray(np.concatenate([lane, ~lane], 0).astype(np.float32)).astype(BF16)
    zero = jnp.zeros((2, width), BF16)
    uw_rows = jnp.concatenate(split_rows(mix_gain) + split_rows(mix_shift) + [zero], 0)

    line = Line()
    dp_size = lax.axis_size("dp")
    place = lax.axis_index("dp").astype(jnp.int32)
    count = dp_size // 2
    around = lax.rem(place // 2 + count - 1 - jnp.arange(count, dtype=jnp.int32), count)
    mine_ids, other_ids = 2 * around + lax.rem(place, 2), 2 * around + 1 - lax.rem(place, 2)

    def tied(products):
        (lefts, rights), others = products[0], products[1:]
        return [([line.tie(lefts[0])] + lefts[1:], rights)] + others

    def full(products):
        grad = full_grad(tied(products))
        line.mark(grad)
        return grad

    every = lambda items, name: [item[name] for item in items]

    ones, twos, threes = [], [], []
    for c in range(chunks):
        found = front(
            orders[c], lengths, line.tie(tokens3), pre_gain, pre_shift, qkv_weight, qkv_bias, tables, mask, mix_gain, uw_rows,
            out_weight,
        )
        own, first, qkv, mixed, small = found[:5]
        one = dict(own=own, first=first, qkv=qkv, mixed=mixed, parts=found[5:])
        line.mark(small)
        one["small"] = small
        if c == 0:
            one["total"] = Total(line, one["parts"], bits)
            one["sums"] = Small(small, bits)
        ones.append(one)
    sums0 = ones[0]["sums"]
    if bits > 1:
        ones[0]["total"].advance()
    for c in range(1, chunks):
        ones[c]["total"] = Total(line, [line.tie(part) for part in ones[c]["parts"]], bits)
    sums0.held[0] = line.tie(sums0.held[0])
    sums0.step()
    cot3 = cotangent.reshape(pairs, SLOT, D)
    cots = []
    for c in range(chunks):
        cots.append(line.tie(cot3)[orders[c]].reshape(-1, D))
        line.mark(cots[-1])
    totals = every(ones, "total")
    line.mark(*line.last, *sums0.pieces())
    for step in range(1, bits):
        totals[0].advance()
    back = hidden_back([line.tie(cots[0])] + cots[1:], down_weight)
    line.mark(back)
    for one in ones[1:]:
        one["sums"] = Small(line.tie(one["small"]), bits)
    done = [bits] + [0] * (chunks - 1)
    steps_of(totals, bits, done, 2 * bits - 1)
    for one in ones[1:]:
        line.mark(*line.last, one["sums"].got)
        one["sums"].step()
    uw_total = both_vectors(sums0.pieces())

    def mid_of(c):
        two = twos[c]
        low, grad, vecs = hidden_mid(c, line.tie(two["active"]), two["slope"], back, two["sums"], hid_gain, hid_shift)
        two.update(low=low, grad=grad, vecs=functools.reduce(jnp.add, [vecs[k] for k in range(blocks)]))
        line.mark(vecs)

    def hidden_of(c):
        parts = hidden_grad(line.tie(twos[c]["grad"]), up_weight)
        line.mark(parts[0])
        return parts

    totals[0].gather()
    for other in ones[1:]:
        line.mark(*line.last, *other["sums"].pieces())
    for c in range(chunks):
        one = ones[c]
        mid, second, stat = middle_norm(
            line.tie(one["own"]), totals[c].pieces(), one["sums"].pieces(), uw_total, out_bias, ffn_gain, ffn_shift
        )
        line.mark(stat)
        if c == 0:
            for total in totals[1:]:
                total.advance()
                total.gather()
        active, slope, sums = hidden_front(c, line.tie(second), up_weight, up_bias, back, hid_gain)
        line.mark(sums)
        twos.append(dict(middle=mid, second=second, stat=stat, active=active, slope=slope, sums=all_pieces(sums, bits)))
        if c == 0:
            line.mark(sums, *twos[0]["sums"][1:])
            for total in totals[1:]:
                for step in range(1, bits):
                    total.gather()
        else:
            twos[0]["total"].advance()
            line.mark(*line.last, *twos[c]["sums"][1:])
        mid_of(c)
        if c > 0:
            line.mark(*line.last, *twos[0]["total"].got)
        if c == 0 and chunks > 1:
            twos[0]["total"] = Total(line, hidden_of(0), bits)
    lows = every(twos, "low")
    down_grad = full([(lows, cots)])
    down_part = lax.psum_scatter(down_grad, "dp", scatter_dimension=1, tiled=True)
    up_products = [(every(twos, "second"), every(twos, "grad"))]
    sent = ring_grads(other_ids, tied(up_products))[0]
    line.mark(sent)
    sent = lax.ppermute(sent, "dp", [(d, d ^ 1) for d in range(dp_size)])
    if chunks > 1:
        for step in range(1, bits):
            twos[0]["total"].advance()
        twos[0]["total"].gather()
        parts = [None] + [hidden_of(c) for c in range(1, chunks)]
    else:
        twos[0]["total"] = Total(line, hidden_of(0), bits)
        for step in range(bits):
            twos[0]["total"].advance()
        twos[0]["total"].gather()
    ring_first, ring_rest = ring_grads(mine_ids, tied(up_products), sent)
    line.mark(ring_rest)
    ring = Ring(line, ring_first, ring_rest, dp_size)
    for step in range(1, bits):
        twos[0]["total"].gather()
    for c in range(1, chunks):
        twos[c]["total"] = Total(line, [line.tie(part) for part in parts[c]], bits)
    totals = every(twos, "total")
    result = result_part(jnp.concatenate(orders), [line.tie(lows[0])] + lows[1:], down_weight)
    line.mark(result)

    for c in range(chunks):
        one, two = ones[c], twos[c]
        grad, low, stat2, vecs = middle_back(
            line.tie(one["own"]), cots[c], two["total"].pieces(), two["middle"], two["stat"], uw_total, out_bias, ffn_gain
        )
        line.mark(stat2)
        if c == 0:
            for total in totals[1:]:
                total.advance()
        found = attention_back(
            orders[c], lengths, line.tie(low), stat2, one["mixed"], one["qkv"], one["own"], mix_gain, mix_shift, out_weight,
            qkv_weight, tables, mask,
        )
        line.mark(found[2])
        three = dict(grad=grad, low=low, vecs=tree_sum(vecs), mix_low=found[0], dproj=found[1])
        three["narrow"] = tree_sum(found[2])
        three["wide"] = tree_sum(found[3])
        parts = found[4:]
        if c == 0 and chunks > 1:
            for total in totals[1:]:
                for step in range(1, bits):
                    total.advance()
                for step in range(bits):
                    total.gather()
            for total in totals[1:]:
                line.mark(*line.last, *total.got)
            up_part = ring.advance()
            result = lax.psum(line.tie(result), "tensor")
            parts = [line.tie(part) for part in parts]
        three["total"] = Total(line, parts, bits)
        threes.append(three)

    first, last = threes[0]["total"], threes[-1]["total"]
    if chunks > 1:
        first.advance()
    add = lambda items, name, size: functools.reduce(jnp.add, [item[name] for item in items])[:size]
    pad = lambda v: jnp.pad(v, ((0, 0), (0, D - v.shape[1])))
    wide = add(threes, "wide", 2)
    got = flip(wide, 0, blocks)
    attention_grad = full(
        [(every(ones, "first"), every(threes, "dproj")), (every(threes, "low"), every(threes, "mix_low"))]
    )
    attention_part = lax.psum_scatter(attention_grad, "dp", scatter_dimension=0, tiled=True)
    if chunks == 1:
        up_part = ring.advance()
        result = lax.psum(line.tie(result), "tensor")
    for step in range(1 if chunks > 1 else 0, bits):
        first.advance()
    first.gather()
    if chunks > 1:
        last.advance()
    for step in range(1, bits):
        first.gather()
    line.mark(*line.last, down_part)
    up_part = ring.advance()
    if chunks > 1:
        for step in range(1, bits):
            last.advance()
        last.gather()
    for bit in range(1, bits):
        wide = line.tie(wide) + got
        got = flip(wide, bit, blocks)
        line.mark(wide)
    if chunks > 1:
        line.mark(*line.last, *last.got)
    hop = lambda v, bit: lax.ppermute(v, "dp", [(d, d ^ (1 << bit)) for d in range(dp_size)])
    dp_bits = dp_size.bit_length() - 1
    tokens_grad, output = None, None
    for c in range(chunks):
        tokens_grad = tokens_back(
            orders[c], line.tie(ones[c]["own"]), threes[c]["grad"], threes[c]["total"].pieces(), pre_gain, tokens_grad, pairs
        )
        line.mark(tokens_grad)
        if c == 0:
            wide = line.tie(wide) + got
            vecs = jnp.concatenate(
                [pad(add(twos, "vecs", 3)), add(threes, "vecs", 4), pad(add(threes, "narrow", 3)), wide], 0
            )
            line.mark(vecs)
            got = hop(vecs, 0)
            if chunks > 1:
                for step in range(1, bits):
                    last.gather()
            vecs = line.tie(vecs) + got
            line.mark(vecs)
            got = hop(vecs, 1)
    for bit in range(2, dp_bits):
        vecs = line.tie(vecs) + got
        line.mark(vecs)
        got = hop(vecs, bit)
    for step in range(2, count - 1):
        up_part = ring.advance()
    for c in range(chunks):
        output = output_of(orders[c], line.tie(twos[c]["middle"]), result, down_bias, output)
        line.mark(output)
    vecs = vecs + got
    hid_vecs, mid_vecs, narrow, wide = vecs[:3], vecs[3:7], vecs[7:10], vecs[10:12]
    qkv_part = jnp.swapaxes(attention_part[:, : 3 * width].reshape(-1, 3, width), 0, 1)
    out_part = jnp.transpose(attention_part[:, 3 * width :])
    units = hid_gain.shape[1]
    return (
        output.reshape(-1, D),
        tokens_grad.reshape(-1, D),
        wide[0],
        wide[1],
        qkv_part,
        narrow[2, : 3 * width].reshape(3, width),
        narrow[0, :width],
        narrow[1, :width],
        out_part,
        mid_vecs[2],
        mid_vecs[0],
        mid_vecs[1],
        up_part,
        hid_vecs[2, :units],
        hid_vecs[0, :units],
        hid_vecs[1, :units],
        down_part,
        mid_vecs[3],
    )


def solution(mesh):
    in_specs = (
        P("dp", None),
        P("dp"),
        P("dp", None),
        P(),
        P(),
        P(None, None, "tensor"),
        P(None, "tensor"),
        P("tensor"),
        P("tensor"),
        P("tensor", None),
        P(),
        P(),
        P(),
        P(None, "tensor"),
        P("tensor"),
        P("tensor"),
        P("tensor"),
        P("tensor", None),
        P(),
    )
    out_specs = (
        P("dp", None),
        P("dp", None),
        P(),
        P(),
        P(None, "dp", "tensor"),
        P(None, "tensor"),
        P("tensor"),
        P("tensor"),
        P("tensor", "dp"),
        P(),
        P(),
        P(),
        P("dp", "tensor"),
        P("tensor"),
        P("tensor"),
        P("tensor"),
        P("tensor", "dp"),
        P(),
    )
    return jax.shard_map(body, mesh=mesh, in_specs=in_specs, out_specs=out_specs, check_vma=False)
```

```python
import functools
import math

import jax
import jax.numpy as jnp
import numpy as np
from jax import lax
from jax.experimental import pallas as pl
from jax.experimental.pallas import tpu as pltpu
from jax.sharding import PartitionSpec as P

D = 2048
HD = 64
FF = 8192
SLOT = 128
IMG = 64
SCALE_BASE = 512
HALF = D // 2

eps = 1e-05
root_half = 0.7071067811865476
inv_root_two_pi = 0.3989422804014327
masked_score = -1e30
MEGA = 1 << 20

COST = {
    "front": 15.6,
    "middle_norm": 7.5,
    "hidden_back": 400.0,
    "hidden_front": 14.7,
    "hidden_mid": 400.0,
    "hidden_grad": 7.0,
    "full_grad": 15.0,
    "ring_grads": 12.0,
    "result_part": 400.0,
    "middle_back": 11.0,
    "attention_back": 21.7,
    "tokens_back": 8.5,
    "output": 6.0,
}
WORK = 5.5e+07

F32 = jnp.float32
BF16 = jnp.bfloat16
NN = (((1,), (0,)), ((), ()))
NT = (((1,), (1,)), ((), ()))
TN = (((0,), (0,)), ((), ()))


def rounded(value):
    return value.astype(BF16)


def mul(left, right, dims=NN):
    return lax.dot_general(left, right, dims, preferred_element_type=F32)


def xpos_tables():
    place = np.arange(SLOT, dtype=np.float64)[:, None]
    lane = np.arange(128)[None, :]
    index = (lane % HD) // 2
    angle = place * 10000.0 ** (-2.0 * index / HD)
    zeta = (2.0 * index + 0.4 * HD) / (1.4 * HD)
    growth = zeta ** ((place - SLOT // 2) / SCALE_BASE)
    even = lane % 2 == 0
    found = []
    for factor in (growth / math.sqrt(HD), 1.0 / growth):
        found += [
            np.cos(angle) * factor,
            np.where(even, -np.sin(angle), 0.0) * factor,
            np.where(even, 0.0, np.sin(angle)) * factor,
        ]
    return jnp.asarray(np.tile(np.stack(found), (1, 2, 1)).astype(np.float32))


def rotate(value, tables, base, sign):
    up = pltpu.roll(value, 127, axis=1)
    down = pltpu.roll(value, 1, axis=1)
    turned = up * tables[base + 1] + down * tables[base + 2]
    return value * tables[base] + turned if sign > 0 else value * tables[base] - turned


def columns_of(parts):
    return jnp.transpose(parts)


def rows_of(columns):
    size = columns[0].shape[0]
    lane = lax.broadcasted_iota(jnp.int32, (size, 128), 1)
    tile = jnp.zeros((size, 128), F32)
    for at, column in enumerate(columns):
        tile = jnp.where(lane == at, column, tile)
    return jnp.transpose(tile)[:8]


def norm_parts(value):
    mean = jnp.mean(value, axis=-1, keepdims=True)
    var = jnp.mean(value * value, axis=-1, keepdims=True) - mean * mean
    inverse = lax.rsqrt(var + eps)
    return (value - mean) * inverse, inverse


def sum_rows(value):
    return jnp.sum(value, axis=0, keepdims=True)


def whole(array, **kw):
    rank = array.ndim
    return (array, array.shape, lambda *at: (0,) * rank)


def run(kernel, grid, ins, outs, scratch=(), prefetch=(), after=(), alias=None, limit=56, name=None):
    prefetch = tuple(prefetch)

    def body(*refs):
        refs = list(refs)
        first = len(prefetch) + len(ins)
        del refs[first : first + len(after)]
        kernel(*refs)

    in_specs = []
    for array, block, where in ins:
        if block is None:
            in_specs.append(pl.BlockSpec(memory_space=pl.ANY))
        elif tuple(block) == tuple(array.shape):
            in_specs.append(pl.BlockSpec(block, where, pipeline_mode=pl.Buffered(1)))
        else:
            in_specs.append(pl.BlockSpec(block, where))
    in_specs += [pl.BlockSpec(memory_space=pl.ANY)] * len(after)
    out_specs = [pl.BlockSpec(block, where) for shape, dtype, block, where in outs]
    out_shape = [jax.ShapeDtypeStruct(shape, dtype) for shape, dtype, block, where in outs]
    return pl.pallas_call(
        body,
        grid_spec=pltpu.PrefetchScalarGridSpec(
            num_scalar_prefetch=len(prefetch),
            grid=grid,
            in_specs=in_specs,
            out_specs=out_specs,
            scratch_shapes=list(scratch),
        ),
        out_shape=out_shape,
        input_output_aliases=alias or {},
        compiler_params=pltpu.CompilerParams(
            dimension_semantics=("arbitrary",) * len(grid), vmem_limit_bytes=limit * MEGA
        ),
        cost_estimate=pl.CostEstimate(flops=int(COST[name] * WORK), bytes_accessed=1000, transcendentals=0),
        name=name,
    )(*prefetch, *[array for array, block, where in ins], *after)


def flip(value, bit, size):
    return lax.ppermute(value, "tensor", [(t, t ^ (1 << bit)) for t in range(size)])


def all_pieces(own, bits):
    size = 1 << bits
    return [own] + [lax.ppermute(own, "tensor", [(t, t ^ k) for t in range(size)]) for k in range(1, size)]


class Line:
    def __init__(self):
        self.last = None

    def tie(self, value):
        if self.last is None:
            return value
        return lax.optimization_barrier((value,) + self.last)[0]

    def mark(self, *values):
        self.last = values


class Total:
    def __init__(self, line, parts, bits):
        self.line, self.bits = line, bits
        self.orders = [list(range(bits)), list(range(bits))[::-1]]
        self.left = [[bit for bit in range(bits) if bit != order[0]] for order in self.orders]
        self.keep = [parts[0], parts[2]]
        self.got = [flip(parts[1], self.orders[0][0], 1 << bits), flip(parts[3], self.orders[1][0], 1 << bits)]
        self.step = 1

    def advance(self):
        line, size = self.line, 1 << self.bits
        if self.step == self.bits:
            for half in range(2):
                self.keep[half] = line.tie(self.keep[half]) + self.got[half]
                line.mark(self.keep[half])
            return
        picks = []
        for half in range(2):
            left, bit = self.left[half], self.orders[half][self.step]
            keep, got = self.keep[half], self.got[half]
            cube = (2,) * len(left) + keep.shape[1:]
            axis = len(left) - 1 - left.index(bit)
            shape = (keep.shape[0] // 2,) + keep.shape[1:]
            pick = lambda value, at, cube=cube, axis=axis, shape=shape: lax.index_in_dim(
                value.reshape(cube), at, axis, keepdims=False
            ).reshape(shape)
            send = pick(line.tie(keep), 1) + pick(got, 1)
            line.mark(send)
            picks.append((pick, keep, got))
            self.got[half] = flip(send, bit, size)
            left.remove(bit)
        for half in range(2):
            pick, keep, got = picks[half]
            self.keep[half] = pick(line.tie(keep), 0) + pick(got, 0)
            line.mark(self.keep[half])
        self.step += 1

    def gather(self):
        size = 1 << self.bits
        if self.step == self.bits:
            self.held = [[0], [0]]
            self.step += 1
        else:
            for half in range(2):
                self.keep[half] = jnp.concatenate([self.line.tie(self.keep[half]), self.got[half]], 0)
                self.line.mark(self.keep[half])
                self.held[half] = self.held[half] + [block | self.last[half] for block in self.held[half]]
        self.last = [1 << self.orders[half].pop() for half in range(2)]
        self.got = [flip(self.keep[half], self.last[half].bit_length() - 1, size) for half in range(2)]

    def pieces(self):
        arrays, where = [], []
        for half in range(2):
            arrays += [self.keep[half], self.got[half]]
            found = {block: (2 * half, at) for at, block in enumerate(self.held[half])}
            found.update({block | self.last[half]: (2 * half + 1, at) for at, block in enumerate(self.held[half])})
            where.append(found)
        return arrays, where


class Ring:
    def __init__(self, line, first, rest, size):
        self.line, self.rest, self.size = line, rest, size
        self.step = 0
        self.got = self.send(first)

    def send(self, value):
        return lax.ppermute(value, "dp", [(d, (d + 2) % self.size) for d in range(self.size)])

    def advance(self):
        value = self.line.tie(self.rest)[self.step] + self.got
        self.line.mark(value)
        self.step += 1
        if self.step < self.size // 2 - 1:
            self.got = self.send(value)
        return value


def butterfly(value, bits):
    for bit in range(bits):
        value = value + flip(value, bit, 1 << bits)
    return value


def tree_sum(value):
    while value.shape[0] > 1:
        value = value.reshape((value.shape[0] // 2, 2) + value.shape[1:])
        value = value[:, 0] + value[:, 1]
    return value[0]


class Small:
    def __init__(self, own, bits):
        self.bits, self.bit, self.held = bits, 0, [own]
        self.got = None
        self.step()

    def step(self):
        if self.got is not None:
            many = len(self.held)
            self.held = self.held + [self.got[at] for at in range(many)]
        if self.bit < self.bits:
            self.got = flip(jnp.stack(self.held), self.bit, 1 << self.bits)
            self.bit += 1

    def pieces(self):
        while len(self.held) < 1 << self.bits:
            self.step()
        return self.held


def both_vectors(pieces):
    level = [piece[8:] for piece in pieces]
    while len(level) > 1:
        level = [level[at] + level[at + 1] for at in range(0, len(level), 2)]
    many = D // level[0].shape[1]
    return jnp.stack([level[0][:many].reshape(-1), level[0][4 : 4 + many].reshape(-1)])


def combine(pieces, block, blocks):
    level = [pieces[other][:8, (block ^ other) * SLOT : (block ^ other) * SLOT + SLOT] for other in range(blocks)]
    while len(level) > 1:
        level = [level[at] + level[at + 1] for at in range(0, len(level), 2)]
    return level[0]


def attention_scores(query, both_keys, length):
    scores = mul(query, both_keys, NT)
    row = lax.broadcasted_iota(jnp.int32, scores.shape, 0)
    place = lax.broadcasted_iota(jnp.int32, scores.shape, 1) % SLOT
    scores = jnp.where((place <= row) & (place < IMG + length), scores, masked_score)
    parts = []
    for at in range(2):
        part = scores[:, at * SLOT : (at + 1) * SLOT]
        expd = jnp.exp(part - jnp.max(part, axis=-1, keepdims=True))
        parts.append(expd / jnp.sum(expd, axis=-1, keepdims=True))
    return parts


def split_heads(value, mask):
    return jnp.concatenate([value * mask[0:1], value * mask[1:2]], axis=0)


def store_parts(refs, value, step, steps, only=None):
    left_keep, left_send, right_keep, right_send = refs
    left_keep[0] = value[:SLOT, :HALF]
    left_send[0] = value[SLOT:, :HALF]

    @pl.when(step < steps // 2)
    def _():
        right_keep[0] = value[:SLOT, HALF:]
        right_keep[1] = value[SLOT:, HALF:]

    @pl.when(step >= steps // 2)
    def _():
        right_send[0] = value[:SLOT, HALF:]
        right_send[1] = value[SLOT:, HALF:]


def part_outs(blocks):
    half = blocks // 2
    steps = blocks // 2
    shape = (half, SLOT, HALF)
    low = max(steps // 2, 1)
    return [
        (shape, F32, (1, SLOT, HALF), lambda s, *_: (s, 0, 0)),
        (shape, F32, (1, SLOT, HALF), lambda s, *_: (s, 0, 0)),
        (shape, F32, (2, SLOT, HALF), lambda s, *_: (jnp.minimum(s, low - 1), 0, 0)),
        (shape, F32, (2, SLOT, HALF), lambda s, *_: (jnp.maximum(s - steps // 2, 0), 0, 0)),
    ]


def front(order, lengths, tokens, gain, shift, weight, bias, tables, mask, mix_gain, uw_rows, out_weight, after=()):
    blocks = order.shape[0]
    steps = blocks // 2
    width = weight.shape[2]
    groups = width // 128
    rows = blocks * SLOT

    def kernel(order_ref, length_ref, x0, x1, g, b, w, wb, tab, msk, mg, uwr, ow, own, first, qkv, mixed, small, *parts_uw):
        step = pl.program_id(0)
        parts, uw = parts_uw[:4], parts_uw[4]

        @pl.when(step == 0)
        def _():
            found = mul(uwr[...], ow[...])
            uw[0:1] = found[0:1] + found[1:2] + found[2:3]
            uw[1:2] = found[3:4] + found[4:5] + found[5:6]
            small[8:] = jnp.zeros((8, rows), F32)
            for at in range(D // rows):
                c = slice(at * rows, at * rows + rows)
                small[8 + at : 9 + at] = uw[0:1, c]
                small[12 + at : 13 + at] = uw[1:2, c]

        x = jnp.concatenate([x0[0], x1[0]], axis=0)
        own[...] = x
        hat, _ = norm_parts(x.astype(F32))
        one = rounded(hat * g[...] + b[...])
        first[...] = one
        for c in range(3):
            proj = mul(one, w[c]) + wb[c : c + 1]
            for group in range(groups):
                part = proj[:, group * 128 : group * 128 + 128]
                if c < 2:
                    part = rotate(part, tab, 3 * c, 1)
                at = c * width + group * 128
                qkv[:, at : at + 128] = rounded(part)
        for pair in range(2):
            r = slice(pair * SLOT, pair * SLOT + SLOT)
            length = length_ref[order_ref[2 * step + pair]]
            for group in range(groups):
                at = group * 128
                query = qkv[r, at : at + 128]
                keys = split_heads(qkv[r, width + at : width + at + 128], msk)
                values = split_heads(qkv[r, 2 * width + at : 2 * width + at + 128], msk)
                probs = attention_scores(query, keys, length)
                mixed[r, at : at + 128] = mul(rounded(jnp.concatenate(probs, axis=1)), values)
        m = mixed[...]
        total = jnp.sum(m, axis=-1, keepdims=True)
        here = pl.ds(pl.multiple_of(step * 2 * SLOT, 2 * SLOT), 2 * SLOT)
        small[:8, here] = rows_of([total, jnp.sum(m * m, axis=-1, keepdims=True)])
        middle = total * (1.0 / width)
        partial = mul(rounded((m - middle) * mg[...]), ow[...]) + middle * uw[0:1]
        store_parts(parts, partial, step, steps)

    row2 = lambda s, *_: (s, 0)
    pair_of = lambda offset: lambda s, order_ref, length_ref: (order_ref[2 * s + offset], 0, 0)
    return run(
        kernel,
        (steps,),
        [
            (tokens, (1, SLOT, D), pair_of(0)),
            (tokens, (1, SLOT, D), pair_of(1)),
            whole(gain), whole(shift), whole(weight), whole(bias), whole(tables), whole(mask),
            whole(mix_gain), whole(uw_rows), whole(out_weight),
        ],
        [
            ((rows, D), BF16, (2 * SLOT, D), row2),
            ((rows, D), BF16, (2 * SLOT, D), row2),
            ((rows, 3 * width), BF16, (2 * SLOT, 3 * width), row2),
            ((rows, width), F32, (2 * SLOT, width), row2),
            ((16, rows), F32, (16, rows), lambda s, *_: (0, 0)),
        ]
        + part_outs(blocks),
        scratch=[pltpu.VMEM((8, D), F32)],
        prefetch=(order, lengths),
        after=after,
        name="front",
    )


def pieces_in(pieces):
    return [whole(piece) for piece in pieces[0]]


def load_pieces(refs, where, total, step, blocks):
    for block in range(blocks):

        @pl.when(step == block)
        def _(block=block):
            for half in range(2):
                array, at = where[half][block]
                total[:, half * HALF : half * HALF + HALF] = refs[array][at]


def middle_norm(own, pieces, sums, uw, out_bias, gain, shift, after=()):
    blocks = len(pieces[1][0])
    rows = blocks * SLOT

    def kernel(*refs):
        x, parts, stats = refs[0], refs[1:5], refs[5 : 5 + blocks]
        uw_ref, bias, g, b, mid, second, stat, total, tot8 = refs[5 + blocks :]
        step = pl.program_id(0)
        load_pieces(parts, pieces[1], total, step, blocks)
        for block in range(blocks):

            @pl.when(step == block)
            def _(block=block):
                tot8[...] = combine(stats, block, blocks)

        cols = columns_of(tot8[...])
        mean = cols[:, 0:1] * (1.0 / D)
        inverse = lax.rsqrt(cols[:, 1:2] * (1.0 / D) - mean * mean + eps)
        branch = inverse * (total[...] - mean * uw_ref[0:1]) + uw_ref[1:2]
        value = x[...].astype(F32) + branch + bias[...]
        mid[...] = value
        hat, _ = norm_parts(value)
        second[...] = rounded(hat * g[...] + b[...])
        lane = lax.broadcasted_iota(jnp.int32, (SLOT, 128), 1)
        stat[...] = jnp.where(lane == 0, mean, inverse)

    row = lambda k, *_: (k, 0)
    return run(
        kernel,
        (blocks,),
        [(own, (SLOT, D), row)]
        + pieces_in(pieces)
        + [whole(part) for part in sums]
        + [whole(uw), whole(out_bias), whole(gain), whole(shift)],
        [
            ((rows, D), F32, (SLOT, D), row),
            ((rows, D), BF16, (SLOT, D), row),
            ((rows, 128), F32, (SLOT, 128), row),
        ],
        scratch=[pltpu.VMEM((SLOT, D), F32), pltpu.VMEM((8, SLOT), F32)],
        after=after,
        name="middle_norm",
    )


def hidden_back(cots, down_weight):
    many, rows, units = len(cots), cots[0].shape[0], down_weight.shape[0]
    tile = min(512, units)

    def kernel(*refs):
        w, out = refs[many:]
        for at in range(many):
            out[at * rows : at * rows + rows] = rounded(mul(refs[at][...], w[...], NT))

    return run(
        kernel,
        (units // tile,),
        [whole(cot) for cot in cots] + [(down_weight, (tile, D), lambda j: (j, 0))],
        [((many * rows, units), BF16, (many * rows, tile), lambda j: (0, j))],
        name="hidden_back",
    )[0]


def hidden_front(chunk, second, up_weight, up_bias, back, gain, after=()):
    rows, units = second.shape[0], up_weight.shape[1]
    tile = 512
    steps = units // tile

    def part_of(c, s_ref, w, b, hb, g, act, slp):
        hidden = mul(s_ref[...], w[:, c]) + b[:, c]
        tail = jnp.exp(-0.5 * hidden * hidden)
        t = 1.0 / (1.0 + (0.3275911 * root_half) * jnp.abs(hidden))
        poly = 1.061405429 * t - 1.453152027
        poly = poly * t + 1.421413741
        poly = poly * t - 0.284496736
        poly = poly * t + 0.254829592
        half = 0.5 * poly * t * tail
        phi = jnp.where(hidden >= 0.0, 1.0 - half, half)
        active = hidden * phi
        act[:, c] = rounded(active)
        slp[:, c] = rounded(phi + hidden * (inv_root_two_pi * tail))
        scaled = hb[:, c].astype(F32) * g[:, c]
        return [value[:, :128] + value[:, 128:] for value in (active, active * active, scaled, scaled * active)]

    def kernel(s_ref, w, b, hb, g, act, slp, sums, acc):
        step = pl.program_id(0)
        found = [part_of(slice(at, at + 256), s_ref, w, b, hb, g, act, slp) for at in range(0, tile, 256)]

        @pl.when(step == 0)
        def _():
            for at in range(4):
                acc[at] = found[0][at] + found[1][at]

        @pl.when(step > 0)
        def _():
            for at in range(4):
                acc[at] += found[0][at] + found[1][at]

        @pl.when(step == steps - 1)
        def _():
            for block in range(rows // SLOT):
                r = slice(block * SLOT, block * SLOT + SLOT)
                sums[:, r] = rows_of([jnp.sum(acc[at, r], axis=-1, keepdims=True) for at in range(4)])

    return run(
        kernel,
        (steps,),
        [
            whole(second),
            (up_weight, (D, tile), lambda j: (0, j)),
            (up_bias, (1, tile), lambda j: (0, j)),
            (back, (rows, tile), lambda j: (chunk, j)),
            (gain, (1, tile), lambda j: (0, j)),
        ],
        [
            ((rows, units), BF16, (rows, tile), lambda j: (0, j)),
            ((rows, units), BF16, (rows, tile), lambda j: (0, j)),
            ((8, rows), F32, (8, rows), lambda j: (0, 0)),
        ],
        scratch=[pltpu.VMEM((4, rows, 128), F32)],
        after=after,
        name="hidden_front",
    )


def hidden_mid(chunk, active, slope, back, sums, gain, shift):
    blocks = len(sums)
    rows, units = active.shape

    def kernel(act, slp, hb, *refs):
        stats = refs[:blocks]
        g, b, low, grad, vecs, tot8 = refs[blocks:]
        step = pl.program_id(0)
        for block in range(blocks):

            @pl.when(step == block)
            def _(block=block):
                tot8[...] = combine(stats, block, blocks)

        cols = columns_of(tot8[...]) * (1.0 / FF)
        mean = cols[:, 0:1]
        inverse = lax.rsqrt(cols[:, 1:2] - mean * mean + eps)
        one = cols[:, 2:3]
        two = inverse * (cols[:, 3:4] - mean * one)
        for at in range(0, units, 256):
            c = slice(at, at + 256)
            hat = (act[:, c].astype(F32) - mean) * inverse
            low[:, c] = rounded(hat * g[:, c] + b[:, c])
            raw = hb[:, c].astype(F32)
            grown = rounded(inverse * (raw * g[:, c] - one - hat * two) * slp[:, c].astype(F32))
            grad[:, c] = grown
            vecs[0, 0:1, c] = sum_rows(raw * hat)
            vecs[0, 1:2, c] = sum_rows(raw)
            vecs[0, 2:3, c] = sum_rows(grown.astype(F32))

    row = lambda k: (k, 0)
    return run(
        kernel,
        (blocks,),
        [
            (active, (SLOT, units), row),
            (slope, (SLOT, units), row),
            (back, (SLOT, units), lambda k: (chunk * blocks + k, 0)),
        ]
        + [whole(part) for part in sums]
        + [whole(gain), whole(shift)],
        [
            ((rows, units), BF16, (SLOT, units), row),
            ((rows, units), BF16, (SLOT, units), row),
            ((blocks, 8, units), F32, (1, 8, units), lambda k: (k, 0, 0)),
        ],
        scratch=[pltpu.VMEM((8, SLOT), F32)],
        name="hidden_mid",
    )


def hidden_grad(grad, up_weight):
    rows, units = grad.shape
    blocks = rows // SLOT
    tile = 512
    steps = D // tile
    half = steps // 2

    def kernel(gr, w, left_keep, left_send, right_keep, right_send):
        step = pl.program_id(0)
        value = mul(gr[...], w[...], NT)

        @pl.when(step < half)
        def _():
            for block in range(blocks):
                r = slice(block * SLOT, block * SLOT + SLOT)
                (left_send if block & 1 else left_keep)[block // 2] = value[r]

        @pl.when(step >= half)
        def _():
            for block in range(blocks):
                r = slice(block * SLOT, block * SLOT + SLOT)
                (right_send if block >= blocks // 2 else right_keep)[block % (blocks // 2)] = value[r]

    shape = (blocks // 2, SLOT, HALF)
    block_shape = (blocks // 2, SLOT, tile)
    lefts = lambda j: (0, 0, jnp.minimum(j, half - 1))
    rights = lambda j: (0, 0, jnp.maximum(j - half, 0))
    return run(
        kernel,
        (steps,),
        [whole(grad), (up_weight, (tile, units), lambda j: (j, 0))],
        [
            (shape, F32, block_shape, lefts),
            (shape, F32, block_shape, lefts),
            (shape, F32, block_shape, rights),
            (shape, F32, block_shape, rights),
        ],
        name="hidden_grad",
    )


def result_part(order, lows, down_weight):
    pairs = order.shape[0]
    units = down_weight.shape[0]
    many = len(lows)
    rows = lows[0].shape[0]
    each = rows // SLOT
    tile = 256

    def kernel(order_ref, *refs):
        w, out = refs[many:]
        for at in range(many):
            value = mul(refs[at][...], w[...])
            for block in range(each):
                out[order_ref[at * each + block]] = value[block * SLOT : block * SLOT + SLOT]

    return run(
        kernel,
        (D // tile,),
        [whole(low) for low in lows] + [(down_weight, (units, tile), lambda j, *_: (0, j))],
        [((pairs, SLOT, D), F32, (pairs, SLOT, tile), lambda j, *_: (0, 0, j))],
        prefetch=(order,),
        name="result_part",
    )[0]


def middle_back(own, cot, pieces, middle, stat, uw, out_bias, gain, after=()):
    blocks = len(pieces[1][0])
    rows = blocks * SLOT

    def kernel(*refs):
        x, c, parts = refs[0], refs[1], refs[2:6]
        mid, st, uw_ref, bias, g, grad, low, stat2, vecs, total = refs[6:]
        load_pieces(parts, pieces[1], total, pl.program_id(0), blocks)
        value = mid[...]
        hat, inverse = norm_parts(value)
        sec = total[...]
        scaled = sec * g[...]
        up = c[...].astype(F32)
        out = up + inverse * (
            scaled
            - jnp.mean(scaled, axis=-1, keepdims=True)
            - hat * jnp.mean(scaled * hat, axis=-1, keepdims=True)
        )
        grad[...] = out
        lowered = rounded(out)
        low[...] = lowered
        low32 = lowered.astype(F32)
        one = jnp.mean(low32 * uw_ref[0:1], axis=-1, keepdims=True)
        moved = value - x[...].astype(F32) - bias[...] - uw_ref[1:2]
        two = jnp.mean(low32 * moved, axis=-1, keepdims=True)
        lane = lax.broadcasted_iota(jnp.int32, (SLOT, 128), 1)
        stat2[...] = jnp.where(lane == 2, one, jnp.where(lane == 3, two, st[...]))
        vecs[0, 0:1] = sum_rows(sec * hat)
        vecs[0, 1:2] = sum_rows(sec)
        vecs[0, 2:3] = sum_rows(out)
        vecs[0, 3:4] = sum_rows(up)

    row = lambda k, *_: (k, 0)
    return run(
        kernel,
        (blocks,),
        [(own, (SLOT, D), row), (cot, (SLOT, D), row)]
        + pieces_in(pieces)
        + [(middle, (SLOT, D), row), (stat, (SLOT, 128), row), whole(uw), whole(out_bias), whole(gain)],
        [
            ((rows, D), F32, (SLOT, D), row),
            ((rows, D), BF16, (SLOT, D), row),
            ((rows, 128), F32, (SLOT, 128), row),
            ((blocks, 8, D), F32, (1, 8, D), lambda k, *_: (k, 0, 0)),
        ],
        scratch=[pltpu.VMEM((SLOT, D), F32)],
        after=after,
        name="middle_back",
    )


def attention_back(order, lengths, low, stat, mixed, qkv, own, mix_gain, mix_shift, out_weight, weight, tables, mask, after=()):
    blocks = order.shape[0]
    steps = blocks // 2
    width = out_weight.shape[0]
    groups = width // 128
    rows = blocks * SLOT

    def kernel(
        order_ref, length_ref, low_ref, st, mx, qkv_ref, x, mg, ms, ow, w, tab, msk,
        mix_low, dproj, vecs, wide, left_keep, left_send, right_keep, right_send, dmixed,
    ):
        step = pl.program_id(0)
        mean, inverse, one, two = (st[:, at : at + 1] for at in range(4))
        back = mul(low_ref[...], ow[...], NT)
        hat = (mx[...] - mean) * inverse
        mix_low[...] = rounded(hat * mg[...] + ms[...])
        dmixed[...] = rounded(inverse * (back * mg[...] - one - hat * two))
        vecs[0, 0:1, :width] = sum_rows(back * hat)
        vecs[0, 1:2, :width] = sum_rows(back)
        first_half = lax.broadcasted_iota(jnp.int32, (SLOT, 128), 1) < HD
        for pair in range(2):
            r = slice(pair * SLOT, pair * SLOT + SLOT)
            length = length_ref[order_ref[2 * step + pair]]
            for group in range(groups):
                at = group * 128
                query = qkv_ref[r, at : at + 128]
                keys = split_heads(qkv_ref[r, width + at : width + at + 128], msk)
                values = split_heads(qkv_ref[r, 2 * width + at : 2 * width + at + 128], msk)
                grad = dmixed[r, at : at + 128]
                probs = attention_scores(query, keys, length)
                dprobs = mul(grad, values, NT)
                dscores = []
                for i in range(2):
                    dp = dprobs[:, i * SLOT : (i + 1) * SLOT]
                    carried = jnp.sum(probs[i] * dp, axis=-1, keepdims=True)
                    dscores.append(rounded(probs[i] * (dp - carried)))
                dscores = jnp.concatenate(dscores, axis=1)
                dquery = mul(dscores, keys)
                dkey = mul(dscores, query, TN)
                dvalue = mul(rounded(jnp.concatenate(probs, axis=1)), grad, TN)
                dkey = jnp.where(first_half, dkey[:SLOT], dkey[SLOT:])
                dvalue = jnp.where(first_half, dvalue[:SLOT], dvalue[SLOT:])
                tabs = [tab[i, :SLOT] for i in range(6)]
                dproj[r, at : at + 128] = rounded(rotate(dquery, tabs, 0, -1))
                dproj[r, width + at : width + at + 128] = rounded(rotate(dkey, tabs, 3, -1))
                dproj[r, 2 * width + at : 2 * width + at + 128] = rounded(dvalue)
        vecs[0, 2:3] = sum_rows(dproj[...].astype(F32))
        partial = mul(dproj[:, :width], w[0], NT)
        for c in (1, 2):
            partial += mul(dproj[:, c * width : (c + 1) * width], w[c], NT)
        pre_hat, _ = norm_parts(x[...].astype(F32))
        grown = partial * pre_hat
        wide[0, 0:1] = sum_rows(grown[:SLOT]) + sum_rows(grown[SLOT:])
        wide[0, 1:2] = sum_rows(partial[:SLOT]) + sum_rows(partial[SLOT:])
        store_parts((left_keep, left_send, right_keep, right_send), partial, step, steps)

    row2 = lambda s, *_: (s, 0)
    return run(
        kernel,
        (steps,),
        [
            (low, (2 * SLOT, D), row2),
            (stat, (2 * SLOT, 128), row2),
            (mixed, (2 * SLOT, width), row2),
            (qkv, (2 * SLOT, 3 * width), row2),
            (own, (2 * SLOT, D), row2),
            whole(mix_gain), whole(mix_shift), whole(out_weight), whole(weight), whole(tables), whole(mask),
        ],
        [
            ((rows, width), BF16, (2 * SLOT, width), row2),
            ((rows, 3 * width), BF16, (2 * SLOT, 3 * width), row2),
            ((steps, 8, 3 * width), F32, (1, 8, 3 * width), lambda s, *_: (s, 0, 0)),
            ((steps, 8, D), F32, (1, 8, D), lambda s, *_: (s, 0, 0)),
        ]
        + part_outs(blocks),
        scratch=[pltpu.VMEM((2 * SLOT, width), BF16)],
        prefetch=(order, lengths),
        after=after,
        name="attention_back",
    )


def tokens_back(order, own, grad, pieces, gain, before, pairs, after=()):
    blocks = len(pieces[1][0])

    def kernel(order_ref, x, gr, *refs):
        parts = refs[:4]
        g = refs[4]
        out, total = refs[-2:]
        load_pieces(parts, pieces[1], total, pl.program_id(0), blocks)
        hat, inverse = norm_parts(x[...].astype(F32))
        scaled = total[...] * g[...]
        out[0] = gr[...] + inverse * (
            scaled
            - jnp.mean(scaled, axis=-1, keepdims=True)
            - hat * jnp.mean(scaled * hat, axis=-1, keepdims=True)
        )

    row = lambda k, *_: (k, 0)
    ins = [(own, (SLOT, D), row), (grad, (SLOT, D), row)] + pieces_in(pieces) + [whole(gain)]
    alias = None
    if before is not None:
        alias = {1 + len(ins): 0}
        ins = ins + [(before, None, None)]
    return run(
        kernel,
        (blocks,),
        ins,
        [((pairs, SLOT, D), F32, (1, SLOT, D), lambda k, o: (o[k], 0, 0))],
        scratch=[pltpu.VMEM((SLOT, D), F32)],
        prefetch=(order,),
        after=after,
        alias=alias,
        name="tokens_back",
    )[0]


def output_of(order, middle, result, bias, before, after=()):
    blocks = order.shape[0]

    def kernel(order_ref, mid, res, b, *refs):
        out = refs[-1]
        out[0] = rounded(mid[...] + res[0] + b[...])

    ins = [
        (middle, (SLOT, D), lambda k, *_: (k, 0)),
        (result, (1, SLOT, D), lambda k, o: (o[k], 0, 0)),
        whole(bias),
    ]
    alias = None
    if before is not None:
        alias = {1 + len(ins): 0}
        ins = ins + [(before, None, None)]
    return run(
        kernel,
        (blocks,),
        ins,
        [(result.shape, BF16, (1, SLOT, D), lambda k, o: (o[k], 0, 0))],
        prefetch=(order,),
        after=after,
        alias=alias,
        name="output",
    )[0]


def ring_grads(ids, products, got=None):
    count, many = ids.shape[0], len(products[0][0])
    rows = products[0][0][0].shape[0]
    widths = [rights[0].shape[1] for lefts, rights in products]
    block = D // (2 * count)
    shape = (block, sum(widths))

    def kernel(ids_ref, *refs):
        outs = refs[2 * many * len(products) + (got is not None) :]
        step = pl.program_id(0)
        start = 0
        for at, width in enumerate(widths):
            left, right = (refs[(2 * at + side) * many : (2 * at + side + 1) * many] for side in range(2))
            value = mul(left[0][...], right[0][...], TN)
            for k in range(1, many):
                value += mul(left[k][...], right[k][...], TN)
            c = slice(start, start + width)
            start += width
            if got is None:
                outs[0][0, :, c] = value
                continue
            value += refs[2 * many * len(products)][0, :, c]

            @pl.when(step == 0)
            def _(value=value, c=c):
                outs[0][:, c] = value

            @pl.when(step > 0)
            def _(value=value, c=c):
                outs[1][0, :, c] = value

    fixed = lambda i, *_: (0, 0)
    moving = lambda i, ids_ref: (0, ids_ref[i])
    lead = lambda i, *_: (i, 0, 0)
    ins = []
    for lefts, rights in products:
        ins += [(left, (rows, block), moving) for left in lefts]
        ins += [(right, right.shape, fixed) for right in rights]
    if got is None:
        outs = [((count,) + shape, F32, (1,) + shape, lead)]
    else:
        ins += [(got, (1,) + shape, lead)]
        outs = [
            (shape, F32, shape, fixed),
            ((count - 1,) + shape, F32, (1,) + shape, lambda i, *_: (jnp.maximum(i - 1, 0), 0, 0)),
        ]
    return run(kernel, (count,), ins, outs, prefetch=(ids,), name="ring_grads")


def full_grad(products):
    many, block = len(products[0][0]), 512
    rows, tall = products[0][0][0].shape
    widths = [rights[0].shape[1] for lefts, rights in products]

    def kernel(*refs):
        out, start = refs[-1], 0
        for at, width in enumerate(widths):
            left, right = (refs[(2 * at + side) * many : (2 * at + side + 1) * many] for side in range(2))
            value = mul(left[0][...], right[0][...], TN)
            for k in range(1, many):
                value += mul(left[k][...], right[k][...], TN)
            out[:, start : start + width] = value
            start += width

    ins = []
    for lefts, rights in products:
        ins += [(left, (rows, block), lambda i: (0, i)) for left in lefts]
        ins += [(right, right.shape, lambda i: (0, 0)) for right in rights]
    wide = sum(widths)
    return run(
        kernel, (tall // block,), ins, [((tall, wide), F32, (block, wide), lambda i: (i, 0))], name="full_grad"
    )[0]


def steps_of(totals, bits, done, until):
    done = list(done)

    def step(at):
        if done[at] < bits:
            totals[at].advance()
        else:
            totals[at].gather()
        done[at] += 1
        if done[at] == bits and until == 2 * bits:
            totals[at].gather()
            done[at] += 1

    limits = [until] + [until if until == 2 * bits else bits - 1] * (len(totals) - 1)
    while any(have < limit for have, limit in zip(done, limits)):
        for at in range(len(totals)):
            if done[at] < limits[at]:
                step(at)


def split_rows(value):
    found = []
    for _ in range(3):
        part = lax.reduce_precision(value, 8, 7)
        found.append(part.astype(BF16))
        value = value - part
    return found


def body(
    tokens,
    lengths,
    cotangent,
    pre_gain,
    pre_shift,
    qkv_weight,
    qkv_bias,
    mix_gain,
    mix_shift,
    out_weight,
    out_bias,
    ffn_gain,
    ffn_shift,
    up_weight,
    up_bias,
    hid_gain,
    hid_shift,
    down_weight,
    down_bias,
):
    pairs = lengths.shape[0]
    blocks = lax.axis_size("tensor")
    bits = blocks.bit_length() - 1
    chunks = pairs // blocks
    width = qkv_weight.shape[2]
    mine = lax.axis_index("tensor").astype(jnp.int32)
    orders = [jnp.arange(c * blocks, (c + 1) * blocks, dtype=jnp.int32) ^ mine for c in range(chunks)]
    tokens3 = tokens.reshape(pairs, SLOT, D)
    row = lambda v: v.reshape(1, -1)
    pre_gain, pre_shift, mix_gain, mix_shift = map(row, (pre_gain, pre_shift, mix_gain, mix_shift))
    out_bias, ffn_gain, ffn_shift, up_bias = map(row, (out_bias, ffn_gain, ffn_shift, up_bias))
    hid_gain, hid_shift, down_bias = map(row, (hid_gain, hid_shift, down_bias))
    tables = xpos_tables()
    lane = np.arange(128)[None, :] < HD
    mask = jnp.asarray(np.concatenate([lane, ~lane], 0).astype(np.float32)).astype(BF16)
    zero = jnp.zeros((2, width), BF16)
    uw_rows = jnp.concatenate(split_rows(mix_gain) + split_rows(mix_shift) + [zero], 0)

    line = Line()
    dp_size = lax.axis_size("dp")
    place = lax.axis_index("dp").astype(jnp.int32)
    count = dp_size // 2
    around = lax.rem(place // 2 + count - 1 - jnp.arange(count, dtype=jnp.int32), count)
    mine_ids, other_ids = 2 * around + lax.rem(place, 2), 2 * around + 1 - lax.rem(place, 2)

    def tied(products):
        (lefts, rights), others = products[0], products[1:]
        return [([line.tie(lefts[0])] + lefts[1:], rights)] + others

    def full(products):
        grad = full_grad(tied(products))
        line.mark(grad)
        return grad

    every = lambda items, name: [item[name] for item in items]

    ones, twos, threes = [], [], []
    for c in range(chunks):
        found = front(
            orders[c], lengths, line.tie(tokens3), pre_gain, pre_shift, qkv_weight, qkv_bias, tables, mask, mix_gain, uw_rows,
            out_weight,
        )
        own, first, qkv, mixed, small = found[:5]
        one = dict(own=own, first=first, qkv=qkv, mixed=mixed, parts=found[5:])
        line.mark(small)
        one["small"] = small
        if c == 0:
            one["total"] = Total(line, one["parts"], bits)
            one["sums"] = Small(small, bits)
        ones.append(one)
    sums0 = ones[0]["sums"]
    if bits > 1:
        ones[0]["total"].advance()
    for c in range(1, chunks):
        ones[c]["total"] = Total(line, [line.tie(part) for part in ones[c]["parts"]], bits)
    sums0.held[0] = line.tie(sums0.held[0])
    sums0.step()
    cot3 = cotangent.reshape(pairs, SLOT, D)
    cots = []
    for c in range(chunks):
        cots.append(line.tie(cot3)[orders[c]].reshape(-1, D))
        line.mark(cots[-1])
    totals = every(ones, "total")
    line.mark(*line.last, *sums0.pieces())
    for step in range(1, bits):
        totals[0].advance()
    back = hidden_back([line.tie(cots[0])] + cots[1:], down_weight)
    line.mark(back)
    for one in ones[1:]:
        one["sums"] = Small(line.tie(one["small"]), bits)
    done = [bits] + [0] * (chunks - 1)
    steps_of(totals, bits, done, 2 * bits - 1)
    for one in ones[1:]:
        line.mark(*line.last, one["sums"].got)
        one["sums"].step()
    uw_total = both_vectors(sums0.pieces())

    def mid_of(c):
        two = twos[c]
        low, grad, vecs = hidden_mid(c, line.tie(two["active"]), two["slope"], back, two["sums"], hid_gain, hid_shift)
        two.update(low=low, grad=grad, vecs=functools.reduce(jnp.add, [vecs[k] for k in range(blocks)]))
        line.mark(vecs)

    def hidden_of(c):
        parts = hidden_grad(line.tie(twos[c]["grad"]), up_weight)
        line.mark(parts[0])
        return parts

    totals[0].gather()
    for c in range(chunks):
        one = ones[c]
        mid, second, stat = middle_norm(
            line.tie(one["own"]), totals[c].pieces(), one["sums"].pieces(), uw_total, out_bias, ffn_gain, ffn_shift
        )
        line.mark(stat)
        if c == 0:
            for total in totals[1:]:
                total.advance()
                total.gather()
            for other in ones[1:]:
                line.mark(*line.last, *other["sums"].pieces())
        active, slope, sums = hidden_front(c, line.tie(second), up_weight, up_bias, back, hid_gain)
        line.mark(sums)
        twos.append(dict(middle=mid, second=second, stat=stat, active=active, slope=slope, sums=all_pieces(sums, bits)))
        if c == 0:
            for total in totals[1:]:
                for step in range(1, bits):
                    total.gather()
            line.mark(*line.last, *twos[0]["sums"][1:])
        else:
            twos[0]["total"].advance()
            line.mark(*line.last, *twos[c]["sums"][1:])
        mid_of(c)
        if c > 0:
            line.mark(*line.last, *twos[0]["total"].got)
        if c == 0 and chunks > 1:
            twos[0]["total"] = Total(line, hidden_of(0), bits)
    lows = every(twos, "low")
    down_grad = full([(lows, cots)])
    down_part = lax.psum_scatter(down_grad, "dp", scatter_dimension=1, tiled=True)
    up_products = [(every(twos, "second"), every(twos, "grad"))]
    sent = ring_grads(other_ids, tied(up_products))[0]
    line.mark(sent)
    sent = lax.ppermute(sent, "dp", [(d, d ^ 1) for d in range(dp_size)])
    if chunks > 1:
        for step in range(1, bits):
            twos[0]["total"].advance()
        twos[0]["total"].gather()
        parts = [None] + [hidden_of(c) for c in range(1, chunks)]
    else:
        twos[0]["total"] = Total(line, hidden_of(0), bits)
        for step in range(bits):
            twos[0]["total"].advance()
        twos[0]["total"].gather()
    ring_first, ring_rest = ring_grads(mine_ids, tied(up_products), sent)
    line.mark(ring_rest)
    ring = Ring(line, ring_first, ring_rest, dp_size)
    for step in range(1, bits):
        twos[0]["total"].gather()
    for c in range(1, chunks):
        twos[c]["total"] = Total(line, [line.tie(part) for part in parts[c]], bits)
    totals = every(twos, "total")
    result = result_part(jnp.concatenate(orders), [line.tie(lows[0])] + lows[1:], down_weight)
    line.mark(result)

    for c in range(chunks):
        one, two = ones[c], twos[c]
        grad, low, stat2, vecs = middle_back(
            line.tie(one["own"]), cots[c], two["total"].pieces(), two["middle"], two["stat"], uw_total, out_bias, ffn_gain
        )
        line.mark(stat2)
        if c == 0:
            for total in totals[1:]:
                total.advance()
        found = attention_back(
            orders[c], lengths, line.tie(low), stat2, one["mixed"], one["qkv"], one["own"], mix_gain, mix_shift, out_weight,
            qkv_weight, tables, mask,
        )
        line.mark(found[2])
        three = dict(grad=grad, low=low, vecs=tree_sum(vecs), mix_low=found[0], dproj=found[1])
        three["narrow"] = tree_sum(found[2])
        three["wide"] = tree_sum(found[3])
        parts = found[4:]
        if c == 0 and chunks > 1:
            for total in totals[1:]:
                for step in range(1, bits):
                    total.advance()
                for step in range(bits):
                    total.gather()
            for total in totals[1:]:
                line.mark(*line.last, *total.got)
            up_part = ring.advance()
            result = lax.psum(line.tie(result), "tensor")
            parts = [line.tie(part) for part in parts]
        three["total"] = Total(line, parts, bits)
        threes.append(three)

    first, last = threes[0]["total"], threes[-1]["total"]
    add = lambda items, name, size: functools.reduce(jnp.add, [item[name] for item in items])[:size]
    pad = lambda v: jnp.pad(v, ((0, 0), (0, D - v.shape[1])))
    wide = add(threes, "wide", 2)
    got = flip(wide, 0, blocks)
    attention_grad = full(
        [(every(ones, "first"), every(threes, "dproj")), (every(threes, "low"), every(threes, "mix_low"))]
    )
    if chunks == 1:
        up_part = ring.advance()
        result = lax.psum(line.tie(result), "tensor")
    for step in range(bits):
        first.advance()
    first.gather()
    if chunks > 1:
        last.advance()
    line.mark(*line.last, down_part)
    up_part = ring.advance()
    attention_part = lax.psum_scatter(line.tie(attention_grad), "dp", scatter_dimension=0, tiled=True)
    for step in range(1, bits):
        first.gather()
    if chunks > 1:
        for step in range(1, bits):
            last.advance()
        last.gather()
    for bit in range(1, bits):
        wide = line.tie(wide) + got
        got = flip(wide, bit, blocks)
        line.mark(wide)
    if chunks > 1:
        line.mark(*line.last, *last.got)
    hop = lambda v, bit: lax.ppermute(v, "dp", [(d, d ^ (1 << bit)) for d in range(dp_size)])
    dp_bits = dp_size.bit_length() - 1
    tokens_grad, output = None, None
    for c in range(chunks):
        tokens_grad = tokens_back(
            orders[c], line.tie(ones[c]["own"]), threes[c]["grad"], threes[c]["total"].pieces(), pre_gain, tokens_grad, pairs
        )
        line.mark(tokens_grad)
        if c == 0:
            wide = line.tie(wide) + got
            vecs = jnp.concatenate(
                [pad(add(twos, "vecs", 3)), add(threes, "vecs", 4), pad(add(threes, "narrow", 3)), wide], 0
            )
            line.mark(vecs)
            got = hop(vecs, 0)
            for step in range(2, count - 1):
                up_part = ring.advance()
            if chunks > 1:
                for step in range(1, bits):
                    last.gather()
            vecs = line.tie(vecs) + got
            line.mark(vecs)
            got = hop(vecs, 1)
    for bit in range(2, dp_bits):
        vecs = line.tie(vecs) + got
        line.mark(vecs)
        got = hop(vecs, bit)
    for c in range(chunks):
        output = output_of(orders[c], line.tie(twos[c]["middle"]), result, down_bias, output)
        line.mark(output)
    vecs = vecs + got
    hid_vecs, mid_vecs, narrow, wide = vecs[:3], vecs[3:7], vecs[7:10], vecs[10:12]
    qkv_part = jnp.swapaxes(attention_part[:, : 3 * width].reshape(-1, 3, width), 0, 1)
    out_part = jnp.transpose(attention_part[:, 3 * width :])
    units = hid_gain.shape[1]
    return (
        output.reshape(-1, D),
        tokens_grad.reshape(-1, D),
        wide[0],
        wide[1],
        qkv_part,
        narrow[2, : 3 * width].reshape(3, width),
        narrow[0, :width],
        narrow[1, :width],
        out_part,
        mid_vecs[2],
        mid_vecs[0],
        mid_vecs[1],
        up_part,
        hid_vecs[2, :units],
        hid_vecs[0, :units],
        hid_vecs[1, :units],
        down_part,
        mid_vecs[3],
    )


def solution(mesh):
    in_specs = (
        P("dp", None),
        P("dp"),
        P("dp", None),
        P(),
        P(),
        P(None, None, "tensor"),
        P(None, "tensor"),
        P("tensor"),
        P("tensor"),
        P("tensor", None),
        P(),
        P(),
        P(),
        P(None, "tensor"),
        P("tensor"),
        P("tensor"),
        P("tensor"),
        P("tensor", None),
        P(),
    )
    out_specs = (
        P("dp", None),
        P("dp", None),
        P(),
        P(),
        P(None, "dp", "tensor"),
        P(None, "tensor"),
        P("tensor"),
        P("tensor"),
        P("tensor", "dp"),
        P(),
        P(),
        P(),
        P("dp", "tensor"),
        P("tensor"),
        P("tensor"),
        P("tensor"),
        P("tensor", "dp"),
        P(),
    )
    return jax.shard_map(body, mesh=mesh, in_specs=in_specs, out_specs=out_specs, check_vma=False)
```

```python
import functools
import math

import jax
import jax.numpy as jnp
import numpy as np
from jax import lax
from jax.experimental import pallas as pl
from jax.experimental.pallas import tpu as pltpu
from jax.sharding import PartitionSpec as P

D = 2048
HD = 64
FF = 8192
SLOT = 128
IMG = 64
SCALE_BASE = 512
HALF = D // 2

eps = 1e-05
root_half = 0.7071067811865476
inv_root_two_pi = 0.3989422804014327
masked_score = -1e30
MEGA = 1 << 20

COST = {
    "front": 15.6,
    "middle_norm": 400.0,
    "hidden_back": 400.0,
    "hidden_front": 14.7,
    "hidden_mid": 400.0,
    "hidden_grad": 7.0,
    "full_grad": 15.0,
    "ring_grads": 12.0,
    "result_part": 400.0,
    "middle_back": 11.0,
    "attention_back": 21.7,
    "tokens_back": 8.5,
    "output": 6.0,
}
WORK = 5.5e+07

F32 = jnp.float32
BF16 = jnp.bfloat16
NN = (((1,), (0,)), ((), ()))
NT = (((1,), (1,)), ((), ()))
TN = (((0,), (0,)), ((), ()))


def rounded(value):
    return value.astype(BF16)


def mul(left, right, dims=NN):
    return lax.dot_general(left, right, dims, preferred_element_type=F32)


def xpos_tables():
    place = np.arange(SLOT, dtype=np.float64)[:, None]
    lane = np.arange(128)[None, :]
    index = (lane % HD) // 2
    angle = place * 10000.0 ** (-2.0 * index / HD)
    zeta = (2.0 * index + 0.4 * HD) / (1.4 * HD)
    growth = zeta ** ((place - SLOT // 2) / SCALE_BASE)
    even = lane % 2 == 0
    found = []
    for factor in (growth / math.sqrt(HD), 1.0 / growth):
        found += [
            np.cos(angle) * factor,
            np.where(even, -np.sin(angle), 0.0) * factor,
            np.where(even, 0.0, np.sin(angle)) * factor,
        ]
    return jnp.asarray(np.tile(np.stack(found), (1, 2, 1)).astype(np.float32))


def rotate(value, tables, base, sign):
    up = pltpu.roll(value, 127, axis=1)
    down = pltpu.roll(value, 1, axis=1)
    turned = up * tables[base + 1] + down * tables[base + 2]
    return value * tables[base] + turned if sign > 0 else value * tables[base] - turned


def columns_of(parts):
    return jnp.transpose(parts)


def rows_of(columns):
    size = columns[0].shape[0]
    lane = lax.broadcasted_iota(jnp.int32, (size, 128), 1)
    tile = jnp.zeros((size, 128), F32)
    for at, column in enumerate(columns):
        tile = jnp.where(lane == at, column, tile)
    return jnp.transpose(tile)[:8]


def norm_parts(value):
    mean = jnp.mean(value, axis=-1, keepdims=True)
    var = jnp.mean(value * value, axis=-1, keepdims=True) - mean * mean
    inverse = lax.rsqrt(var + eps)
    return (value - mean) * inverse, inverse


def sum_rows(value):
    return jnp.sum(value, axis=0, keepdims=True)


def whole(array, **kw):
    rank = array.ndim
    return (array, array.shape, lambda *at: (0,) * rank)


def run(kernel, grid, ins, outs, scratch=(), prefetch=(), after=(), alias=None, limit=56, name=None):
    prefetch = tuple(prefetch)

    def body(*refs):
        refs = list(refs)
        first = len(prefetch) + len(ins)
        del refs[first : first + len(after)]
        kernel(*refs)

    in_specs = []
    for array, block, where in ins:
        if block is None:
            in_specs.append(pl.BlockSpec(memory_space=pl.ANY))
        elif tuple(block) == tuple(array.shape):
            in_specs.append(pl.BlockSpec(block, where, pipeline_mode=pl.Buffered(1)))
        else:
            in_specs.append(pl.BlockSpec(block, where))
    in_specs += [pl.BlockSpec(memory_space=pl.ANY)] * len(after)
    out_specs = [pl.BlockSpec(block, where) for shape, dtype, block, where in outs]
    out_shape = [jax.ShapeDtypeStruct(shape, dtype) for shape, dtype, block, where in outs]
    return pl.pallas_call(
        body,
        grid_spec=pltpu.PrefetchScalarGridSpec(
            num_scalar_prefetch=len(prefetch),
            grid=grid,
            in_specs=in_specs,
            out_specs=out_specs,
            scratch_shapes=list(scratch),
        ),
        out_shape=out_shape,
        input_output_aliases=alias or {},
        compiler_params=pltpu.CompilerParams(
            dimension_semantics=("arbitrary",) * len(grid), vmem_limit_bytes=limit * MEGA
        ),
        cost_estimate=pl.CostEstimate(flops=int(COST[name] * WORK), bytes_accessed=1000, transcendentals=0),
        name=name,
    )(*prefetch, *[array for array, block, where in ins], *after)


def flip(value, bit, size):
    return lax.ppermute(value, "tensor", [(t, t ^ (1 << bit)) for t in range(size)])


def all_pieces(own, bits):
    size = 1 << bits
    return [own] + [lax.ppermute(own, "tensor", [(t, t ^ k) for t in range(size)]) for k in range(1, size)]


class Line:
    def __init__(self):
        self.last = None

    def tie(self, value):
        if self.last is None:
            return value
        return lax.optimization_barrier((value,) + self.last)[0]

    def mark(self, *values):
        self.last = values


class Total:
    def __init__(self, line, parts, bits):
        self.line, self.bits = line, bits
        self.orders = [list(range(bits)), list(range(bits))[::-1]]
        self.left = [[bit for bit in range(bits) if bit != order[0]] for order in self.orders]
        self.keep = [parts[0], parts[2]]
        self.got = [flip(parts[1], self.orders[0][0], 1 << bits), flip(parts[3], self.orders[1][0], 1 << bits)]
        self.step = 1

    def advance(self):
        line, size = self.line, 1 << self.bits
        if self.step == self.bits:
            for half in range(2):
                self.keep[half] = line.tie(self.keep[half]) + self.got[half]
                line.mark(self.keep[half])
            return
        picks = []
        for half in range(2):
            left, bit = self.left[half], self.orders[half][self.step]
            keep, got = self.keep[half], self.got[half]
            cube = (2,) * len(left) + keep.shape[1:]
            axis = len(left) - 1 - left.index(bit)
            shape = (keep.shape[0] // 2,) + keep.shape[1:]
            pick = lambda value, at, cube=cube, axis=axis, shape=shape: lax.index_in_dim(
                value.reshape(cube), at, axis, keepdims=False
            ).reshape(shape)
            send = pick(line.tie(keep), 1) + pick(got, 1)
            line.mark(send)
            picks.append((pick, keep, got))
            self.got[half] = flip(send, bit, size)
            left.remove(bit)
        for half in range(2):
            pick, keep, got = picks[half]
            self.keep[half] = pick(line.tie(keep), 0) + pick(got, 0)
            line.mark(self.keep[half])
        self.step += 1

    def gather(self):
        size = 1 << self.bits
        if self.step == self.bits:
            self.held = [[0], [0]]
            self.step += 1
        else:
            for half in range(2):
                self.keep[half] = jnp.concatenate([self.line.tie(self.keep[half]), self.got[half]], 0)
                self.line.mark(self.keep[half])
                self.held[half] = self.held[half] + [block | self.last[half] for block in self.held[half]]
        self.last = [1 << self.orders[half].pop() for half in range(2)]
        self.got = [flip(self.keep[half], self.last[half].bit_length() - 1, size) for half in range(2)]

    def pieces(self):
        arrays, where = [], []
        for half in range(2):
            arrays += [self.keep[half], self.got[half]]
            found = {block: (2 * half, at) for at, block in enumerate(self.held[half])}
            found.update({block | self.last[half]: (2 * half + 1, at) for at, block in enumerate(self.held[half])})
            where.append(found)
        return arrays, where


class Ring:
    def __init__(self, line, first, rest, size):
        self.line, self.rest, self.size = line, rest, size
        self.step = 0
        self.got = self.send(first)

    def send(self, value):
        return lax.ppermute(value, "dp", [(d, (d + 2) % self.size) for d in range(self.size)])

    def advance(self):
        value = self.line.tie(self.rest)[self.step] + self.got
        self.line.mark(value)
        self.step += 1
        if self.step < self.size // 2 - 1:
            self.got = self.send(value)
        return value


def butterfly(value, bits):
    for bit in range(bits):
        value = value + flip(value, bit, 1 << bits)
    return value


def tree_sum(value):
    while value.shape[0] > 1:
        value = value.reshape((value.shape[0] // 2, 2) + value.shape[1:])
        value = value[:, 0] + value[:, 1]
    return value[0]


class Small:
    def __init__(self, own, bits):
        self.bits, self.bit, self.held = bits, 0, [own]
        self.got = None
        self.step()

    def step(self):
        if self.got is not None:
            many = len(self.held)
            self.held = self.held + [self.got[at] for at in range(many)]
        if self.bit < self.bits:
            self.got = flip(jnp.stack(self.held), self.bit, 1 << self.bits)
            self.bit += 1

    def pieces(self):
        while len(self.held) < 1 << self.bits:
            self.step()
        return self.held


def both_vectors(pieces):
    level = [piece[8:] for piece in pieces]
    while len(level) > 1:
        level = [level[at] + level[at + 1] for at in range(0, len(level), 2)]
    many = D // level[0].shape[1]
    return jnp.stack([level[0][:many].reshape(-1), level[0][4 : 4 + many].reshape(-1)])


def combine(pieces, block, blocks):
    level = [pieces[other][:8, (block ^ other) * SLOT : (block ^ other) * SLOT + SLOT] for other in range(blocks)]
    while len(level) > 1:
        level = [level[at] + level[at + 1] for at in range(0, len(level), 2)]
    return level[0]


def attention_scores(query, both_keys, length):
    scores = mul(query, both_keys, NT)
    row = lax.broadcasted_iota(jnp.int32, scores.shape, 0)
    place = lax.broadcasted_iota(jnp.int32, scores.shape, 1) % SLOT
    scores = jnp.where((place <= row) & (place < IMG + length), scores, masked_score)
    parts = []
    for at in range(2):
        part = scores[:, at * SLOT : (at + 1) * SLOT]
        expd = jnp.exp(part - jnp.max(part, axis=-1, keepdims=True))
        parts.append(expd / jnp.sum(expd, axis=-1, keepdims=True))
    return parts


def split_heads(value, mask):
    return jnp.concatenate([value * mask[0:1], value * mask[1:2]], axis=0)


def store_parts(refs, value, step, steps, only=None):
    left_keep, left_send, right_keep, right_send = refs
    left_keep[0] = value[:SLOT, :HALF]
    left_send[0] = value[SLOT:, :HALF]

    @pl.when(step < steps // 2)
    def _():
        right_keep[0] = value[:SLOT, HALF:]
        right_keep[1] = value[SLOT:, HALF:]

    @pl.when(step >= steps // 2)
    def _():
        right_send[0] = value[:SLOT, HALF:]
        right_send[1] = value[SLOT:, HALF:]


def part_outs(blocks):
    half = blocks // 2
    steps = blocks // 2
    shape = (half, SLOT, HALF)
    low = max(steps // 2, 1)
    return [
        (shape, F32, (1, SLOT, HALF), lambda s, *_: (s, 0, 0)),
        (shape, F32, (1, SLOT, HALF), lambda s, *_: (s, 0, 0)),
        (shape, F32, (2, SLOT, HALF), lambda s, *_: (jnp.minimum(s, low - 1), 0, 0)),
        (shape, F32, (2, SLOT, HALF), lambda s, *_: (jnp.maximum(s - steps // 2, 0), 0, 0)),
    ]


def front(order, lengths, tokens, gain, shift, weight, bias, tables, mask, mix_gain, uw_rows, out_weight, after=()):
    blocks = order.shape[0]
    steps = blocks // 2
    width = weight.shape[2]
    groups = width // 128
    rows = blocks * SLOT

    def kernel(order_ref, length_ref, x0, x1, g, b, w, wb, tab, msk, mg, uwr, ow, own, first, qkv, mixed, small, *parts_uw):
        step = pl.program_id(0)
        parts, uw = parts_uw[:4], parts_uw[4]

        @pl.when(step == 0)
        def _():
            found = mul(uwr[...], ow[...])
            uw[0:1] = found[0:1] + found[1:2] + found[2:3]
            uw[1:2] = found[3:4] + found[4:5] + found[5:6]
            small[8:] = jnp.zeros((8, rows), F32)
            for at in range(D // rows):
                c = slice(at * rows, at * rows + rows)
                small[8 + at : 9 + at] = uw[0:1, c]
                small[12 + at : 13 + at] = uw[1:2, c]

        x = jnp.concatenate([x0[0], x1[0]], axis=0)
        own[...] = x
        hat, _ = norm_parts(x.astype(F32))
        one = rounded(hat * g[...] + b[...])
        first[...] = one
        for c in range(3):
            proj = mul(one, w[c]) + wb[c : c + 1]
            for group in range(groups):
                part = proj[:, group * 128 : group * 128 + 128]
                if c < 2:
                    part = rotate(part, tab, 3 * c, 1)
                at = c * width + group * 128
                qkv[:, at : at + 128] = rounded(part)
        for pair in range(2):
            r = slice(pair * SLOT, pair * SLOT + SLOT)
            length = length_ref[order_ref[2 * step + pair]]
            for group in range(groups):
                at = group * 128
                query = qkv[r, at : at + 128]
                keys = split_heads(qkv[r, width + at : width + at + 128], msk)
                values = split_heads(qkv[r, 2 * width + at : 2 * width + at + 128], msk)
                probs = attention_scores(query, keys, length)
                mixed[r, at : at + 128] = mul(rounded(jnp.concatenate(probs, axis=1)), values)
        m = mixed[...]
        total = jnp.sum(m, axis=-1, keepdims=True)
        here = pl.ds(pl.multiple_of(step * 2 * SLOT, 2 * SLOT), 2 * SLOT)
        small[:8, here] = rows_of([total, jnp.sum(m * m, axis=-1, keepdims=True)])
        middle = total * (1.0 / width)
        partial = mul(rounded((m - middle) * mg[...]), ow[...]) + middle * uw[0:1]
        store_parts(parts, partial, step, steps)

    row2 = lambda s, *_: (s, 0)
    pair_of = lambda offset: lambda s, order_ref, length_ref: (order_ref[2 * s + offset], 0, 0)
    return run(
        kernel,
        (steps,),
        [
            (tokens, (1, SLOT, D), pair_of(0)),
            (tokens, (1, SLOT, D), pair_of(1)),
            whole(gain), whole(shift), whole(weight), whole(bias), whole(tables), whole(mask),
            whole(mix_gain), whole(uw_rows), whole(out_weight),
        ],
        [
            ((rows, D), BF16, (2 * SLOT, D), row2),
            ((rows, D), BF16, (2 * SLOT, D), row2),
            ((rows, 3 * width), BF16, (2 * SLOT, 3 * width), row2),
            ((rows, width), F32, (2 * SLOT, width), row2),
            ((16, rows), F32, (16, rows), lambda s, *_: (0, 0)),
        ]
        + part_outs(blocks),
        scratch=[pltpu.VMEM((8, D), F32)],
        prefetch=(order, lengths),
        after=after,
        name="front",
    )


def pieces_in(pieces):
    return [whole(piece) for piece in pieces[0]]


def load_pieces(refs, where, total, step, blocks):
    for block in range(blocks):

        @pl.when(step == block)
        def _(block=block):
            for half in range(2):
                array, at = where[half][block]
                total[:, half * HALF : half * HALF + HALF] = refs[array][at]


def middle_norm(own, pieces, sums, uw, out_bias, gain, shift, after=()):
    blocks = len(pieces[1][0])
    rows = blocks * SLOT

    def kernel(*refs):
        x, parts, stats = refs[0], refs[1:5], refs[5 : 5 + blocks]
        uw_ref, bias, g, b, mid, second, stat, total, tot8 = refs[5 + blocks :]
        step = pl.program_id(0)
        load_pieces(parts, pieces[1], total, step, blocks)
        for block in range(blocks):

            @pl.when(step == block)
            def _(block=block):
                tot8[...] = combine(stats, block, blocks)

        cols = columns_of(tot8[...])
        mean = cols[:, 0:1] * (1.0 / D)
        inverse = lax.rsqrt(cols[:, 1:2] * (1.0 / D) - mean * mean + eps)
        branch = inverse * (total[...] - mean * uw_ref[0:1]) + uw_ref[1:2]
        value = x[...].astype(F32) + branch + bias[...]
        mid[...] = value
        hat, _ = norm_parts(value)
        second[...] = rounded(hat * g[...] + b[...])
        lane = lax.broadcasted_iota(jnp.int32, (SLOT, 128), 1)
        stat[...] = jnp.where(lane == 0, mean, inverse)

    row = lambda k, *_: (k, 0)
    return run(
        kernel,
        (blocks,),
        [(own, (SLOT, D), row)]
        + pieces_in(pieces)
        + [whole(part) for part in sums]
        + [whole(uw), whole(out_bias), whole(gain), whole(shift)],
        [
            ((rows, D), F32, (SLOT, D), row),
            ((rows, D), BF16, (SLOT, D), row),
            ((rows, 128), F32, (SLOT, 128), row),
        ],
        scratch=[pltpu.VMEM((SLOT, D), F32), pltpu.VMEM((8, SLOT), F32)],
        after=after,
        name="middle_norm",
    )


def hidden_back(cots, down_weight):
    many, rows, units = len(cots), cots[0].shape[0], down_weight.shape[0]
    tile = min(512, units)

    def kernel(*refs):
        w, out = refs[many:]
        for at in range(many):
            out[at * rows : at * rows + rows] = rounded(mul(refs[at][...], w[...], NT))

    return run(
        kernel,
        (units // tile,),
        [whole(cot) for cot in cots] + [(down_weight, (tile, D), lambda j: (j, 0))],
        [((many * rows, units), BF16, (many * rows, tile), lambda j: (0, j))],
        name="hidden_back",
    )[0]


def hidden_front(chunk, second, up_weight, up_bias, back, gain, after=()):
    rows, units = second.shape[0], up_weight.shape[1]
    tile = 512
    steps = units // tile

    def part_of(c, s_ref, w, b, hb, g, act, slp):
        hidden = mul(s_ref[...], w[:, c]) + b[:, c]
        tail = jnp.exp(-0.5 * hidden * hidden)
        t = 1.0 / (1.0 + (0.3275911 * root_half) * jnp.abs(hidden))
        poly = 1.061405429 * t - 1.453152027
        poly = poly * t + 1.421413741
        poly = poly * t - 0.284496736
        poly = poly * t + 0.254829592
        half = 0.5 * poly * t * tail
        phi = jnp.where(hidden >= 0.0, 1.0 - half, half)
        active = hidden * phi
        act[:, c] = rounded(active)
        slp[:, c] = rounded(phi + hidden * (inv_root_two_pi * tail))
        scaled = hb[:, c].astype(F32) * g[:, c]
        return [value[:, :128] + value[:, 128:] for value in (active, active * active, scaled, scaled * active)]

    def kernel(s_ref, w, b, hb, g, act, slp, sums, acc):
        step = pl.program_id(0)
        found = [part_of(slice(at, at + 256), s_ref, w, b, hb, g, act, slp) for at in range(0, tile, 256)]

        @pl.when(step == 0)
        def _():
            for at in range(4):
                acc[at] = found[0][at] + found[1][at]

        @pl.when(step > 0)
        def _():
            for at in range(4):
                acc[at] += found[0][at] + found[1][at]

        @pl.when(step == steps - 1)
        def _():
            for block in range(rows // SLOT):
                r = slice(block * SLOT, block * SLOT + SLOT)
                sums[:, r] = rows_of([jnp.sum(acc[at, r], axis=-1, keepdims=True) for at in range(4)])

    return run(
        kernel,
        (steps,),
        [
            whole(second),
            (up_weight, (D, tile), lambda j: (0, j)),
            (up_bias, (1, tile), lambda j: (0, j)),
            (back, (rows, tile), lambda j: (chunk, j)),
            (gain, (1, tile), lambda j: (0, j)),
        ],
        [
            ((rows, units), BF16, (rows, tile), lambda j: (0, j)),
            ((rows, units), BF16, (rows, tile), lambda j: (0, j)),
            ((8, rows), F32, (8, rows), lambda j: (0, 0)),
        ],
        scratch=[pltpu.VMEM((4, rows, 128), F32)],
        after=after,
        name="hidden_front",
    )


def hidden_mid(chunk, active, slope, back, sums, gain, shift):
    blocks = len(sums)
    rows, units = active.shape

    def kernel(act, slp, hb, *refs):
        stats = refs[:blocks]
        g, b, low, grad, vecs, tot8 = refs[blocks:]
        step = pl.program_id(0)
        for block in range(blocks):

            @pl.when(step == block)
            def _(block=block):
                tot8[...] = combine(stats, block, blocks)

        cols = columns_of(tot8[...]) * (1.0 / FF)
        mean = cols[:, 0:1]
        inverse = lax.rsqrt(cols[:, 1:2] - mean * mean + eps)
        one = cols[:, 2:3]
        two = inverse * (cols[:, 3:4] - mean * one)
        for at in range(0, units, 256):
            c = slice(at, at + 256)
            hat = (act[:, c].astype(F32) - mean) * inverse
            low[:, c] = rounded(hat * g[:, c] + b[:, c])
            raw = hb[:, c].astype(F32)
            grown = rounded(inverse * (raw * g[:, c] - one - hat * two) * slp[:, c].astype(F32))
            grad[:, c] = grown
            vecs[0, 0:1, c] = sum_rows(raw * hat)
            vecs[0, 1:2, c] = sum_rows(raw)
            vecs[0, 2:3, c] = sum_rows(grown.astype(F32))

    row = lambda k: (k, 0)
    return run(
        kernel,
        (blocks,),
        [
            (active, (SLOT, units), row),
            (slope, (SLOT, units), row),
            (back, (SLOT, units), lambda k: (chunk * blocks + k, 0)),
        ]
        + [whole(part) for part in sums]
        + [whole(gain), whole(shift)],
        [
            ((rows, units), BF16, (SLOT, units), row),
            ((rows, units), BF16, (SLOT, units), row),
            ((blocks, 8, units), F32, (1, 8, units), lambda k: (k, 0, 0)),
        ],
        scratch=[pltpu.VMEM((8, SLOT), F32)],
        name="hidden_mid",
    )


def hidden_grad(grad, up_weight):
    rows, units = grad.shape
    blocks = rows // SLOT
    tile = 512
    steps = D // tile
    half = steps // 2

    def kernel(gr, w, left_keep, left_send, right_keep, right_send):
        step = pl.program_id(0)
        value = mul(gr[...], w[...], NT)

        @pl.when(step < half)
        def _():
            for block in range(blocks):
                r = slice(block * SLOT, block * SLOT + SLOT)
                (left_send if block & 1 else left_keep)[block // 2] = value[r]

        @pl.when(step >= half)
        def _():
            for block in range(blocks):
                r = slice(block * SLOT, block * SLOT + SLOT)
                (right_send if block >= blocks // 2 else right_keep)[block % (blocks // 2)] = value[r]

    shape = (blocks // 2, SLOT, HALF)
    block_shape = (blocks // 2, SLOT, tile)
    lefts = lambda j: (0, 0, jnp.minimum(j, half - 1))
    rights = lambda j: (0, 0, jnp.maximum(j - half, 0))
    return run(
        kernel,
        (steps,),
        [whole(grad), (up_weight, (tile, units), lambda j: (j, 0))],
        [
            (shape, F32, block_shape, lefts),
            (shape, F32, block_shape, lefts),
            (shape, F32, block_shape, rights),
            (shape, F32, block_shape, rights),
        ],
        name="hidden_grad",
    )


def result_part(order, lows, down_weight):
    pairs = order.shape[0]
    units = down_weight.shape[0]
    many = len(lows)
    rows = lows[0].shape[0]
    each = rows // SLOT
    tile = 256

    def kernel(order_ref, *refs):
        w, out = refs[many:]
        for at in range(many):
            value = mul(refs[at][...], w[...])
            for block in range(each):
                out[order_ref[at * each + block]] = value[block * SLOT : block * SLOT + SLOT]

    return run(
        kernel,
        (D // tile,),
        [whole(low) for low in lows] + [(down_weight, (units, tile), lambda j, *_: (0, j))],
        [((pairs, SLOT, D), F32, (pairs, SLOT, tile), lambda j, *_: (0, 0, j))],
        prefetch=(order,),
        name="result_part",
    )[0]


def middle_back(own, cot, pieces, middle, stat, uw, out_bias, gain, after=()):
    blocks = len(pieces[1][0])
    rows = blocks * SLOT

    def kernel(*refs):
        x, c, parts = refs[0], refs[1], refs[2:6]
        mid, st, uw_ref, bias, g, grad, low, stat2, vecs, total = refs[6:]
        load_pieces(parts, pieces[1], total, pl.program_id(0), blocks)
        value = mid[...]
        hat, inverse = norm_parts(value)
        sec = total[...]
        scaled = sec * g[...]
        up = c[...].astype(F32)
        out = up + inverse * (
            scaled
            - jnp.mean(scaled, axis=-1, keepdims=True)
            - hat * jnp.mean(scaled * hat, axis=-1, keepdims=True)
        )
        grad[...] = out
        lowered = rounded(out)
        low[...] = lowered
        low32 = lowered.astype(F32)
        one = jnp.mean(low32 * uw_ref[0:1], axis=-1, keepdims=True)
        moved = value - x[...].astype(F32) - bias[...] - uw_ref[1:2]
        two = jnp.mean(low32 * moved, axis=-1, keepdims=True)
        lane = lax.broadcasted_iota(jnp.int32, (SLOT, 128), 1)
        stat2[...] = jnp.where(lane == 2, one, jnp.where(lane == 3, two, st[...]))
        vecs[0, 0:1] = sum_rows(sec * hat)
        vecs[0, 1:2] = sum_rows(sec)
        vecs[0, 2:3] = sum_rows(out)
        vecs[0, 3:4] = sum_rows(up)

    row = lambda k, *_: (k, 0)
    return run(
        kernel,
        (blocks,),
        [(own, (SLOT, D), row), (cot, (SLOT, D), row)]
        + pieces_in(pieces)
        + [(middle, (SLOT, D), row), (stat, (SLOT, 128), row), whole(uw), whole(out_bias), whole(gain)],
        [
            ((rows, D), F32, (SLOT, D), row),
            ((rows, D), BF16, (SLOT, D), row),
            ((rows, 128), F32, (SLOT, 128), row),
            ((blocks, 8, D), F32, (1, 8, D), lambda k, *_: (k, 0, 0)),
        ],
        scratch=[pltpu.VMEM((SLOT, D), F32)],
        after=after,
        name="middle_back",
    )


def attention_back(order, lengths, low, stat, mixed, qkv, own, mix_gain, mix_shift, out_weight, weight, tables, mask, after=()):
    blocks = order.shape[0]
    steps = blocks // 2
    width = out_weight.shape[0]
    groups = width // 128
    rows = blocks * SLOT

    def kernel(
        order_ref, length_ref, low_ref, st, mx, qkv_ref, x, mg, ms, ow, w, tab, msk,
        mix_low, dproj, vecs, wide, left_keep, left_send, right_keep, right_send, dmixed,
    ):
        step = pl.program_id(0)
        mean, inverse, one, two = (st[:, at : at + 1] for at in range(4))
        back = mul(low_ref[...], ow[...], NT)
        hat = (mx[...] - mean) * inverse
        mix_low[...] = rounded(hat * mg[...] + ms[...])
        dmixed[...] = rounded(inverse * (back * mg[...] - one - hat * two))
        vecs[0, 0:1, :width] = sum_rows(back * hat)
        vecs[0, 1:2, :width] = sum_rows(back)
        first_half = lax.broadcasted_iota(jnp.int32, (SLOT, 128), 1) < HD
        for pair in range(2):
            r = slice(pair * SLOT, pair * SLOT + SLOT)
            length = length_ref[order_ref[2 * step + pair]]
            for group in range(groups):
                at = group * 128
                query = qkv_ref[r, at : at + 128]
                keys = split_heads(qkv_ref[r, width + at : width + at + 128], msk)
                values = split_heads(qkv_ref[r, 2 * width + at : 2 * width + at + 128], msk)
                grad = dmixed[r, at : at + 128]
                probs = attention_scores(query, keys, length)
                dprobs = mul(grad, values, NT)
                dscores = []
                for i in range(2):
                    dp = dprobs[:, i * SLOT : (i + 1) * SLOT]
                    carried = jnp.sum(probs[i] * dp, axis=-1, keepdims=True)
                    dscores.append(rounded(probs[i] * (dp - carried)))
                dscores = jnp.concatenate(dscores, axis=1)
                dquery = mul(dscores, keys)
                dkey = mul(dscores, query, TN)
                dvalue = mul(rounded(jnp.concatenate(probs, axis=1)), grad, TN)
                dkey = jnp.where(first_half, dkey[:SLOT], dkey[SLOT:])
                dvalue = jnp.where(first_half, dvalue[:SLOT], dvalue[SLOT:])
                tabs = [tab[i, :SLOT] for i in range(6)]
                dproj[r, at : at + 128] = rounded(rotate(dquery, tabs, 0, -1))
                dproj[r, width + at : width + at + 128] = rounded(rotate(dkey, tabs, 3, -1))
                dproj[r, 2 * width + at : 2 * width + at + 128] = rounded(dvalue)
        vecs[0, 2:3] = sum_rows(dproj[...].astype(F32))
        partial = mul(dproj[:, :width], w[0], NT)
        for c in (1, 2):
            partial += mul(dproj[:, c * width : (c + 1) * width], w[c], NT)
        pre_hat, _ = norm_parts(x[...].astype(F32))
        grown = partial * pre_hat
        wide[0, 0:1] = sum_rows(grown[:SLOT]) + sum_rows(grown[SLOT:])
        wide[0, 1:2] = sum_rows(partial[:SLOT]) + sum_rows(partial[SLOT:])
        store_parts((left_keep, left_send, right_keep, right_send), partial, step, steps)

    row2 = lambda s, *_: (s, 0)
    return run(
        kernel,
        (steps,),
        [
            (low, (2 * SLOT, D), row2),
            (stat, (2 * SLOT, 128), row2),
            (mixed, (2 * SLOT, width), row2),
            (qkv, (2 * SLOT, 3 * width), row2),
            (own, (2 * SLOT, D), row2),
            whole(mix_gain), whole(mix_shift), whole(out_weight), whole(weight), whole(tables), whole(mask),
        ],
        [
            ((rows, width), BF16, (2 * SLOT, width), row2),
            ((rows, 3 * width), BF16, (2 * SLOT, 3 * width), row2),
            ((steps, 8, 3 * width), F32, (1, 8, 3 * width), lambda s, *_: (s, 0, 0)),
            ((steps, 8, D), F32, (1, 8, D), lambda s, *_: (s, 0, 0)),
        ]
        + part_outs(blocks),
        scratch=[pltpu.VMEM((2 * SLOT, width), BF16)],
        prefetch=(order, lengths),
        after=after,
        name="attention_back",
    )


def tokens_back(order, own, grad, pieces, gain, before, pairs, after=()):
    blocks = len(pieces[1][0])

    def kernel(order_ref, x, gr, *refs):
        parts = refs[:4]
        g = refs[4]
        out, total = refs[-2:]
        load_pieces(parts, pieces[1], total, pl.program_id(0), blocks)
        hat, inverse = norm_parts(x[...].astype(F32))
        scaled = total[...] * g[...]
        out[0] = gr[...] + inverse * (
            scaled
            - jnp.mean(scaled, axis=-1, keepdims=True)
            - hat * jnp.mean(scaled * hat, axis=-1, keepdims=True)
        )

    row = lambda k, *_: (k, 0)
    ins = [(own, (SLOT, D), row), (grad, (SLOT, D), row)] + pieces_in(pieces) + [whole(gain)]
    alias = None
    if before is not None:
        alias = {1 + len(ins): 0}
        ins = ins + [(before, None, None)]
    return run(
        kernel,
        (blocks,),
        ins,
        [((pairs, SLOT, D), F32, (1, SLOT, D), lambda k, o: (o[k], 0, 0))],
        scratch=[pltpu.VMEM((SLOT, D), F32)],
        prefetch=(order,),
        after=after,
        alias=alias,
        name="tokens_back",
    )[0]


def output_of(order, middle, result, bias, before, after=()):
    blocks = order.shape[0]

    def kernel(order_ref, mid, res, b, *refs):
        out = refs[-1]
        out[0] = rounded(mid[...] + res[0] + b[...])

    ins = [
        (middle, (SLOT, D), lambda k, *_: (k, 0)),
        (result, (1, SLOT, D), lambda k, o: (o[k], 0, 0)),
        whole(bias),
    ]
    alias = None
    if before is not None:
        alias = {1 + len(ins): 0}
        ins = ins + [(before, None, None)]
    return run(
        kernel,
        (blocks,),
        ins,
        [(result.shape, BF16, (1, SLOT, D), lambda k, o: (o[k], 0, 0))],
        prefetch=(order,),
        after=after,
        alias=alias,
        name="output",
    )[0]


def ring_grads(ids, products, got=None):
    count, many = ids.shape[0], len(products[0][0])
    rows = products[0][0][0].shape[0]
    widths = [rights[0].shape[1] for lefts, rights in products]
    block = D // (2 * count)
    shape = (block, sum(widths))

    def kernel(ids_ref, *refs):
        outs = refs[2 * many * len(products) + (got is not None) :]
        step = pl.program_id(0)
        start = 0
        for at, width in enumerate(widths):
            left, right = (refs[(2 * at + side) * many : (2 * at + side + 1) * many] for side in range(2))
            value = mul(left[0][...], right[0][...], TN)
            for k in range(1, many):
                value += mul(left[k][...], right[k][...], TN)
            c = slice(start, start + width)
            start += width
            if got is None:
                outs[0][0, :, c] = value
                continue
            value += refs[2 * many * len(products)][0, :, c]

            @pl.when(step == 0)
            def _(value=value, c=c):
                outs[0][:, c] = value

            @pl.when(step > 0)
            def _(value=value, c=c):
                outs[1][0, :, c] = value

    fixed = lambda i, *_: (0, 0)
    moving = lambda i, ids_ref: (0, ids_ref[i])
    lead = lambda i, *_: (i, 0, 0)
    ins = []
    for lefts, rights in products:
        ins += [(left, (rows, block), moving) for left in lefts]
        ins += [(right, right.shape, fixed) for right in rights]
    if got is None:
        outs = [((count,) + shape, F32, (1,) + shape, lead)]
    else:
        ins += [(got, (1,) + shape, lead)]
        outs = [
            (shape, F32, shape, fixed),
            ((count - 1,) + shape, F32, (1,) + shape, lambda i, *_: (jnp.maximum(i - 1, 0), 0, 0)),
        ]
    return run(kernel, (count,), ins, outs, prefetch=(ids,), name="ring_grads")


def full_grad(products):
    many, block = len(products[0][0]), 512
    rows, tall = products[0][0][0].shape
    widths = [rights[0].shape[1] for lefts, rights in products]

    def kernel(*refs):
        out, start = refs[-1], 0
        for at, width in enumerate(widths):
            left, right = (refs[(2 * at + side) * many : (2 * at + side + 1) * many] for side in range(2))
            value = mul(left[0][...], right[0][...], TN)
            for k in range(1, many):
                value += mul(left[k][...], right[k][...], TN)
            out[:, start : start + width] = value
            start += width

    ins = []
    for lefts, rights in products:
        ins += [(left, (rows, block), lambda i: (0, i)) for left in lefts]
        ins += [(right, right.shape, lambda i: (0, 0)) for right in rights]
    wide = sum(widths)
    return run(
        kernel, (tall // block,), ins, [((tall, wide), F32, (block, wide), lambda i: (i, 0))], name="full_grad"
    )[0]


def steps_of(totals, bits, done, until):
    done = list(done)

    def step(at):
        if done[at] < bits:
            totals[at].advance()
        else:
            totals[at].gather()
        done[at] += 1
        if done[at] == bits and until == 2 * bits:
            totals[at].gather()
            done[at] += 1

    limits = [until] + [until if until == 2 * bits else bits - 1] * (len(totals) - 1)
    while any(have < limit for have, limit in zip(done, limits)):
        for at in range(len(totals)):
            if done[at] < limits[at]:
                step(at)


def split_rows(value):
    found = []
    for _ in range(3):
        part = lax.reduce_precision(value, 8, 7)
        found.append(part.astype(BF16))
        value = value - part
    return found


def body(
    tokens,
    lengths,
    cotangent,
    pre_gain,
    pre_shift,
    qkv_weight,
    qkv_bias,
    mix_gain,
    mix_shift,
    out_weight,
    out_bias,
    ffn_gain,
    ffn_shift,
    up_weight,
    up_bias,
    hid_gain,
    hid_shift,
    down_weight,
    down_bias,
):
    pairs = lengths.shape[0]
    blocks = lax.axis_size("tensor")
    bits = blocks.bit_length() - 1
    chunks = pairs // blocks
    width = qkv_weight.shape[2]
    mine = lax.axis_index("tensor").astype(jnp.int32)
    orders = [jnp.arange(c * blocks, (c + 1) * blocks, dtype=jnp.int32) ^ mine for c in range(chunks)]
    tokens3 = tokens.reshape(pairs, SLOT, D)
    row = lambda v: v.reshape(1, -1)
    pre_gain, pre_shift, mix_gain, mix_shift = map(row, (pre_gain, pre_shift, mix_gain, mix_shift))
    out_bias, ffn_gain, ffn_shift, up_bias = map(row, (out_bias, ffn_gain, ffn_shift, up_bias))
    hid_gain, hid_shift, down_bias = map(row, (hid_gain, hid_shift, down_bias))
    tables = xpos_tables()
    lane = np.arange(128)[None, :] < HD
    mask = jnp.asarray(np.concatenate([lane, ~lane], 0).astype(np.float32)).astype(BF16)
    zero = jnp.zeros((2, width), BF16)
    uw_rows = jnp.concatenate(split_rows(mix_gain) + split_rows(mix_shift) + [zero], 0)

    line = Line()
    dp_size = lax.axis_size("dp")
    place = lax.axis_index("dp").astype(jnp.int32)
    count = dp_size // 2
    around = lax.rem(place // 2 + count - 1 - jnp.arange(count, dtype=jnp.int32), count)
    mine_ids, other_ids = 2 * around + lax.rem(place, 2), 2 * around + 1 - lax.rem(place, 2)

    def tied(products):
        (lefts, rights), others = products[0], products[1:]
        return [([line.tie(lefts[0])] + lefts[1:], rights)] + others

    def full(products):
        grad = full_grad(tied(products))
        line.mark(grad)
        return grad

    every = lambda items, name: [item[name] for item in items]

    ones, twos, threes = [], [], []
    for c in range(chunks):
        found = front(
            orders[c], lengths, line.tie(tokens3), pre_gain, pre_shift, qkv_weight, qkv_bias, tables, mask, mix_gain, uw_rows,
            out_weight,
        )
        own, first, qkv, mixed, small = found[:5]
        one = dict(own=own, first=first, qkv=qkv, mixed=mixed, parts=found[5:])
        line.mark(small)
        one["small"] = small
        if c == 0:
            one["total"] = Total(line, one["parts"], bits)
            one["sums"] = Small(small, bits)
        ones.append(one)
    sums0 = ones[0]["sums"]
    if bits > 1:
        ones[0]["total"].advance()
    for c in range(1, chunks):
        ones[c]["total"] = Total(line, [line.tie(part) for part in ones[c]["parts"]], bits)
    sums0.held[0] = line.tie(sums0.held[0])
    sums0.step()
    cot3 = cotangent.reshape(pairs, SLOT, D)
    cots = []
    for c in range(chunks):
        cots.append(line.tie(cot3)[orders[c]].reshape(-1, D))
        line.mark(cots[-1])
    totals = every(ones, "total")
    line.mark(*line.last, *sums0.pieces())
    for step in range(1, bits):
        totals[0].advance()
    back = hidden_back([line.tie(cots[0])] + cots[1:], down_weight)
    line.mark(back)
    for one in ones[1:]:
        one["sums"] = Small(line.tie(one["small"]), bits)
    done = [bits] + [0] * (chunks - 1)
    steps_of(totals, bits, done, 2 * bits - 1)
    for one in ones[1:]:
        line.mark(*line.last, one["sums"].got)
        one["sums"].step()
    uw_total = both_vectors(sums0.pieces())

    def mid_of(c):
        two = twos[c]
        low, grad, vecs = hidden_mid(c, line.tie(two["active"]), two["slope"], back, two["sums"], hid_gain, hid_shift)
        two.update(low=low, grad=grad, vecs=functools.reduce(jnp.add, [vecs[k] for k in range(blocks)]))
        line.mark(vecs)

    def hidden_of(c):
        parts = hidden_grad(line.tie(twos[c]["grad"]), up_weight)
        line.mark(parts[0])
        return parts

    totals[0].gather()
    for other in ones[1:]:
        line.mark(*line.last, *other["sums"].pieces())
    for c in range(chunks):
        one = ones[c]
        mid, second, stat = middle_norm(
            line.tie(one["own"]), totals[c].pieces(), one["sums"].pieces(), uw_total, out_bias, ffn_gain, ffn_shift
        )
        line.mark(stat)
        if c == 0:
            for total in totals[1:]:
                total.advance()
                total.gather()
        active, slope, sums = hidden_front(c, line.tie(second), up_weight, up_bias, back, hid_gain)
        line.mark(sums)
        twos.append(dict(middle=mid, second=second, stat=stat, active=active, slope=slope, sums=all_pieces(sums, bits)))
        if c == 0:
            for total in totals[1:]:
                for step in range(1, bits):
                    total.gather()
            line.mark(*line.last, *twos[0]["sums"][1:])
        else:
            twos[0]["total"].advance()
            line.mark(*line.last, *twos[c]["sums"][1:])
        mid_of(c)
        if c > 0:
            line.mark(*line.last, *twos[0]["total"].got)
        if c == 0 and chunks > 1:
            twos[0]["total"] = Total(line, hidden_of(0), bits)
    lows = every(twos, "low")
    down_grad = full([(lows, cots)])
    down_part = lax.psum_scatter(down_grad, "dp", scatter_dimension=1, tiled=True)
    up_products = [(every(twos, "second"), every(twos, "grad"))]
    sent = ring_grads(other_ids, tied(up_products))[0]
    line.mark(sent)
    sent = lax.ppermute(sent, "dp", [(d, d ^ 1) for d in range(dp_size)])
    if chunks > 1:
        for step in range(1, bits):
            twos[0]["total"].advance()
        twos[0]["total"].gather()
        parts = [None] + [hidden_of(c) for c in range(1, chunks)]
    else:
        twos[0]["total"] = Total(line, hidden_of(0), bits)
        for step in range(bits):
            twos[0]["total"].advance()
        twos[0]["total"].gather()
    ring_first, ring_rest = ring_grads(mine_ids, tied(up_products), sent)
    line.mark(ring_rest)
    ring = Ring(line, ring_first, ring_rest, dp_size)
    for step in range(1, bits):
        twos[0]["total"].gather()
    for c in range(1, chunks):
        twos[c]["total"] = Total(line, [line.tie(part) for part in parts[c]], bits)
    totals = every(twos, "total")
    result = result_part(jnp.concatenate(orders), [line.tie(lows[0])] + lows[1:], down_weight)
    line.mark(result)

    for c in range(chunks):
        one, two = ones[c], twos[c]
        grad, low, stat2, vecs = middle_back(
            line.tie(one["own"]), cots[c], two["total"].pieces(), two["middle"], two["stat"], uw_total, out_bias, ffn_gain
        )
        line.mark(stat2)
        if c == 0:
            for total in totals[1:]:
                total.advance()
        found = attention_back(
            orders[c], lengths, line.tie(low), stat2, one["mixed"], one["qkv"], one["own"], mix_gain, mix_shift, out_weight,
            qkv_weight, tables, mask,
        )
        line.mark(found[2])
        three = dict(grad=grad, low=low, vecs=tree_sum(vecs), mix_low=found[0], dproj=found[1])
        three["narrow"] = tree_sum(found[2])
        three["wide"] = tree_sum(found[3])
        parts = found[4:]
        if c == 0 and chunks > 1:
            for total in totals[1:]:
                for step in range(1, bits):
                    total.advance()
                for step in range(bits):
                    total.gather()
            for total in totals[1:]:
                line.mark(*line.last, *total.got)
            up_part = ring.advance()
            result = lax.psum(line.tie(result), "tensor")
            parts = [line.tie(part) for part in parts]
        three["total"] = Total(line, parts, bits)
        threes.append(three)

    first, last = threes[0]["total"], threes[-1]["total"]
    add = lambda items, name, size: functools.reduce(jnp.add, [item[name] for item in items])[:size]
    pad = lambda v: jnp.pad(v, ((0, 0), (0, D - v.shape[1])))
    wide = add(threes, "wide", 2)
    got = flip(wide, 0, blocks)
    attention_grad = full(
        [(every(ones, "first"), every(threes, "dproj")), (every(threes, "low"), every(threes, "mix_low"))]
    )
    if chunks == 1:
        up_part = ring.advance()
        result = lax.psum(line.tie(result), "tensor")
    line.mark(*line.last, down_part, *(first.got + last.got if chunks > 1 else []))
    up_part = ring.advance()
    attention_part = lax.psum_scatter(line.tie(attention_grad), "dp", scatter_dimension=0, tiled=True)
    for step in range(bits):
        first.advance()
    first.gather()
    if chunks > 1:
        last.advance()
    for step in range(1, bits):
        first.gather()
    if chunks > 1:
        for step in range(1, bits):
            last.advance()
        last.gather()
    for bit in range(1, bits):
        wide = line.tie(wide) + got
        got = flip(wide, bit, blocks)
        line.mark(wide)
    if chunks > 1:
        line.mark(*line.last, *last.got)
    hop = lambda v, bit: lax.ppermute(v, "dp", [(d, d ^ (1 << bit)) for d in range(dp_size)])
    dp_bits = dp_size.bit_length() - 1
    tokens_grad, output = None, None
    for c in range(chunks):
        tokens_grad = tokens_back(
            orders[c], line.tie(ones[c]["own"]), threes[c]["grad"], threes[c]["total"].pieces(), pre_gain, tokens_grad, pairs
        )
        line.mark(tokens_grad)
        if c == 0:
            wide = line.tie(wide) + got
            vecs = jnp.concatenate(
                [pad(add(twos, "vecs", 3)), add(threes, "vecs", 4), pad(add(threes, "narrow", 3)), wide], 0
            )
            line.mark(vecs)
            got = hop(vecs, 0)
            for step in range(2, count - 1):
                up_part = ring.advance()
            if chunks > 1:
                for step in range(1, bits):
                    last.gather()
            vecs = line.tie(vecs) + got
            line.mark(vecs)
            got = hop(vecs, 1)
    for bit in range(2, dp_bits):
        vecs = line.tie(vecs) + got
        line.mark(vecs)
        got = hop(vecs, bit)
    for c in range(chunks):
        output = output_of(orders[c], line.tie(twos[c]["middle"]), result, down_bias, output)
        line.mark(output)
    vecs = vecs + got
    hid_vecs, mid_vecs, narrow, wide = vecs[:3], vecs[3:7], vecs[7:10], vecs[10:12]
    qkv_part = jnp.swapaxes(attention_part[:, : 3 * width].reshape(-1, 3, width), 0, 1)
    out_part = jnp.transpose(attention_part[:, 3 * width :])
    units = hid_gain.shape[1]
    return (
        output.reshape(-1, D),
        tokens_grad.reshape(-1, D),
        wide[0],
        wide[1],
        qkv_part,
        narrow[2, : 3 * width].reshape(3, width),
        narrow[0, :width],
        narrow[1, :width],
        out_part,
        mid_vecs[2],
        mid_vecs[0],
        mid_vecs[1],
        up_part,
        hid_vecs[2, :units],
        hid_vecs[0, :units],
        hid_vecs[1, :units],
        down_part,
        mid_vecs[3],
    )


def solution(mesh):
    in_specs = (
        P("dp", None),
        P("dp"),
        P("dp", None),
        P(),
        P(),
        P(None, None, "tensor"),
        P(None, "tensor"),
        P("tensor"),
        P("tensor"),
        P("tensor", None),
        P(),
        P(),
        P(),
        P(None, "tensor"),
        P("tensor"),
        P("tensor"),
        P("tensor"),
        P("tensor", None),
        P(),
    )
    out_specs = (
        P("dp", None),
        P("dp", None),
        P(),
        P(),
        P(None, "dp", "tensor"),
        P(None, "tensor"),
        P("tensor"),
        P("tensor"),
        P("tensor", "dp"),
        P(),
        P(),
        P(),
        P("dp", "tensor"),
        P("tensor"),
        P("tensor"),
        P("tensor"),
        P("tensor", "dp"),
        P(),
    )
    return jax.shard_map(body, mesh=mesh, in_specs=in_specs, out_specs=out_specs, check_vma=False)
```

```python
import functools
import math

import jax
import jax.numpy as jnp
import numpy as np
from jax import lax
from jax.experimental import pallas as pl
from jax.experimental.pallas import tpu as pltpu
from jax.sharding import PartitionSpec as P

D = 2048
HD = 64
FF = 8192
SLOT = 128
IMG = 64
SCALE_BASE = 512
HALF = D // 2

eps = 1e-05
root_half = 0.7071067811865476
inv_root_two_pi = 0.3989422804014327
masked_score = -1e30
MEGA = 1 << 20

COST = {
    "front": 15.6,
    "middle_norm": 400.0,
    "hidden_back": 400.0,
    "hidden_front": 14.7,
    "hidden_mid": 400.0,
    "hidden_grad": 7.0,
    "full_grad": 15.0,
    "ring_grads": 12.0,
    "result_part": 400.0,
    "middle_back": 11.0,
    "attention_back": 21.7,
    "tokens_back": 8.5,
    "output": 6.0,
}
WORK = 5.5e+07

F32 = jnp.float32
BF16 = jnp.bfloat16
NN = (((1,), (0,)), ((), ()))
NT = (((1,), (1,)), ((), ()))
TN = (((0,), (0,)), ((), ()))


def rounded(value):
    return value.astype(BF16)


def mul(left, right, dims=NN):
    return lax.dot_general(left, right, dims, preferred_element_type=F32)


def xpos_tables():
    place = np.arange(SLOT, dtype=np.float64)[:, None]
    lane = np.arange(128)[None, :]
    index = (lane % HD) // 2
    angle = place * 10000.0 ** (-2.0 * index / HD)
    zeta = (2.0 * index + 0.4 * HD) / (1.4 * HD)
    growth = zeta ** ((place - SLOT // 2) / SCALE_BASE)
    even = lane % 2 == 0
    found = []
    for factor in (growth / math.sqrt(HD), 1.0 / growth):
        found += [
            np.cos(angle) * factor,
            np.where(even, -np.sin(angle), 0.0) * factor,
            np.where(even, 0.0, np.sin(angle)) * factor,
        ]
    return jnp.asarray(np.tile(np.stack(found), (1, 2, 1)).astype(np.float32))


def rotate(value, tables, base, sign):
    up = pltpu.roll(value, 127, axis=1)
    down = pltpu.roll(value, 1, axis=1)
    turned = up * tables[base + 1] + down * tables[base + 2]
    return value * tables[base] + turned if sign > 0 else value * tables[base] - turned


def columns_of(parts):
    return jnp.transpose(parts)


def rows_of(columns):
    size = columns[0].shape[0]
    lane = lax.broadcasted_iota(jnp.int32, (size, 128), 1)
    tile = jnp.zeros((size, 128), F32)
    for at, column in enumerate(columns):
        tile = jnp.where(lane == at, column, tile)
    return jnp.transpose(tile)[:8]


def norm_parts(value):
    mean = jnp.mean(value, axis=-1, keepdims=True)
    var = jnp.mean(value * value, axis=-1, keepdims=True) - mean * mean
    inverse = lax.rsqrt(var + eps)
    return (value - mean) * inverse, inverse


def sum_rows(value):
    return jnp.sum(value, axis=0, keepdims=True)


def whole(array, **kw):
    rank = array.ndim
    return (array, array.shape, lambda *at: (0,) * rank)


def run(kernel, grid, ins, outs, scratch=(), prefetch=(), after=(), alias=None, limit=56, name=None):
    prefetch = tuple(prefetch)

    def body(*refs):
        refs = list(refs)
        first = len(prefetch) + len(ins)
        del refs[first : first + len(after)]
        kernel(*refs)

    in_specs = []
    for array, block, where in ins:
        if block is None:
            in_specs.append(pl.BlockSpec(memory_space=pl.ANY))
        elif tuple(block) == tuple(array.shape):
            in_specs.append(pl.BlockSpec(block, where, pipeline_mode=pl.Buffered(1)))
        else:
            in_specs.append(pl.BlockSpec(block, where))
    in_specs += [pl.BlockSpec(memory_space=pl.ANY)] * len(after)
    out_specs = [pl.BlockSpec(block, where) for shape, dtype, block, where in outs]
    out_shape = [jax.ShapeDtypeStruct(shape, dtype) for shape, dtype, block, where in outs]
    return pl.pallas_call(
        body,
        grid_spec=pltpu.PrefetchScalarGridSpec(
            num_scalar_prefetch=len(prefetch),
            grid=grid,
            in_specs=in_specs,
            out_specs=out_specs,
            scratch_shapes=list(scratch),
        ),
        out_shape=out_shape,
        input_output_aliases=alias or {},
        compiler_params=pltpu.CompilerParams(
            dimension_semantics=("arbitrary",) * len(grid), vmem_limit_bytes=limit * MEGA
        ),
        cost_estimate=pl.CostEstimate(flops=int(COST[name] * WORK), bytes_accessed=1000, transcendentals=0),
        name=name,
    )(*prefetch, *[array for array, block, where in ins], *after)


def flip(value, bit, size):
    return lax.ppermute(value, "tensor", [(t, t ^ (1 << bit)) for t in range(size)])


def all_pieces(own, bits):
    size = 1 << bits
    return [own] + [lax.ppermute(own, "tensor", [(t, t ^ k) for t in range(size)]) for k in range(1, size)]


class Line:
    def __init__(self):
        self.last = None

    def tie(self, value):
        if self.last is None:
            return value
        return lax.optimization_barrier((value,) + self.last)[0]

    def mark(self, *values):
        self.last = values


class Total:
    def __init__(self, line, parts, bits):
        self.line, self.bits = line, bits
        self.orders = [list(range(bits)), list(range(bits))[::-1]]
        self.left = [[bit for bit in range(bits) if bit != order[0]] for order in self.orders]
        self.keep = [parts[0], parts[2]]
        self.got = [flip(parts[1], self.orders[0][0], 1 << bits), flip(parts[3], self.orders[1][0], 1 << bits)]
        self.step = 1

    def advance(self):
        line, size = self.line, 1 << self.bits
        if self.step == self.bits:
            for half in range(2):
                self.keep[half] = line.tie(self.keep[half]) + self.got[half]
                line.mark(self.keep[half])
            return
        picks = []
        for half in range(2):
            left, bit = self.left[half], self.orders[half][self.step]
            keep, got = self.keep[half], self.got[half]
            cube = (2,) * len(left) + keep.shape[1:]
            axis = len(left) - 1 - left.index(bit)
            shape = (keep.shape[0] // 2,) + keep.shape[1:]
            pick = lambda value, at, cube=cube, axis=axis, shape=shape: lax.index_in_dim(
                value.reshape(cube), at, axis, keepdims=False
            ).reshape(shape)
            send = pick(line.tie(keep), 1) + pick(got, 1)
            line.mark(send)
            picks.append((pick, keep, got))
            self.got[half] = flip(send, bit, size)
            left.remove(bit)
        for half in range(2):
            pick, keep, got = picks[half]
            self.keep[half] = pick(line.tie(keep), 0) + pick(got, 0)
            line.mark(self.keep[half])
        self.step += 1

    def gather(self):
        size = 1 << self.bits
        if self.step == self.bits:
            self.held = [[0], [0]]
            self.step += 1
        else:
            for half in range(2):
                self.keep[half] = jnp.concatenate([self.line.tie(self.keep[half]), self.got[half]], 0)
                self.line.mark(self.keep[half])
                self.held[half] = self.held[half] + [block | self.last[half] for block in self.held[half]]
        self.last = [1 << self.orders[half].pop() for half in range(2)]
        self.got = [flip(self.keep[half], self.last[half].bit_length() - 1, size) for half in range(2)]

    def pieces(self):
        arrays, where = [], []
        for half in range(2):
            arrays += [self.keep[half], self.got[half]]
            found = {block: (2 * half, at) for at, block in enumerate(self.held[half])}
            found.update({block | self.last[half]: (2 * half + 1, at) for at, block in enumerate(self.held[half])})
            where.append(found)
        return arrays, where


class Ring:
    def __init__(self, line, first, rest, size):
        self.line, self.rest, self.size = line, rest, size
        self.step = 0
        self.got = self.send(first)

    def send(self, value):
        return lax.ppermute(value, "dp", [(d, (d + 2) % self.size) for d in range(self.size)])

    def advance(self):
        value = self.line.tie(self.rest)[self.step] + self.got
        self.line.mark(value)
        self.step += 1
        if self.step < self.size // 2 - 1:
            self.got = self.send(value)
        return value


def butterfly(value, bits):
    for bit in range(bits):
        value = value + flip(value, bit, 1 << bits)
    return value


def tree_sum(value):
    while value.shape[0] > 1:
        value = value.reshape((value.shape[0] // 2, 2) + value.shape[1:])
        value = value[:, 0] + value[:, 1]
    return value[0]


class Small:
    def __init__(self, own, bits):
        self.bits, self.bit, self.held = bits, 0, [own]
        self.got = None
        self.step()

    def step(self):
        if self.got is not None:
            many = len(self.held)
            self.held = self.held + [self.got[at] for at in range(many)]
        if self.bit < self.bits:
            self.got = flip(jnp.stack(self.held), self.bit, 1 << self.bits)
            self.bit += 1

    def pieces(self):
        while len(self.held) < 1 << self.bits:
            self.step()
        return self.held


def both_vectors(pieces):
    level = [piece[8:] for piece in pieces]
    while len(level) > 1:
        level = [level[at] + level[at + 1] for at in range(0, len(level), 2)]
    many = D // level[0].shape[1]
    return jnp.stack([level[0][:many].reshape(-1), level[0][4 : 4 + many].reshape(-1)])


def combine(pieces, block, blocks):
    level = [pieces[other][:8, (block ^ other) * SLOT : (block ^ other) * SLOT + SLOT] for other in range(blocks)]
    while len(level) > 1:
        level = [level[at] + level[at + 1] for at in range(0, len(level), 2)]
    return level[0]


def attention_scores(query, both_keys, length):
    scores = mul(query, both_keys, NT)
    row = lax.broadcasted_iota(jnp.int32, scores.shape, 0)
    place = lax.broadcasted_iota(jnp.int32, scores.shape, 1) % SLOT
    scores = jnp.where((place <= row) & (place < IMG + length), scores, masked_score)
    parts = []
    for at in range(2):
        part = scores[:, at * SLOT : (at + 1) * SLOT]
        expd = jnp.exp(part - jnp.max(part, axis=-1, keepdims=True))
        parts.append(expd / jnp.sum(expd, axis=-1, keepdims=True))
    return parts


def split_heads(value, mask):
    return jnp.concatenate([value * mask[0:1], value * mask[1:2]], axis=0)


def store_parts(refs, value, step, steps, only=None):
    left_keep, left_send, right_keep, right_send = refs
    left_keep[0] = value[:SLOT, :HALF]
    left_send[0] = value[SLOT:, :HALF]

    @pl.when(step < steps // 2)
    def _():
        right_keep[0] = value[:SLOT, HALF:]
        right_keep[1] = value[SLOT:, HALF:]

    @pl.when(step >= steps // 2)
    def _():
        right_send[0] = value[:SLOT, HALF:]
        right_send[1] = value[SLOT:, HALF:]


def part_outs(blocks):
    half = blocks // 2
    steps = blocks // 2
    shape = (half, SLOT, HALF)
    low = max(steps // 2, 1)
    return [
        (shape, F32, (1, SLOT, HALF), lambda s, *_: (s, 0, 0)),
        (shape, F32, (1, SLOT, HALF), lambda s, *_: (s, 0, 0)),
        (shape, F32, (2, SLOT, HALF), lambda s, *_: (jnp.minimum(s, low - 1), 0, 0)),
        (shape, F32, (2, SLOT, HALF), lambda s, *_: (jnp.maximum(s - steps // 2, 0), 0, 0)),
    ]


def front(order, lengths, tokens, gain, shift, weight, bias, tables, mask, mix_gain, uw_rows, out_weight, after=()):
    blocks = order.shape[0]
    steps = blocks // 2
    width = weight.shape[2]
    groups = width // 128
    rows = blocks * SLOT

    def kernel(order_ref, length_ref, x0, x1, g, b, w, wb, tab, msk, mg, uwr, ow, own, first, qkv, mixed, small, *parts_uw):
        step = pl.program_id(0)
        parts, uw = parts_uw[:4], parts_uw[4]

        @pl.when(step == 0)
        def _():
            found = mul(uwr[...], ow[...])
            uw[0:1] = found[0:1] + found[1:2] + found[2:3]
            uw[1:2] = found[3:4] + found[4:5] + found[5:6]
            small[8:] = jnp.zeros((8, rows), F32)
            for at in range(D // rows):
                c = slice(at * rows, at * rows + rows)
                small[8 + at : 9 + at] = uw[0:1, c]
                small[12 + at : 13 + at] = uw[1:2, c]

        x = jnp.concatenate([x0[0], x1[0]], axis=0)
        own[...] = x
        hat, _ = norm_parts(x.astype(F32))
        one = rounded(hat * g[...] + b[...])
        first[...] = one
        for c in range(3):
            proj = mul(one, w[c]) + wb[c : c + 1]
            for group in range(groups):
                part = proj[:, group * 128 : group * 128 + 128]
                if c < 2:
                    part = rotate(part, tab, 3 * c, 1)
                at = c * width + group * 128
                qkv[:, at : at + 128] = rounded(part)
        for pair in range(2):
            r = slice(pair * SLOT, pair * SLOT + SLOT)
            length = length_ref[order_ref[2 * step + pair]]
            for group in range(groups):
                at = group * 128
                query = qkv[r, at : at + 128]
                keys = split_heads(qkv[r, width + at : width + at + 128], msk)
                values = split_heads(qkv[r, 2 * width + at : 2 * width + at + 128], msk)
                probs = attention_scores(query, keys, length)
                mixed[r, at : at + 128] = mul(rounded(jnp.concatenate(probs, axis=1)), values)
        m = mixed[...]
        total = jnp.sum(m, axis=-1, keepdims=True)
        here = pl.ds(pl.multiple_of(step * 2 * SLOT, 2 * SLOT), 2 * SLOT)
        small[:8, here] = rows_of([total, jnp.sum(m * m, axis=-1, keepdims=True)])
        middle = total * (1.0 / width)
        partial = mul(rounded((m - middle) * mg[...]), ow[...]) + middle * uw[0:1]
        store_parts(parts, partial, step, steps)

    row2 = lambda s, *_: (s, 0)
    pair_of = lambda offset: lambda s, order_ref, length_ref: (order_ref[2 * s + offset], 0, 0)
    return run(
        kernel,
        (steps,),
        [
            (tokens, (1, SLOT, D), pair_of(0)),
            (tokens, (1, SLOT, D), pair_of(1)),
            whole(gain), whole(shift), whole(weight), whole(bias), whole(tables), whole(mask),
            whole(mix_gain), whole(uw_rows), whole(out_weight),
        ],
        [
            ((rows, D), BF16, (2 * SLOT, D), row2),
            ((rows, D), BF16, (2 * SLOT, D), row2),
            ((rows, 3 * width), BF16, (2 * SLOT, 3 * width), row2),
            ((rows, width), F32, (2 * SLOT, width), row2),
            ((16, rows), F32, (16, rows), lambda s, *_: (0, 0)),
        ]
        + part_outs(blocks),
        scratch=[pltpu.VMEM((8, D), F32)],
        prefetch=(order, lengths),
        after=after,
        name="front",
    )


def pieces_in(pieces):
    return [whole(piece) for piece in pieces[0]]


def load_pieces(refs, where, total, step, blocks):
    for block in range(blocks):

        @pl.when(step == block)
        def _(block=block):
            for half in range(2):
                array, at = where[half][block]
                total[:, half * HALF : half * HALF + HALF] = refs[array][at]


def middle_norm(own, pieces, sums, uw, out_bias, gain, shift, after=()):
    blocks = len(pieces[1][0])
    rows = blocks * SLOT

    def kernel(*refs):
        x, parts, stats = refs[0], refs[1:5], refs[5 : 5 + blocks]
        uw_ref, bias, g, b, mid, second, stat, total, tot8 = refs[5 + blocks :]
        step = pl.program_id(0)
        load_pieces(parts, pieces[1], total, step, blocks)
        for block in range(blocks):

            @pl.when(step == block)
            def _(block=block):
                tot8[...] = combine(stats, block, blocks)

        cols = columns_of(tot8[...])
        mean = cols[:, 0:1] * (1.0 / D)
        inverse = lax.rsqrt(cols[:, 1:2] * (1.0 / D) - mean * mean + eps)
        branch = inverse * (total[...] - mean * uw_ref[0:1]) + uw_ref[1:2]
        value = x[...].astype(F32) + branch + bias[...]
        mid[...] = value
        hat, _ = norm_parts(value)
        second[...] = rounded(hat * g[...] + b[...])
        lane = lax.broadcasted_iota(jnp.int32, (SLOT, 128), 1)
        stat[...] = jnp.where(lane == 0, mean, inverse)

    row = lambda k, *_: (k, 0)
    return run(
        kernel,
        (blocks,),
        [(own, (SLOT, D), row)]
        + pieces_in(pieces)
        + [whole(part) for part in sums]
        + [whole(uw), whole(out_bias), whole(gain), whole(shift)],
        [
            ((rows, D), F32, (SLOT, D), row),
            ((rows, D), BF16, (SLOT, D), row),
            ((rows, 128), F32, (SLOT, 128), row),
        ],
        scratch=[pltpu.VMEM((SLOT, D), F32), pltpu.VMEM((8, SLOT), F32)],
        after=after,
        name="middle_norm",
    )


def hidden_back(cots, down_weight):
    many, rows, units = len(cots), cots[0].shape[0], down_weight.shape[0]
    tile = min(512, units)

    def kernel(*refs):
        w, out = refs[many:]
        for at in range(many):
            out[at * rows : at * rows + rows] = rounded(mul(refs[at][...], w[...], NT))

    return run(
        kernel,
        (units // tile,),
        [whole(cot) for cot in cots] + [(down_weight, (tile, D), lambda j: (j, 0))],
        [((many * rows, units), BF16, (many * rows, tile), lambda j: (0, j))],
        name="hidden_back",
    )[0]


def hidden_front(chunk, second, up_weight, up_bias, back, gain, after=()):
    rows, units = second.shape[0], up_weight.shape[1]
    tile = 512
    steps = units // tile

    def part_of(c, s_ref, w, b, hb, g, act, slp):
        hidden = mul(s_ref[...], w[:, c]) + b[:, c]
        tail = jnp.exp(-0.5 * hidden * hidden)
        t = 1.0 / (1.0 + (0.3275911 * root_half) * jnp.abs(hidden))
        poly = 1.061405429 * t - 1.453152027
        poly = poly * t + 1.421413741
        poly = poly * t - 0.284496736
        poly = poly * t + 0.254829592
        half = 0.5 * poly * t * tail
        phi = jnp.where(hidden >= 0.0, 1.0 - half, half)
        active = hidden * phi
        act[:, c] = rounded(active)
        slp[:, c] = rounded(phi + hidden * (inv_root_two_pi * tail))
        scaled = hb[:, c].astype(F32) * g[:, c]
        return [value[:, :128] + value[:, 128:] for value in (active, active * active, scaled, scaled * active)]

    def kernel(s_ref, w, b, hb, g, act, slp, sums, acc):
        step = pl.program_id(0)
        found = [part_of(slice(at, at + 256), s_ref, w, b, hb, g, act, slp) for at in range(0, tile, 256)]

        @pl.when(step == 0)
        def _():
            for at in range(4):
                acc[at] = found[0][at] + found[1][at]

        @pl.when(step > 0)
        def _():
            for at in range(4):
                acc[at] += found[0][at] + found[1][at]

        @pl.when(step == steps - 1)
        def _():
            for block in range(rows // SLOT):
                r = slice(block * SLOT, block * SLOT + SLOT)
                sums[:, r] = rows_of([jnp.sum(acc[at, r], axis=-1, keepdims=True) for at in range(4)])

    return run(
        kernel,
        (steps,),
        [
            whole(second),
            (up_weight, (D, tile), lambda j: (0, j)),
            (up_bias, (1, tile), lambda j: (0, j)),
            (back, (rows, tile), lambda j: (chunk, j)),
            (gain, (1, tile), lambda j: (0, j)),
        ],
        [
            ((rows, units), BF16, (rows, tile), lambda j: (0, j)),
            ((rows, units), BF16, (rows, tile), lambda j: (0, j)),
            ((8, rows), F32, (8, rows), lambda j: (0, 0)),
        ],
        scratch=[pltpu.VMEM((4, rows, 128), F32)],
        after=after,
        name="hidden_front",
    )


def hidden_mid(chunk, active, slope, back, sums, gain, shift):
    blocks = len(sums)
    rows, units = active.shape

    def kernel(act, slp, hb, *refs):
        stats = refs[:blocks]
        g, b, low, grad, vecs, tot8 = refs[blocks:]
        step = pl.program_id(0)
        for block in range(blocks):

            @pl.when(step == block)
            def _(block=block):
                tot8[...] = combine(stats, block, blocks)

        cols = columns_of(tot8[...]) * (1.0 / FF)
        mean = cols[:, 0:1]
        inverse = lax.rsqrt(cols[:, 1:2] - mean * mean + eps)
        one = cols[:, 2:3]
        two = inverse * (cols[:, 3:4] - mean * one)
        for at in range(0, units, 256):
            c = slice(at, at + 256)
            hat = (act[:, c].astype(F32) - mean) * inverse
            low[:, c] = rounded(hat * g[:, c] + b[:, c])
            raw = hb[:, c].astype(F32)
            grown = rounded(inverse * (raw * g[:, c] - one - hat * two) * slp[:, c].astype(F32))
            grad[:, c] = grown
            vecs[0, 0:1, c] = sum_rows(raw * hat)
            vecs[0, 1:2, c] = sum_rows(raw)
            vecs[0, 2:3, c] = sum_rows(grown.astype(F32))

    row = lambda k: (k, 0)
    return run(
        kernel,
        (blocks,),
        [
            (active, (SLOT, units), row),
            (slope, (SLOT, units), row),
            (back, (SLOT, units), lambda k: (chunk * blocks + k, 0)),
        ]
        + [whole(part) for part in sums]
        + [whole(gain), whole(shift)],
        [
            ((rows, units), BF16, (SLOT, units), row),
            ((rows, units), BF16, (SLOT, units), row),
            ((blocks, 8, units), F32, (1, 8, units), lambda k: (k, 0, 0)),
        ],
        scratch=[pltpu.VMEM((8, SLOT), F32)],
        name="hidden_mid",
    )


def hidden_grad(grad, up_weight):
    rows, units = grad.shape
    blocks = rows // SLOT
    tile = 512
    steps = D // tile
    half = steps // 2

    def kernel(gr, w, left_keep, left_send, right_keep, right_send):
        step = pl.program_id(0)
        value = mul(gr[...], w[...], NT)

        @pl.when(step < half)
        def _():
            for block in range(blocks):
                r = slice(block * SLOT, block * SLOT + SLOT)
                (left_send if block & 1 else left_keep)[block // 2] = value[r]

        @pl.when(step >= half)
        def _():
            for block in range(blocks):
                r = slice(block * SLOT, block * SLOT + SLOT)
                (right_send if block >= blocks // 2 else right_keep)[block % (blocks // 2)] = value[r]

    shape = (blocks // 2, SLOT, HALF)
    block_shape = (blocks // 2, SLOT, tile)
    lefts = lambda j: (0, 0, jnp.minimum(j, half - 1))
    rights = lambda j: (0, 0, jnp.maximum(j - half, 0))
    return run(
        kernel,
        (steps,),
        [whole(grad), (up_weight, (tile, units), lambda j: (j, 0))],
        [
            (shape, F32, block_shape, lefts),
            (shape, F32, block_shape, lefts),
            (shape, F32, block_shape, rights),
            (shape, F32, block_shape, rights),
        ],
        name="hidden_grad",
    )


def result_part(order, lows, down_weight):
    pairs = order.shape[0]
    units = down_weight.shape[0]
    many = len(lows)
    rows = lows[0].shape[0]
    each = rows // SLOT
    tile = 256

    def kernel(order_ref, *refs):
        w, out = refs[many:]
        for at in range(many):
            value = mul(refs[at][...], w[...])
            for block in range(each):
                out[order_ref[at * each + block]] = value[block * SLOT : block * SLOT + SLOT]

    return run(
        kernel,
        (D // tile,),
        [whole(low) for low in lows] + [(down_weight, (units, tile), lambda j, *_: (0, j))],
        [((pairs, SLOT, D), F32, (pairs, SLOT, tile), lambda j, *_: (0, 0, j))],
        prefetch=(order,),
        name="result_part",
    )[0]


def middle_back(own, cot, pieces, middle, stat, uw, out_bias, gain, after=()):
    blocks = len(pieces[1][0])
    rows = blocks * SLOT

    def kernel(*refs):
        x, c, parts = refs[0], refs[1], refs[2:6]
        mid, st, uw_ref, bias, g, grad, low, stat2, vecs, total = refs[6:]
        load_pieces(parts, pieces[1], total, pl.program_id(0), blocks)
        value = mid[...]
        hat, inverse = norm_parts(value)
        sec = total[...]
        scaled = sec * g[...]
        up = c[...].astype(F32)
        out = up + inverse * (
            scaled
            - jnp.mean(scaled, axis=-1, keepdims=True)
            - hat * jnp.mean(scaled * hat, axis=-1, keepdims=True)
        )
        grad[...] = out
        lowered = rounded(out)
        low[...] = lowered
        low32 = lowered.astype(F32)
        one = jnp.mean(low32 * uw_ref[0:1], axis=-1, keepdims=True)
        moved = value - x[...].astype(F32) - bias[...] - uw_ref[1:2]
        two = jnp.mean(low32 * moved, axis=-1, keepdims=True)
        lane = lax.broadcasted_iota(jnp.int32, (SLOT, 128), 1)
        stat2[...] = jnp.where(lane == 2, one, jnp.where(lane == 3, two, st[...]))
        vecs[0, 0:1] = sum_rows(sec * hat)
        vecs[0, 1:2] = sum_rows(sec)
        vecs[0, 2:3] = sum_rows(out)
        vecs[0, 3:4] = sum_rows(up)

    row = lambda k, *_: (k, 0)
    return run(
        kernel,
        (blocks,),
        [(own, (SLOT, D), row), (cot, (SLOT, D), row)]
        + pieces_in(pieces)
        + [(middle, (SLOT, D), row), (stat, (SLOT, 128), row), whole(uw), whole(out_bias), whole(gain)],
        [
            ((rows, D), F32, (SLOT, D), row),
            ((rows, D), BF16, (SLOT, D), row),
            ((rows, 128), F32, (SLOT, 128), row),
            ((blocks, 8, D), F32, (1, 8, D), lambda k, *_: (k, 0, 0)),
        ],
        scratch=[pltpu.VMEM((SLOT, D), F32)],
        after=after,
        name="middle_back",
    )


def attention_back(order, lengths, low, stat, mixed, qkv, own, mix_gain, mix_shift, out_weight, weight, tables, mask, after=()):
    blocks = order.shape[0]
    steps = blocks // 2
    width = out_weight.shape[0]
    groups = width // 128
    rows = blocks * SLOT

    def kernel(
        order_ref, length_ref, low_ref, st, mx, qkv_ref, x, mg, ms, ow, w, tab, msk,
        mix_low, dproj, vecs, wide, left_keep, left_send, right_keep, right_send, dmixed,
    ):
        step = pl.program_id(0)
        mean, inverse, one, two = (st[:, at : at + 1] for at in range(4))
        back = mul(low_ref[...], ow[...], NT)
        hat = (mx[...] - mean) * inverse
        mix_low[...] = rounded(hat * mg[...] + ms[...])
        dmixed[...] = rounded(inverse * (back * mg[...] - one - hat * two))
        vecs[0, 0:1, :width] = sum_rows(back * hat)
        vecs[0, 1:2, :width] = sum_rows(back)
        first_half = lax.broadcasted_iota(jnp.int32, (SLOT, 128), 1) < HD
        for pair in range(2):
            r = slice(pair * SLOT, pair * SLOT + SLOT)
            length = length_ref[order_ref[2 * step + pair]]
            for group in range(groups):
                at = group * 128
                query = qkv_ref[r, at : at + 128]
                keys = split_heads(qkv_ref[r, width + at : width + at + 128], msk)
                values = split_heads(qkv_ref[r, 2 * width + at : 2 * width + at + 128], msk)
                grad = dmixed[r, at : at + 128]
                probs = attention_scores(query, keys, length)
                dprobs = mul(grad, values, NT)
                dscores = []
                for i in range(2):
                    dp = dprobs[:, i * SLOT : (i + 1) * SLOT]
                    carried = jnp.sum(probs[i] * dp, axis=-1, keepdims=True)
                    dscores.append(rounded(probs[i] * (dp - carried)))
                dscores = jnp.concatenate(dscores, axis=1)
                dquery = mul(dscores, keys)
                dkey = mul(dscores, query, TN)
                dvalue = mul(rounded(jnp.concatenate(probs, axis=1)), grad, TN)
                dkey = jnp.where(first_half, dkey[:SLOT], dkey[SLOT:])
                dvalue = jnp.where(first_half, dvalue[:SLOT], dvalue[SLOT:])
                tabs = [tab[i, :SLOT] for i in range(6)]
                dproj[r, at : at + 128] = rounded(rotate(dquery, tabs, 0, -1))
                dproj[r, width + at : width + at + 128] = rounded(rotate(dkey, tabs, 3, -1))
                dproj[r, 2 * width + at : 2 * width + at + 128] = rounded(dvalue)
        vecs[0, 2:3] = sum_rows(dproj[...].astype(F32))
        partial = mul(dproj[:, :width], w[0], NT)
        for c in (1, 2):
            partial += mul(dproj[:, c * width : (c + 1) * width], w[c], NT)
        pre_hat, _ = norm_parts(x[...].astype(F32))
        grown = partial * pre_hat
        wide[0, 0:1] = sum_rows(grown[:SLOT]) + sum_rows(grown[SLOT:])
        wide[0, 1:2] = sum_rows(partial[:SLOT]) + sum_rows(partial[SLOT:])
        store_parts((left_keep, left_send, right_keep, right_send), partial, step, steps)

    row2 = lambda s, *_: (s, 0)
    return run(
        kernel,
        (steps,),
        [
            (low, (2 * SLOT, D), row2),
            (stat, (2 * SLOT, 128), row2),
            (mixed, (2 * SLOT, width), row2),
            (qkv, (2 * SLOT, 3 * width), row2),
            (own, (2 * SLOT, D), row2),
            whole(mix_gain), whole(mix_shift), whole(out_weight), whole(weight), whole(tables), whole(mask),
        ],
        [
            ((rows, width), BF16, (2 * SLOT, width), row2),
            ((rows, 3 * width), BF16, (2 * SLOT, 3 * width), row2),
            ((steps, 8, 3 * width), F32, (1, 8, 3 * width), lambda s, *_: (s, 0, 0)),
            ((steps, 8, D), F32, (1, 8, D), lambda s, *_: (s, 0, 0)),
        ]
        + part_outs(blocks),
        scratch=[pltpu.VMEM((2 * SLOT, width), BF16)],
        prefetch=(order, lengths),
        after=after,
        name="attention_back",
    )


def tokens_back(order, own, grad, pieces, gain, before, pairs, after=()):
    blocks = len(pieces[1][0])

    def kernel(order_ref, x, gr, *refs):
        parts = refs[:4]
        g = refs[4]
        out, total = refs[-2:]
        load_pieces(parts, pieces[1], total, pl.program_id(0), blocks)
        hat, inverse = norm_parts(x[...].astype(F32))
        scaled = total[...] * g[...]
        out[0] = gr[...] + inverse * (
            scaled
            - jnp.mean(scaled, axis=-1, keepdims=True)
            - hat * jnp.mean(scaled * hat, axis=-1, keepdims=True)
        )

    row = lambda k, *_: (k, 0)
    ins = [(own, (SLOT, D), row), (grad, (SLOT, D), row)] + pieces_in(pieces) + [whole(gain)]
    alias = None
    if before is not None:
        alias = {1 + len(ins): 0}
        ins = ins + [(before, None, None)]
    return run(
        kernel,
        (blocks,),
        ins,
        [((pairs, SLOT, D), F32, (1, SLOT, D), lambda k, o: (o[k], 0, 0))],
        scratch=[pltpu.VMEM((SLOT, D), F32)],
        prefetch=(order,),
        after=after,
        alias=alias,
        name="tokens_back",
    )[0]


def output_of(order, middle, result, bias, before, after=()):
    blocks = order.shape[0]

    def kernel(order_ref, mid, res, b, *refs):
        out = refs[-1]
        out[0] = rounded(mid[...] + res[0] + b[...])

    ins = [
        (middle, (SLOT, D), lambda k, *_: (k, 0)),
        (result, (1, SLOT, D), lambda k, o: (o[k], 0, 0)),
        whole(bias),
    ]
    alias = None
    if before is not None:
        alias = {1 + len(ins): 0}
        ins = ins + [(before, None, None)]
    return run(
        kernel,
        (blocks,),
        ins,
        [(result.shape, BF16, (1, SLOT, D), lambda k, o: (o[k], 0, 0))],
        prefetch=(order,),
        after=after,
        alias=alias,
        name="output",
    )[0]


def ring_grads(ids, products, got=None):
    count, many = ids.shape[0], len(products[0][0])
    rows = products[0][0][0].shape[0]
    widths = [rights[0].shape[1] for lefts, rights in products]
    block = D // (2 * count)
    shape = (block, sum(widths))

    def kernel(ids_ref, *refs):
        outs = refs[2 * many * len(products) + (got is not None) :]
        step = pl.program_id(0)
        start = 0
        for at, width in enumerate(widths):
            left, right = (refs[(2 * at + side) * many : (2 * at + side + 1) * many] for side in range(2))
            value = mul(left[0][...], right[0][...], TN)
            for k in range(1, many):
                value += mul(left[k][...], right[k][...], TN)
            c = slice(start, start + width)
            start += width
            if got is None:
                outs[0][0, :, c] = value
                continue
            value += refs[2 * many * len(products)][0, :, c]

            @pl.when(step == 0)
            def _(value=value, c=c):
                outs[0][:, c] = value

            @pl.when(step > 0)
            def _(value=value, c=c):
                outs[1][0, :, c] = value

    fixed = lambda i, *_: (0, 0)
    moving = lambda i, ids_ref: (0, ids_ref[i])
    lead = lambda i, *_: (i, 0, 0)
    ins = []
    for lefts, rights in products:
        ins += [(left, (rows, block), moving) for left in lefts]
        ins += [(right, right.shape, fixed) for right in rights]
    if got is None:
        outs = [((count,) + shape, F32, (1,) + shape, lead)]
    else:
        ins += [(got, (1,) + shape, lead)]
        outs = [
            (shape, F32, shape, fixed),
            ((count - 1,) + shape, F32, (1,) + shape, lambda i, *_: (jnp.maximum(i - 1, 0), 0, 0)),
        ]
    return run(kernel, (count,), ins, outs, prefetch=(ids,), name="ring_grads")


def full_grad(products):
    many, block = len(products[0][0]), 512
    rows, tall = products[0][0][0].shape
    widths = [rights[0].shape[1] for lefts, rights in products]

    def kernel(*refs):
        out, start = refs[-1], 0
        for at, width in enumerate(widths):
            left, right = (refs[(2 * at + side) * many : (2 * at + side + 1) * many] for side in range(2))
            value = mul(left[0][...], right[0][...], TN)
            for k in range(1, many):
                value += mul(left[k][...], right[k][...], TN)
            out[:, start : start + width] = value
            start += width

    ins = []
    for lefts, rights in products:
        ins += [(left, (rows, block), lambda i: (0, i)) for left in lefts]
        ins += [(right, right.shape, lambda i: (0, 0)) for right in rights]
    wide = sum(widths)
    return run(
        kernel, (tall // block,), ins, [((tall, wide), F32, (block, wide), lambda i: (i, 0))], name="full_grad"
    )[0]


def steps_of(totals, bits, done, until):
    done = list(done)

    def step(at):
        if done[at] < bits:
            totals[at].advance()
        else:
            totals[at].gather()
        done[at] += 1
        if done[at] == bits and until == 2 * bits:
            totals[at].gather()
            done[at] += 1

    limits = [until] + [until if until == 2 * bits else bits - 1] * (len(totals) - 1)
    while any(have < limit for have, limit in zip(done, limits)):
        for at in range(len(totals)):
            if done[at] < limits[at]:
                step(at)


def split_rows(value):
    found = []
    for _ in range(3):
        part = lax.reduce_precision(value, 8, 7)
        found.append(part.astype(BF16))
        value = value - part
    return found


def body(
    tokens,
    lengths,
    cotangent,
    pre_gain,
    pre_shift,
    qkv_weight,
    qkv_bias,
    mix_gain,
    mix_shift,
    out_weight,
    out_bias,
    ffn_gain,
    ffn_shift,
    up_weight,
    up_bias,
    hid_gain,
    hid_shift,
    down_weight,
    down_bias,
):
    pairs = lengths.shape[0]
    blocks = lax.axis_size("tensor")
    bits = blocks.bit_length() - 1
    chunks = pairs // blocks
    width = qkv_weight.shape[2]
    mine = lax.axis_index("tensor").astype(jnp.int32)
    orders = [jnp.arange(c * blocks, (c + 1) * blocks, dtype=jnp.int32) ^ mine for c in range(chunks)]
    tokens3 = tokens.reshape(pairs, SLOT, D)
    row = lambda v: v.reshape(1, -1)
    pre_gain, pre_shift, mix_gain, mix_shift = map(row, (pre_gain, pre_shift, mix_gain, mix_shift))
    out_bias, ffn_gain, ffn_shift, up_bias = map(row, (out_bias, ffn_gain, ffn_shift, up_bias))
    hid_gain, hid_shift, down_bias = map(row, (hid_gain, hid_shift, down_bias))
    tables = xpos_tables()
    lane = np.arange(128)[None, :] < HD
    mask = jnp.asarray(np.concatenate([lane, ~lane], 0).astype(np.float32)).astype(BF16)
    zero = jnp.zeros((2, width), BF16)
    uw_rows = jnp.concatenate(split_rows(mix_gain) + split_rows(mix_shift) + [zero], 0)

    line = Line()
    dp_size = lax.axis_size("dp")
    place = lax.axis_index("dp").astype(jnp.int32)
    count = dp_size // 2
    around = lax.rem(place // 2 + count - 1 - jnp.arange(count, dtype=jnp.int32), count)
    mine_ids, other_ids = 2 * around + lax.rem(place, 2), 2 * around + 1 - lax.rem(place, 2)

    def tied(products):
        (lefts, rights), others = products[0], products[1:]
        return [([line.tie(lefts[0])] + lefts[1:], rights)] + others

    def full(products):
        grad = full_grad(tied(products))
        line.mark(grad)
        return grad

    every = lambda items, name: [item[name] for item in items]

    ones, twos, threes = [], [], []
    for c in range(chunks):
        found = front(
            orders[c], lengths, line.tie(tokens3), pre_gain, pre_shift, qkv_weight, qkv_bias, tables, mask, mix_gain, uw_rows,
            out_weight,
        )
        own, first, qkv, mixed, small = found[:5]
        one = dict(own=own, first=first, qkv=qkv, mixed=mixed, parts=found[5:])
        line.mark(small)
        one["small"] = small
        if c == 0:
            one["total"] = Total(line, one["parts"], bits)
            one["sums"] = Small(small, bits)
        ones.append(one)
    sums0 = ones[0]["sums"]
    if bits > 1:
        ones[0]["total"].advance()
    for c in range(1, chunks):
        ones[c]["total"] = Total(line, [line.tie(part) for part in ones[c]["parts"]], bits)
    sums0.held[0] = line.tie(sums0.held[0])
    sums0.step()
    cot3 = cotangent.reshape(pairs, SLOT, D)
    cots = []
    for c in range(chunks):
        cots.append(line.tie(cot3)[orders[c]].reshape(-1, D))
        line.mark(cots[-1])
    totals = every(ones, "total")
    line.mark(*line.last, *sums0.pieces())
    for step in range(1, bits):
        totals[0].advance()
    back = hidden_back([line.tie(cots[0])] + cots[1:], down_weight)
    line.mark(back)
    for one in ones[1:]:
        one["sums"] = Small(line.tie(one["small"]), bits)
    done = [bits] + [0] * (chunks - 1)
    steps_of(totals, bits, done, 2 * bits - 1)
    for one in ones[1:]:
        line.mark(*line.last, one["sums"].got)
        one["sums"].step()
    uw_total = both_vectors(sums0.pieces())

    def mid_of(c):
        two = twos[c]
        low, grad, vecs = hidden_mid(c, line.tie(two["active"]), two["slope"], back, two["sums"], hid_gain, hid_shift)
        two.update(low=low, grad=grad, vecs=functools.reduce(jnp.add, [vecs[k] for k in range(blocks)]))
        line.mark(vecs)

    def hidden_of(c):
        parts = hidden_grad(line.tie(twos[c]["grad"]), up_weight)
        line.mark(parts[0])
        return parts

    totals[0].gather()
    for other in ones[1:]:
        line.mark(*line.last, *other["sums"].pieces())
    for c in range(chunks):
        one = ones[c]
        mid, second, stat = middle_norm(
            line.tie(one["own"]), totals[c].pieces(), one["sums"].pieces(), uw_total, out_bias, ffn_gain, ffn_shift
        )
        line.mark(stat)
        if c == 0:
            for total in totals[1:]:
                total.advance()
                total.gather()
        active, slope, sums = hidden_front(c, line.tie(second), up_weight, up_bias, back, hid_gain)
        line.mark(sums)
        twos.append(dict(middle=mid, second=second, stat=stat, active=active, slope=slope, sums=all_pieces(sums, bits)))
        if c == 0:
            for total in totals[1:]:
                for step in range(1, bits):
                    total.gather()
            line.mark(*line.last, *twos[0]["sums"][1:])
        else:
            twos[0]["total"].advance()
            line.mark(*line.last, *twos[c]["sums"][1:])
        mid_of(c)
        if c > 0:
            line.mark(*line.last, *twos[0]["total"].got)
        if c == 0 and chunks > 1:
            twos[0]["total"] = Total(line, hidden_of(0), bits)
    lows = every(twos, "low")
    down_grad = full([(lows, cots)])
    down_part = lax.psum_scatter(down_grad, "dp", scatter_dimension=1, tiled=True)
    up_products = [(every(twos, "second"), every(twos, "grad"))]
    sent = ring_grads(other_ids, tied(up_products))[0]
    line.mark(sent)
    sent = lax.ppermute(sent, "dp", [(d, d ^ 1) for d in range(dp_size)])
    if chunks > 1:
        for step in range(1, bits):
            twos[0]["total"].advance()
        twos[0]["total"].gather()
        parts = [None] + [hidden_of(c) for c in range(1, chunks)]
    else:
        twos[0]["total"] = Total(line, hidden_of(0), bits)
        for step in range(bits):
            twos[0]["total"].advance()
        twos[0]["total"].gather()
    ring_first, ring_rest = ring_grads(mine_ids, tied(up_products), sent)
    line.mark(ring_rest)
    ring = Ring(line, ring_first, ring_rest, dp_size)
    for step in range(1, bits):
        twos[0]["total"].gather()
    for c in range(1, chunks):
        twos[c]["total"] = Total(line, [line.tie(part) for part in parts[c]], bits)
    totals = every(twos, "total")
    result = result_part(jnp.concatenate(orders), [line.tie(lows[0])] + lows[1:], down_weight)
    line.mark(result)

    for c in range(chunks):
        one, two = ones[c], twos[c]
        grad, low, stat2, vecs = middle_back(
            line.tie(one["own"]), cots[c], two["total"].pieces(), two["middle"], two["stat"], uw_total, out_bias, ffn_gain
        )
        line.mark(stat2)
        if c == 0:
            for total in totals[1:]:
                total.advance()
        found = attention_back(
            orders[c], lengths, line.tie(low), stat2, one["mixed"], one["qkv"], one["own"], mix_gain, mix_shift, out_weight,
            qkv_weight, tables, mask,
        )
        line.mark(found[2])
        three = dict(grad=grad, low=low, vecs=tree_sum(vecs), mix_low=found[0], dproj=found[1])
        three["narrow"] = tree_sum(found[2])
        three["wide"] = tree_sum(found[3])
        parts = found[4:]
        if c == 0 and chunks > 1:
            for total in totals[1:]:
                for step in range(1, bits):
                    total.advance()
                for step in range(bits):
                    total.gather()
            for total in totals[1:]:
                line.mark(*line.last, *total.got)
            up_part = ring.advance()
            result = lax.psum(line.tie(result), "tensor")
            parts = [line.tie(part) for part in parts]
        three["total"] = Total(line, parts, bits)
        threes.append(three)

    first, last = threes[0]["total"], threes[-1]["total"]
    add = lambda items, name, size: functools.reduce(jnp.add, [item[name] for item in items])[:size]
    pad = lambda v: jnp.pad(v, ((0, 0), (0, D - v.shape[1])))
    wide = add(threes, "wide", 2)
    got = flip(wide, 0, blocks)
    if chunks > 1:
        line.mark(*line.last, *first.got)
    attention_grad = full(
        [(every(ones, "first"), every(threes, "dproj")), (every(threes, "low"), every(threes, "mix_low"))]
    )
    if chunks == 1:
        up_part = ring.advance()
        result = lax.psum(line.tie(result), "tensor")
    attention_part = lax.psum_scatter(attention_grad, "dp", scatter_dimension=0, tiled=True)
    for step in range(bits):
        first.advance()
    first.gather()
    if chunks > 1:
        last.advance()
    for step in range(1, bits):
        first.gather()
    line.mark(*line.last, down_part)
    up_part = ring.advance()
    if chunks > 1:
        for step in range(1, bits):
            last.advance()
        last.gather()
    for bit in range(1, bits):
        wide = line.tie(wide) + got
        got = flip(wide, bit, blocks)
        line.mark(wide)
    if chunks > 1:
        line.mark(*line.last, *last.got)
    hop = lambda v, bit: lax.ppermute(v, "dp", [(d, d ^ (1 << bit)) for d in range(dp_size)])
    dp_bits = dp_size.bit_length() - 1
    tokens_grad, output = None, None
    for c in range(chunks):
        tokens_grad = tokens_back(
            orders[c], line.tie(ones[c]["own"]), threes[c]["grad"], threes[c]["total"].pieces(), pre_gain, tokens_grad, pairs
        )
        line.mark(tokens_grad)
        if c == 0:
            wide = line.tie(wide) + got
            vecs = jnp.concatenate(
                [pad(add(twos, "vecs", 3)), add(threes, "vecs", 4), pad(add(threes, "narrow", 3)), wide], 0
            )
            line.mark(vecs)
            got = hop(vecs, 0)
            for step in range(2, count - 1):
                up_part = ring.advance()
            if chunks > 1:
                for step in range(1, bits):
                    last.gather()
            vecs = line.tie(vecs) + got
            line.mark(vecs)
            got = hop(vecs, 1)
    for bit in range(2, dp_bits):
        vecs = line.tie(vecs) + got
        line.mark(vecs)
        got = hop(vecs, bit)
    for c in range(chunks):
        output = output_of(orders[c], line.tie(twos[c]["middle"]), result, down_bias, output)
        line.mark(output)
    vecs = vecs + got
    hid_vecs, mid_vecs, narrow, wide = vecs[:3], vecs[3:7], vecs[7:10], vecs[10:12]
    qkv_part = jnp.swapaxes(attention_part[:, : 3 * width].reshape(-1, 3, width), 0, 1)
    out_part = jnp.transpose(attention_part[:, 3 * width :])
    units = hid_gain.shape[1]
    return (
        output.reshape(-1, D),
        tokens_grad.reshape(-1, D),
        wide[0],
        wide[1],
        qkv_part,
        narrow[2, : 3 * width].reshape(3, width),
        narrow[0, :width],
        narrow[1, :width],
        out_part,
        mid_vecs[2],
        mid_vecs[0],
        mid_vecs[1],
        up_part,
        hid_vecs[2, :units],
        hid_vecs[0, :units],
        hid_vecs[1, :units],
        down_part,
        mid_vecs[3],
    )


def solution(mesh):
    in_specs = (
        P("dp", None),
        P("dp"),
        P("dp", None),
        P(),
        P(),
        P(None, None, "tensor"),
        P(None, "tensor"),
        P("tensor"),
        P("tensor"),
        P("tensor", None),
        P(),
        P(),
        P(),
        P(None, "tensor"),
        P("tensor"),
        P("tensor"),
        P("tensor"),
        P("tensor", None),
        P(),
    )
    out_specs = (
        P("dp", None),
        P("dp", None),
        P(),
        P(),
        P(None, "dp", "tensor"),
        P(None, "tensor"),
        P("tensor"),
        P("tensor"),
        P("tensor", "dp"),
        P(),
        P(),
        P(),
        P("dp", "tensor"),
        P("tensor"),
        P("tensor"),
        P("tensor"),
        P("tensor", "dp"),
        P(),
    )
    return jax.shard_map(body, mesh=mesh, in_specs=in_specs, out_specs=out_specs, check_vma=False)
```

```python
import functools
import math

import jax
import jax.numpy as jnp
import numpy as np
from jax import lax
from jax.experimental import pallas as pl
from jax.experimental.pallas import tpu as pltpu
from jax.sharding import PartitionSpec as P

D = 2048
HD = 64
FF = 8192
SLOT = 128
IMG = 64
SCALE_BASE = 512
HALF = D // 2

eps = 1e-05
root_half = 0.7071067811865476
inv_root_two_pi = 0.3989422804014327
masked_score = -1e30
MEGA = 1 << 20

COST = {
    "front": 15.6,
    "middle_norm": 400.0,
    "hidden_back": 400.0,
    "hidden_front": 14.7,
    "hidden_mid": 400.0,
    "hidden_grad": 7.0,
    "full_grad": 15.0,
    "ring_grads": 12.0,
    "result_part": 400.0,
    "middle_back": 11.0,
    "attention_back": 21.7,
    "tokens_back": 2450.0,
    "output": 6.0,
}
WORK = 5.5e+07

F32 = jnp.float32
BF16 = jnp.bfloat16
NN = (((1,), (0,)), ((), ()))
NT = (((1,), (1,)), ((), ()))
TN = (((0,), (0,)), ((), ()))


def rounded(value):
    return value.astype(BF16)


def mul(left, right, dims=NN):
    return lax.dot_general(left, right, dims, preferred_element_type=F32)


def xpos_tables():
    place = np.arange(SLOT, dtype=np.float64)[:, None]
    lane = np.arange(128)[None, :]
    index = (lane % HD) // 2
    angle = place * 10000.0 ** (-2.0 * index / HD)
    zeta = (2.0 * index + 0.4 * HD) / (1.4 * HD)
    growth = zeta ** ((place - SLOT // 2) / SCALE_BASE)
    even = lane % 2 == 0
    found = []
    for factor in (growth / math.sqrt(HD), 1.0 / growth):
        found += [
            np.cos(angle) * factor,
            np.where(even, -np.sin(angle), 0.0) * factor,
            np.where(even, 0.0, np.sin(angle)) * factor,
        ]
    return jnp.asarray(np.tile(np.stack(found), (1, 2, 1)).astype(np.float32))


def rotate(value, tables, base, sign):
    up = pltpu.roll(value, 127, axis=1)
    down = pltpu.roll(value, 1, axis=1)
    turned = up * tables[base + 1] + down * tables[base + 2]
    return value * tables[base] + turned if sign > 0 else value * tables[base] - turned


def columns_of(parts):
    return jnp.transpose(parts)


def rows_of(columns):
    size = columns[0].shape[0]
    lane = lax.broadcasted_iota(jnp.int32, (size, 128), 1)
    tile = jnp.zeros((size, 128), F32)
    for at, column in enumerate(columns):
        tile = jnp.where(lane == at, column, tile)
    return jnp.transpose(tile)[:8]


def norm_parts(value):
    mean = jnp.mean(value, axis=-1, keepdims=True)
    var = jnp.mean(value * value, axis=-1, keepdims=True) - mean * mean
    inverse = lax.rsqrt(var + eps)
    return (value - mean) * inverse, inverse


def sum_rows(value):
    return jnp.sum(value, axis=0, keepdims=True)


def whole(array, **kw):
    rank = array.ndim
    return (array, array.shape, lambda *at: (0,) * rank)


def run(kernel, grid, ins, outs, scratch=(), prefetch=(), after=(), alias=None, limit=56, name=None):
    prefetch = tuple(prefetch)

    def body(*refs):
        refs = list(refs)
        first = len(prefetch) + len(ins)
        del refs[first : first + len(after)]
        kernel(*refs)

    in_specs = []
    for array, block, where in ins:
        if block is None:
            in_specs.append(pl.BlockSpec(memory_space=pl.ANY))
        elif tuple(block) == tuple(array.shape):
            in_specs.append(pl.BlockSpec(block, where, pipeline_mode=pl.Buffered(1)))
        else:
            in_specs.append(pl.BlockSpec(block, where))
    in_specs += [pl.BlockSpec(memory_space=pl.ANY)] * len(after)
    out_specs = [pl.BlockSpec(block, where) for shape, dtype, block, where in outs]
    out_shape = [jax.ShapeDtypeStruct(shape, dtype) for shape, dtype, block, where in outs]
    return pl.pallas_call(
        body,
        grid_spec=pltpu.PrefetchScalarGridSpec(
            num_scalar_prefetch=len(prefetch),
            grid=grid,
            in_specs=in_specs,
            out_specs=out_specs,
            scratch_shapes=list(scratch),
        ),
        out_shape=out_shape,
        input_output_aliases=alias or {},
        compiler_params=pltpu.CompilerParams(
            dimension_semantics=("arbitrary",) * len(grid), vmem_limit_bytes=limit * MEGA
        ),
        cost_estimate=pl.CostEstimate(flops=int(COST[name] * WORK), bytes_accessed=1000, transcendentals=0),
        name=name,
    )(*prefetch, *[array for array, block, where in ins], *after)


def flip(value, bit, size):
    return lax.ppermute(value, "tensor", [(t, t ^ (1 << bit)) for t in range(size)])


def all_pieces(own, bits):
    size = 1 << bits
    return [own] + [lax.ppermute(own, "tensor", [(t, t ^ k) for t in range(size)]) for k in range(1, size)]


class Line:
    def __init__(self):
        self.last = None

    def tie(self, value):
        if self.last is None:
            return value
        return lax.optimization_barrier((value,) + self.last)[0]

    def mark(self, *values):
        self.last = values


class Total:
    def __init__(self, line, parts, bits):
        self.line, self.bits = line, bits
        self.orders = [list(range(bits)), list(range(bits))[::-1]]
        self.left = [[bit for bit in range(bits) if bit != order[0]] for order in self.orders]
        self.keep = [parts[0], parts[2]]
        self.got = [flip(parts[1], self.orders[0][0], 1 << bits), flip(parts[3], self.orders[1][0], 1 << bits)]
        self.step = 1

    def advance(self):
        line, size = self.line, 1 << self.bits
        if self.step == self.bits:
            for half in range(2):
                self.keep[half] = line.tie(self.keep[half]) + self.got[half]
                line.mark(self.keep[half])
            return
        picks = []
        for half in range(2):
            left, bit = self.left[half], self.orders[half][self.step]
            keep, got = self.keep[half], self.got[half]
            cube = (2,) * len(left) + keep.shape[1:]
            axis = len(left) - 1 - left.index(bit)
            shape = (keep.shape[0] // 2,) + keep.shape[1:]
            pick = lambda value, at, cube=cube, axis=axis, shape=shape: lax.index_in_dim(
                value.reshape(cube), at, axis, keepdims=False
            ).reshape(shape)
            send = pick(line.tie(keep), 1) + pick(got, 1)
            line.mark(send)
            picks.append((pick, keep, got))
            self.got[half] = flip(send, bit, size)
            left.remove(bit)
        for half in range(2):
            pick, keep, got = picks[half]
            self.keep[half] = pick(line.tie(keep), 0) + pick(got, 0)
            line.mark(self.keep[half])
        self.step += 1

    def gather(self):
        size = 1 << self.bits
        if self.step == self.bits:
            self.held = [[0], [0]]
            self.step += 1
        else:
            for half in range(2):
                self.keep[half] = jnp.concatenate([self.line.tie(self.keep[half]), self.got[half]], 0)
                self.line.mark(self.keep[half])
                self.held[half] = self.held[half] + [block | self.last[half] for block in self.held[half]]
        self.last = [1 << self.orders[half].pop() for half in range(2)]
        self.got = [flip(self.keep[half], self.last[half].bit_length() - 1, size) for half in range(2)]

    def pieces(self):
        arrays, where = [], []
        for half in range(2):
            arrays += [self.keep[half], self.got[half]]
            found = {block: (2 * half, at) for at, block in enumerate(self.held[half])}
            found.update({block | self.last[half]: (2 * half + 1, at) for at, block in enumerate(self.held[half])})
            where.append(found)
        return arrays, where


class Ring:
    def __init__(self, line, first, rest, size):
        self.line, self.rest, self.size = line, rest, size
        self.step = 0
        self.got = self.send(first)

    def send(self, value):
        return lax.ppermute(value, "dp", [(d, (d + 2) % self.size) for d in range(self.size)])

    def advance(self):
        value = self.line.tie(self.rest)[self.step] + self.got
        self.line.mark(value)
        self.step += 1
        if self.step < self.size // 2 - 1:
            self.got = self.send(value)
        return value


def butterfly(value, bits):
    for bit in range(bits):
        value = value + flip(value, bit, 1 << bits)
    return value


def tree_sum(value):
    while value.shape[0] > 1:
        value = value.reshape((value.shape[0] // 2, 2) + value.shape[1:])
        value = value[:, 0] + value[:, 1]
    return value[0]


class Small:
    def __init__(self, own, bits):
        self.bits, self.bit, self.held = bits, 0, [own]
        self.got = None
        self.step()

    def step(self):
        if self.got is not None:
            many = len(self.held)
            self.held = self.held + [self.got[at] for at in range(many)]
        if self.bit < self.bits:
            self.got = flip(jnp.stack(self.held), self.bit, 1 << self.bits)
            self.bit += 1

    def pieces(self):
        while len(self.held) < 1 << self.bits:
            self.step()
        return self.held


def both_vectors(pieces):
    level = [piece[8:] for piece in pieces]
    while len(level) > 1:
        level = [level[at] + level[at + 1] for at in range(0, len(level), 2)]
    many = D // level[0].shape[1]
    return jnp.stack([level[0][:many].reshape(-1), level[0][4 : 4 + many].reshape(-1)])


def combine(pieces, block, blocks):
    level = [pieces[other][:8, (block ^ other) * SLOT : (block ^ other) * SLOT + SLOT] for other in range(blocks)]
    while len(level) > 1:
        level = [level[at] + level[at + 1] for at in range(0, len(level), 2)]
    return level[0]


def attention_scores(query, both_keys, length):
    scores = mul(query, both_keys, NT)
    row = lax.broadcasted_iota(jnp.int32, scores.shape, 0)
    place = lax.broadcasted_iota(jnp.int32, scores.shape, 1) % SLOT
    scores = jnp.where((place <= row) & (place < IMG + length), scores, masked_score)
    parts = []
    for at in range(2):
        part = scores[:, at * SLOT : (at + 1) * SLOT]
        expd = jnp.exp(part - jnp.max(part, axis=-1, keepdims=True))
        parts.append(expd / jnp.sum(expd, axis=-1, keepdims=True))
    return parts


def split_heads(value, mask):
    return jnp.concatenate([value * mask[0:1], value * mask[1:2]], axis=0)


def store_parts(refs, value, step, steps, only=None):
    left_keep, left_send, right_keep, right_send = refs
    left_keep[0] = value[:SLOT, :HALF]
    left_send[0] = value[SLOT:, :HALF]

    @pl.when(step < steps // 2)
    def _():
        right_keep[0] = value[:SLOT, HALF:]
        right_keep[1] = value[SLOT:, HALF:]

    @pl.when(step >= steps // 2)
    def _():
        right_send[0] = value[:SLOT, HALF:]
        right_send[1] = value[SLOT:, HALF:]


def part_outs(blocks):
    half = blocks // 2
    steps = blocks // 2
    shape = (half, SLOT, HALF)
    low = max(steps // 2, 1)
    return [
        (shape, F32, (1, SLOT, HALF), lambda s, *_: (s, 0, 0)),
        (shape, F32, (1, SLOT, HALF), lambda s, *_: (s, 0, 0)),
        (shape, F32, (2, SLOT, HALF), lambda s, *_: (jnp.minimum(s, low - 1), 0, 0)),
        (shape, F32, (2, SLOT, HALF), lambda s, *_: (jnp.maximum(s - steps // 2, 0), 0, 0)),
    ]


def front(order, lengths, tokens, gain, shift, weight, bias, tables, mask, mix_gain, uw_rows, out_weight, after=()):
    blocks = order.shape[0]
    steps = blocks // 2
    width = weight.shape[2]
    groups = width // 128
    rows = blocks * SLOT

    def kernel(order_ref, length_ref, x0, x1, g, b, w, wb, tab, msk, mg, uwr, ow, own, first, qkv, mixed, small, *parts_uw):
        step = pl.program_id(0)
        parts, uw = parts_uw[:4], parts_uw[4]

        @pl.when(step == 0)
        def _():
            found = mul(uwr[...], ow[...])
            uw[0:1] = found[0:1] + found[1:2] + found[2:3]
            uw[1:2] = found[3:4] + found[4:5] + found[5:6]
            small[8:] = jnp.zeros((8, rows), F32)
            for at in range(D // rows):
                c = slice(at * rows, at * rows + rows)
                small[8 + at : 9 + at] = uw[0:1, c]
                small[12 + at : 13 + at] = uw[1:2, c]

        x = jnp.concatenate([x0[0], x1[0]], axis=0)
        own[...] = x
        hat, _ = norm_parts(x.astype(F32))
        one = rounded(hat * g[...] + b[...])
        first[...] = one
        for c in range(3):
            proj = mul(one, w[c]) + wb[c : c + 1]
            for group in range(groups):
                part = proj[:, group * 128 : group * 128 + 128]
                if c < 2:
                    part = rotate(part, tab, 3 * c, 1)
                at = c * width + group * 128
                qkv[:, at : at + 128] = rounded(part)
        for pair in range(2):
            r = slice(pair * SLOT, pair * SLOT + SLOT)
            length = length_ref[order_ref[2 * step + pair]]
            for group in range(groups):
                at = group * 128
                query = qkv[r, at : at + 128]
                keys = split_heads(qkv[r, width + at : width + at + 128], msk)
                values = split_heads(qkv[r, 2 * width + at : 2 * width + at + 128], msk)
                probs = attention_scores(query, keys, length)
                mixed[r, at : at + 128] = mul(rounded(jnp.concatenate(probs, axis=1)), values)
        m = mixed[...]
        total = jnp.sum(m, axis=-1, keepdims=True)
        here = pl.ds(pl.multiple_of(step * 2 * SLOT, 2 * SLOT), 2 * SLOT)
        small[:8, here] = rows_of([total, jnp.sum(m * m, axis=-1, keepdims=True)])
        middle = total * (1.0 / width)
        partial = mul(rounded((m - middle) * mg[...]), ow[...]) + middle * uw[0:1]
        store_parts(parts, partial, step, steps)

    row2 = lambda s, *_: (s, 0)
    pair_of = lambda offset: lambda s, order_ref, length_ref: (order_ref[2 * s + offset], 0, 0)
    return run(
        kernel,
        (steps,),
        [
            (tokens, (1, SLOT, D), pair_of(0)),
            (tokens, (1, SLOT, D), pair_of(1)),
            whole(gain), whole(shift), whole(weight), whole(bias), whole(tables), whole(mask),
            whole(mix_gain), whole(uw_rows), whole(out_weight),
        ],
        [
            ((rows, D), BF16, (2 * SLOT, D), row2),
            ((rows, D), BF16, (2 * SLOT, D), row2),
            ((rows, 3 * width), BF16, (2 * SLOT, 3 * width), row2),
            ((rows, width), F32, (2 * SLOT, width), row2),
            ((16, rows), F32, (16, rows), lambda s, *_: (0, 0)),
        ]
        + part_outs(blocks),
        scratch=[pltpu.VMEM((8, D), F32)],
        prefetch=(order, lengths),
        after=after,
        name="front",
    )


def pieces_in(pieces):
    return [whole(piece) for piece in pieces[0]]


def load_pieces(refs, where, total, step, blocks):
    for block in range(blocks):

        @pl.when(step == block)
        def _(block=block):
            for half in range(2):
                array, at = where[half][block]
                total[:, half * HALF : half * HALF + HALF] = refs[array][at]


def middle_norm(own, pieces, sums, uw, out_bias, gain, shift, after=()):
    blocks = len(pieces[1][0])
    rows = blocks * SLOT

    def kernel(*refs):
        x, parts, stats = refs[0], refs[1:5], refs[5 : 5 + blocks]
        uw_ref, bias, g, b, mid, second, stat, total, tot8 = refs[5 + blocks :]
        step = pl.program_id(0)
        load_pieces(parts, pieces[1], total, step, blocks)
        for block in range(blocks):

            @pl.when(step == block)
            def _(block=block):
                tot8[...] = combine(stats, block, blocks)

        cols = columns_of(tot8[...])
        mean = cols[:, 0:1] * (1.0 / D)
        inverse = lax.rsqrt(cols[:, 1:2] * (1.0 / D) - mean * mean + eps)
        branch = inverse * (total[...] - mean * uw_ref[0:1]) + uw_ref[1:2]
        value = x[...].astype(F32) + branch + bias[...]
        mid[...] = value
        hat, _ = norm_parts(value)
        second[...] = rounded(hat * g[...] + b[...])
        lane = lax.broadcasted_iota(jnp.int32, (SLOT, 128), 1)
        stat[...] = jnp.where(lane == 0, mean, inverse)

    row = lambda k, *_: (k, 0)
    return run(
        kernel,
        (blocks,),
        [(own, (SLOT, D), row)]
        + pieces_in(pieces)
        + [whole(part) for part in sums]
        + [whole(uw), whole(out_bias), whole(gain), whole(shift)],
        [
            ((rows, D), F32, (SLOT, D), row),
            ((rows, D), BF16, (SLOT, D), row),
            ((rows, 128), F32, (SLOT, 128), row),
        ],
        scratch=[pltpu.VMEM((SLOT, D), F32), pltpu.VMEM((8, SLOT), F32)],
        after=after,
        name="middle_norm",
    )


def hidden_back(cots, down_weight):
    many, rows, units = len(cots), cots[0].shape[0], down_weight.shape[0]
    tile = min(512, units)

    def kernel(*refs):
        w, out = refs[many:]
        for at in range(many):
            out[at * rows : at * rows + rows] = rounded(mul(refs[at][...], w[...], NT))

    return run(
        kernel,
        (units // tile,),
        [whole(cot) for cot in cots] + [(down_weight, (tile, D), lambda j: (j, 0))],
        [((many * rows, units), BF16, (many * rows, tile), lambda j: (0, j))],
        name="hidden_back",
    )[0]


def hidden_front(chunk, second, up_weight, up_bias, back, gain, after=()):
    rows, units = second.shape[0], up_weight.shape[1]
    tile = 512
    steps = units // tile

    def part_of(c, s_ref, w, b, hb, g, act, slp):
        hidden = mul(s_ref[...], w[:, c]) + b[:, c]
        tail = jnp.exp(-0.5 * hidden * hidden)
        t = 1.0 / (1.0 + (0.3275911 * root_half) * jnp.abs(hidden))
        poly = 1.061405429 * t - 1.453152027
        poly = poly * t + 1.421413741
        poly = poly * t - 0.284496736
        poly = poly * t + 0.254829592
        half = 0.5 * poly * t * tail
        phi = jnp.where(hidden >= 0.0, 1.0 - half, half)
        active = hidden * phi
        act[:, c] = rounded(active)
        slp[:, c] = rounded(phi + hidden * (inv_root_two_pi * tail))
        scaled = hb[:, c].astype(F32) * g[:, c]
        return [value[:, :128] + value[:, 128:] for value in (active, active * active, scaled, scaled * active)]

    def kernel(s_ref, w, b, hb, g, act, slp, sums, acc):
        step = pl.program_id(0)
        found = [part_of(slice(at, at + 256), s_ref, w, b, hb, g, act, slp) for at in range(0, tile, 256)]

        @pl.when(step == 0)
        def _():
            for at in range(4):
                acc[at] = found[0][at] + found[1][at]

        @pl.when(step > 0)
        def _():
            for at in range(4):
                acc[at] += found[0][at] + found[1][at]

        @pl.when(step == steps - 1)
        def _():
            for block in range(rows // SLOT):
                r = slice(block * SLOT, block * SLOT + SLOT)
                sums[:, r] = rows_of([jnp.sum(acc[at, r], axis=-1, keepdims=True) for at in range(4)])

    return run(
        kernel,
        (steps,),
        [
            whole(second),
            (up_weight, (D, tile), lambda j: (0, j)),
            (up_bias, (1, tile), lambda j: (0, j)),
            (back, (rows, tile), lambda j: (chunk, j)),
            (gain, (1, tile), lambda j: (0, j)),
        ],
        [
            ((rows, units), BF16, (rows, tile), lambda j: (0, j)),
            ((rows, units), BF16, (rows, tile), lambda j: (0, j)),
            ((8, rows), F32, (8, rows), lambda j: (0, 0)),
        ],
        scratch=[pltpu.VMEM((4, rows, 128), F32)],
        after=after,
        name="hidden_front",
    )


def hidden_mid(chunk, active, slope, back, sums, gain, shift):
    blocks = len(sums)
    rows, units = active.shape

    def kernel(act, slp, hb, *refs):
        stats = refs[:blocks]
        g, b, low, grad, vecs, tot8 = refs[blocks:]
        step = pl.program_id(0)
        for block in range(blocks):

            @pl.when(step == block)
            def _(block=block):
                tot8[...] = combine(stats, block, blocks)

        cols = columns_of(tot8[...]) * (1.0 / FF)
        mean = cols[:, 0:1]
        inverse = lax.rsqrt(cols[:, 1:2] - mean * mean + eps)
        one = cols[:, 2:3]
        two = inverse * (cols[:, 3:4] - mean * one)
        for at in range(0, units, 256):
            c = slice(at, at + 256)
            hat = (act[:, c].astype(F32) - mean) * inverse
            low[:, c] = rounded(hat * g[:, c] + b[:, c])
            raw = hb[:, c].astype(F32)
            grown = rounded(inverse * (raw * g[:, c] - one - hat * two) * slp[:, c].astype(F32))
            grad[:, c] = grown
            vecs[0, 0:1, c] = sum_rows(raw * hat)
            vecs[0, 1:2, c] = sum_rows(raw)
            vecs[0, 2:3, c] = sum_rows(grown.astype(F32))

    row = lambda k: (k, 0)
    return run(
        kernel,
        (blocks,),
        [
            (active, (SLOT, units), row),
            (slope, (SLOT, units), row),
            (back, (SLOT, units), lambda k: (chunk * blocks + k, 0)),
        ]
        + [whole(part) for part in sums]
        + [whole(gain), whole(shift)],
        [
            ((rows, units), BF16, (SLOT, units), row),
            ((rows, units), BF16, (SLOT, units), row),
            ((blocks, 8, units), F32, (1, 8, units), lambda k: (k, 0, 0)),
        ],
        scratch=[pltpu.VMEM((8, SLOT), F32)],
        name="hidden_mid",
    )


def hidden_grad(grad, up_weight):
    rows, units = grad.shape
    blocks = rows // SLOT
    tile = 512
    steps = D // tile
    half = steps // 2

    def kernel(gr, w, left_keep, left_send, right_keep, right_send):
        step = pl.program_id(0)
        value = mul(gr[...], w[...], NT)

        @pl.when(step < half)
        def _():
            for block in range(blocks):
                r = slice(block * SLOT, block * SLOT + SLOT)
                (left_send if block & 1 else left_keep)[block // 2] = value[r]

        @pl.when(step >= half)
        def _():
            for block in range(blocks):
                r = slice(block * SLOT, block * SLOT + SLOT)
                (right_send if block >= blocks // 2 else right_keep)[block % (blocks // 2)] = value[r]

    shape = (blocks // 2, SLOT, HALF)
    block_shape = (blocks // 2, SLOT, tile)
    lefts = lambda j: (0, 0, jnp.minimum(j, half - 1))
    rights = lambda j: (0, 0, jnp.maximum(j - half, 0))
    return run(
        kernel,
        (steps,),
        [whole(grad), (up_weight, (tile, units), lambda j: (j, 0))],
        [
            (shape, F32, block_shape, lefts),
            (shape, F32, block_shape, lefts),
            (shape, F32, block_shape, rights),
            (shape, F32, block_shape, rights),
        ],
        name="hidden_grad",
    )


def result_part(order, lows, down_weight):
    pairs = order.shape[0]
    units = down_weight.shape[0]
    many = len(lows)
    rows = lows[0].shape[0]
    each = rows // SLOT
    tile = 256

    def kernel(order_ref, *refs):
        w, out = refs[many:]
        for at in range(many):
            value = mul(refs[at][...], w[...])
            for block in range(each):
                out[order_ref[at * each + block]] = value[block * SLOT : block * SLOT + SLOT]

    return run(
        kernel,
        (D // tile,),
        [whole(low) for low in lows] + [(down_weight, (units, tile), lambda j, *_: (0, j))],
        [((pairs, SLOT, D), F32, (pairs, SLOT, tile), lambda j, *_: (0, 0, j))],
        prefetch=(order,),
        name="result_part",
    )[0]


def middle_back(own, cot, pieces, middle, stat, uw, out_bias, gain, after=()):
    blocks = len(pieces[1][0])
    rows = blocks * SLOT

    def kernel(*refs):
        x, c, parts = refs[0], refs[1], refs[2:6]
        mid, st, uw_ref, bias, g, grad, low, stat2, vecs, total = refs[6:]
        load_pieces(parts, pieces[1], total, pl.program_id(0), blocks)
        value = mid[...]
        hat, inverse = norm_parts(value)
        sec = total[...]
        scaled = sec * g[...]
        up = c[...].astype(F32)
        out = up + inverse * (
            scaled
            - jnp.mean(scaled, axis=-1, keepdims=True)
            - hat * jnp.mean(scaled * hat, axis=-1, keepdims=True)
        )
        grad[...] = out
        lowered = rounded(out)
        low[...] = lowered
        low32 = lowered.astype(F32)
        one = jnp.mean(low32 * uw_ref[0:1], axis=-1, keepdims=True)
        moved = value - x[...].astype(F32) - bias[...] - uw_ref[1:2]
        two = jnp.mean(low32 * moved, axis=-1, keepdims=True)
        lane = lax.broadcasted_iota(jnp.int32, (SLOT, 128), 1)
        stat2[...] = jnp.where(lane == 2, one, jnp.where(lane == 3, two, st[...]))
        vecs[0, 0:1] = sum_rows(sec * hat)
        vecs[0, 1:2] = sum_rows(sec)
        vecs[0, 2:3] = sum_rows(out)
        vecs[0, 3:4] = sum_rows(up)

    row = lambda k, *_: (k, 0)
    return run(
        kernel,
        (blocks,),
        [(own, (SLOT, D), row), (cot, (SLOT, D), row)]
        + pieces_in(pieces)
        + [(middle, (SLOT, D), row), (stat, (SLOT, 128), row), whole(uw), whole(out_bias), whole(gain)],
        [
            ((rows, D), F32, (SLOT, D), row),
            ((rows, D), BF16, (SLOT, D), row),
            ((rows, 128), F32, (SLOT, 128), row),
            ((blocks, 8, D), F32, (1, 8, D), lambda k, *_: (k, 0, 0)),
        ],
        scratch=[pltpu.VMEM((SLOT, D), F32)],
        after=after,
        name="middle_back",
    )


def attention_back(order, lengths, low, stat, mixed, qkv, own, mix_gain, mix_shift, out_weight, weight, tables, mask, after=()):
    blocks = order.shape[0]
    steps = blocks // 2
    width = out_weight.shape[0]
    groups = width // 128
    rows = blocks * SLOT

    def kernel(
        order_ref, length_ref, low_ref, st, mx, qkv_ref, x, mg, ms, ow, w, tab, msk,
        mix_low, dproj, vecs, wide, left_keep, left_send, right_keep, right_send, dmixed,
    ):
        step = pl.program_id(0)
        mean, inverse, one, two = (st[:, at : at + 1] for at in range(4))
        back = mul(low_ref[...], ow[...], NT)
        hat = (mx[...] - mean) * inverse
        mix_low[...] = rounded(hat * mg[...] + ms[...])
        dmixed[...] = rounded(inverse * (back * mg[...] - one - hat * two))
        vecs[0, 0:1, :width] = sum_rows(back * hat)
        vecs[0, 1:2, :width] = sum_rows(back)
        first_half = lax.broadcasted_iota(jnp.int32, (SLOT, 128), 1) < HD
        for pair in range(2):
            r = slice(pair * SLOT, pair * SLOT + SLOT)
            length = length_ref[order_ref[2 * step + pair]]
            for group in range(groups):
                at = group * 128
                query = qkv_ref[r, at : at + 128]
                keys = split_heads(qkv_ref[r, width + at : width + at + 128], msk)
                values = split_heads(qkv_ref[r, 2 * width + at : 2 * width + at + 128], msk)
                grad = dmixed[r, at : at + 128]
                probs = attention_scores(query, keys, length)
                dprobs = mul(grad, values, NT)
                dscores = []
                for i in range(2):
                    dp = dprobs[:, i * SLOT : (i + 1) * SLOT]
                    carried = jnp.sum(probs[i] * dp, axis=-1, keepdims=True)
                    dscores.append(rounded(probs[i] * (dp - carried)))
                dscores = jnp.concatenate(dscores, axis=1)
                dquery = mul(dscores, keys)
                dkey = mul(dscores, query, TN)
                dvalue = mul(rounded(jnp.concatenate(probs, axis=1)), grad, TN)
                dkey = jnp.where(first_half, dkey[:SLOT], dkey[SLOT:])
                dvalue = jnp.where(first_half, dvalue[:SLOT], dvalue[SLOT:])
                tabs = [tab[i, :SLOT] for i in range(6)]
                dproj[r, at : at + 128] = rounded(rotate(dquery, tabs, 0, -1))
                dproj[r, width + at : width + at + 128] = rounded(rotate(dkey, tabs, 3, -1))
                dproj[r, 2 * width + at : 2 * width + at + 128] = rounded(dvalue)
        vecs[0, 2:3] = sum_rows(dproj[...].astype(F32))
        partial = mul(dproj[:, :width], w[0], NT)
        for c in (1, 2):
            partial += mul(dproj[:, c * width : (c + 1) * width], w[c], NT)
        pre_hat, _ = norm_parts(x[...].astype(F32))
        grown = partial * pre_hat
        wide[0, 0:1] = sum_rows(grown[:SLOT]) + sum_rows(grown[SLOT:])
        wide[0, 1:2] = sum_rows(partial[:SLOT]) + sum_rows(partial[SLOT:])
        store_parts((left_keep, left_send, right_keep, right_send), partial, step, steps)

    row2 = lambda s, *_: (s, 0)
    return run(
        kernel,
        (steps,),
        [
            (low, (2 * SLOT, D), row2),
            (stat, (2 * SLOT, 128), row2),
            (mixed, (2 * SLOT, width), row2),
            (qkv, (2 * SLOT, 3 * width), row2),
            (own, (2 * SLOT, D), row2),
            whole(mix_gain), whole(mix_shift), whole(out_weight), whole(weight), whole(tables), whole(mask),
        ],
        [
            ((rows, width), BF16, (2 * SLOT, width), row2),
            ((rows, 3 * width), BF16, (2 * SLOT, 3 * width), row2),
            ((steps, 8, 3 * width), F32, (1, 8, 3 * width), lambda s, *_: (s, 0, 0)),
            ((steps, 8, D), F32, (1, 8, D), lambda s, *_: (s, 0, 0)),
        ]
        + part_outs(blocks),
        scratch=[pltpu.VMEM((2 * SLOT, width), BF16)],
        prefetch=(order, lengths),
        after=after,
        name="attention_back",
    )


def tokens_back(order, own, grad, pieces, gain, before, pairs, after=()):
    blocks = len(pieces[1][0])

    def kernel(order_ref, x, gr, *refs):
        parts = refs[:4]
        g = refs[4]
        out, total = refs[-2:]
        load_pieces(parts, pieces[1], total, pl.program_id(0), blocks)
        hat, inverse = norm_parts(x[...].astype(F32))
        scaled = total[...] * g[...]
        out[0] = gr[...] + inverse * (
            scaled
            - jnp.mean(scaled, axis=-1, keepdims=True)
            - hat * jnp.mean(scaled * hat, axis=-1, keepdims=True)
        )

    row = lambda k, *_: (k, 0)
    ins = [(own, (SLOT, D), row), (grad, (SLOT, D), row)] + pieces_in(pieces) + [whole(gain)]
    alias = None
    if before is not None:
        alias = {1 + len(ins): 0}
        ins = ins + [(before, None, None)]
    return run(
        kernel,
        (blocks,),
        ins,
        [((pairs, SLOT, D), F32, (1, SLOT, D), lambda k, o: (o[k], 0, 0))],
        scratch=[pltpu.VMEM((SLOT, D), F32)],
        prefetch=(order,),
        after=after,
        alias=alias,
        name="tokens_back",
    )[0]


def output_of(order, middle, result, bias, before, after=()):
    blocks = order.shape[0]

    def kernel(order_ref, mid, res, b, *refs):
        out = refs[-1]
        out[0] = rounded(mid[...] + res[0] + b[...])

    ins = [
        (middle, (SLOT, D), lambda k, *_: (k, 0)),
        (result, (1, SLOT, D), lambda k, o: (o[k], 0, 0)),
        whole(bias),
    ]
    alias = None
    if before is not None:
        alias = {1 + len(ins): 0}
        ins = ins + [(before, None, None)]
    return run(
        kernel,
        (blocks,),
        ins,
        [(result.shape, BF16, (1, SLOT, D), lambda k, o: (o[k], 0, 0))],
        prefetch=(order,),
        after=after,
        alias=alias,
        name="output",
    )[0]


def ring_grads(ids, products, got=None):
    count, many = ids.shape[0], len(products[0][0])
    rows = products[0][0][0].shape[0]
    widths = [rights[0].shape[1] for lefts, rights in products]
    block = D // (2 * count)
    shape = (block, sum(widths))

    def kernel(ids_ref, *refs):
        outs = refs[2 * many * len(products) + (got is not None) :]
        step = pl.program_id(0)
        start = 0
        for at, width in enumerate(widths):
            left, right = (refs[(2 * at + side) * many : (2 * at + side + 1) * many] for side in range(2))
            value = mul(left[0][...], right[0][...], TN)
            for k in range(1, many):
                value += mul(left[k][...], right[k][...], TN)
            c = slice(start, start + width)
            start += width
            if got is None:
                outs[0][0, :, c] = value
                continue
            value += refs[2 * many * len(products)][0, :, c]

            @pl.when(step == 0)
            def _(value=value, c=c):
                outs[0][:, c] = value

            @pl.when(step > 0)
            def _(value=value, c=c):
                outs[1][0, :, c] = value

    fixed = lambda i, *_: (0, 0)
    moving = lambda i, ids_ref: (0, ids_ref[i])
    lead = lambda i, *_: (i, 0, 0)
    ins = []
    for lefts, rights in products:
        ins += [(left, (rows, block), moving) for left in lefts]
        ins += [(right, right.shape, fixed) for right in rights]
    if got is None:
        outs = [((count,) + shape, F32, (1,) + shape, lead)]
    else:
        ins += [(got, (1,) + shape, lead)]
        outs = [
            (shape, F32, shape, fixed),
            ((count - 1,) + shape, F32, (1,) + shape, lambda i, *_: (jnp.maximum(i - 1, 0), 0, 0)),
        ]
    return run(kernel, (count,), ins, outs, prefetch=(ids,), name="ring_grads")


def full_grad(products):
    many, block = len(products[0][0]), 512
    rows, tall = products[0][0][0].shape
    widths = [rights[0].shape[1] for lefts, rights in products]

    def kernel(*refs):
        out, start = refs[-1], 0
        for at, width in enumerate(widths):
            left, right = (refs[(2 * at + side) * many : (2 * at + side + 1) * many] for side in range(2))
            value = mul(left[0][...], right[0][...], TN)
            for k in range(1, many):
                value += mul(left[k][...], right[k][...], TN)
            out[:, start : start + width] = value
            start += width

    ins = []
    for lefts, rights in products:
        ins += [(left, (rows, block), lambda i: (0, i)) for left in lefts]
        ins += [(right, right.shape, lambda i: (0, 0)) for right in rights]
    wide = sum(widths)
    return run(
        kernel, (tall // block,), ins, [((tall, wide), F32, (block, wide), lambda i: (i, 0))], name="full_grad"
    )[0]


def steps_of(totals, bits, done, until):
    done = list(done)

    def step(at):
        if done[at] < bits:
            totals[at].advance()
        else:
            totals[at].gather()
        done[at] += 1
        if done[at] == bits and until == 2 * bits:
            totals[at].gather()
            done[at] += 1

    limits = [until] + [until if until == 2 * bits else bits - 1] * (len(totals) - 1)
    while any(have < limit for have, limit in zip(done, limits)):
        for at in range(len(totals)):
            if done[at] < limits[at]:
                step(at)


def split_rows(value):
    found = []
    for _ in range(3):
        part = lax.reduce_precision(value, 8, 7)
        found.append(part.astype(BF16))
        value = value - part
    return found


def body(
    tokens,
    lengths,
    cotangent,
    pre_gain,
    pre_shift,
    qkv_weight,
    qkv_bias,
    mix_gain,
    mix_shift,
    out_weight,
    out_bias,
    ffn_gain,
    ffn_shift,
    up_weight,
    up_bias,
    hid_gain,
    hid_shift,
    down_weight,
    down_bias,
):
    pairs = lengths.shape[0]
    blocks = lax.axis_size("tensor")
    bits = blocks.bit_length() - 1
    chunks = pairs // blocks
    width = qkv_weight.shape[2]
    mine = lax.axis_index("tensor").astype(jnp.int32)
    orders = [jnp.arange(c * blocks, (c + 1) * blocks, dtype=jnp.int32) ^ mine for c in range(chunks)]
    tokens3 = tokens.reshape(pairs, SLOT, D)
    row = lambda v: v.reshape(1, -1)
    pre_gain, pre_shift, mix_gain, mix_shift = map(row, (pre_gain, pre_shift, mix_gain, mix_shift))
    out_bias, ffn_gain, ffn_shift, up_bias = map(row, (out_bias, ffn_gain, ffn_shift, up_bias))
    hid_gain, hid_shift, down_bias = map(row, (hid_gain, hid_shift, down_bias))
    tables = xpos_tables()
    lane = np.arange(128)[None, :] < HD
    mask = jnp.asarray(np.concatenate([lane, ~lane], 0).astype(np.float32)).astype(BF16)
    zero = jnp.zeros((2, width), BF16)
    uw_rows = jnp.concatenate(split_rows(mix_gain) + split_rows(mix_shift) + [zero], 0)

    line = Line()
    dp_size = lax.axis_size("dp")
    place = lax.axis_index("dp").astype(jnp.int32)
    count = dp_size // 2
    around = lax.rem(place // 2 + count - 1 - jnp.arange(count, dtype=jnp.int32), count)
    mine_ids, other_ids = 2 * around + lax.rem(place, 2), 2 * around + 1 - lax.rem(place, 2)

    def tied(products):
        (lefts, rights), others = products[0], products[1:]
        return [([line.tie(lefts[0])] + lefts[1:], rights)] + others

    def full(products):
        grad = full_grad(tied(products))
        line.mark(grad)
        return grad

    every = lambda items, name: [item[name] for item in items]

    ones, twos, threes = [], [], []
    for c in range(chunks):
        found = front(
            orders[c], lengths, line.tie(tokens3), pre_gain, pre_shift, qkv_weight, qkv_bias, tables, mask, mix_gain, uw_rows,
            out_weight,
        )
        own, first, qkv, mixed, small = found[:5]
        one = dict(own=own, first=first, qkv=qkv, mixed=mixed, parts=found[5:])
        line.mark(small)
        one["small"] = small
        if c == 0:
            one["total"] = Total(line, one["parts"], bits)
            one["sums"] = Small(small, bits)
        ones.append(one)
    sums0 = ones[0]["sums"]
    if bits > 1:
        ones[0]["total"].advance()
    for c in range(1, chunks):
        ones[c]["total"] = Total(line, [line.tie(part) for part in ones[c]["parts"]], bits)
    sums0.held[0] = line.tie(sums0.held[0])
    sums0.step()
    cot3 = cotangent.reshape(pairs, SLOT, D)
    cots = []
    for c in range(chunks):
        cots.append(line.tie(cot3)[orders[c]].reshape(-1, D))
        line.mark(cots[-1])
    totals = every(ones, "total")
    line.mark(*line.last, *sums0.pieces())
    for step in range(1, bits):
        totals[0].advance()
    back = hidden_back([line.tie(cots[0])] + cots[1:], down_weight)
    line.mark(back)
    for one in ones[1:]:
        one["sums"] = Small(line.tie(one["small"]), bits)
    done = [bits] + [0] * (chunks - 1)
    steps_of(totals, bits, done, 2 * bits - 1)
    for one in ones[1:]:
        line.mark(*line.last, one["sums"].got)
        one["sums"].step()
    uw_total = both_vectors(sums0.pieces())

    def mid_of(c):
        two = twos[c]
        low, grad, vecs = hidden_mid(c, line.tie(two["active"]), two["slope"], back, two["sums"], hid_gain, hid_shift)
        two.update(low=low, grad=grad, vecs=functools.reduce(jnp.add, [vecs[k] for k in range(blocks)]))
        line.mark(vecs)

    def hidden_of(c):
        parts = hidden_grad(line.tie(twos[c]["grad"]), up_weight)
        line.mark(parts[0])
        return parts

    totals[0].gather()
    for other in ones[1:]:
        line.mark(*line.last, *other["sums"].pieces())
    for c in range(chunks):
        one = ones[c]
        mid, second, stat = middle_norm(
            line.tie(one["own"]), totals[c].pieces(), one["sums"].pieces(), uw_total, out_bias, ffn_gain, ffn_shift
        )
        line.mark(stat)
        if c == 0:
            for total in totals[1:]:
                total.advance()
                total.gather()
        active, slope, sums = hidden_front(c, line.tie(second), up_weight, up_bias, back, hid_gain)
        line.mark(sums)
        twos.append(dict(middle=mid, second=second, stat=stat, active=active, slope=slope, sums=all_pieces(sums, bits)))
        if c == 0:
            for total in totals[1:]:
                for step in range(1, bits):
                    total.gather()
            line.mark(*line.last, *twos[0]["sums"][1:])
        else:
            twos[0]["total"].advance()
            line.mark(*line.last, *twos[c]["sums"][1:])
        mid_of(c)
        if c > 0:
            line.mark(*line.last, *twos[0]["total"].got)
        if c == 0 and chunks > 1:
            twos[0]["total"] = Total(line, hidden_of(0), bits)
    lows = every(twos, "low")
    down_grad = full([(lows, cots)])
    down_part = lax.psum_scatter(down_grad, "dp", scatter_dimension=1, tiled=True)
    up_products = [(every(twos, "second"), every(twos, "grad"))]
    sent = ring_grads(other_ids, tied(up_products))[0]
    line.mark(sent)
    sent = lax.ppermute(sent, "dp", [(d, d ^ 1) for d in range(dp_size)])
    if chunks > 1:
        for step in range(1, bits):
            twos[0]["total"].advance()
        twos[0]["total"].gather()
        parts = [None] + [hidden_of(c) for c in range(1, chunks)]
    else:
        twos[0]["total"] = Total(line, hidden_of(0), bits)
        for step in range(bits):
            twos[0]["total"].advance()
        twos[0]["total"].gather()
    ring_first, ring_rest = ring_grads(mine_ids, tied(up_products), sent)
    line.mark(ring_rest)
    ring = Ring(line, ring_first, ring_rest, dp_size)
    for step in range(1, bits):
        twos[0]["total"].gather()
    for c in range(1, chunks):
        twos[c]["total"] = Total(line, [line.tie(part) for part in parts[c]], bits)
    totals = every(twos, "total")
    result = result_part(jnp.concatenate(orders), [line.tie(lows[0])] + lows[1:], down_weight)
    line.mark(result)

    for c in range(chunks):
        one, two = ones[c], twos[c]
        grad, low, stat2, vecs = middle_back(
            line.tie(one["own"]), cots[c], two["total"].pieces(), two["middle"], two["stat"], uw_total, out_bias, ffn_gain
        )
        line.mark(stat2)
        if c == 0:
            for total in totals[1:]:
                total.advance()
        found = attention_back(
            orders[c], lengths, line.tie(low), stat2, one["mixed"], one["qkv"], one["own"], mix_gain, mix_shift, out_weight,
            qkv_weight, tables, mask,
        )
        line.mark(found[2])
        three = dict(grad=grad, low=low, vecs=tree_sum(vecs), mix_low=found[0], dproj=found[1])
        three["narrow"] = tree_sum(found[2])
        three["wide"] = tree_sum(found[3])
        parts = found[4:]
        if c == 0 and chunks > 1:
            for total in totals[1:]:
                for step in range(1, bits):
                    total.advance()
                for step in range(bits):
                    total.gather()
            for total in totals[1:]:
                line.mark(*line.last, *total.got)
            up_part = ring.advance()
            result = lax.psum(line.tie(result), "tensor")
            parts = [line.tie(part) for part in parts]
        three["total"] = Total(line, parts, bits)
        threes.append(three)

    first, last = threes[0]["total"], threes[-1]["total"]
    add = lambda items, name, size: functools.reduce(jnp.add, [item[name] for item in items])[:size]
    pad = lambda v: jnp.pad(v, ((0, 0), (0, D - v.shape[1])))
    wide = add(threes, "wide", 2)
    got = flip(wide, 0, blocks)
    if chunks > 1:
        line.mark(*line.last, *first.got)
    attention_grad = full(
        [(every(ones, "first"), every(threes, "dproj")), (every(threes, "low"), every(threes, "mix_low"))]
    )
    if chunks == 1:
        up_part = ring.advance()
        result = lax.psum(line.tie(result), "tensor")
    attention_part = lax.psum_scatter(attention_grad, "dp", scatter_dimension=0, tiled=True)
    for step in range(bits):
        first.advance()
    first.gather()
    if chunks > 1:
        last.advance()
    for step in range(1, bits):
        first.gather()
    line.mark(*line.last, down_part)
    up_part = ring.advance()
    if chunks > 1:
        for step in range(1, bits):
            last.advance()
        last.gather()
    for bit in range(1, bits):
        wide = line.tie(wide) + got
        got = flip(wide, bit, blocks)
        line.mark(wide)
    if chunks > 1:
        line.mark(*line.last, *last.got)
    hop = lambda v, bit: lax.ppermute(v, "dp", [(d, d ^ (1 << bit)) for d in range(dp_size)])
    dp_bits = dp_size.bit_length() - 1
    tokens_grad, output = None, None
    for c in range(chunks):
        tokens_grad = tokens_back(
            orders[c], line.tie(ones[c]["own"]), threes[c]["grad"], threes[c]["total"].pieces(), pre_gain, tokens_grad, pairs
        )
        line.mark(tokens_grad)
        if c == 0:
            wide = line.tie(wide) + got
            vecs = jnp.concatenate(
                [pad(add(twos, "vecs", 3)), add(threes, "vecs", 4), pad(add(threes, "narrow", 3)), wide], 0
            )
            line.mark(vecs)
            got = hop(vecs, 0)
            for step in range(2, count - 1):
                up_part = ring.advance()
            if chunks > 1:
                for step in range(1, bits):
                    last.gather()
            vecs = line.tie(vecs) + got
            line.mark(vecs)
            got = hop(vecs, 1)
    for bit in range(2, dp_bits):
        vecs = line.tie(vecs) + got
        line.mark(vecs)
        got = hop(vecs, bit)
    for c in range(chunks):
        output = output_of(orders[c], line.tie(twos[c]["middle"]), result, down_bias, output)
        line.mark(output)
    vecs = vecs + got
    hid_vecs, mid_vecs, narrow, wide = vecs[:3], vecs[3:7], vecs[7:10], vecs[10:12]
    qkv_part = jnp.swapaxes(attention_part[:, : 3 * width].reshape(-1, 3, width), 0, 1)
    out_part = jnp.transpose(attention_part[:, 3 * width :])
    units = hid_gain.shape[1]
    return (
        output.reshape(-1, D),
        tokens_grad.reshape(-1, D),
        wide[0],
        wide[1],
        qkv_part,
        narrow[2, : 3 * width].reshape(3, width),
        narrow[0, :width],
        narrow[1, :width],
        out_part,
        mid_vecs[2],
        mid_vecs[0],
        mid_vecs[1],
        up_part,
        hid_vecs[2, :units],
        hid_vecs[0, :units],
        hid_vecs[1, :units],
        down_part,
        mid_vecs[3],
    )


def solution(mesh):
    in_specs = (
        P("dp", None),
        P("dp"),
        P("dp", None),
        P(),
        P(),
        P(None, None, "tensor"),
        P(None, "tensor"),
        P("tensor"),
        P("tensor"),
        P("tensor", None),
        P(),
        P(),
        P(),
        P(None, "tensor"),
        P("tensor"),
        P("tensor"),
        P("tensor"),
        P("tensor", None),
        P(),
    )
    out_specs = (
        P("dp", None),
        P("dp", None),
        P(),
        P(),
        P(None, "dp", "tensor"),
        P(None, "tensor"),
        P("tensor"),
        P("tensor"),
        P("tensor", "dp"),
        P(),
        P(),
        P(),
        P("dp", "tensor"),
        P("tensor"),
        P("tensor"),
        P("tensor"),
        P("tensor", "dp"),
        P(),
    )
    return jax.shard_map(body, mesh=mesh, in_specs=in_specs, out_specs=out_specs, check_vma=False)
```

```python
import functools
import math

import jax
import jax.numpy as jnp
import numpy as np
from jax import lax
from jax.experimental import pallas as pl
from jax.experimental.pallas import tpu as pltpu
from jax.sharding import PartitionSpec as P

D = 2048
HD = 64
FF = 8192
SLOT = 128
IMG = 64
SCALE_BASE = 512
HALF = D // 2

eps = 1e-05
root_half = 0.7071067811865476
inv_root_two_pi = 0.3989422804014327
masked_score = -1e30
MEGA = 1 << 20

COST = {
    "front": 15.6,
    "middle_norm": 400.0,
    "hidden_back": 400.0,
    "hidden_front": 14.7,
    "hidden_mid": 400.0,
    "hidden_grad": 7.0,
    "full_grad": 15.0,
    "ring_grads": 12.0,
    "result_part": 400.0,
    "middle_back": 11.0,
    "attention_back": 21.7,
    "tokens_back": 8.5,
    "output": 6.0,
    "attention_outputs": 2.0,
}
WORK = 5.5e+07

F32 = jnp.float32
BF16 = jnp.bfloat16
NN = (((1,), (0,)), ((), ()))
NT = (((1,), (1,)), ((), ()))
TN = (((0,), (0,)), ((), ()))


def rounded(value):
    return value.astype(BF16)


def mul(left, right, dims=NN):
    return lax.dot_general(left, right, dims, preferred_element_type=F32)


def xpos_tables():
    place = np.arange(SLOT, dtype=np.float64)[:, None]
    lane = np.arange(128)[None, :]
    index = (lane % HD) // 2
    angle = place * 10000.0 ** (-2.0 * index / HD)
    zeta = (2.0 * index + 0.4 * HD) / (1.4 * HD)
    growth = zeta ** ((place - SLOT // 2) / SCALE_BASE)
    even = lane % 2 == 0
    found = []
    for factor in (growth / math.sqrt(HD), 1.0 / growth):
        found += [
            np.cos(angle) * factor,
            np.where(even, -np.sin(angle), 0.0) * factor,
            np.where(even, 0.0, np.sin(angle)) * factor,
        ]
    return jnp.asarray(np.tile(np.stack(found), (1, 2, 1)).astype(np.float32))


def rotate(value, tables, base, sign):
    up = pltpu.roll(value, 127, axis=1)
    down = pltpu.roll(value, 1, axis=1)
    turned = up * tables[base + 1] + down * tables[base + 2]
    return value * tables[base] + turned if sign > 0 else value * tables[base] - turned


def columns_of(parts):
    return jnp.transpose(parts)


def rows_of(columns):
    size = columns[0].shape[0]
    lane = lax.broadcasted_iota(jnp.int32, (size, 128), 1)
    tile = jnp.zeros((size, 128), F32)
    for at, column in enumerate(columns):
        tile = jnp.where(lane == at, column, tile)
    return jnp.transpose(tile)[:8]


def norm_parts(value):
    mean = jnp.mean(value, axis=-1, keepdims=True)
    var = jnp.mean(value * value, axis=-1, keepdims=True) - mean * mean
    inverse = lax.rsqrt(var + eps)
    return (value - mean) * inverse, inverse


def sum_rows(value):
    return jnp.sum(value, axis=0, keepdims=True)


def whole(array, **kw):
    rank = array.ndim
    return (array, array.shape, lambda *at: (0,) * rank)


def run(kernel, grid, ins, outs, scratch=(), prefetch=(), after=(), alias=None, limit=56, name=None):
    prefetch = tuple(prefetch)

    def body(*refs):
        refs = list(refs)
        first = len(prefetch) + len(ins)
        del refs[first : first + len(after)]
        kernel(*refs)

    in_specs = []
    for array, block, where in ins:
        if block is None:
            in_specs.append(pl.BlockSpec(memory_space=pl.ANY))
        elif tuple(block) == tuple(array.shape):
            in_specs.append(pl.BlockSpec(block, where, pipeline_mode=pl.Buffered(1)))
        else:
            in_specs.append(pl.BlockSpec(block, where))
    in_specs += [pl.BlockSpec(memory_space=pl.ANY)] * len(after)
    out_specs = [pl.BlockSpec(block, where) for shape, dtype, block, where in outs]
    out_shape = [jax.ShapeDtypeStruct(shape, dtype) for shape, dtype, block, where in outs]
    return pl.pallas_call(
        body,
        grid_spec=pltpu.PrefetchScalarGridSpec(
            num_scalar_prefetch=len(prefetch),
            grid=grid,
            in_specs=in_specs,
            out_specs=out_specs,
            scratch_shapes=list(scratch),
        ),
        out_shape=out_shape,
        input_output_aliases=alias or {},
        compiler_params=pltpu.CompilerParams(
            dimension_semantics=("arbitrary",) * len(grid), vmem_limit_bytes=limit * MEGA
        ),
        cost_estimate=pl.CostEstimate(flops=int(COST[name] * WORK), bytes_accessed=1000, transcendentals=0),
        name=name,
    )(*prefetch, *[array for array, block, where in ins], *after)


def flip(value, bit, size):
    return lax.ppermute(value, "tensor", [(t, t ^ (1 << bit)) for t in range(size)])


def all_pieces(own, bits):
    size = 1 << bits
    return [own] + [lax.ppermute(own, "tensor", [(t, t ^ k) for t in range(size)]) for k in range(1, size)]


class Line:
    def __init__(self):
        self.last = None

    def tie(self, value):
        if self.last is None:
            return value
        return lax.optimization_barrier((value,) + self.last)[0]

    def mark(self, *values):
        self.last = values


class Total:
    def __init__(self, line, parts, bits):
        self.line, self.bits = line, bits
        self.orders = [list(range(bits)), list(range(bits))[::-1]]
        self.left = [[bit for bit in range(bits) if bit != order[0]] for order in self.orders]
        self.keep = [parts[0], parts[2]]
        self.got = [flip(parts[1], self.orders[0][0], 1 << bits), flip(parts[3], self.orders[1][0], 1 << bits)]
        self.step = 1

    def advance(self):
        line, size = self.line, 1 << self.bits
        if self.step == self.bits:
            for half in range(2):
                self.keep[half] = line.tie(self.keep[half]) + self.got[half]
                line.mark(self.keep[half])
            return
        picks = []
        for half in range(2):
            left, bit = self.left[half], self.orders[half][self.step]
            keep, got = self.keep[half], self.got[half]
            cube = (2,) * len(left) + keep.shape[1:]
            axis = len(left) - 1 - left.index(bit)
            shape = (keep.shape[0] // 2,) + keep.shape[1:]
            pick = lambda value, at, cube=cube, axis=axis, shape=shape: lax.index_in_dim(
                value.reshape(cube), at, axis, keepdims=False
            ).reshape(shape)
            send = pick(line.tie(keep), 1) + pick(got, 1)
            line.mark(send)
            picks.append((pick, keep, got))
            self.got[half] = flip(send, bit, size)
            left.remove(bit)
        for half in range(2):
            pick, keep, got = picks[half]
            self.keep[half] = pick(line.tie(keep), 0) + pick(got, 0)
            line.mark(self.keep[half])
        self.step += 1

    def gather(self):
        size = 1 << self.bits
        if self.step == self.bits:
            self.held = [[0], [0]]
            self.step += 1
        else:
            for half in range(2):
                self.keep[half] = jnp.concatenate([self.line.tie(self.keep[half]), self.got[half]], 0)
                self.line.mark(self.keep[half])
                self.held[half] = self.held[half] + [block | self.last[half] for block in self.held[half]]
        self.last = [1 << self.orders[half].pop() for half in range(2)]
        self.got = [flip(self.keep[half], self.last[half].bit_length() - 1, size) for half in range(2)]

    def pieces(self):
        arrays, where = [], []
        for half in range(2):
            arrays += [self.keep[half], self.got[half]]
            found = {block: (2 * half, at) for at, block in enumerate(self.held[half])}
            found.update({block | self.last[half]: (2 * half + 1, at) for at, block in enumerate(self.held[half])})
            where.append(found)
        return arrays, where


class Ring:
    def __init__(self, line, first, rest, size):
        self.line, self.rest, self.size = line, rest, size
        self.step = 0
        self.got = self.send(first)

    def send(self, value):
        return lax.ppermute(value, "dp", [(d, (d + 2) % self.size) for d in range(self.size)])

    def advance(self):
        value = self.line.tie(self.rest)[self.step] + self.got
        self.line.mark(value)
        self.step += 1
        if self.step < self.size // 2 - 1:
            self.got = self.send(value)
        return value


def butterfly(value, bits):
    for bit in range(bits):
        value = value + flip(value, bit, 1 << bits)
    return value


def tree_sum(value):
    while value.shape[0] > 1:
        value = value.reshape((value.shape[0] // 2, 2) + value.shape[1:])
        value = value[:, 0] + value[:, 1]
    return value[0]


class Small:
    def __init__(self, own, bits):
        self.bits, self.bit, self.held = bits, 0, [own]
        self.got = None
        self.step()

    def step(self):
        if self.got is not None:
            many = len(self.held)
            self.held = self.held + [self.got[at] for at in range(many)]
        if self.bit < self.bits:
            self.got = flip(jnp.stack(self.held), self.bit, 1 << self.bits)
            self.bit += 1

    def pieces(self):
        while len(self.held) < 1 << self.bits:
            self.step()
        return self.held


def both_vectors(pieces):
    level = [piece[8:] for piece in pieces]
    while len(level) > 1:
        level = [level[at] + level[at + 1] for at in range(0, len(level), 2)]
    many = D // level[0].shape[1]
    return jnp.stack([level[0][:many].reshape(-1), level[0][4 : 4 + many].reshape(-1)])


def combine(pieces, block, blocks):
    level = [pieces[other][:8, (block ^ other) * SLOT : (block ^ other) * SLOT + SLOT] for other in range(blocks)]
    while len(level) > 1:
        level = [level[at] + level[at + 1] for at in range(0, len(level), 2)]
    return level[0]


def attention_scores(query, both_keys, length):
    scores = mul(query, both_keys, NT)
    row = lax.broadcasted_iota(jnp.int32, scores.shape, 0)
    place = lax.broadcasted_iota(jnp.int32, scores.shape, 1) % SLOT
    scores = jnp.where((place <= row) & (place < IMG + length), scores, masked_score)
    parts = []
    for at in range(2):
        part = scores[:, at * SLOT : (at + 1) * SLOT]
        expd = jnp.exp(part - jnp.max(part, axis=-1, keepdims=True))
        parts.append(expd / jnp.sum(expd, axis=-1, keepdims=True))
    return parts


def split_heads(value, mask):
    return jnp.concatenate([value * mask[0:1], value * mask[1:2]], axis=0)


def store_parts(refs, value, step, steps, only=None):
    left_keep, left_send, right_keep, right_send = refs
    left_keep[0] = value[:SLOT, :HALF]
    left_send[0] = value[SLOT:, :HALF]

    @pl.when(step < steps // 2)
    def _():
        right_keep[0] = value[:SLOT, HALF:]
        right_keep[1] = value[SLOT:, HALF:]

    @pl.when(step >= steps // 2)
    def _():
        right_send[0] = value[:SLOT, HALF:]
        right_send[1] = value[SLOT:, HALF:]


def part_outs(blocks):
    half = blocks // 2
    steps = blocks // 2
    shape = (half, SLOT, HALF)
    low = max(steps // 2, 1)
    return [
        (shape, F32, (1, SLOT, HALF), lambda s, *_: (s, 0, 0)),
        (shape, F32, (1, SLOT, HALF), lambda s, *_: (s, 0, 0)),
        (shape, F32, (2, SLOT, HALF), lambda s, *_: (jnp.minimum(s, low - 1), 0, 0)),
        (shape, F32, (2, SLOT, HALF), lambda s, *_: (jnp.maximum(s - steps // 2, 0), 0, 0)),
    ]


def front(order, lengths, tokens, gain, shift, weight, bias, tables, mask, mix_gain, uw_rows, out_weight, after=()):
    blocks = order.shape[0]
    steps = blocks // 2
    width = weight.shape[2]
    groups = width // 128
    rows = blocks * SLOT

    def kernel(order_ref, length_ref, x0, x1, g, b, w, wb, tab, msk, mg, uwr, ow, own, first, qkv, mixed, small, *parts_uw):
        step = pl.program_id(0)
        parts, uw = parts_uw[:4], parts_uw[4]

        @pl.when(step == 0)
        def _():
            found = mul(uwr[...], ow[...])
            uw[0:1] = found[0:1] + found[1:2] + found[2:3]
            uw[1:2] = found[3:4] + found[4:5] + found[5:6]
            small[8:] = jnp.zeros((8, rows), F32)
            for at in range(D // rows):
                c = slice(at * rows, at * rows + rows)
                small[8 + at : 9 + at] = uw[0:1, c]
                small[12 + at : 13 + at] = uw[1:2, c]

        x = jnp.concatenate([x0[0], x1[0]], axis=0)
        own[...] = x
        hat, _ = norm_parts(x.astype(F32))
        one = rounded(hat * g[...] + b[...])
        first[...] = one
        for c in range(3):
            proj = mul(one, w[c]) + wb[c : c + 1]
            for group in range(groups):
                part = proj[:, group * 128 : group * 128 + 128]
                if c < 2:
                    part = rotate(part, tab, 3 * c, 1)
                at = c * width + group * 128
                qkv[:, at : at + 128] = rounded(part)
        for pair in range(2):
            r = slice(pair * SLOT, pair * SLOT + SLOT)
            length = length_ref[order_ref[2 * step + pair]]
            for group in range(groups):
                at = group * 128
                query = qkv[r, at : at + 128]
                keys = split_heads(qkv[r, width + at : width + at + 128], msk)
                values = split_heads(qkv[r, 2 * width + at : 2 * width + at + 128], msk)
                probs = attention_scores(query, keys, length)
                mixed[r, at : at + 128] = mul(rounded(jnp.concatenate(probs, axis=1)), values)
        m = mixed[...]
        total = jnp.sum(m, axis=-1, keepdims=True)
        here = pl.ds(pl.multiple_of(step * 2 * SLOT, 2 * SLOT), 2 * SLOT)
        small[:8, here] = rows_of([total, jnp.sum(m * m, axis=-1, keepdims=True)])
        middle = total * (1.0 / width)
        partial = mul(rounded((m - middle) * mg[...]), ow[...]) + middle * uw[0:1]
        store_parts(parts, partial, step, steps)

    row2 = lambda s, *_: (s, 0)
    pair_of = lambda offset: lambda s, order_ref, length_ref: (order_ref[2 * s + offset], 0, 0)
    return run(
        kernel,
        (steps,),
        [
            (tokens, (1, SLOT, D), pair_of(0)),
            (tokens, (1, SLOT, D), pair_of(1)),
            whole(gain), whole(shift), whole(weight), whole(bias), whole(tables), whole(mask),
            whole(mix_gain), whole(uw_rows), whole(out_weight),
        ],
        [
            ((rows, D), BF16, (2 * SLOT, D), row2),
            ((rows, D), BF16, (2 * SLOT, D), row2),
            ((rows, 3 * width), BF16, (2 * SLOT, 3 * width), row2),
            ((rows, width), F32, (2 * SLOT, width), row2),
            ((16, rows), F32, (16, rows), lambda s, *_: (0, 0)),
        ]
        + part_outs(blocks),
        scratch=[pltpu.VMEM((8, D), F32)],
        prefetch=(order, lengths),
        after=after,
        name="front",
    )


def pieces_in(pieces):
    return [whole(piece) for piece in pieces[0]]


def load_pieces(refs, where, total, step, blocks):
    for block in range(blocks):

        @pl.when(step == block)
        def _(block=block):
            for half in range(2):
                array, at = where[half][block]
                total[:, half * HALF : half * HALF + HALF] = refs[array][at]


def middle_norm(own, pieces, sums, uw, out_bias, gain, shift, after=()):
    blocks = len(pieces[1][0])
    rows = blocks * SLOT

    def kernel(*refs):
        x, parts, stats = refs[0], refs[1:5], refs[5 : 5 + blocks]
        uw_ref, bias, g, b, mid, second, stat, total, tot8 = refs[5 + blocks :]
        step = pl.program_id(0)
        load_pieces(parts, pieces[1], total, step, blocks)
        for block in range(blocks):

            @pl.when(step == block)
            def _(block=block):
                tot8[...] = combine(stats, block, blocks)

        cols = columns_of(tot8[...])
        mean = cols[:, 0:1] * (1.0 / D)
        inverse = lax.rsqrt(cols[:, 1:2] * (1.0 / D) - mean * mean + eps)
        branch = inverse * (total[...] - mean * uw_ref[0:1]) + uw_ref[1:2]
        value = x[...].astype(F32) + branch + bias[...]
        mid[...] = value
        hat, _ = norm_parts(value)
        second[...] = rounded(hat * g[...] + b[...])
        lane = lax.broadcasted_iota(jnp.int32, (SLOT, 128), 1)
        stat[...] = jnp.where(lane == 0, mean, inverse)

    row = lambda k, *_: (k, 0)
    return run(
        kernel,
        (blocks,),
        [(own, (SLOT, D), row)]
        + pieces_in(pieces)
        + [whole(part) for part in sums]
        + [whole(uw), whole(out_bias), whole(gain), whole(shift)],
        [
            ((rows, D), F32, (SLOT, D), row),
            ((rows, D), BF16, (SLOT, D), row),
            ((rows, 128), F32, (SLOT, 128), row),
        ],
        scratch=[pltpu.VMEM((SLOT, D), F32), pltpu.VMEM((8, SLOT), F32)],
        after=after,
        name="middle_norm",
    )


def hidden_back(cots, down_weight):
    many, rows, units = len(cots), cots[0].shape[0], down_weight.shape[0]
    tile = min(512, units)

    def kernel(*refs):
        w, out = refs[many:]
        for at in range(many):
            out[at * rows : at * rows + rows] = rounded(mul(refs[at][...], w[...], NT))

    return run(
        kernel,
        (units // tile,),
        [whole(cot) for cot in cots] + [(down_weight, (tile, D), lambda j: (j, 0))],
        [((many * rows, units), BF16, (many * rows, tile), lambda j: (0, j))],
        name="hidden_back",
    )[0]


def hidden_front(chunk, second, up_weight, up_bias, back, gain, after=()):
    rows, units = second.shape[0], up_weight.shape[1]
    tile = 512
    steps = units // tile

    def part_of(c, s_ref, w, b, hb, g, act, slp):
        hidden = mul(s_ref[...], w[:, c]) + b[:, c]
        tail = jnp.exp(-0.5 * hidden * hidden)
        t = 1.0 / (1.0 + (0.3275911 * root_half) * jnp.abs(hidden))
        poly = 1.061405429 * t - 1.453152027
        poly = poly * t + 1.421413741
        poly = poly * t - 0.284496736
        poly = poly * t + 0.254829592
        half = 0.5 * poly * t * tail
        phi = jnp.where(hidden >= 0.0, 1.0 - half, half)
        active = hidden * phi
        act[:, c] = rounded(active)
        slp[:, c] = rounded(phi + hidden * (inv_root_two_pi * tail))
        scaled = hb[:, c].astype(F32) * g[:, c]
        return [value[:, :128] + value[:, 128:] for value in (active, active * active, scaled, scaled * active)]

    def kernel(s_ref, w, b, hb, g, act, slp, sums, acc):
        step = pl.program_id(0)
        found = [part_of(slice(at, at + 256), s_ref, w, b, hb, g, act, slp) for at in range(0, tile, 256)]

        @pl.when(step == 0)
        def _():
            for at in range(4):
                acc[at] = found[0][at] + found[1][at]

        @pl.when(step > 0)
        def _():
            for at in range(4):
                acc[at] += found[0][at] + found[1][at]

        @pl.when(step == steps - 1)
        def _():
            for block in range(rows // SLOT):
                r = slice(block * SLOT, block * SLOT + SLOT)
                sums[:, r] = rows_of([jnp.sum(acc[at, r], axis=-1, keepdims=True) for at in range(4)])

    return run(
        kernel,
        (steps,),
        [
            whole(second),
            (up_weight, (D, tile), lambda j: (0, j)),
            (up_bias, (1, tile), lambda j: (0, j)),
            (back, (rows, tile), lambda j: (chunk, j)),
            (gain, (1, tile), lambda j: (0, j)),
        ],
        [
            ((rows, units), BF16, (rows, tile), lambda j: (0, j)),
            ((rows, units), BF16, (rows, tile), lambda j: (0, j)),
            ((8, rows), F32, (8, rows), lambda j: (0, 0)),
        ],
        scratch=[pltpu.VMEM((4, rows, 128), F32)],
        after=after,
        name="hidden_front",
    )


def hidden_mid(chunk, active, slope, back, sums, gain, shift):
    blocks = len(sums)
    rows, units = active.shape

    def kernel(act, slp, hb, *refs):
        stats = refs[:blocks]
        g, b, low, grad, vecs, tot8 = refs[blocks:]
        step = pl.program_id(0)
        for block in range(blocks):

            @pl.when(step == block)
            def _(block=block):
                tot8[...] = combine(stats, block, blocks)

        cols = columns_of(tot8[...]) * (1.0 / FF)
        mean = cols[:, 0:1]
        inverse = lax.rsqrt(cols[:, 1:2] - mean * mean + eps)
        one = cols[:, 2:3]
        two = inverse * (cols[:, 3:4] - mean * one)
        for at in range(0, units, 256):
            c = slice(at, at + 256)
            hat = (act[:, c].astype(F32) - mean) * inverse
            low[:, c] = rounded(hat * g[:, c] + b[:, c])
            raw = hb[:, c].astype(F32)
            grown = rounded(inverse * (raw * g[:, c] - one - hat * two) * slp[:, c].astype(F32))
            grad[:, c] = grown
            vecs[0, 0:1, c] = sum_rows(raw * hat)
            vecs[0, 1:2, c] = sum_rows(raw)
            vecs[0, 2:3, c] = sum_rows(grown.astype(F32))

    row = lambda k: (k, 0)
    return run(
        kernel,
        (blocks,),
        [
            (active, (SLOT, units), row),
            (slope, (SLOT, units), row),
            (back, (SLOT, units), lambda k: (chunk * blocks + k, 0)),
        ]
        + [whole(part) for part in sums]
        + [whole(gain), whole(shift)],
        [
            ((rows, units), BF16, (SLOT, units), row),
            ((rows, units), BF16, (SLOT, units), row),
            ((blocks, 8, units), F32, (1, 8, units), lambda k: (k, 0, 0)),
        ],
        scratch=[pltpu.VMEM((8, SLOT), F32)],
        name="hidden_mid",
    )


def hidden_grad(grad, up_weight):
    rows, units = grad.shape
    blocks = rows // SLOT
    tile = 512
    steps = D // tile
    half = steps // 2

    def kernel(gr, w, left_keep, left_send, right_keep, right_send):
        step = pl.program_id(0)
        value = mul(gr[...], w[...], NT)

        @pl.when(step < half)
        def _():
            for block in range(blocks):
                r = slice(block * SLOT, block * SLOT + SLOT)
                (left_send if block & 1 else left_keep)[block // 2] = value[r]

        @pl.when(step >= half)
        def _():
            for block in range(blocks):
                r = slice(block * SLOT, block * SLOT + SLOT)
                (right_send if block >= blocks // 2 else right_keep)[block % (blocks // 2)] = value[r]

    shape = (blocks // 2, SLOT, HALF)
    block_shape = (blocks // 2, SLOT, tile)
    lefts = lambda j: (0, 0, jnp.minimum(j, half - 1))
    rights = lambda j: (0, 0, jnp.maximum(j - half, 0))
    return run(
        kernel,
        (steps,),
        [whole(grad), (up_weight, (tile, units), lambda j: (j, 0))],
        [
            (shape, F32, block_shape, lefts),
            (shape, F32, block_shape, lefts),
            (shape, F32, block_shape, rights),
            (shape, F32, block_shape, rights),
        ],
        name="hidden_grad",
    )


def result_part(order, lows, down_weight):
    pairs = order.shape[0]
    units = down_weight.shape[0]
    many = len(lows)
    rows = lows[0].shape[0]
    each = rows // SLOT
    tile = 256

    def kernel(order_ref, *refs):
        w, out = refs[many:]
        for at in range(many):
            value = mul(refs[at][...], w[...])
            for block in range(each):
                out[order_ref[at * each + block]] = value[block * SLOT : block * SLOT + SLOT]

    return run(
        kernel,
        (D // tile,),
        [whole(low) for low in lows] + [(down_weight, (units, tile), lambda j, *_: (0, j))],
        [((pairs, SLOT, D), F32, (pairs, SLOT, tile), lambda j, *_: (0, 0, j))],
        prefetch=(order,),
        name="result_part",
    )[0]


def middle_back(own, cot, pieces, middle, stat, uw, out_bias, gain, after=()):
    blocks = len(pieces[1][0])
    rows = blocks * SLOT

    def kernel(*refs):
        x, c, parts = refs[0], refs[1], refs[2:6]
        mid, st, uw_ref, bias, g, grad, low, stat2, vecs, total = refs[6:]
        load_pieces(parts, pieces[1], total, pl.program_id(0), blocks)
        value = mid[...]
        hat, inverse = norm_parts(value)
        sec = total[...]
        scaled = sec * g[...]
        up = c[...].astype(F32)
        out = up + inverse * (
            scaled
            - jnp.mean(scaled, axis=-1, keepdims=True)
            - hat * jnp.mean(scaled * hat, axis=-1, keepdims=True)
        )
        grad[...] = out
        lowered = rounded(out)
        low[...] = lowered
        low32 = lowered.astype(F32)
        one = jnp.mean(low32 * uw_ref[0:1], axis=-1, keepdims=True)
        moved = value - x[...].astype(F32) - bias[...] - uw_ref[1:2]
        two = jnp.mean(low32 * moved, axis=-1, keepdims=True)
        lane = lax.broadcasted_iota(jnp.int32, (SLOT, 128), 1)
        stat2[...] = jnp.where(lane == 2, one, jnp.where(lane == 3, two, st[...]))
        vecs[0, 0:1] = sum_rows(sec * hat)
        vecs[0, 1:2] = sum_rows(sec)
        vecs[0, 2:3] = sum_rows(out)
        vecs[0, 3:4] = sum_rows(up)

    row = lambda k, *_: (k, 0)
    return run(
        kernel,
        (blocks,),
        [(own, (SLOT, D), row), (cot, (SLOT, D), row)]
        + pieces_in(pieces)
        + [(middle, (SLOT, D), row), (stat, (SLOT, 128), row), whole(uw), whole(out_bias), whole(gain)],
        [
            ((rows, D), F32, (SLOT, D), row),
            ((rows, D), BF16, (SLOT, D), row),
            ((rows, 128), F32, (SLOT, 128), row),
            ((blocks, 8, D), F32, (1, 8, D), lambda k, *_: (k, 0, 0)),
        ],
        scratch=[pltpu.VMEM((SLOT, D), F32)],
        after=after,
        name="middle_back",
    )


def attention_back(order, lengths, low, stat, mixed, qkv, own, mix_gain, mix_shift, out_weight, weight, tables, mask, after=()):
    blocks = order.shape[0]
    steps = blocks // 2
    width = out_weight.shape[0]
    groups = width // 128
    rows = blocks * SLOT

    def kernel(
        order_ref, length_ref, low_ref, st, mx, qkv_ref, x, mg, ms, ow, w, tab, msk,
        mix_low, dproj, vecs, wide, left_keep, left_send, right_keep, right_send, dmixed,
    ):
        step = pl.program_id(0)
        mean, inverse, one, two = (st[:, at : at + 1] for at in range(4))
        back = mul(low_ref[...], ow[...], NT)
        hat = (mx[...] - mean) * inverse
        mix_low[...] = rounded(hat * mg[...] + ms[...])
        dmixed[...] = rounded(inverse * (back * mg[...] - one - hat * two))
        vecs[0, 0:1, :width] = sum_rows(back * hat)
        vecs[0, 1:2, :width] = sum_rows(back)
        first_half = lax.broadcasted_iota(jnp.int32, (SLOT, 128), 1) < HD
        for pair in range(2):
            r = slice(pair * SLOT, pair * SLOT + SLOT)
            length = length_ref[order_ref[2 * step + pair]]
            for group in range(groups):
                at = group * 128
                query = qkv_ref[r, at : at + 128]
                keys = split_heads(qkv_ref[r, width + at : width + at + 128], msk)
                values = split_heads(qkv_ref[r, 2 * width + at : 2 * width + at + 128], msk)
                grad = dmixed[r, at : at + 128]
                probs = attention_scores(query, keys, length)
                dprobs = mul(grad, values, NT)
                dscores = []
                for i in range(2):
                    dp = dprobs[:, i * SLOT : (i + 1) * SLOT]
                    carried = jnp.sum(probs[i] * dp, axis=-1, keepdims=True)
                    dscores.append(rounded(probs[i] * (dp - carried)))
                dscores = jnp.concatenate(dscores, axis=1)
                dquery = mul(dscores, keys)
                dkey = mul(dscores, query, TN)
                dvalue = mul(rounded(jnp.concatenate(probs, axis=1)), grad, TN)
                dkey = jnp.where(first_half, dkey[:SLOT], dkey[SLOT:])
                dvalue = jnp.where(first_half, dvalue[:SLOT], dvalue[SLOT:])
                tabs = [tab[i, :SLOT] for i in range(6)]
                dproj[r, at : at + 128] = rounded(rotate(dquery, tabs, 0, -1))
                dproj[r, width + at : width + at + 128] = rounded(rotate(dkey, tabs, 3, -1))
                dproj[r, 2 * width + at : 2 * width + at + 128] = rounded(dvalue)
        vecs[0, 2:3] = sum_rows(dproj[...].astype(F32))
        partial = mul(dproj[:, :width], w[0], NT)
        for c in (1, 2):
            partial += mul(dproj[:, c * width : (c + 1) * width], w[c], NT)
        pre_hat, _ = norm_parts(x[...].astype(F32))
        grown = partial * pre_hat
        wide[0, 0:1] = sum_rows(grown[:SLOT]) + sum_rows(grown[SLOT:])
        wide[0, 1:2] = sum_rows(partial[:SLOT]) + sum_rows(partial[SLOT:])
        store_parts((left_keep, left_send, right_keep, right_send), partial, step, steps)

    row2 = lambda s, *_: (s, 0)
    return run(
        kernel,
        (steps,),
        [
            (low, (2 * SLOT, D), row2),
            (stat, (2 * SLOT, 128), row2),
            (mixed, (2 * SLOT, width), row2),
            (qkv, (2 * SLOT, 3 * width), row2),
            (own, (2 * SLOT, D), row2),
            whole(mix_gain), whole(mix_shift), whole(out_weight), whole(weight), whole(tables), whole(mask),
        ],
        [
            ((rows, width), BF16, (2 * SLOT, width), row2),
            ((rows, 3 * width), BF16, (2 * SLOT, 3 * width), row2),
            ((steps, 8, 3 * width), F32, (1, 8, 3 * width), lambda s, *_: (s, 0, 0)),
            ((steps, 8, D), F32, (1, 8, D), lambda s, *_: (s, 0, 0)),
        ]
        + part_outs(blocks),
        scratch=[pltpu.VMEM((2 * SLOT, width), BF16)],
        prefetch=(order, lengths),
        after=after,
        name="attention_back",
    )


def tokens_back(order, own, grad, pieces, gain, before, pairs, after=()):
    blocks = len(pieces[1][0])

    def kernel(order_ref, x, gr, *refs):
        parts = refs[:4]
        g = refs[4]
        out, total = refs[-2:]
        load_pieces(parts, pieces[1], total, pl.program_id(0), blocks)
        hat, inverse = norm_parts(x[...].astype(F32))
        scaled = total[...] * g[...]
        out[0] = gr[...] + inverse * (
            scaled
            - jnp.mean(scaled, axis=-1, keepdims=True)
            - hat * jnp.mean(scaled * hat, axis=-1, keepdims=True)
        )

    row = lambda k, *_: (k, 0)
    ins = [(own, (SLOT, D), row), (grad, (SLOT, D), row)] + pieces_in(pieces) + [whole(gain)]
    alias = None
    if before is not None:
        alias = {1 + len(ins): 0}
        ins = ins + [(before, None, None)]
    return run(
        kernel,
        (blocks,),
        ins,
        [((pairs, SLOT, D), F32, (1, SLOT, D), lambda k, o: (o[k], 0, 0))],
        scratch=[pltpu.VMEM((SLOT, D), F32)],
        prefetch=(order,),
        after=after,
        alias=alias,
        name="tokens_back",
    )[0]


def output_of(order, middle, result, bias, before, after=()):
    blocks = order.shape[0]

    def kernel(order_ref, mid, res, b, *refs):
        out = refs[-1]
        out[0] = rounded(mid[...] + res[0] + b[...])

    ins = [
        (middle, (SLOT, D), lambda k, *_: (k, 0)),
        (result, (1, SLOT, D), lambda k, o: (o[k], 0, 0)),
        whole(bias),
    ]
    alias = None
    if before is not None:
        alias = {1 + len(ins): 0}
        ins = ins + [(before, None, None)]
    return run(
        kernel,
        (blocks,),
        ins,
        [(result.shape, BF16, (1, SLOT, D), lambda k, o: (o[k], 0, 0))],
        prefetch=(order,),
        after=after,
        alias=alias,
        name="output",
    )[0]


def ring_grads(ids, products, got=None):
    count, many = ids.shape[0], len(products[0][0])
    rows = products[0][0][0].shape[0]
    widths = [rights[0].shape[1] for lefts, rights in products]
    block = D // (2 * count)
    shape = (block, sum(widths))

    def kernel(ids_ref, *refs):
        outs = refs[2 * many * len(products) + (got is not None) :]
        step = pl.program_id(0)
        start = 0
        for at, width in enumerate(widths):
            left, right = (refs[(2 * at + side) * many : (2 * at + side + 1) * many] for side in range(2))
            value = mul(left[0][...], right[0][...], TN)
            for k in range(1, many):
                value += mul(left[k][...], right[k][...], TN)
            c = slice(start, start + width)
            start += width
            if got is None:
                outs[0][0, :, c] = value
                continue
            value += refs[2 * many * len(products)][0, :, c]

            @pl.when(step == 0)
            def _(value=value, c=c):
                outs[0][:, c] = value

            @pl.when(step > 0)
            def _(value=value, c=c):
                outs[1][0, :, c] = value

    fixed = lambda i, *_: (0, 0)
    moving = lambda i, ids_ref: (0, ids_ref[i])
    lead = lambda i, *_: (i, 0, 0)
    ins = []
    for lefts, rights in products:
        ins += [(left, (rows, block), moving) for left in lefts]
        ins += [(right, right.shape, fixed) for right in rights]
    if got is None:
        outs = [((count,) + shape, F32, (1,) + shape, lead)]
    else:
        ins += [(got, (1,) + shape, lead)]
        outs = [
            (shape, F32, shape, fixed),
            ((count - 1,) + shape, F32, (1,) + shape, lambda i, *_: (jnp.maximum(i - 1, 0), 0, 0)),
        ]
    return run(kernel, (count,), ins, outs, prefetch=(ids,), name="ring_grads")


def full_grad(products):
    many, block = len(products[0][0]), 512
    rows, tall = products[0][0][0].shape
    widths = [rights[0].shape[1] for lefts, rights in products]

    def kernel(*refs):
        out, start = refs[-1], 0
        for at, width in enumerate(widths):
            left, right = (refs[(2 * at + side) * many : (2 * at + side + 1) * many] for side in range(2))
            value = mul(left[0][...], right[0][...], TN)
            for k in range(1, many):
                value += mul(left[k][...], right[k][...], TN)
            out[:, start : start + width] = value
            start += width

    ins = []
    for lefts, rights in products:
        ins += [(left, (rows, block), lambda i: (0, i)) for left in lefts]
        ins += [(right, right.shape, lambda i: (0, 0)) for right in rights]
    wide = sum(widths)
    return run(
        kernel, (tall // block,), ins, [((tall, wide), F32, (block, wide), lambda i: (i, 0))], name="full_grad"
    )[0]


def steps_of(totals, bits, done, until):
    done = list(done)

    def step(at):
        if done[at] < bits:
            totals[at].advance()
        else:
            totals[at].gather()
        done[at] += 1
        if done[at] == bits and until == 2 * bits:
            totals[at].gather()
            done[at] += 1

    limits = [until] + [until if until == 2 * bits else bits - 1] * (len(totals) - 1)
    while any(have < limit for have, limit in zip(done, limits)):
        for at in range(len(totals)):
            if done[at] < limits[at]:
                step(at)


def attention_outputs(part, width):
    rows = part.shape[0]

    def kernel(p, qkv, out):
        for c in range(3):
            qkv[c] = p[:, c * width : (c + 1) * width]
        out[...] = jnp.transpose(p[:, 3 * width :])

    return run(
        kernel,
        (1,),
        [whole(part)],
        [
            ((3, rows, width), F32, (3, rows, width), lambda i: (0, 0, 0)),
            ((width, rows), F32, (width, rows), lambda i: (0, 0)),
        ],
        name="attention_outputs",
    )


def split_rows(value):
    found = []
    for _ in range(3):
        part = lax.reduce_precision(value, 8, 7)
        found.append(part.astype(BF16))
        value = value - part
    return found


def body(
    tokens,
    lengths,
    cotangent,
    pre_gain,
    pre_shift,
    qkv_weight,
    qkv_bias,
    mix_gain,
    mix_shift,
    out_weight,
    out_bias,
    ffn_gain,
    ffn_shift,
    up_weight,
    up_bias,
    hid_gain,
    hid_shift,
    down_weight,
    down_bias,
):
    pairs = lengths.shape[0]
    blocks = lax.axis_size("tensor")
    bits = blocks.bit_length() - 1
    chunks = pairs // blocks
    width = qkv_weight.shape[2]
    mine = lax.axis_index("tensor").astype(jnp.int32)
    orders = [jnp.arange(c * blocks, (c + 1) * blocks, dtype=jnp.int32) ^ mine for c in range(chunks)]
    tokens3 = tokens.reshape(pairs, SLOT, D)
    row = lambda v: v.reshape(1, -1)
    pre_gain, pre_shift, mix_gain, mix_shift = map(row, (pre_gain, pre_shift, mix_gain, mix_shift))
    out_bias, ffn_gain, ffn_shift, up_bias = map(row, (out_bias, ffn_gain, ffn_shift, up_bias))
    hid_gain, hid_shift, down_bias = map(row, (hid_gain, hid_shift, down_bias))
    tables = xpos_tables()
    lane = np.arange(128)[None, :] < HD
    mask = jnp.asarray(np.concatenate([lane, ~lane], 0).astype(np.float32)).astype(BF16)
    zero = jnp.zeros((2, width), BF16)
    uw_rows = jnp.concatenate(split_rows(mix_gain) + split_rows(mix_shift) + [zero], 0)

    line = Line()
    dp_size = lax.axis_size("dp")
    place = lax.axis_index("dp").astype(jnp.int32)
    count = dp_size // 2
    around = lax.rem(place // 2 + count - 1 - jnp.arange(count, dtype=jnp.int32), count)
    mine_ids, other_ids = 2 * around + lax.rem(place, 2), 2 * around + 1 - lax.rem(place, 2)

    def tied(products):
        (lefts, rights), others = products[0], products[1:]
        return [([line.tie(lefts[0])] + lefts[1:], rights)] + others

    def full(products):
        grad = full_grad(tied(products))
        line.mark(grad)
        return grad

    every = lambda items, name: [item[name] for item in items]

    ones, twos, threes = [], [], []
    for c in range(chunks):
        found = front(
            orders[c], lengths, line.tie(tokens3), pre_gain, pre_shift, qkv_weight, qkv_bias, tables, mask, mix_gain, uw_rows,
            out_weight,
        )
        own, first, qkv, mixed, small = found[:5]
        one = dict(own=own, first=first, qkv=qkv, mixed=mixed, parts=found[5:])
        line.mark(small)
        one["small"] = small
        if c == 0:
            one["total"] = Total(line, one["parts"], bits)
            one["sums"] = Small(small, bits)
        ones.append(one)
    sums0 = ones[0]["sums"]
    if bits > 1:
        ones[0]["total"].advance()
    for c in range(1, chunks):
        ones[c]["total"] = Total(line, [line.tie(part) for part in ones[c]["parts"]], bits)
    sums0.held[0] = line.tie(sums0.held[0])
    sums0.step()
    cot3 = cotangent.reshape(pairs, SLOT, D)
    cots = []
    for c in range(chunks):
        cots.append(line.tie(cot3)[orders[c]].reshape(-1, D))
        line.mark(cots[-1])
    totals = every(ones, "total")
    line.mark(*line.last, *sums0.pieces())
    for step in range(1, bits):
        totals[0].advance()
    back = hidden_back([line.tie(cots[0])] + cots[1:], down_weight)
    line.mark(back)
    for one in ones[1:]:
        one["sums"] = Small(line.tie(one["small"]), bits)
    done = [bits] + [0] * (chunks - 1)
    steps_of(totals, bits, done, 2 * bits - 1)
    for one in ones[1:]:
        line.mark(*line.last, one["sums"].got)
        one["sums"].step()
    uw_total = both_vectors(sums0.pieces())

    def mid_of(c):
        two = twos[c]
        low, grad, vecs = hidden_mid(c, line.tie(two["active"]), two["slope"], back, two["sums"], hid_gain, hid_shift)
        two.update(low=low, grad=grad, vecs=functools.reduce(jnp.add, [vecs[k] for k in range(blocks)]))
        line.mark(vecs)

    def hidden_of(c):
        parts = hidden_grad(line.tie(twos[c]["grad"]), up_weight)
        line.mark(parts[0])
        return parts

    totals[0].gather()
    for other in ones[1:]:
        line.mark(*line.last, *other["sums"].pieces())
    for c in range(chunks):
        one = ones[c]
        mid, second, stat = middle_norm(
            line.tie(one["own"]), totals[c].pieces(), one["sums"].pieces(), uw_total, out_bias, ffn_gain, ffn_shift
        )
        line.mark(stat)
        if c == 0:
            for total in totals[1:]:
                total.advance()
                total.gather()
        active, slope, sums = hidden_front(c, line.tie(second), up_weight, up_bias, back, hid_gain)
        line.mark(sums)
        twos.append(dict(middle=mid, second=second, stat=stat, active=active, slope=slope, sums=all_pieces(sums, bits)))
        if c == 0:
            for total in totals[1:]:
                for step in range(1, bits):
                    total.gather()
            line.mark(*line.last, *twos[0]["sums"][1:])
        else:
            twos[0]["total"].advance()
            line.mark(*line.last, *twos[c]["sums"][1:])
        mid_of(c)
        if c > 0:
            line.mark(*line.last, *twos[0]["total"].got)
        if c == 0 and chunks > 1:
            twos[0]["total"] = Total(line, hidden_of(0), bits)
    lows = every(twos, "low")
    down_grad = full([(lows, cots)])
    down_part = lax.psum_scatter(down_grad, "dp", scatter_dimension=1, tiled=True)
    up_products = [(every(twos, "second"), every(twos, "grad"))]
    sent = ring_grads(other_ids, tied(up_products))[0]
    line.mark(sent)
    sent = lax.ppermute(sent, "dp", [(d, d ^ 1) for d in range(dp_size)])
    if chunks > 1:
        for step in range(1, bits):
            twos[0]["total"].advance()
        twos[0]["total"].gather()
        parts = [None] + [hidden_of(c) for c in range(1, chunks)]
    else:
        twos[0]["total"] = Total(line, hidden_of(0), bits)
        for step in range(bits):
            twos[0]["total"].advance()
        twos[0]["total"].gather()
    ring_first, ring_rest = ring_grads(mine_ids, tied(up_products), sent)
    line.mark(ring_rest)
    ring = Ring(line, ring_first, ring_rest, dp_size)
    for step in range(1, bits):
        twos[0]["total"].gather()
    for c in range(1, chunks):
        twos[c]["total"] = Total(line, [line.tie(part) for part in parts[c]], bits)
    totals = every(twos, "total")
    result = result_part(jnp.concatenate(orders), [line.tie(lows[0])] + lows[1:], down_weight)
    line.mark(result)

    for c in range(chunks):
        one, two = ones[c], twos[c]
        grad, low, stat2, vecs = middle_back(
            line.tie(one["own"]), cots[c], two["total"].pieces(), two["middle"], two["stat"], uw_total, out_bias, ffn_gain
        )
        line.mark(stat2)
        if c == 0:
            for total in totals[1:]:
                total.advance()
        found = attention_back(
            orders[c], lengths, line.tie(low), stat2, one["mixed"], one["qkv"], one["own"], mix_gain, mix_shift, out_weight,
            qkv_weight, tables, mask,
        )
        line.mark(found[2])
        three = dict(grad=grad, low=low, vecs=tree_sum(vecs), mix_low=found[0], dproj=found[1])
        three["narrow"] = tree_sum(found[2])
        three["wide"] = tree_sum(found[3])
        parts = found[4:]
        if c == 0 and chunks > 1:
            for total in totals[1:]:
                for step in range(1, bits):
                    total.advance()
                for step in range(bits):
                    total.gather()
            for total in totals[1:]:
                line.mark(*line.last, *total.got)
            up_part = ring.advance()
            result = lax.psum(line.tie(result), "tensor")
            parts = [line.tie(part) for part in parts]
        three["total"] = Total(line, parts, bits)
        threes.append(three)

    first, last = threes[0]["total"], threes[-1]["total"]
    add = lambda items, name, size: functools.reduce(jnp.add, [item[name] for item in items])[:size]
    pad = lambda v: jnp.pad(v, ((0, 0), (0, D - v.shape[1])))
    wide = add(threes, "wide", 2)
    got = flip(wide, 0, blocks)
    if chunks > 1:
        line.mark(*line.last, *first.got)
    attention_grad = full(
        [(every(ones, "first"), every(threes, "dproj")), (every(threes, "low"), every(threes, "mix_low"))]
    )
    if chunks == 1:
        up_part = ring.advance()
        result = lax.psum(line.tie(result), "tensor")
    attention_part = lax.psum_scatter(attention_grad, "dp", scatter_dimension=0, tiled=True)
    for step in range(bits):
        first.advance()
    first.gather()
    if chunks > 1:
        last.advance()
    for step in range(1, bits):
        first.gather()
    line.mark(*line.last, down_part)
    up_part = ring.advance()
    if chunks > 1:
        for step in range(1, bits):
            last.advance()
        last.gather()
    for bit in range(1, bits):
        wide = line.tie(wide) + got
        got = flip(wide, bit, blocks)
        line.mark(wide)
    if chunks > 1:
        line.mark(*line.last, *last.got)
    hop = lambda v, bit: lax.ppermute(v, "dp", [(d, d ^ (1 << bit)) for d in range(dp_size)])
    dp_bits = dp_size.bit_length() - 1
    tokens_grad, output = None, None
    for c in range(chunks):
        tokens_grad = tokens_back(
            orders[c], line.tie(ones[c]["own"]), threes[c]["grad"], threes[c]["total"].pieces(), pre_gain, tokens_grad, pairs
        )
        line.mark(tokens_grad)
        if c == 0:
            wide = line.tie(wide) + got
            vecs = jnp.concatenate(
                [pad(add(twos, "vecs", 3)), add(threes, "vecs", 4), pad(add(threes, "narrow", 3)), wide], 0
            )
            line.mark(vecs)
            got = hop(vecs, 0)
            for step in range(2, count - 1):
                up_part = ring.advance()
            if chunks > 1:
                for step in range(1, bits):
                    last.gather()
            vecs = line.tie(vecs) + got
            line.mark(vecs)
            got = hop(vecs, 1)
    for bit in range(2, dp_bits):
        vecs = line.tie(vecs) + got
        line.mark(vecs)
        got = hop(vecs, bit)
    for c in range(chunks):
        output = output_of(orders[c], line.tie(twos[c]["middle"]), result, down_bias, output)
        line.mark(output)
    vecs = vecs + got
    hid_vecs, mid_vecs, narrow, wide = vecs[:3], vecs[3:7], vecs[7:10], vecs[10:12]
    qkv_part, out_part = attention_outputs(attention_part, width)
    units = hid_gain.shape[1]
    return (
        output.reshape(-1, D),
        tokens_grad.reshape(-1, D),
        wide[0],
        wide[1],
        qkv_part,
        narrow[2, : 3 * width].reshape(3, width),
        narrow[0, :width],
        narrow[1, :width],
        out_part,
        mid_vecs[2],
        mid_vecs[0],
        mid_vecs[1],
        up_part,
        hid_vecs[2, :units],
        hid_vecs[0, :units],
        hid_vecs[1, :units],
        down_part,
        mid_vecs[3],
    )


def solution(mesh):
    in_specs = (
        P("dp", None),
        P("dp"),
        P("dp", None),
        P(),
        P(),
        P(None, None, "tensor"),
        P(None, "tensor"),
        P("tensor"),
        P("tensor"),
        P("tensor", None),
        P(),
        P(),
        P(),
        P(None, "tensor"),
        P("tensor"),
        P("tensor"),
        P("tensor"),
        P("tensor", None),
        P(),
    )
    out_specs = (
        P("dp", None),
        P("dp", None),
        P(),
        P(),
        P(None, "dp", "tensor"),
        P(None, "tensor"),
        P("tensor"),
        P("tensor"),
        P("tensor", "dp"),
        P(),
        P(),
        P(),
        P("dp", "tensor"),
        P("tensor"),
        P("tensor"),
        P("tensor"),
        P("tensor", "dp"),
        P(),
    )
    return jax.shard_map(body, mesh=mesh, in_specs=in_specs, out_specs=out_specs, check_vma=False)
```

```python
import functools
import math

import jax
import jax.numpy as jnp
import numpy as np
from jax import lax
from jax.experimental import pallas as pl
from jax.experimental.pallas import tpu as pltpu
from jax.sharding import PartitionSpec as P

D = 2048
HD = 64
FF = 8192
SLOT = 128
IMG = 64
SCALE_BASE = 512
HALF = D // 2

eps = 1e-05
root_half = 0.7071067811865476
inv_root_two_pi = 0.3989422804014327
masked_score = -1e30
MEGA = 1 << 20

COST = {
    "front": 15.6,
    "middle_norm": 400.0,
    "hidden_back": 400.0,
    "hidden_front": 14.7,
    "hidden_mid": 400.0,
    "hidden_low": 400.0,
    "hidden_grad": 7.0,
    "full_grad": 15.0,
    "ring_grads": 12.0,
    "result_part": 400.0,
    "middle_back": 11.0,
    "attention_back": 21.7,
    "tokens_back": 8.5,
    "output": 6.0,
    "attention_outputs": 2.0,
}
WORK = 5.5e+07

F32 = jnp.float32
BF16 = jnp.bfloat16
NN = (((1,), (0,)), ((), ()))
NT = (((1,), (1,)), ((), ()))
TN = (((0,), (0,)), ((), ()))


def rounded(value):
    return value.astype(BF16)


def mul(left, right, dims=NN):
    return lax.dot_general(left, right, dims, preferred_element_type=F32)


def xpos_tables():
    place = np.arange(SLOT, dtype=np.float64)[:, None]
    lane = np.arange(128)[None, :]
    index = (lane % HD) // 2
    angle = place * 10000.0 ** (-2.0 * index / HD)
    zeta = (2.0 * index + 0.4 * HD) / (1.4 * HD)
    growth = zeta ** ((place - SLOT // 2) / SCALE_BASE)
    even = lane % 2 == 0
    found = []
    for factor in (growth / math.sqrt(HD), 1.0 / growth):
        found += [
            np.cos(angle) * factor,
            np.where(even, -np.sin(angle), 0.0) * factor,
            np.where(even, 0.0, np.sin(angle)) * factor,
        ]
    return jnp.asarray(np.tile(np.stack(found), (1, 2, 1)).astype(np.float32))


def rotate(value, tables, base, sign):
    up = pltpu.roll(value, 127, axis=1)
    down = pltpu.roll(value, 1, axis=1)
    turned = up * tables[base + 1] + down * tables[base + 2]
    return value * tables[base] + turned if sign > 0 else value * tables[base] - turned


def columns_of(parts):
    return jnp.transpose(parts)


def rows_of(columns):
    size = columns[0].shape[0]
    lane = lax.broadcasted_iota(jnp.int32, (size, 128), 1)
    tile = jnp.zeros((size, 128), F32)
    for at, column in enumerate(columns):
        tile = jnp.where(lane == at, column, tile)
    return jnp.transpose(tile)[:8]


def norm_parts(value):
    mean = jnp.mean(value, axis=-1, keepdims=True)
    var = jnp.mean(value * value, axis=-1, keepdims=True) - mean * mean
    inverse = lax.rsqrt(var + eps)
    return (value - mean) * inverse, inverse


def sum_rows(value):
    return jnp.sum(value, axis=0, keepdims=True)


def whole(array, **kw):
    rank = array.ndim
    return (array, array.shape, lambda *at: (0,) * rank)


def run(kernel, grid, ins, outs, scratch=(), prefetch=(), after=(), alias=None, limit=56, name=None):
    prefetch = tuple(prefetch)

    def body(*refs):
        refs = list(refs)
        first = len(prefetch) + len(ins)
        del refs[first : first + len(after)]
        kernel(*refs)

    in_specs = []
    for array, block, where in ins:
        if block is None:
            in_specs.append(pl.BlockSpec(memory_space=pl.ANY))
        elif tuple(block) == tuple(array.shape):
            in_specs.append(pl.BlockSpec(block, where, pipeline_mode=pl.Buffered(1)))
        else:
            in_specs.append(pl.BlockSpec(block, where))
    in_specs += [pl.BlockSpec(memory_space=pl.ANY)] * len(after)
    out_specs = [pl.BlockSpec(block, where) for shape, dtype, block, where in outs]
    out_shape = [jax.ShapeDtypeStruct(shape, dtype) for shape, dtype, block, where in outs]
    return pl.pallas_call(
        body,
        grid_spec=pltpu.PrefetchScalarGridSpec(
            num_scalar_prefetch=len(prefetch),
            grid=grid,
            in_specs=in_specs,
            out_specs=out_specs,
            scratch_shapes=list(scratch),
        ),
        out_shape=out_shape,
        input_output_aliases=alias or {},
        compiler_params=pltpu.CompilerParams(
            dimension_semantics=("arbitrary",) * len(grid), vmem_limit_bytes=limit * MEGA
        ),
        cost_estimate=pl.CostEstimate(flops=int(COST[name] * WORK), bytes_accessed=1000, transcendentals=0),
        name=name,
    )(*prefetch, *[array for array, block, where in ins], *after)


def flip(value, bit, size):
    return lax.ppermute(value, "tensor", [(t, t ^ (1 << bit)) for t in range(size)])


def all_pieces(own, bits):
    size = 1 << bits
    return [own] + [lax.ppermute(own, "tensor", [(t, t ^ k) for t in range(size)]) for k in range(1, size)]


class Line:
    def __init__(self):
        self.last = None

    def tie(self, value):
        if self.last is None:
            return value
        return lax.optimization_barrier((value,) + self.last)[0]

    def mark(self, *values):
        self.last = values


class Total:
    def __init__(self, line, parts, bits):
        self.line, self.bits = line, bits
        self.orders = [list(range(bits)), list(range(bits))[::-1]]
        self.left = [[bit for bit in range(bits) if bit != order[0]] for order in self.orders]
        self.keep = [parts[0], parts[2]]
        self.got = [flip(parts[1], self.orders[0][0], 1 << bits), flip(parts[3], self.orders[1][0], 1 << bits)]
        self.step = 1

    def advance(self):
        line, size = self.line, 1 << self.bits
        if self.step == self.bits:
            for half in range(2):
                self.keep[half] = line.tie(self.keep[half]) + self.got[half]
                line.mark(self.keep[half])
            return
        picks = []
        for half in range(2):
            left, bit = self.left[half], self.orders[half][self.step]
            keep, got = self.keep[half], self.got[half]
            cube = (2,) * len(left) + keep.shape[1:]
            axis = len(left) - 1 - left.index(bit)
            shape = (keep.shape[0] // 2,) + keep.shape[1:]
            pick = lambda value, at, cube=cube, axis=axis, shape=shape: lax.index_in_dim(
                value.reshape(cube), at, axis, keepdims=False
            ).reshape(shape)
            send = pick(line.tie(keep), 1) + pick(got, 1)
            line.mark(send)
            picks.append((pick, keep, got))
            self.got[half] = flip(send, bit, size)
            left.remove(bit)
        for half in range(2):
            pick, keep, got = picks[half]
            self.keep[half] = pick(line.tie(keep), 0) + pick(got, 0)
            line.mark(self.keep[half])
        self.step += 1

    def gather(self):
        size = 1 << self.bits
        if self.step == self.bits:
            self.held = [[0], [0]]
            self.step += 1
        else:
            for half in range(2):
                self.keep[half] = jnp.concatenate([self.line.tie(self.keep[half]), self.got[half]], 0)
                self.line.mark(self.keep[half])
                self.held[half] = self.held[half] + [block | self.last[half] for block in self.held[half]]
        self.last = [1 << self.orders[half].pop() for half in range(2)]
        self.got = [flip(self.keep[half], self.last[half].bit_length() - 1, size) for half in range(2)]

    def pieces(self):
        arrays, where = [], []
        for half in range(2):
            arrays += [self.keep[half], self.got[half]]
            found = {block: (2 * half, at) for at, block in enumerate(self.held[half])}
            found.update({block | self.last[half]: (2 * half + 1, at) for at, block in enumerate(self.held[half])})
            where.append(found)
        return arrays, where


class Ring:
    def __init__(self, line, first, rest, size):
        self.line, self.rest, self.size = line, rest, size
        self.step = 0
        self.got = self.send(first)

    def send(self, value):
        return lax.ppermute(value, "dp", [(d, (d + 2) % self.size) for d in range(self.size)])

    def advance(self):
        value = self.line.tie(self.rest)[self.step] + self.got
        self.line.mark(value)
        self.step += 1
        if self.step < self.size // 2 - 1:
            self.got = self.send(value)
        return value


def butterfly(value, bits):
    for bit in range(bits):
        value = value + flip(value, bit, 1 << bits)
    return value


def tree_sum(value):
    while value.shape[0] > 1:
        value = value.reshape((value.shape[0] // 2, 2) + value.shape[1:])
        value = value[:, 0] + value[:, 1]
    return value[0]


class Small:
    def __init__(self, own, bits):
        self.bits, self.bit, self.held = bits, 0, [own]
        self.got = None
        self.step()

    def step(self):
        if self.got is not None:
            many = len(self.held)
            self.held = self.held + [self.got[at] for at in range(many)]
        if self.bit < self.bits:
            self.got = flip(jnp.stack(self.held), self.bit, 1 << self.bits)
            self.bit += 1

    def pieces(self):
        while len(self.held) < 1 << self.bits:
            self.step()
        return self.held


def both_vectors(pieces):
    level = [piece[8:] for piece in pieces]
    while len(level) > 1:
        level = [level[at] + level[at + 1] for at in range(0, len(level), 2)]
    many = D // level[0].shape[1]
    return jnp.stack([level[0][:many].reshape(-1), level[0][4 : 4 + many].reshape(-1)])


def combine(pieces, block, blocks):
    level = [pieces[other][:8, (block ^ other) * SLOT : (block ^ other) * SLOT + SLOT] for other in range(blocks)]
    while len(level) > 1:
        level = [level[at] + level[at + 1] for at in range(0, len(level), 2)]
    return level[0]


def attention_scores(query, both_keys, length):
    scores = mul(query, both_keys, NT)
    row = lax.broadcasted_iota(jnp.int32, scores.shape, 0)
    place = lax.broadcasted_iota(jnp.int32, scores.shape, 1) % SLOT
    scores = jnp.where((place <= row) & (place < IMG + length), scores, masked_score)
    parts = []
    for at in range(2):
        part = scores[:, at * SLOT : (at + 1) * SLOT]
        expd = jnp.exp(part - jnp.max(part, axis=-1, keepdims=True))
        parts.append(expd / jnp.sum(expd, axis=-1, keepdims=True))
    return parts


def split_heads(value, mask):
    return jnp.concatenate([value * mask[0:1], value * mask[1:2]], axis=0)


def store_parts(refs, value, step, steps, only=None):
    left_keep, left_send, right_keep, right_send = refs
    left_keep[0] = value[:SLOT, :HALF]
    left_send[0] = value[SLOT:, :HALF]

    @pl.when(step < steps // 2)
    def _():
        right_keep[0] = value[:SLOT, HALF:]
        right_keep[1] = value[SLOT:, HALF:]

    @pl.when(step >= steps // 2)
    def _():
        right_send[0] = value[:SLOT, HALF:]
        right_send[1] = value[SLOT:, HALF:]


def part_outs(blocks):
    half = blocks // 2
    steps = blocks // 2
    shape = (half, SLOT, HALF)
    low = max(steps // 2, 1)
    return [
        (shape, F32, (1, SLOT, HALF), lambda s, *_: (s, 0, 0)),
        (shape, F32, (1, SLOT, HALF), lambda s, *_: (s, 0, 0)),
        (shape, F32, (2, SLOT, HALF), lambda s, *_: (jnp.minimum(s, low - 1), 0, 0)),
        (shape, F32, (2, SLOT, HALF), lambda s, *_: (jnp.maximum(s - steps // 2, 0), 0, 0)),
    ]


def front(order, lengths, tokens, gain, shift, weight, bias, tables, mask, mix_gain, uw_rows, out_weight, after=()):
    blocks = order.shape[0]
    steps = blocks // 2
    width = weight.shape[2]
    groups = width // 128
    rows = blocks * SLOT

    def kernel(order_ref, length_ref, x0, x1, g, b, w, wb, tab, msk, mg, uwr, ow, own, first, qkv, mixed, small, *parts_uw):
        step = pl.program_id(0)
        parts, uw = parts_uw[:4], parts_uw[4]

        @pl.when(step == 0)
        def _():
            found = mul(uwr[...], ow[...])
            uw[0:1] = found[0:1] + found[1:2] + found[2:3]
            uw[1:2] = found[3:4] + found[4:5] + found[5:6]
            small[8:] = jnp.zeros((8, rows), F32)
            for at in range(D // rows):
                c = slice(at * rows, at * rows + rows)
                small[8 + at : 9 + at] = uw[0:1, c]
                small[12 + at : 13 + at] = uw[1:2, c]

        x = jnp.concatenate([x0[0], x1[0]], axis=0)
        own[...] = x
        hat, _ = norm_parts(x.astype(F32))
        one = rounded(hat * g[...] + b[...])
        first[...] = one
        for c in range(3):
            proj = mul(one, w[c]) + wb[c : c + 1]
            for group in range(groups):
                part = proj[:, group * 128 : group * 128 + 128]
                if c < 2:
                    part = rotate(part, tab, 3 * c, 1)
                at = c * width + group * 128
                qkv[:, at : at + 128] = rounded(part)
        for pair in range(2):
            r = slice(pair * SLOT, pair * SLOT + SLOT)
            length = length_ref[order_ref[2 * step + pair]]
            for group in range(groups):
                at = group * 128
                query = qkv[r, at : at + 128]
                keys = split_heads(qkv[r, width + at : width + at + 128], msk)
                values = split_heads(qkv[r, 2 * width + at : 2 * width + at + 128], msk)
                probs = attention_scores(query, keys, length)
                mixed[r, at : at + 128] = mul(rounded(jnp.concatenate(probs, axis=1)), values)
        m = mixed[...]
        total = jnp.sum(m, axis=-1, keepdims=True)
        here = pl.ds(pl.multiple_of(step * 2 * SLOT, 2 * SLOT), 2 * SLOT)
        small[:8, here] = rows_of([total, jnp.sum(m * m, axis=-1, keepdims=True)])
        middle = total * (1.0 / width)
        partial = mul(rounded((m - middle) * mg[...]), ow[...]) + middle * uw[0:1]
        store_parts(parts, partial, step, steps)

    row2 = lambda s, *_: (s, 0)
    pair_of = lambda offset: lambda s, order_ref, length_ref: (order_ref[2 * s + offset], 0, 0)
    return run(
        kernel,
        (steps,),
        [
            (tokens, (1, SLOT, D), pair_of(0)),
            (tokens, (1, SLOT, D), pair_of(1)),
            whole(gain), whole(shift), whole(weight), whole(bias), whole(tables), whole(mask),
            whole(mix_gain), whole(uw_rows), whole(out_weight),
        ],
        [
            ((rows, D), BF16, (2 * SLOT, D), row2),
            ((rows, D), BF16, (2 * SLOT, D), row2),
            ((rows, 3 * width), BF16, (2 * SLOT, 3 * width), row2),
            ((rows, width), F32, (2 * SLOT, width), row2),
            ((16, rows), F32, (16, rows), lambda s, *_: (0, 0)),
        ]
        + part_outs(blocks),
        scratch=[pltpu.VMEM((8, D), F32)],
        prefetch=(order, lengths),
        after=after,
        name="front",
    )


def pieces_in(pieces):
    return [whole(piece) for piece in pieces[0]]


def load_pieces(refs, where, total, step, blocks):
    for block in range(blocks):

        @pl.when(step == block)
        def _(block=block):
            for half in range(2):
                array, at = where[half][block]
                total[:, half * HALF : half * HALF + HALF] = refs[array][at]


def middle_norm(own, pieces, sums, uw, out_bias, gain, shift, after=()):
    blocks = len(pieces[1][0])
    rows = blocks * SLOT

    def kernel(*refs):
        x, parts, stats = refs[0], refs[1:5], refs[5 : 5 + blocks]
        uw_ref, bias, g, b, mid, second, stat, total, tot8 = refs[5 + blocks :]
        step = pl.program_id(0)
        load_pieces(parts, pieces[1], total, step, blocks)
        for block in range(blocks):

            @pl.when(step == block)
            def _(block=block):
                tot8[...] = combine(stats, block, blocks)

        cols = columns_of(tot8[...])
        mean = cols[:, 0:1] * (1.0 / D)
        inverse = lax.rsqrt(cols[:, 1:2] * (1.0 / D) - mean * mean + eps)
        branch = inverse * (total[...] - mean * uw_ref[0:1]) + uw_ref[1:2]
        value = x[...].astype(F32) + branch + bias[...]
        mid[...] = value
        hat, _ = norm_parts(value)
        second[...] = rounded(hat * g[...] + b[...])
        lane = lax.broadcasted_iota(jnp.int32, (SLOT, 128), 1)
        stat[...] = jnp.where(lane == 0, mean, inverse)

    row = lambda k, *_: (k, 0)
    return run(
        kernel,
        (blocks,),
        [(own, (SLOT, D), row)]
        + pieces_in(pieces)
        + [whole(part) for part in sums]
        + [whole(uw), whole(out_bias), whole(gain), whole(shift)],
        [
            ((rows, D), F32, (SLOT, D), row),
            ((rows, D), BF16, (SLOT, D), row),
            ((rows, 128), F32, (SLOT, 128), row),
        ],
        scratch=[pltpu.VMEM((SLOT, D), F32), pltpu.VMEM((8, SLOT), F32)],
        after=after,
        name="middle_norm",
    )


def hidden_back(cots, down_weight):
    many, rows, units = len(cots), cots[0].shape[0], down_weight.shape[0]
    tile = min(512, units)

    def kernel(*refs):
        w, out = refs[many:]
        for at in range(many):
            out[at * rows : at * rows + rows] = rounded(mul(refs[at][...], w[...], NT))

    return run(
        kernel,
        (units // tile,),
        [whole(cot) for cot in cots] + [(down_weight, (tile, D), lambda j: (j, 0))],
        [((many * rows, units), BF16, (many * rows, tile), lambda j: (0, j))],
        name="hidden_back",
    )[0]


def hidden_front(chunk, second, up_weight, up_bias, back, gain, after=()):
    rows, units = second.shape[0], up_weight.shape[1]
    tile = 512
    steps = units // tile

    def part_of(c, s_ref, w, b, hb, g, act, slp):
        hidden = mul(s_ref[...], w[:, c]) + b[:, c]
        tail = jnp.exp(-0.5 * hidden * hidden)
        t = 1.0 / (1.0 + (0.3275911 * root_half) * jnp.abs(hidden))
        poly = 1.061405429 * t - 1.453152027
        poly = poly * t + 1.421413741
        poly = poly * t - 0.284496736
        poly = poly * t + 0.254829592
        half = 0.5 * poly * t * tail
        phi = jnp.where(hidden >= 0.0, 1.0 - half, half)
        active = hidden * phi
        act[:, c] = rounded(active)
        slp[:, c] = rounded(phi + hidden * (inv_root_two_pi * tail))
        scaled = hb[:, c].astype(F32) * g[:, c]
        return [value[:, :128] + value[:, 128:] for value in (active, active * active, scaled, scaled * active)]

    def kernel(s_ref, w, b, hb, g, act, slp, sums, acc):
        step = pl.program_id(0)
        found = [part_of(slice(at, at + 256), s_ref, w, b, hb, g, act, slp) for at in range(0, tile, 256)]

        @pl.when(step == 0)
        def _():
            for at in range(4):
                acc[at] = found[0][at] + found[1][at]

        @pl.when(step > 0)
        def _():
            for at in range(4):
                acc[at] += found[0][at] + found[1][at]

        @pl.when(step == steps - 1)
        def _():
            for block in range(rows // SLOT):
                r = slice(block * SLOT, block * SLOT + SLOT)
                sums[:, r] = rows_of([jnp.sum(acc[at, r], axis=-1, keepdims=True) for at in range(4)])

    return run(
        kernel,
        (steps,),
        [
            whole(second),
            (up_weight, (D, tile), lambda j: (0, j)),
            (up_bias, (1, tile), lambda j: (0, j)),
            (back, (rows, tile), lambda j: (chunk, j)),
            (gain, (1, tile), lambda j: (0, j)),
        ],
        [
            ((rows, units), BF16, (rows, tile), lambda j: (0, j)),
            ((rows, units), BF16, (rows, tile), lambda j: (0, j)),
            ((8, rows), F32, (8, rows), lambda j: (0, 0)),
        ],
        scratch=[pltpu.VMEM((4, rows, 128), F32)],
        after=after,
        name="hidden_front",
    )


def hidden_low(active, sums, gain, shift):
    blocks = len(sums)
    rows, units = active.shape

    def kernel(act, *refs):
        stats = refs[:blocks]
        g, b, low, tot8 = refs[blocks:]
        step = pl.program_id(0)
        for block in range(blocks):

            @pl.when(step == block)
            def _(block=block):
                tot8[...] = combine(stats, block, blocks)

        cols = columns_of(tot8[...]) * (1.0 / FF)
        mean = cols[:, 0:1]
        inverse = lax.rsqrt(cols[:, 1:2] - mean * mean + eps)
        for at in range(0, units, 256):
            c = slice(at, at + 256)
            hat = (act[:, c].astype(F32) - mean) * inverse
            low[:, c] = rounded(hat * g[:, c] + b[:, c])

    row = lambda k: (k, 0)
    return run(
        kernel,
        (blocks,),
        [(active, (SLOT, units), row)] + [whole(part) for part in sums] + [whole(gain), whole(shift)],
        [((rows, units), BF16, (SLOT, units), row)],
        scratch=[pltpu.VMEM((8, SLOT), F32)],
        name="hidden_low",
    )[0]


def hidden_mid(chunk, active, slope, back, sums, gain, shift):
    blocks = len(sums)
    rows, units = active.shape

    def kernel(act, slp, hb, *refs):
        stats = refs[:blocks]
        g, b, low, grad, vecs, tot8 = refs[blocks:]
        step = pl.program_id(0)
        for block in range(blocks):

            @pl.when(step == block)
            def _(block=block):
                tot8[...] = combine(stats, block, blocks)

        cols = columns_of(tot8[...]) * (1.0 / FF)
        mean = cols[:, 0:1]
        inverse = lax.rsqrt(cols[:, 1:2] - mean * mean + eps)
        one = cols[:, 2:3]
        two = inverse * (cols[:, 3:4] - mean * one)
        for at in range(0, units, 256):
            c = slice(at, at + 256)
            hat = (act[:, c].astype(F32) - mean) * inverse
            low[:, c] = rounded(hat * g[:, c] + b[:, c])
            raw = hb[:, c].astype(F32)
            grown = rounded(inverse * (raw * g[:, c] - one - hat * two) * slp[:, c].astype(F32))
            grad[:, c] = grown
            vecs[0, 0:1, c] = sum_rows(raw * hat)
            vecs[0, 1:2, c] = sum_rows(raw)
            vecs[0, 2:3, c] = sum_rows(grown.astype(F32))

    row = lambda k: (k, 0)
    return run(
        kernel,
        (blocks,),
        [
            (active, (SLOT, units), row),
            (slope, (SLOT, units), row),
            (back, (SLOT, units), lambda k: (chunk * blocks + k, 0)),
        ]
        + [whole(part) for part in sums]
        + [whole(gain), whole(shift)],
        [
            ((rows, units), BF16, (SLOT, units), row),
            ((rows, units), BF16, (SLOT, units), row),
            ((blocks, 8, units), F32, (1, 8, units), lambda k: (k, 0, 0)),
        ],
        scratch=[pltpu.VMEM((8, SLOT), F32)],
        name="hidden_mid",
    )


def hidden_grad(grad, up_weight):
    rows, units = grad.shape
    blocks = rows // SLOT
    tile = 512
    steps = D // tile
    half = steps // 2

    def kernel(gr, w, left_keep, left_send, right_keep, right_send):
        step = pl.program_id(0)
        value = mul(gr[...], w[...], NT)

        @pl.when(step < half)
        def _():
            for block in range(blocks):
                r = slice(block * SLOT, block * SLOT + SLOT)
                (left_send if block & 1 else left_keep)[block // 2] = value[r]

        @pl.when(step >= half)
        def _():
            for block in range(blocks):
                r = slice(block * SLOT, block * SLOT + SLOT)
                (right_send if block >= blocks // 2 else right_keep)[block % (blocks // 2)] = value[r]

    shape = (blocks // 2, SLOT, HALF)
    block_shape = (blocks // 2, SLOT, tile)
    lefts = lambda j: (0, 0, jnp.minimum(j, half - 1))
    rights = lambda j: (0, 0, jnp.maximum(j - half, 0))
    return run(
        kernel,
        (steps,),
        [whole(grad), (up_weight, (tile, units), lambda j: (j, 0))],
        [
            (shape, F32, block_shape, lefts),
            (shape, F32, block_shape, lefts),
            (shape, F32, block_shape, rights),
            (shape, F32, block_shape, rights),
        ],
        name="hidden_grad",
    )


def result_part(order, lows, down_weight):
    pairs = order.shape[0]
    units = down_weight.shape[0]
    many = len(lows)
    rows = lows[0].shape[0]
    each = rows // SLOT
    tile = 256

    def kernel(order_ref, *refs):
        w, out = refs[many:]
        for at in range(many):
            value = mul(refs[at][...], w[...])
            for block in range(each):
                out[order_ref[at * each + block]] = value[block * SLOT : block * SLOT + SLOT]

    return run(
        kernel,
        (D // tile,),
        [whole(low) for low in lows] + [(down_weight, (units, tile), lambda j, *_: (0, j))],
        [((pairs, SLOT, D), F32, (pairs, SLOT, tile), lambda j, *_: (0, 0, j))],
        prefetch=(order,),
        name="result_part",
    )[0]


def middle_back(own, cot, pieces, middle, stat, uw, out_bias, gain, after=()):
    blocks = len(pieces[1][0])
    rows = blocks * SLOT

    def kernel(*refs):
        x, c, parts = refs[0], refs[1], refs[2:6]
        mid, st, uw_ref, bias, g, grad, low, stat2, vecs, total = refs[6:]
        load_pieces(parts, pieces[1], total, pl.program_id(0), blocks)
        value = mid[...]
        hat, inverse = norm_parts(value)
        sec = total[...]
        scaled = sec * g[...]
        up = c[...].astype(F32)
        out = up + inverse * (
            scaled
            - jnp.mean(scaled, axis=-1, keepdims=True)
            - hat * jnp.mean(scaled * hat, axis=-1, keepdims=True)
        )
        grad[...] = out
        lowered = rounded(out)
        low[...] = lowered
        low32 = lowered.astype(F32)
        one = jnp.mean(low32 * uw_ref[0:1], axis=-1, keepdims=True)
        moved = value - x[...].astype(F32) - bias[...] - uw_ref[1:2]
        two = jnp.mean(low32 * moved, axis=-1, keepdims=True)
        lane = lax.broadcasted_iota(jnp.int32, (SLOT, 128), 1)
        stat2[...] = jnp.where(lane == 2, one, jnp.where(lane == 3, two, st[...]))
        vecs[0, 0:1] = sum_rows(sec * hat)
        vecs[0, 1:2] = sum_rows(sec)
        vecs[0, 2:3] = sum_rows(out)
        vecs[0, 3:4] = sum_rows(up)

    row = lambda k, *_: (k, 0)
    return run(
        kernel,
        (blocks,),
        [(own, (SLOT, D), row), (cot, (SLOT, D), row)]
        + pieces_in(pieces)
        + [(middle, (SLOT, D), row), (stat, (SLOT, 128), row), whole(uw), whole(out_bias), whole(gain)],
        [
            ((rows, D), F32, (SLOT, D), row),
            ((rows, D), BF16, (SLOT, D), row),
            ((rows, 128), F32, (SLOT, 128), row),
            ((blocks, 8, D), F32, (1, 8, D), lambda k, *_: (k, 0, 0)),
        ],
        scratch=[pltpu.VMEM((SLOT, D), F32)],
        after=after,
        name="middle_back",
    )


def attention_back(order, lengths, low, stat, mixed, qkv, own, mix_gain, mix_shift, out_weight, weight, tables, mask, after=()):
    blocks = order.shape[0]
    steps = blocks // 2
    width = out_weight.shape[0]
    groups = width // 128
    rows = blocks * SLOT

    def kernel(
        order_ref, length_ref, low_ref, st, mx, qkv_ref, x, mg, ms, ow, w, tab, msk,
        mix_low, dproj, vecs, wide, left_keep, left_send, right_keep, right_send, dmixed,
    ):
        step = pl.program_id(0)
        mean, inverse, one, two = (st[:, at : at + 1] for at in range(4))
        back = mul(low_ref[...], ow[...], NT)
        hat = (mx[...] - mean) * inverse
        mix_low[...] = rounded(hat * mg[...] + ms[...])
        dmixed[...] = rounded(inverse * (back * mg[...] - one - hat * two))
        vecs[0, 0:1, :width] = sum_rows(back * hat)
        vecs[0, 1:2, :width] = sum_rows(back)
        first_half = lax.broadcasted_iota(jnp.int32, (SLOT, 128), 1) < HD
        for pair in range(2):
            r = slice(pair * SLOT, pair * SLOT + SLOT)
            length = length_ref[order_ref[2 * step + pair]]
            for group in range(groups):
                at = group * 128
                query = qkv_ref[r, at : at + 128]
                keys = split_heads(qkv_ref[r, width + at : width + at + 128], msk)
                values = split_heads(qkv_ref[r, 2 * width + at : 2 * width + at + 128], msk)
                grad = dmixed[r, at : at + 128]
                probs = attention_scores(query, keys, length)
                dprobs = mul(grad, values, NT)
                dscores = []
                for i in range(2):
                    dp = dprobs[:, i * SLOT : (i + 1) * SLOT]
                    carried = jnp.sum(probs[i] * dp, axis=-1, keepdims=True)
                    dscores.append(rounded(probs[i] * (dp - carried)))
                dscores = jnp.concatenate(dscores, axis=1)
                dquery = mul(dscores, keys)
                dkey = mul(dscores, query, TN)
                dvalue = mul(rounded(jnp.concatenate(probs, axis=1)), grad, TN)
                dkey = jnp.where(first_half, dkey[:SLOT], dkey[SLOT:])
                dvalue = jnp.where(first_half, dvalue[:SLOT], dvalue[SLOT:])
                tabs = [tab[i, :SLOT] for i in range(6)]
                dproj[r, at : at + 128] = rounded(rotate(dquery, tabs, 0, -1))
                dproj[r, width + at : width + at + 128] = rounded(rotate(dkey, tabs, 3, -1))
                dproj[r, 2 * width + at : 2 * width + at + 128] = rounded(dvalue)
        vecs[0, 2:3] = sum_rows(dproj[...].astype(F32))
        partial = mul(dproj[:, :width], w[0], NT)
        for c in (1, 2):
            partial += mul(dproj[:, c * width : (c + 1) * width], w[c], NT)
        pre_hat, _ = norm_parts(x[...].astype(F32))
        grown = partial * pre_hat
        wide[0, 0:1] = sum_rows(grown[:SLOT]) + sum_rows(grown[SLOT:])
        wide[0, 1:2] = sum_rows(partial[:SLOT]) + sum_rows(partial[SLOT:])
        store_parts((left_keep, left_send, right_keep, right_send), partial, step, steps)

    row2 = lambda s, *_: (s, 0)
    return run(
        kernel,
        (steps,),
        [
            (low, (2 * SLOT, D), row2),
            (stat, (2 * SLOT, 128), row2),
            (mixed, (2 * SLOT, width), row2),
            (qkv, (2 * SLOT, 3 * width), row2),
            (own, (2 * SLOT, D), row2),
            whole(mix_gain), whole(mix_shift), whole(out_weight), whole(weight), whole(tables), whole(mask),
        ],
        [
            ((rows, width), BF16, (2 * SLOT, width), row2),
            ((rows, 3 * width), BF16, (2 * SLOT, 3 * width), row2),
            ((steps, 8, 3 * width), F32, (1, 8, 3 * width), lambda s, *_: (s, 0, 0)),
            ((steps, 8, D), F32, (1, 8, D), lambda s, *_: (s, 0, 0)),
        ]
        + part_outs(blocks),
        scratch=[pltpu.VMEM((2 * SLOT, width), BF16)],
        prefetch=(order, lengths),
        after=after,
        name="attention_back",
    )


def tokens_back(order, own, grad, pieces, gain, before, pairs, after=()):
    blocks = len(pieces[1][0])

    def kernel(order_ref, x, gr, *refs):
        parts = refs[:4]
        g = refs[4]
        out, total = refs[-2:]
        load_pieces(parts, pieces[1], total, pl.program_id(0), blocks)
        hat, inverse = norm_parts(x[...].astype(F32))
        scaled = total[...] * g[...]
        out[0] = gr[...] + inverse * (
            scaled
            - jnp.mean(scaled, axis=-1, keepdims=True)
            - hat * jnp.mean(scaled * hat, axis=-1, keepdims=True)
        )

    row = lambda k, *_: (k, 0)
    ins = [(own, (SLOT, D), row), (grad, (SLOT, D), row)] + pieces_in(pieces) + [whole(gain)]
    alias = None
    if before is not None:
        alias = {1 + len(ins): 0}
        ins = ins + [(before, None, None)]
    return run(
        kernel,
        (blocks,),
        ins,
        [((pairs, SLOT, D), F32, (1, SLOT, D), lambda k, o: (o[k], 0, 0))],
        scratch=[pltpu.VMEM((SLOT, D), F32)],
        prefetch=(order,),
        after=after,
        alias=alias,
        name="tokens_back",
    )[0]


def output_of(order, middle, result, bias, before, after=()):
    blocks = order.shape[0]

    def kernel(order_ref, mid, res, b, *refs):
        out = refs[-1]
        out[0] = rounded(mid[...] + res[0] + b[...])

    ins = [
        (middle, (SLOT, D), lambda k, *_: (k, 0)),
        (result, (1, SLOT, D), lambda k, o: (o[k], 0, 0)),
        whole(bias),
    ]
    alias = None
    if before is not None:
        alias = {1 + len(ins): 0}
        ins = ins + [(before, None, None)]
    return run(
        kernel,
        (blocks,),
        ins,
        [(result.shape, BF16, (1, SLOT, D), lambda k, o: (o[k], 0, 0))],
        prefetch=(order,),
        after=after,
        alias=alias,
        name="output",
    )[0]


def ring_grads(ids, products, got=None):
    count, many = ids.shape[0], len(products[0][0])
    rows = products[0][0][0].shape[0]
    widths = [rights[0].shape[1] for lefts, rights in products]
    block = D // (2 * count)
    shape = (block, sum(widths))

    def kernel(ids_ref, *refs):
        outs = refs[2 * many * len(products) + (got is not None) :]
        step = pl.program_id(0)
        start = 0
        for at, width in enumerate(widths):
            left, right = (refs[(2 * at + side) * many : (2 * at + side + 1) * many] for side in range(2))
            value = mul(left[0][...], right[0][...], TN)
            for k in range(1, many):
                value += mul(left[k][...], right[k][...], TN)
            c = slice(start, start + width)
            start += width
            if got is None:
                outs[0][0, :, c] = value
                continue
            value += refs[2 * many * len(products)][0, :, c]

            @pl.when(step == 0)
            def _(value=value, c=c):
                outs[0][:, c] = value

            @pl.when(step > 0)
            def _(value=value, c=c):
                outs[1][0, :, c] = value

    fixed = lambda i, *_: (0, 0)
    moving = lambda i, ids_ref: (0, ids_ref[i])
    lead = lambda i, *_: (i, 0, 0)
    ins = []
    for lefts, rights in products:
        ins += [(left, (rows, block), moving) for left in lefts]
        ins += [(right, right.shape, fixed) for right in rights]
    if got is None:
        outs = [((count,) + shape, F32, (1,) + shape, lead)]
    else:
        ins += [(got, (1,) + shape, lead)]
        outs = [
            (shape, F32, shape, fixed),
            ((count - 1,) + shape, F32, (1,) + shape, lambda i, *_: (jnp.maximum(i - 1, 0), 0, 0)),
        ]
    return run(kernel, (count,), ins, outs, prefetch=(ids,), name="ring_grads")


def full_grad(products):
    many, block = len(products[0][0]), 512
    rows, tall = products[0][0][0].shape
    widths = [rights[0].shape[1] for lefts, rights in products]

    def kernel(*refs):
        out, start = refs[-1], 0
        for at, width in enumerate(widths):
            left, right = (refs[(2 * at + side) * many : (2 * at + side + 1) * many] for side in range(2))
            value = mul(left[0][...], right[0][...], TN)
            for k in range(1, many):
                value += mul(left[k][...], right[k][...], TN)
            out[:, start : start + width] = value
            start += width

    ins = []
    for lefts, rights in products:
        ins += [(left, (rows, block), lambda i: (0, i)) for left in lefts]
        ins += [(right, right.shape, lambda i: (0, 0)) for right in rights]
    wide = sum(widths)
    return run(
        kernel, (tall // block,), ins, [((tall, wide), F32, (block, wide), lambda i: (i, 0))], name="full_grad"
    )[0]


def steps_of(totals, bits, done, until):
    done = list(done)

    def step(at):
        if done[at] < bits:
            totals[at].advance()
        else:
            totals[at].gather()
        done[at] += 1
        if done[at] == bits and until == 2 * bits:
            totals[at].gather()
            done[at] += 1

    limits = [until] + [until if until == 2 * bits else bits - 1] * (len(totals) - 1)
    while any(have < limit for have, limit in zip(done, limits)):
        for at in range(len(totals)):
            if done[at] < limits[at]:
                step(at)


def attention_outputs(part, width):
    rows = part.shape[0]

    def kernel(p, qkv, out):
        for c in range(3):
            qkv[c] = p[:, c * width : (c + 1) * width]
        out[...] = jnp.transpose(p[:, 3 * width :])

    return run(
        kernel,
        (1,),
        [whole(part)],
        [
            ((3, rows, width), F32, (3, rows, width), lambda i: (0, 0, 0)),
            ((width, rows), F32, (width, rows), lambda i: (0, 0)),
        ],
        name="attention_outputs",
    )


def split_rows(value):
    found = []
    for _ in range(3):
        part = lax.reduce_precision(value, 8, 7)
        found.append(part.astype(BF16))
        value = value - part
    return found


def body(
    tokens,
    lengths,
    cotangent,
    pre_gain,
    pre_shift,
    qkv_weight,
    qkv_bias,
    mix_gain,
    mix_shift,
    out_weight,
    out_bias,
    ffn_gain,
    ffn_shift,
    up_weight,
    up_bias,
    hid_gain,
    hid_shift,
    down_weight,
    down_bias,
):
    pairs = lengths.shape[0]
    blocks = lax.axis_size("tensor")
    bits = blocks.bit_length() - 1
    chunks = pairs // blocks
    width = qkv_weight.shape[2]
    mine = lax.axis_index("tensor").astype(jnp.int32)
    orders = [jnp.arange(c * blocks, (c + 1) * blocks, dtype=jnp.int32) ^ mine for c in range(chunks)]
    tokens3 = tokens.reshape(pairs, SLOT, D)
    row = lambda v: v.reshape(1, -1)
    pre_gain, pre_shift, mix_gain, mix_shift = map(row, (pre_gain, pre_shift, mix_gain, mix_shift))
    out_bias, ffn_gain, ffn_shift, up_bias = map(row, (out_bias, ffn_gain, ffn_shift, up_bias))
    hid_gain, hid_shift, down_bias = map(row, (hid_gain, hid_shift, down_bias))
    tables = xpos_tables()
    lane = np.arange(128)[None, :] < HD
    mask = jnp.asarray(np.concatenate([lane, ~lane], 0).astype(np.float32)).astype(BF16)
    zero = jnp.zeros((2, width), BF16)
    uw_rows = jnp.concatenate(split_rows(mix_gain) + split_rows(mix_shift) + [zero], 0)

    line = Line()
    dp_size = lax.axis_size("dp")
    place = lax.axis_index("dp").astype(jnp.int32)
    count = dp_size // 2
    around = lax.rem(place // 2 + count - 1 - jnp.arange(count, dtype=jnp.int32), count)
    mine_ids, other_ids = 2 * around + lax.rem(place, 2), 2 * around + 1 - lax.rem(place, 2)

    def tied(products):
        (lefts, rights), others = products[0], products[1:]
        return [([line.tie(lefts[0])] + lefts[1:], rights)] + others

    def full(products):
        grad = full_grad(tied(products))
        line.mark(grad)
        return grad

    every = lambda items, name: [item[name] for item in items]

    ones, twos, threes = [], [], []
    for c in range(chunks):
        found = front(
            orders[c], lengths, line.tie(tokens3), pre_gain, pre_shift, qkv_weight, qkv_bias, tables, mask, mix_gain, uw_rows,
            out_weight,
        )
        own, first, qkv, mixed, small = found[:5]
        one = dict(own=own, first=first, qkv=qkv, mixed=mixed, parts=found[5:])
        line.mark(small)
        one["small"] = small
        if c == 0:
            one["total"] = Total(line, one["parts"], bits)
            one["sums"] = Small(small, bits)
        ones.append(one)
    sums0 = ones[0]["sums"]
    if bits > 1:
        ones[0]["total"].advance()
    for c in range(1, chunks):
        ones[c]["total"] = Total(line, [line.tie(part) for part in ones[c]["parts"]], bits)
    sums0.held[0] = line.tie(sums0.held[0])
    sums0.step()
    cot3 = cotangent.reshape(pairs, SLOT, D)
    cots = []
    for c in range(chunks):
        cots.append(line.tie(cot3)[orders[c]].reshape(-1, D))
        line.mark(cots[-1])
    totals = every(ones, "total")
    line.mark(*line.last, *sums0.pieces())
    for step in range(1, bits):
        totals[0].advance()
    back = hidden_back([line.tie(cots[0])] + cots[1:], down_weight)
    line.mark(back)
    for one in ones[1:]:
        one["sums"] = Small(line.tie(one["small"]), bits)
    done = [bits] + [0] * (chunks - 1)
    steps_of(totals, bits, done, 2 * bits - 1)
    for one in ones[1:]:
        line.mark(*line.last, one["sums"].got)
        one["sums"].step()
    uw_total = both_vectors(sums0.pieces())

    def mid_of(c):
        two = twos[c]
        low, grad, vecs = hidden_mid(c, line.tie(two["active"]), two["slope"], back, two["sums"], hid_gain, hid_shift)
        two.update(low=low, grad=grad, vecs=functools.reduce(jnp.add, [vecs[k] for k in range(blocks)]))
        line.mark(vecs)

    def hidden_of(c):
        parts = hidden_grad(line.tie(twos[c]["grad"]), up_weight)
        line.mark(parts[0])
        return parts

    totals[0].gather()
    for other in ones[1:]:
        line.mark(*line.last, *other["sums"].pieces())
    for c in range(chunks):
        one = ones[c]
        mid, second, stat = middle_norm(
            line.tie(one["own"]), totals[c].pieces(), one["sums"].pieces(), uw_total, out_bias, ffn_gain, ffn_shift
        )
        line.mark(stat)
        if c == 0:
            for total in totals[1:]:
                total.advance()
                total.gather()
        active, slope, sums = hidden_front(c, line.tie(second), up_weight, up_bias, back, hid_gain)
        line.mark(sums)
        twos.append(dict(middle=mid, second=second, stat=stat, active=active, slope=slope, sums=all_pieces(sums, bits)))
        if c == 0:
            for total in totals[1:]:
                for step in range(1, bits):
                    total.gather()
            line.mark(*line.last, *twos[0]["sums"][1:])
        else:
            twos[0]["total"].advance()
            line.mark(*line.last, *twos[c]["sums"][1:])
        if c == chunks - 1 and c > 0:
            two = twos[c]
            two["low"] = hidden_low(line.tie(two["active"]), two["sums"], hid_gain, hid_shift)
            line.mark(two["low"])
        else:
            mid_of(c)
        if c > 0:
            line.mark(*line.last, *twos[0]["total"].got)
        if c == 0 and chunks > 1:
            twos[0]["total"] = Total(line, hidden_of(0), bits)
    lows = every(twos, "low")
    down_grad = full([(lows, cots)])
    down_part = lax.psum_scatter(down_grad, "dp", scatter_dimension=1, tiled=True)
    if chunks > 1:
        low = twos[-1]["low"]
        mid_of(chunks - 1)
        twos[-1]["low"] = low
    up_products = [(every(twos, "second"), every(twos, "grad"))]
    sent = ring_grads(other_ids, tied(up_products))[0]
    line.mark(sent)
    sent = lax.ppermute(sent, "dp", [(d, d ^ 1) for d in range(dp_size)])
    if chunks > 1:
        for step in range(1, bits):
            twos[0]["total"].advance()
        twos[0]["total"].gather()
        parts = [None] + [hidden_of(c) for c in range(1, chunks)]
    else:
        twos[0]["total"] = Total(line, hidden_of(0), bits)
        for step in range(bits):
            twos[0]["total"].advance()
        twos[0]["total"].gather()
    ring_first, ring_rest = ring_grads(mine_ids, tied(up_products), sent)
    line.mark(ring_rest)
    ring = Ring(line, ring_first, ring_rest, dp_size)
    for step in range(1, bits):
        twos[0]["total"].gather()
    for c in range(1, chunks):
        twos[c]["total"] = Total(line, [line.tie(part) for part in parts[c]], bits)
    totals = every(twos, "total")
    result = result_part(jnp.concatenate(orders), [line.tie(lows[0])] + lows[1:], down_weight)
    line.mark(result)

    for c in range(chunks):
        one, two = ones[c], twos[c]
        grad, low, stat2, vecs = middle_back(
            line.tie(one["own"]), cots[c], two["total"].pieces(), two["middle"], two["stat"], uw_total, out_bias, ffn_gain
        )
        line.mark(stat2)
        if c == 0:
            for total in totals[1:]:
                total.advance()
        found = attention_back(
            orders[c], lengths, line.tie(low), stat2, one["mixed"], one["qkv"], one["own"], mix_gain, mix_shift, out_weight,
            qkv_weight, tables, mask,
        )
        line.mark(found[2])
        three = dict(grad=grad, low=low, vecs=tree_sum(vecs), mix_low=found[0], dproj=found[1])
        three["narrow"] = tree_sum(found[2])
        three["wide"] = tree_sum(found[3])
        parts = found[4:]
        if c == 0 and chunks > 1:
            for total in totals[1:]:
                for step in range(1, bits):
                    total.advance()
                for step in range(bits):
                    total.gather()
            for total in totals[1:]:
                line.mark(*line.last, *total.got)
            up_part = ring.advance()
            result = lax.psum(line.tie(result), "tensor")
            parts = [line.tie(part) for part in parts]
        three["total"] = Total(line, parts, bits)
        threes.append(three)

    first, last = threes[0]["total"], threes[-1]["total"]
    add = lambda items, name, size: functools.reduce(jnp.add, [item[name] for item in items])[:size]
    pad = lambda v: jnp.pad(v, ((0, 0), (0, D - v.shape[1])))
    wide = add(threes, "wide", 2)
    got = flip(wide, 0, blocks)
    if chunks > 1:
        line.mark(*line.last, *first.got)
    attention_grad = full(
        [(every(ones, "first"), every(threes, "dproj")), (every(threes, "low"), every(threes, "mix_low"))]
    )
    if chunks == 1:
        up_part = ring.advance()
        result = lax.psum(line.tie(result), "tensor")
    attention_part = lax.psum_scatter(attention_grad, "dp", scatter_dimension=0, tiled=True)
    for step in range(bits):
        first.advance()
    first.gather()
    if chunks > 1:
        last.advance()
    for step in range(1, bits):
        first.gather()
    line.mark(*line.last, down_part)
    up_part = ring.advance()
    if chunks > 1:
        for step in range(1, bits):
            last.advance()
        last.gather()
    for bit in range(1, bits):
        wide = line.tie(wide) + got
        got = flip(wide, bit, blocks)
        line.mark(wide)
    if chunks > 1:
        line.mark(*line.last, *last.got)
    hop = lambda v, bit: lax.ppermute(v, "dp", [(d, d ^ (1 << bit)) for d in range(dp_size)])
    dp_bits = dp_size.bit_length() - 1
    tokens_grad, output = None, None
    for c in range(chunks):
        tokens_grad = tokens_back(
            orders[c], line.tie(ones[c]["own"]), threes[c]["grad"], threes[c]["total"].pieces(), pre_gain, tokens_grad, pairs
        )
        line.mark(tokens_grad)
        if c == 0:
            wide = line.tie(wide) + got
            vecs = jnp.concatenate(
                [pad(add(twos, "vecs", 3)), add(threes, "vecs", 4), pad(add(threes, "narrow", 3)), wide], 0
            )
            line.mark(vecs)
            got = hop(vecs, 0)
            for step in range(2, count - 1):
                up_part = ring.advance()
            if chunks > 1:
                for step in range(1, bits):
                    last.gather()
            vecs = line.tie(vecs) + got
            line.mark(vecs)
            got = hop(vecs, 1)
    for bit in range(2, dp_bits):
        vecs = line.tie(vecs) + got
        line.mark(vecs)
        got = hop(vecs, bit)
    for c in range(chunks):
        output = output_of(orders[c], line.tie(twos[c]["middle"]), result, down_bias, output)
        line.mark(output)
    vecs = vecs + got
    hid_vecs, mid_vecs, narrow, wide = vecs[:3], vecs[3:7], vecs[7:10], vecs[10:12]
    qkv_part, out_part = attention_outputs(attention_part, width)
    units = hid_gain.shape[1]
    return (
        output.reshape(-1, D),
        tokens_grad.reshape(-1, D),
        wide[0],
        wide[1],
        qkv_part,
        narrow[2, : 3 * width].reshape(3, width),
        narrow[0, :width],
        narrow[1, :width],
        out_part,
        mid_vecs[2],
        mid_vecs[0],
        mid_vecs[1],
        up_part,
        hid_vecs[2, :units],
        hid_vecs[0, :units],
        hid_vecs[1, :units],
        down_part,
        mid_vecs[3],
    )


def solution(mesh):
    in_specs = (
        P("dp", None),
        P("dp"),
        P("dp", None),
        P(),
        P(),
        P(None, None, "tensor"),
        P(None, "tensor"),
        P("tensor"),
        P("tensor"),
        P("tensor", None),
        P(),
        P(),
        P(),
        P(None, "tensor"),
        P("tensor"),
        P("tensor"),
        P("tensor"),
        P("tensor", None),
        P(),
    )
    out_specs = (
        P("dp", None),
        P("dp", None),
        P(),
        P(),
        P(None, "dp", "tensor"),
        P(None, "tensor"),
        P("tensor"),
        P("tensor"),
        P("tensor", "dp"),
        P(),
        P(),
        P(),
        P("dp", "tensor"),
        P("tensor"),
        P("tensor"),
        P("tensor"),
        P("tensor", "dp"),
        P(),
    )
    return jax.shard_map(body, mesh=mesh, in_specs=in_specs, out_specs=out_specs, check_vma=False)
```
